32 devices in a mesh: fsdp: 16 (over z, y, x), dp: 2 (over core).
Axes of the slice: x: 2, y: 2, z: 4, core: 2. Of those that a mesh axis runs over, the one named last changes fastest.
Arguments:
- clips_wide: bfloat16 [32, 102, 768], P(('fsdp', 'dp')), may hold values from -6 to 6
- clips_narrow: bfloat16 [64, 51, 768], P(('fsdp', 'dp')), may hold values from -6 to 6
- visible_wide: int32 [32, 102], P(('fsdp', 'dp')), may hold values from 0 to 511, as said below
- visible_narrow: int32 [64, 51], P(('fsdp', 'dp')), may hold values from 0 to 255, as said below
- shift_wide: int32 [32, 2], P(('fsdp', 'dp')), may hold values from 0 to 3
- shift_narrow: int32 [64], P(('fsdp', 'dp')), may hold values from 0 to 3
- enc_norm1: bfloat16 [768], P('fsdp'), may hold values from 0.5 to 1.5
- enc_qkv: bfloat16 [768, 2304], P('fsdp'), may hold values from -0.21875 to 0.21875
- enc_out: bfloat16 [768, 768], P('fsdp'), may hold values from -0.625 to 0.625
- enc_norm2: bfloat16 [768], P('fsdp'), may hold values from 0.5 to 1.5
- enc_up: bfloat16 [768, 3072], P('fsdp'), may hold values from -0.21875 to 0.21875
- enc_down: bfloat16 [3072, 768], P('fsdp'), may hold values from -0.109375 to 0.109375
- embed_proj: bfloat16 [768, 512], P('fsdp'), may hold values from -0.21875 to 0.21875
- mask_token: bfloat16 [512], P('fsdp'), may hold values from -4 to 4
- dec_norm1: bfloat16 [512], P('fsdp'), may hold values from 0.5 to 1.5
- dec_qkv: bfloat16 [512, 1536], P('fsdp'), may hold values from -0.25 to 0.25
- dec_out: bfloat16 [512, 512], P('fsdp'), may hold values from -0.5 to 0.5
- dec_norm2: bfloat16 [512], P('fsdp'), may hold values from 0.5 to 1.5
- dec_up: bfloat16 [512, 2048], P('fsdp'), may hold values from -0.25 to 0.25
- dec_down: bfloat16 [2048, 512], P('fsdp'), may hold values from -0.125 to 0.125
- cotan_wide: bfloat16 [32, 512, 512], P(('fsdp', 'dp')), may hold values from -6 to 6
- cotan_narrow: bfloat16 [64, 256, 512], P(('fsdp', 'dp')), may hold values from -6 to 6
Outputs:
- encoded_wide: bfloat16 [32, 102, 768], P(('fsdp', 'dp'))
- encoded_narrow: bfloat16 [64, 51, 768], P(('fsdp', 'dp'))
- decoded_wide: bfloat16 [32, 512, 512], P(('fsdp', 'dp'))
- decoded_narrow: bfloat16 [64, 256, 512], P(('fsdp', 'dp'))
- grad_wide: float32 [32, 102, 768], P(('fsdp', 'dp'))
- grad_narrow: float32 [64, 51, 768], P(('fsdp', 'dp'))
- grad_enc_norm1: float32 [768], P('fsdp')
- grad_enc_qkv: float32 [768, 2304], P('fsdp')
- grad_enc_out: float32 [768, 768], P('fsdp')
- grad_enc_norm2: float32 [768], P('fsdp')
- grad_enc_up: float32 [768, 3072], P('fsdp')
- grad_enc_down: float32 [3072, 768], P('fsdp')
- grad_embed_proj: float32 [768, 512], P('fsdp')
- grad_mask_token: float32 [512], P('fsdp')
- grad_dec_norm1: float32 [512], P('fsdp')
- grad_dec_qkv: float32 [512, 1536], P('fsdp')
- grad_dec_out: float32 [512, 512], P('fsdp')
- grad_dec_norm2: float32 [512], P('fsdp')
- grad_dec_up: float32 [512, 2048], P('fsdp')
- grad_dec_down: float32 [2048, 512], P('fsdp')
The draws below stay inside these ranges and needn't reach their ends.
Inputs may be any that keep to these rules, and one draw needn't show every extreme that they name: `visible_wide`: each clip's 102 patch numbers are distinct and increasing. `visible_narrow`: each clip's 51 patch numbers are distinct and increasing.
All inputs are finite; a program needn't handle non-finite values.
Results may differ from the reference program's by a relative error of at most 0.024.
Values may be sent and summed in bfloat16 or wider, within the bound.
A program may use at most 192 MiB of HBM per device.

```python
from functools import partial
import jax
import jax.numpy as jnp
from jax import lax

D = 768
HEADS = 12
FF = 3072
DD = 512
DHEADS = 16
DFF = 2048
TIME = 64
COLS_WIDE = 8
COLS_NARROW = 4
WIN = 4
VIS_WIDE = 102
VIS_NARROW = 51
PATCH_WIDE = 512
PATCH_NARROW = 256
CLIPS_WIDE = 32
CLIPS_NARROW = 64


def choose_visible(key, clip_total, patches, keep):
    keys = jax.random.split(key, clip_total)

    def one_clip(clip_key):
        return jax.random.permutation(clip_key, patches)[:keep]
    picks = jax.vmap(one_clip)(keys)
    return jnp.sort(picks, axis=-1).astype(jnp.int32)


def draw_visible_wide(key, part):
    key = jax.random.fold_in(key, 11)
    return choose_visible(key, CLIPS_WIDE, PATCH_WIDE, VIS_WIDE)


def draw_visible_narrow(key, part):
    key = jax.random.fold_in(key, 23)
    return choose_visible(key, CLIPS_NARROW, PATCH_NARROW, VIS_NARROW)


def plant(result, own_key, smallest, largest):
    extent = result.shape
    index_at = [jax.random.randint(jax.random.fold_in(own_key, axis), (), 0, extent[axis]) for axis in range(len(extent))]
    result = result.at[tuple(index_at)].set(smallest)
    longest = extent.index(max(extent))
    index_at[longest] = (index_at[longest] + 1) % extent[longest]
    return result.at[tuple(index_at)].set(largest)


def block_levels(stream_key, dims, pieces, low, top_value):
    def one(position, blocks):
        heights = jax.random.uniform(jax.random.fold_in(jax.random.fold_in(stream_key, 6), position), (blocks,), jnp.float32, low / len(pieces), top_value / len(pieces))
        return jnp.repeat(jnp.exp(heights), dims[position] // blocks).reshape((-1,) + (1,) * (len(dims) - position - 1))

    level = one(*pieces[0])
    for cut in pieces[1:]:
        level = level * one(*cut)
    return level


def noise(stream_key, dims, deviation, limit, pieces=(), held_as=jnp.bfloat16):
    result = jax.random.normal(stream_key, dims, jnp.float32) * deviation
    if len(pieces) > 0:
        result = block_levels(stream_key, dims, pieces, -0.22, 0.18) * result
    return jnp.clip(result, min=-limit, max=limit).astype(held_as)


def setup_inputs(seed: int = 0) -> dict:
    key_of = jax.random.split(jax.random.key(seed), 23)
    return {
        "clips_wide": noise(key_of[0], (CLIPS_WIDE, VIS_WIDE, D), 1.0, 6.0, ((0, 32),)),
        "clips_narrow": noise(key_of[1], (CLIPS_NARROW, VIS_NARROW, D), 1.0, 6.0, ((0, 32),)),
        "visible_wide": draw_visible_wide(jax.random.fold_in(key_of[22], 71), 0),
        "visible_narrow": draw_visible_narrow(jax.random.fold_in(key_of[22], 71), 0),
        "shift_wide": plant(jax.random.randint(key_of[4], (CLIPS_WIDE, 2), 0, WIN), jax.random.fold_in(key_of[4], 1), 0, WIN - 1).astype(jnp.int32),
        "shift_narrow": plant(jax.random.randint(key_of[5], (CLIPS_NARROW,), 0, WIN), jax.random.fold_in(key_of[5], 1), 0, WIN - 1).astype(jnp.int32),
        "enc_norm1": jnp.clip(1.0 + 0.1 * jax.random.normal(key_of[6], (D,), jnp.float32), 0.5, 1.5).astype(jnp.bfloat16),
        "enc_qkv": noise(key_of[7], (D, 3 * D), D ** -0.5, 0.21875, ((0, 16),)),
        "enc_out": noise(key_of[8], (D, D), (D // 8) ** -0.5, 0.625, ((0, 16),)),
        "enc_norm2": jnp.clip(1.0 + 0.1 * jax.random.normal(key_of[9], (D,), jnp.float32), 0.5, 1.5).astype(jnp.bfloat16),
        "enc_up": noise(key_of[10], (D, FF), D ** -0.5, 0.21875, ((0, 16),)),
        "enc_down": noise(key_of[11], (FF, D), FF ** -0.5, 0.109375, ((0, 16),)),
        "embed_proj": noise(key_of[12], (D, DD), D ** -0.5, 0.21875, ((0, 16),)),
        "mask_token": noise(key_of[13], (DD,), 1.0, 4.0, ((0, 16),)),
        "dec_norm1": jnp.clip(1.0 + 0.1 * jax.random.normal(key_of[14], (DD,), jnp.float32), 0.5, 1.5).astype(jnp.bfloat16),
        "dec_qkv": noise(key_of[15], (DD, 3 * DD), DD ** -0.5, 0.25, ((0, 16),)),
        "dec_out": noise(key_of[16], (DD, DD), (DD // 4) ** -0.5, 0.5, ((0, 16),)),
        "dec_norm2": jnp.clip(1.0 + 0.1 * jax.random.normal(key_of[17], (DD,), jnp.float32), 0.5, 1.5).astype(jnp.bfloat16),
        "dec_up": noise(key_of[18], (DD, DFF), DD ** -0.5, 0.25, ((0, 16),)),
        "dec_down": noise(key_of[19], (DFF, DD), DFF ** -0.5, 0.125, ((0, 16),)),
        "cotan_wide": noise(key_of[20], (CLIPS_WIDE, PATCH_WIDE, DD), 1.0, 6.0, ((0, 32),)),
        "cotan_narrow": noise(key_of[21], (CLIPS_NARROW, PATCH_NARROW, DD), 1.0, 6.0, ((0, 32),)),
    }


@jax.custom_vjp
def low(v):
    return lax.optimization_barrier(v.astype(jnp.bfloat16)).astype(jnp.float32)

@jax.custom_vjp
def low_back(v):
    return v

def low_keep(v):
    return (low(v), None)

def low_pass(kept, grad):
    return (grad,)

def back_keep(v):
    return (v, None)

def back_low(kept, grad):
    return (low(grad),)
low.defvjp(low_keep, low_pass)
low_back.defvjp(back_keep, back_low)
EPS = 1e-06
PRECISE = lax.Precision.HIGHEST

def layer_norm(inputs, scales):
    center = lax.optimization_barrier(jnp.mean(inputs, axis=-1, keepdims=True))
    shifted = inputs - center
    spread = lax.optimization_barrier(jnp.mean(shifted * shifted, axis=-1, keepdims=True))
    return shifted * lax.rsqrt(spread + EPS) * scales

def product(former, latter):
    return jnp.einsum('...i,ij->...j', former, latter, precision=PRECISE)

def unchanged(portion):
    return portion

def to_windows(canvas, shifts, columns):
    clip_count = canvas.shape[0]
    features = canvas.shape[-1]
    canvas = canvas.reshape(clip_count, TIME, columns, features)

    def roll_one(portion, offsets):
        portion = jnp.roll(portion, -offsets[0], axis=0)
        return jnp.roll(portion, -offsets[1], axis=1)
    canvas = jax.vmap(roll_one)(canvas, shifts)
    canvas = canvas.reshape(clip_count, TIME // WIN, WIN, columns // WIN, WIN, features)
    canvas = canvas.transpose(0, 1, 3, 2, 4, 5)
    return canvas.reshape(-1, WIN * WIN, features)

def from_windows(windows, shifts, columns):
    features = windows.shape[-1]
    clip_count = windows.shape[0] // (TIME // WIN * (columns // WIN))
    canvas = windows.reshape(clip_count, TIME // WIN, columns // WIN, WIN, WIN, features)
    canvas = canvas.transpose(0, 1, 3, 2, 4, 5).reshape(clip_count, TIME, columns, features)

    def roll_one(portion, offsets):
        portion = jnp.roll(portion, offsets[0], axis=0)
        return jnp.roll(portion, offsets[1], axis=1)
    canvas = jax.vmap(roll_one)(canvas, shifts)
    return canvas.reshape(clip_count, TIME * columns, features)

def attend(queries, key_rows, values, num_heads):
    batches, length, features = queries.shape
    head_size = features // num_heads
    head_shape = (batches, length, num_heads, head_size)
    scores = jnp.einsum('bqhd,bkhd->bhqk', queries.reshape(head_shape), key_rows.reshape(head_shape), precision=PRECISE)
    scores = low_back(scores * head_size ** (-0.5))
    shares = jax.nn.softmax(scores, axis=-1)
    blended = jnp.einsum('bhqk,bkhd->bqhd', low(shares), values.reshape(head_shape), precision=PRECISE)
    return blended.reshape(batches, length, features)

def block(inputs, weights, num_heads, arrange, restore):
    scale_one, w_qkv, w_out, scale_two, w_up, w_down = weights
    features = inputs.shape[-1]
    normed = low(layer_norm(inputs, scale_one))
    projected = low_back(low(product(normed, w_qkv)))
    arranged = arrange(projected)
    blended = attend(arranged[..., :features], arranged[..., features:2 * features], arranged[..., 2 * features:], num_heads)
    blended = low_back(low(restore(blended)))
    middle = inputs + low_back(product(blended, w_out))
    normed_two = low(layer_norm(middle, scale_two))
    raised = low_back(product(normed_two, w_up))
    active = low(jax.nn.gelu(raised, approximate=False))
    return middle + low_back(product(active, w_down))

def forward(params, inputs, visible, shifts, columns):
    encoded = block(inputs, params[:6], HEADS, unchanged, unchanged)
    embedded = low_back(product(low(encoded), params[6]))
    filler = params[7]
    clip_count = inputs.shape[0]
    canvas = jnp.broadcast_to(filler, (clip_count, TIME * columns, filler.shape[0]))
    clip_index = jnp.arange(clip_count, dtype=jnp.int32)[:, None]
    canvas = canvas.at[clip_index, visible].set(embedded)
    arrange = partial(to_windows, shifts=shifts, columns=columns)
    restore = partial(from_windows, shifts=shifts, columns=columns)
    decoded = block(canvas, params[8:], DHEADS, arrange, restore)
    return (encoded, decoded)

def run_kind(params, inputs, visible, shifts, cotangent, columns, group):

    def one_group(totals, portion):
        group_inputs, group_visible, group_shifts, group_cotangent = portion

        def apply(weights, clip_rows):
            return forward(weights, clip_rows, group_visible, group_shifts, columns)
        outputs, pull = jax.vjp(apply, params, group_inputs)
        grad_params, grad_inputs = pull((jnp.zeros_like(outputs[0]), group_cotangent))
        totals = jax.tree.map(jnp.add, totals, grad_params)
        return (totals, (outputs[0].astype(jnp.bfloat16), outputs[1].astype(jnp.bfloat16), grad_inputs))

    def grouped(array):
        return array.reshape((-1, group) + array.shape[1:])

    def ungrouped(array):
        return array.reshape((-1,) + array.shape[2:])
    zeros = jax.tree.map(jnp.zeros_like, params)
    totals, stacked = lax.scan(one_group, zeros, (grouped(inputs), grouped(visible), grouped(shifts), grouped(cotangent)))
    return (totals, (ungrouped(stacked[0]), ungrouped(stacked[1]), ungrouped(stacked[2])))

def reference(clips_wide, clips_narrow, visible_wide, visible_narrow, shift_wide, shift_narrow, enc_norm1, enc_qkv, enc_out, enc_norm2, enc_up, enc_down, embed_proj, mask_token, dec_norm1, dec_qkv, dec_out, dec_norm2, dec_up, dec_down, cotan_wide, cotan_narrow):
    params = tuple((weight_arg.astype(jnp.float32) for weight_arg in (enc_norm1, enc_qkv, enc_out, enc_norm2, enc_up, enc_down, embed_proj, mask_token, dec_norm1, dec_qkv, dec_out, dec_norm2, dec_up, dec_down)))
    narrow_shifts = jnp.stack([shift_narrow, jnp.zeros_like(shift_narrow)], axis=1)
    totals_wide, outs_wide = run_kind(params, clips_wide.astype(jnp.float32), visible_wide, shift_wide, cotan_wide.astype(jnp.float32), COLS_WIDE, 8)
    totals_narrow, outs_narrow = run_kind(params, clips_narrow.astype(jnp.float32), visible_narrow, narrow_shifts, cotan_narrow.astype(jnp.float32), COLS_NARROW, 16)
    grads = [first + second for first, second in zip(totals_wide, totals_narrow)]
    return (outs_wide[0], outs_narrow[0], outs_wide[1], outs_narrow[1], outs_wide[2], outs_narrow[2], grads[0], grads[1], grads[2], grads[3], grads[4], grads[5], grads[6], grads[7], grads[8], grads[9], grads[10], grads[11], grads[12], grads[13])
```

```python
import functools

import jax
import jax.numpy as jnp
from jax import lax
from jax.experimental import pallas as pl
from jax.experimental.pallas import tpu as pltpu
from jax.sharding import PartitionSpec as P

HEADS = 12
DHEADS = 16
TIME = 64
WIN = 4


EPS = 1e-06


MESH = pl.DeviceIdType.MESH


def slots():
    out=[]
    for bx in (0,1):
        for by in (0,1):
            for sgn in (0,1,-1):
                if (bx,by,sgn)!=(0,0,0): out.append((bx,by,sgn))
    return out

def forwards(order,bx,by,sgn):
    differs={'x':bx,'y':by,'z':int(sgn!=0)}
    last=max([j for j,d in enumerate(order) if differs[d]],default=-1)
    dirs=[]
    for j,d in enumerate(order):
        if j>last:
            dirs += ['u','d'] if d=='z' else [d]
    if last>=0 and order[last]=='z':
        dirs.append('u' if sgn<0 else 'd')
    return dirs

def ag_kernel(nz, pieces, nw, *refs):
    ins=refs[:nw]; outs=refs[nw:2*nw]
    send, recv, sib_send, sib_recv, loc = refs[2*nw:]
    f=lax.axis_index("fsdp"); c=lax.axis_index("dp")
    z=f//4; y=(f//2)%2; x=f%2
    xn=(f+1-2*x, c); yn=(f+2-4*y, c); up=(f+4,c); dn=(f-4,c); sib=(f,1-c)
    bar=pltpu.get_barrier_semaphore()
    def sig(dev): pl.semaphore_signal(bar,inc=1,device_id=dev,device_id_type=MESH)
    sig(xn); sig(yn); sig(sib)
    @pl.when(z<nz-1)
    def _(): sig(up)
    @pl.when(z>0)
    def _(): sig(dn)
    pl.semaphore_wait(bar, 3+(z<nz-1).astype(jnp.int32)+(z>0).astype(jnp.int32))
    dest={'x':xn,'y':yn,'u':up,'d':dn}
    ok={'x':None,'y':None,'u':z<nz-1,'d':z>0}
    code={'x':0,'y':1,'u':2,'d':3}
    def rows(w): return ins[w].shape[0]
    def region(i, s, half):
        w,c0,cols,order,share=pieces[i]
        r=rows(w)
        n=ins[w].shape[1]
        col=c0 if not share else pl.multiple_of(half*(n//2)+c0,128)
        return outs[w].at[pl.ds(pl.multiple_of(s*r,r),r), pl.ds(col,cols)]
    def own(i):
        w,c0,cols,order,share=pieces[i]
        n=ins[w].shape[1]
        col=c0 if not share else pl.multiple_of(c*(n//2)+c0,128)
        return ins[w].at[:, pl.ds(col,cols)]
    def remote(i,s,src,d):
        return pltpu.make_async_remote_copy(src_ref=src,dst_ref=region(i,s,c),send_sem=send.at[i,s,code[d]],recv_sem=recv.at[i,s],device_id=dest[d],device_id_type=MESH)
    def sibling(i,s):
        return pltpu.make_async_remote_copy(src_ref=region(i,s,c),dst_ref=region(i,s,c),send_sem=sib_send.at[i,s],recv_sem=sib_recv.at[i,s],device_id=sib,device_id_type=MESH)
    def go(i,s,src,dirs):
        for d in dirs:
            if ok[d] is None: remote(i,s,src,d).start()
            else:
                pl.when(ok[d])(lambda d=d: remote(i,s,src,d).start())
    def wait_sends(i,s,src,dirs):
        for d in dirs:
            if ok[d] is None: remote(i,s,src,d).wait_send()
            else:
                pl.when(ok[d])(lambda d=d: remote(i,s,src,d).wait_send())
    locals_=[]
    for i in range(len(pieces)):
        go(i,f,own(i),forwards(pieces[i][3],0,0,0))
    for w in range(nw):
        r=rows(w)
        cp=pltpu.make_async_copy(ins[w],outs[w].at[pl.ds(pl.multiple_of(f*r,r),r)],loc.at[w]); cp.start(); locals_.append(cp)
    def each(h, i, action):
        for bx,by,sgn in slots():
            k=h-bx-by
            zs=z+sgn*k
            if sgn==0: valid=k==0
            else: valid=(k>=1)&(zs>=0)&(zs<nz)
            s=zs*4+(y+by-2*by*y)*2+(x+bx-2*bx*x)
            pl.when(valid)(lambda s=s,bx=bx,by=by,sgn=sgn: action(i,s,forwards(pieces[i][3],bx,by,sgn)))
    def step(i,s,dirs):
        remote(i,s,region(i,s,c),'x').wait_recv()
        go(i,s,region(i,s,c),dirs)
        if pieces[i][4]: sibling(i,s).start()
    def fin(i,s,dirs):
        wait_sends(i,s,region(i,s,c),dirs)
        if pieces[i][4]:
            sibling(i,s).wait_send()
            pltpu.make_async_remote_copy(src_ref=region(i,s,1-c),dst_ref=region(i,s,1-c),send_sem=sib_send.at[i,s],recv_sem=sib_recv.at[i,s],device_id=sib,device_id_type=MESH).wait_recv()
    @pl.loop(1,nz+2)
    def _(h):
        for i in range(len(pieces)):
            each(h,i,step)
    for i in range(len(pieces)):
        wait_sends(i,f,own(i),forwards(pieces[i][3],0,0,0))
    for cp in locals_: cp.wait()
    @pl.loop(1,nz+2)
    def _(h):
        for i in range(len(pieces)):
            each(h,i,fin)

def all_gather(shards, pieces, nz, cid=1):
    nw=len(shards); npc=len(pieces); n=nz*4
    return pl.pallas_call(functools.partial(ag_kernel,nz,pieces,nw),
        out_shape=[jax.ShapeDtypeStruct((s.shape[0]*n,s.shape[1]),s.dtype) for s in shards],
        in_specs=[pl.BlockSpec(memory_space=pl.ANY)]*nw,
        out_specs=[pl.BlockSpec(memory_space=pl.ANY)]*nw,
        scratch_shapes=[pltpu.SemaphoreType.DMA((npc,n,4)),pltpu.SemaphoreType.DMA((npc,n)),pltpu.SemaphoreType.DMA((npc,n)),pltpu.SemaphoreType.DMA((npc,n)),pltpu.SemaphoreType.DMA((nw,))],
        compiler_params=pltpu.CompilerParams(collective_id=cid,has_side_effects=True),
        name="gather_weights")(*shards)

def slot_count(order, d, nz):
    size={'x':2,'y':2,'z':nz}
    j=order.index('z' if d in 'ud' else d)
    k=1
    for e in order[:j]: k*=size[e]
    return k*(nz+1) if d in 'ud' else k

def slot_index(order, d, nz, pos):
    size={'x':2,'y':2,'z':nz}
    j=order.index('z' if d in 'ud' else d)
    k=0
    for e in order[:j]: k=k*size[e]+pos[e]
    if d in 'ud': k=k*(nz+1)+pos['z']+(1 if d=='d' else 0)
    return k

LEAD = 0
def rs_kernel(nz, pieces, nw, *refs):
    ins=refs[:nw]; vec=refs[nw]; outs=refs[nw+1:2*nw+1]; vout=refs[2*nw+1]
    rest=list(refs[2*nw+2:])
    npc=len(pieces)
    own=[rest.pop(0) for _ in range(npc)]
    sibb=[rest.pop(0) for _ in range(npc)]
    rbuf=[[rest.pop(0) for _ in range(3)] for _ in range(npc)]
    res=[rest.pop(0) for _ in range(npc)]
    vbuf, own_sem, sib_send, sib_recv, send, recv, res_sem, res_send, res_recv, vsend, vrecv = rest
    f=lax.axis_index("fsdp"); c=lax.axis_index("dp")
    z=f//4; y=(f//2)%2; x=f%2
    bits=(nz*4).bit_length()-1
    def flip(b): return f+(1<<b)*(1-2*((f//(1<<b))%2))
    xn=(flip(0), c); yn=(flip(1), c); up=(f+4,c); dn=(f-4,c); sib=(f,1-c)
    bar=pltpu.get_barrier_semaphore()
    def sig(dev): pl.semaphore_signal(bar,inc=1,device_id=dev,device_id_type=MESH)
    sig(xn); sig(yn); sig(sib)
    @pl.when(z<nz-1)
    def _(): sig(up)
    @pl.when(z>0)
    def _(): sig(dn)
    extra=[b for b in range(3,bits)]
    for b in extra: sig((flip(b),c))
    pl.semaphore_wait(bar, 3+len(extra)+(z<nz-1).astype(jnp.int32)+(z>0).astype(jnp.int32))
    dest={'x':xn,'y':yn,'u':up,'d':dn}
    there={'u':z<nz-1,'d':z>0}
    opposite={'u':'d','d':'u','x':'x','y':'y'}
    bufof={'x':0,'y':1,'u':2,'d':2}
    def rws(i): return ins[pieces[i][0]].shape[0]//(nz*4)
    def half(i,h):
        w,c0,cols,order=pieces[i]
        n=ins[w].shape[1]
        return pl.ds(pl.multiple_of(h*(n//2)+c0,128),cols)
    def own_copy(i): return pltpu.make_async_copy(ins[pieces[i][0]].at[:,half(i,c)],own[i],own_sem.at[i])
    def sib_copy(i): return pltpu.make_async_remote_copy(src_ref=ins[pieces[i][0]].at[:,half(i,1-c)],dst_ref=sibb[i],send_sem=sib_send.at[i],recv_sem=sib_recv.at[i],device_id=sib,device_id_type=MESH)
    def vcopy(k):
        dev = sib if k==0 else (flip(k-1),c)
        return pltpu.make_async_remote_copy(src_ref=vbuf.at[0,k],dst_ref=vbuf.at[1,k],send_sem=vsend.at[k],recv_sem=vrecv.at[k],device_id=dev,device_id_type=MESH)
    for i in range(npc):
        sib_copy(i).start(); own_copy(i).start()
    vbuf[0,0]=vec[...]
    vcopy(0).start()
    def blk(i,s): r=rws(i); return pl.ds(pl.multiple_of(s*r,r),r)
    def message(i,s,pos,d):
        order=pieces[i][3]
        b=bufof[d]
        return pltpu.make_async_remote_copy(src_ref=own[i].at[blk(i,s)],dst_ref=rbuf[i][b].at[slot_index(order,opposite[d],nz,pos)],send_sem=send.at[i,s],recv_sem=recv.at[i,b,slot_index(order,opposite[d],nz,pos)],device_id=dest[d],device_id_type=MESH)
    def arrival(i,pos,d):
        order=pieces[i][3]; b=bufof[d]; k=slot_index(order,d,nz,pos)
        return pltpu.make_async_remote_copy(src_ref=rbuf[i][b].at[k],dst_ref=rbuf[i][b].at[k],send_sem=send.at[i,0],recv_sem=recv.at[i,b,k],device_id=sib,device_id_type=MESH)
    def add(i,s,pos,children,final):
        order=pieces[i][3]; r=rws(i)
        ks=[(bufof[d],slot_index(order,d,nz,pos)) for d in children]
        @pl.loop(0,r//16)
        def _(k):
            rr=pl.ds(pl.multiple_of(k*16,16),16)
            gr=pl.ds(pl.multiple_of(s*r+k*16,16),16)
            t=own[i][gr].astype(jnp.float32)+sibb[i][gr].astype(jnp.float32)
            for b,q in ks: t=t+rbuf[i][b][q,rr].astype(jnp.float32)
            if final: res[i][rr]=t
            else: own[i][gr]=t.astype(jnp.bfloat16)
    def parent(order,bx,by,sgn):
        differs={'x':bx,'y':by,'z':int(sgn!=0)}
        last=max(j for j,d in enumerate(order) if differs[d])
        if order[last]=='z': return 'd' if sgn<0 else 'u'
        return order[last]
    def with_children(i,s,pos,children,final):
        sure=[d for d in children if d in 'xy']; maybe=[d for d in children if d in 'ud']
        for d in sure: arrival(i,pos,d).wait_recv()
        for d in maybe: pl.when(there[d])(lambda d=d: arrival(i,pos,d).wait_recv())
        if not maybe: add(i,s,pos,sure,final)
        elif len(maybe)==1:
            pl.when(there[maybe[0]])(lambda: add(i,s,pos,sure+maybe,final))
            pl.when(jnp.logical_not(there[maybe[0]]))(lambda: add(i,s,pos,sure,final))
        else:
            u,d=there['u'],there['d']
            pl.when(u&d)(lambda: add(i,s,pos,sure+['u','d'],final))
            pl.when(u&jnp.logical_not(d))(lambda: add(i,s,pos,sure+['u'],final))
            pl.when(jnp.logical_not(u)&d)(lambda: add(i,s,pos,sure+['d'],final))
            if nz==1: add(i,s,pos,sure,final)
    def each(h,i,leaf,action):
        order=pieces[i][3]
        for bx,by,sgn in slots():
            ch=forwards(order,bx,by,sgn)
            if leaf is not None and (len(ch)==0)!=leaf: continue
            k=h-bx-by
            zs=z+sgn*k
            if sgn==0: valid=k==0
            else: valid=(k>=1)&(zs>=0)&(zs<nz)
            pos={'x':x+bx-2*bx*x,'y':y+by-2*by*y,'z':zs}
            s=zs*4+pos['y']*2+pos['x']
            pl.when(valid)(lambda s=s,pos=pos,ch=ch,p=parent(order,bx,by,sgn): action(i,s,pos,ch,p))
    def work(i,s,pos,ch,p):
        with_children(i,s,pos,ch,False)
        message(i,s,pos,p).start()
    def done(i,s,pos,ch,p):
        message(i,s,pos,p).wait_send()
    top=nz+1
    for i in range(npc):
        own_copy(i).wait(); sib_copy(i).wait_recv()
        for q in range(LEAD+1): each(jnp.int32(top-q),i,True,work)
    @pl.loop(0,top)
    def _(q):
        h=top-q
        for i in range(npc):
            each(h,i,False,work)
        for i in range(npc):
            each(h-LEAD-1,i,True,work)
        for k in range(bits+1):
            @pl.when(q==k)
            def _(k=k):
                vcopy(k).wait()
                vbuf[0,k+1]=vbuf[0,k]+vbuf[1,k]
                if k<bits: vcopy(k+1).start()
    for k in range(top,bits+1):
        vcopy(k).wait()
        vbuf[0,k+1]=vbuf[0,k]+vbuf[1,k]
        if k<bits: vcopy(k+1).start()
    def out_copy(i): return pltpu.make_async_copy(res[i],outs[pieces[i][0]].at[:,half(i,c)],res_sem.at[i])
    def out_sib(i,h): return pltpu.make_async_remote_copy(src_ref=res[i],dst_ref=outs[pieces[i][0]].at[:,half(i,h)],send_sem=res_send.at[i],recv_sem=res_recv.at[i],device_id=sib,device_id_type=MESH)
    for i in range(npc):
        with_children(i,f,{'x':x,'y':y,'z':z},forwards(pieces[i][3],0,0,0),True)
        out_sib(i,c).start(); out_copy(i).start()
    vout[...]=vbuf[0,bits+1]
    for i in range(npc): sib_copy(i).wait_send()
    @pl.loop(0,top)
    def _(q):
        for i in range(npc): each(top-q,i,None,done)
    for i in range(npc):
        out_copy(i).wait(); out_sib(i,c).wait_send(); out_sib(i,1-c).wait_recv()

def reduce_scatter(grads, vec, pieces, nz, cid=2):
    nw=len(grads); npc=len(pieces); n=nz*4; bits=n.bit_length()-1
    shards=[(g.shape[0]//n,g.shape[1]) for g in grads]
    sc=[]
    B=jnp.bfloat16
    for w,c0,cols,o in pieces: sc.append(pltpu.VMEM((shards[w][0]*n,cols),B))
    for w,c0,cols,o in pieces: sc.append(pltpu.VMEM((shards[w][0]*n,cols),B))
    most=1
    for w,c0,cols,o in pieces:
        ns=[slot_count(o,'x',nz),slot_count(o,'y',nz),slot_count(o,'u',nz)]
        most=max(most,*ns)
        for k in ns: sc.append(pltpu.VMEM((k,shards[w][0],cols),B))
    for w,c0,cols,o in pieces: sc.append(pltpu.VMEM((shards[w][0],cols),jnp.float32))
    D=pltpu.SemaphoreType.DMA
    sc += [pltpu.VMEM((2,bits+2)+vec.shape,jnp.float32),D((npc,)),D((npc,)),D((npc,)),D((npc,n)),D((npc,3,most)),D((npc,)),D((npc,)),D((npc,)),D((bits+1,)),D((bits+1,))]
    return pl.pallas_call(functools.partial(rs_kernel,nz,pieces,nw),
        out_shape=[jax.ShapeDtypeStruct(s,jnp.float32) for s in shards]+[jax.ShapeDtypeStruct(vec.shape,jnp.float32)],
        in_specs=[pl.BlockSpec(memory_space=pl.ANY)]*nw+[pl.BlockSpec(memory_space=pltpu.VMEM)],
        out_specs=[pl.BlockSpec(memory_space=pl.ANY)]*nw+[pl.BlockSpec(memory_space=pltpu.VMEM)],
        scratch_shapes=sc,
        compiler_params=pltpu.CompilerParams(collective_id=cid,has_side_effects=True,vmem_limit_bytes=58*2**20),
        name="reduce_gradients")(*grads,vec)

ZXY = ("z", "x", "y")
ZYX = ("z", "y", "x")
XYZ = ("x", "y", "z")
YXZ = ("y", "x", "z")
ROUTES = (
    (7, XYZ), (8, YXZ), (0, ZXY), (3, ZYX), (2, ZXY), (1, ZYX), (5, ZYX), (4, ZYX), (6, ZXY),
)


def gather_pieces(shards):
    pieces = [(w, 0, shards[w].shape[1] // 2, order, True) for w, order in ROUTES]
    return [(len(shards), 0, 128, ZXY, False)] + pieces


def reduce_pieces(shards):
    return [(w, 0, shards[w].shape[1] // 2, order) for w, order in ROUTES]


def whole_tiles(shards):
    return all(s.shape[0] % 16 == 0 and s.shape[1] % 256 == 0 for s in shards)


def gather_all(matrices, vectors, devices):
    if devices % 4 or not whole_tiles(matrices):
        def whole(part):
            return lax.all_gather(part, "fsdp", axis=0, tiled=True)
        return [whole(m) for m in matrices], [whole(v) for v in vectors]
    rows = [jnp.pad(v, (0, 128 - v.shape[0])) for v in vectors]
    packed = jnp.pad(jnp.stack(rows), ((0, 16 - len(rows)), (0, 0)))
    got = all_gather(list(matrices) + [packed], gather_pieces(matrices), devices // 4)
    tiles = got[-1].reshape(devices, 16, 128)
    return got[:-1], [tiles[:, k, : v.shape[0]].reshape(-1) for k, v in enumerate(vectors)]


def reduce_all(grads, vectors, devices):
    if devices % 4 or not whole_tiles([jax.ShapeDtypeStruct((g.shape[0] // devices, g.shape[1]), g.dtype) for g in grads]):
        def share(part):
            part = lax.psum(part.astype(jnp.float32), "dp")
            return lax.psum_scatter(part, "fsdp", scatter_dimension=0, tiled=True)
        return [share(g) for g in grads], [share(v) for v in vectors]
    width = max(v.shape[0] for v in vectors)
    packed = jnp.stack([jnp.pad(v, (0, width - v.shape[0])) for v in vectors])
    packed = jnp.pad(packed, ((0, 8 - len(vectors)), (0, 0)))
    got = reduce_scatter(grads, packed, reduce_pieces(grads), devices // 4)
    me = lax.axis_index("fsdp")
    shares = []
    for k, v in enumerate(vectors):
        n = v.shape[0] // devices
        shares.append(lax.dynamic_slice(got[-1][k], (me * n,), (n,)))
    return got[:-1], shares


def layer_norm(inputs, scales):
    center = jnp.mean(inputs, axis=-1, keepdims=True)
    shifted = inputs - center
    spread = jnp.mean(shifted * shifted, axis=-1, keepdims=True)
    return shifted * lax.rsqrt(spread + EPS) * scales


def gelu_exact(values):
    return jax.nn.gelu(values, approximate=False)


def matmul(former, latter):
    return jnp.dot(former, latter, preferred_element_type=jnp.float32)


def matmul_tn(former, latter):
    return lax.dot_general(
        former, latter, (((0,), (0,)), ((), ())), preferred_element_type=jnp.float32
    )


def matmul_nt(former, latter):
    return lax.dot_general(
        former, latter, (((1,), (1,)), ((), ())), preferred_element_type=jnp.float32
    )


def to_windows(canvas, shifts, columns):
    clip_count = canvas.shape[0]
    features = canvas.shape[-1]
    canvas = canvas.reshape(clip_count, TIME, columns, features)

    def to_roll_one(portion, offsets):
        portion = jnp.roll(portion, -offsets[0], axis=0)
        return jnp.roll(portion, -offsets[1], axis=1)

    canvas = jax.vmap(to_roll_one)(canvas, shifts)
    canvas = canvas.reshape(clip_count, TIME // WIN, WIN, columns // WIN, WIN, features)
    canvas = canvas.transpose(0, 1, 3, 2, 4, 5)
    return canvas.reshape(-1, WIN * WIN, features)


def from_windows(windows, shifts, columns):
    features = windows.shape[-1]
    clip_count = windows.shape[0] // (TIME // WIN * (columns // WIN))
    canvas = windows.reshape(clip_count, TIME // WIN, columns // WIN, WIN, WIN, features)
    canvas = canvas.transpose(0, 1, 3, 2, 4, 5).reshape(clip_count, TIME, columns, features)

    def from_roll_one(portion, offsets):
        portion = jnp.roll(portion, offsets[0], axis=0)
        return jnp.roll(portion, offsets[1], axis=1)

    canvas = jax.vmap(from_roll_one)(canvas, shifts)
    return canvas.reshape(clip_count, TIME * columns, features)


def plain_layout(clip_count, length):

    def arrange(portion):
        return portion.reshape(clip_count, length, portion.shape[-1])

    def restore(portion):
        return portion.reshape(clip_count * length, portion.shape[-1])

    return (clip_count * length, arrange, restore)


def window_layout(clip_count, columns, shifts):

    def arrange(portion):
        return to_windows(
            portion.reshape(clip_count, TIME * columns, portion.shape[-1]), shifts, columns
        )

    def restore(portion):
        return from_windows(portion, shifts, columns).reshape(
            clip_count * TIME * columns, portion.shape[-1]
        )

    return (clip_count * TIME * columns, arrange, restore)


def attend(queries, key_rows, values, num_heads):
    batches, length, features = queries.shape
    head_size = features // num_heads
    head_shape = (batches, length, num_heads, head_size)
    scores = jnp.einsum(
        "bqhd,bkhd->bhqk",
        queries.reshape(head_shape),
        key_rows.reshape(head_shape),
        preferred_element_type=jnp.float32,
    ) * head_size ** (-0.5)
    maximum = jnp.max(scores, axis=-1, keepdims=True)
    weights = jnp.exp(scores - maximum)
    totals = jnp.sum(weights, axis=-1, keepdims=True)
    shares = (weights / totals).astype(jnp.bfloat16)
    blended = jnp.einsum(
        "bhqk,bkhd->bqhd", shares, values.reshape(head_shape), preferred_element_type=jnp.float32
    )
    return (
        blended.astype(jnp.bfloat16).reshape(batches, length, features),
        maximum + jnp.log(totals),
    )


def attend_back(queries, key_rows, values, log_total, grad_blended, num_heads):
    batches, length, features = queries.shape
    head_size = features // num_heads
    scale = head_size ** (-0.5)
    head_shape = (batches, length, num_heads, head_size)
    queries = queries.reshape(head_shape)
    key_rows = key_rows.reshape(head_shape)
    values = values.reshape(head_shape)
    grad_blended = grad_blended.reshape(head_shape)
    scores = (
        jnp.einsum("bqhd,bkhd->bhqk", queries, key_rows, preferred_element_type=jnp.float32) * scale
    )
    shares = jnp.exp(scores - log_total)
    grad_values = jnp.einsum(
        "bhqk,bqhd->bkhd",
        shares.astype(jnp.bfloat16),
        grad_blended,
        preferred_element_type=jnp.float32,
    )
    grad_shares = jnp.einsum(
        "bqhd,bkhd->bhqk", grad_blended, values, preferred_element_type=jnp.float32
    )
    inner = jnp.sum(grad_shares * shares, axis=-1, keepdims=True)
    grad_scores = (shares * (grad_shares - inner)).astype(jnp.bfloat16)
    grad_queries = (
        jnp.einsum("bhqk,bkhd->bqhd", grad_scores, key_rows, preferred_element_type=jnp.float32)
        * scale
    )
    grad_keys = (
        jnp.einsum("bhqk,bqhd->bkhd", grad_scores, queries, preferred_element_type=jnp.float32)
        * scale
    )
    flat_shape = (batches, length, features)
    joined = jnp.concatenate(
        [
            grad_queries.reshape(flat_shape),
            grad_keys.reshape(flat_shape),
            grad_values.reshape(flat_shape),
        ],
        axis=-1,
    )
    return joined.astype(jnp.bfloat16)


def attention_forward(projected, layouts, num_heads):
    features = projected.shape[-1] // 3
    blended_parts = []
    log_totals = []
    offset = 0
    for row_count, arrange, restore in layouts:
        portion = arrange(projected[offset : offset + row_count])
        blended, log_total = attend(
            portion[..., :features],
            portion[..., features : 2 * features],
            portion[..., 2 * features :],
            num_heads,
        )
        blended_parts.append(restore(blended))
        log_totals.append(log_total)
        offset += row_count
    return (jnp.concatenate(blended_parts, 0), log_totals)


def attention_backward(projected, log_totals, grad_blended, layouts, num_heads):
    features = projected.shape[-1] // 3
    gradients = []
    offset = 0
    for position, (row_count, arrange, restore) in enumerate(layouts):
        portion = arrange(projected[offset : offset + row_count])
        grad_portion = arrange(grad_blended[offset : offset + row_count])
        joined = attend_back(
            portion[..., :features],
            portion[..., features : 2 * features],
            portion[..., 2 * features :],
            log_totals[position],
            grad_portion,
            num_heads,
        )
        gradients.append(restore(joined))
        offset += row_count
    return jnp.concatenate(gradients, 0)


def block_forward(inputs, weights, layouts, num_heads):
    gain_one, w_qkv, w_out, gain_two, w_up, w_down = weights
    normed = layer_norm(inputs, gain_one.astype(jnp.float32)).astype(jnp.bfloat16)
    projected = matmul(normed, w_qkv).astype(jnp.bfloat16)
    blended, log_totals = attention_forward(projected, layouts, num_heads)
    middle = inputs + matmul(blended, w_out)
    normed_two = layer_norm(middle, gain_two.astype(jnp.float32)).astype(jnp.bfloat16)
    raised = matmul(normed_two, w_up)
    active = gelu_exact(raised).astype(jnp.bfloat16)
    result = middle + matmul(active, w_down)
    return (
        result,
        (inputs, normed, projected, blended, log_totals, middle, normed_two, raised, active),
    )


def block_backward(grad_result, saved, weights, layouts, num_heads):
    inputs, normed, projected, blended, log_totals, middle, normed_two, raised, active = saved
    gain_one, w_qkv, w_out, gain_two, w_up, w_down = weights
    grad_low = grad_result.astype(jnp.bfloat16)
    grad_down = matmul_tn(active, grad_low)
    grad_active = matmul_nt(grad_low, w_down)
    gelu_value, gelu_pull = jax.vjp(gelu_exact, raised)
    grad_raised = gelu_pull(grad_active)[0].astype(jnp.bfloat16)
    grad_up = matmul_tn(normed_two, grad_raised)
    grad_normed_two = matmul_nt(grad_raised, w_up)
    norm_value, norm_pull = jax.vjp(layer_norm, middle, gain_two.astype(jnp.float32))
    grad_middle, grad_gain_two = norm_pull(grad_normed_two)
    grad_middle = grad_middle + grad_result
    grad_middle_low = grad_middle.astype(jnp.bfloat16)
    grad_out = matmul_tn(blended, grad_middle_low)
    grad_blended = matmul_nt(grad_middle_low, w_out).astype(jnp.bfloat16)
    grad_projected = attention_backward(projected, log_totals, grad_blended, layouts, num_heads)
    grad_qkv = matmul_tn(normed, grad_projected)
    grad_normed = matmul_nt(grad_projected, w_qkv)
    first_value, first_pull = jax.vjp(layer_norm, inputs, gain_one.astype(jnp.float32))
    grad_inputs, grad_gain_one = first_pull(grad_normed)
    return (
        grad_inputs + grad_middle,
        (grad_gain_one, grad_qkv, grad_out, grad_gain_two, grad_up, grad_down),
    )


def place(embedded, visible, filler, patches):
    clip_count = embedded.shape[0]
    canvas = jnp.broadcast_to(filler, (clip_count, patches, filler.shape[0]))
    clip_index = jnp.arange(clip_count, dtype=jnp.int32)[:, None]
    return canvas.at[clip_index, visible].set(embedded)


def masked_sum(grad_canvas, visible):
    clip_count, patches, features = grad_canvas.shape
    clip_index = jnp.arange(clip_count, dtype=jnp.int32)[:, None]
    masked = jnp.ones((clip_count, patches), jnp.float32).at[clip_index, visible].set(0.0)
    return jnp.sum(grad_canvas * masked[:, :, None], axis=(0, 1))


def pick_rows(grad_canvas, visible):
    clip_index = jnp.arange(grad_canvas.shape[0], dtype=jnp.int32)[:, None]
    return grad_canvas[clip_index, visible]


def local(
    clips_wide,
    clips_narrow,
    visible_wide,
    visible_narrow,
    shift_wide,
    shift_narrow,
    enc_norm1,
    enc_qkv,
    enc_out,
    enc_norm2,
    enc_up,
    enc_down,
    embed_proj,
    mask_token,
    dec_norm1,
    dec_qkv,
    dec_out,
    dec_norm2,
    dec_up,
    dec_down,
    cotan_wide,
    cotan_narrow,
):
    wide_count, wide_visible, model_width = clips_wide.shape
    narrow_count, narrow_visible, model_again = clips_narrow.shape
    wide_patches = cotan_wide.shape[1]
    narrow_patches = cotan_narrow.shape[1]
    decoder_width = cotan_wide.shape[2]
    wide_columns = wide_patches // TIME
    narrow_columns = narrow_patches // TIME
    narrow_shifts = jnp.stack([shift_narrow, jnp.zeros_like(shift_narrow)], axis=1)
    enc_layouts = [
        plain_layout(wide_count, wide_visible),
        plain_layout(narrow_count, narrow_visible),
    ]
    dec_layouts = [
        window_layout(wide_count, wide_columns, shift_wide),
        window_layout(narrow_count, narrow_columns, narrow_shifts),
    ]
    devices = lax.axis_size("fsdp")
    matrices = (
        enc_qkv, enc_out, enc_up, enc_down, embed_proj, dec_qkv, dec_out, dec_up, dec_down,
    )
    vectors = (enc_norm1, enc_norm2, mask_token, dec_norm1, dec_norm2)
    m, v = gather_all(matrices, vectors, devices)
    enc_full = (v[0], m[0], m[1], v[1], m[2], m[3], m[4])
    dec_full = (v[2], v[3], m[5], m[6], v[4], m[7], m[8])
    enc_input = jnp.concatenate(
        [clips_wide.reshape(-1, model_width), clips_narrow.reshape(-1, model_width)], 0
    ).astype(jnp.float32)
    encoded, enc_saved = block_forward(enc_input, enc_full[:6], enc_layouts, HEADS)
    encoded_low = encoded.astype(jnp.bfloat16)
    embedded = matmul(encoded_low, enc_full[6])
    wide_rows = wide_count * wide_visible
    filler = dec_full[0].astype(jnp.float32)
    canvas_wide = place(
        embedded[:wide_rows].reshape(wide_count, wide_visible, decoder_width),
        visible_wide,
        filler,
        wide_patches,
    )
    canvas_narrow = place(
        embedded[wide_rows:].reshape(narrow_count, narrow_visible, decoder_width),
        visible_narrow,
        filler,
        narrow_patches,
    )
    dec_input = jnp.concatenate(
        [canvas_wide.reshape(-1, decoder_width), canvas_narrow.reshape(-1, decoder_width)], 0
    )
    decoded, dec_saved = block_forward(dec_input, dec_full[1:], dec_layouts, DHEADS)
    decoded_low = decoded.astype(jnp.bfloat16)
    grad_decoded = jnp.concatenate(
        [cotan_wide.reshape(-1, decoder_width), cotan_narrow.reshape(-1, decoder_width)], 0
    ).astype(jnp.float32)
    dec_back = dec_full[1:]
    grad_canvas, dec_grads = block_backward(grad_decoded, dec_saved, dec_back, dec_layouts, DHEADS)
    wide_patch_rows = wide_count * wide_patches
    grad_canvas_wide = grad_canvas[:wide_patch_rows].reshape(
        wide_count, wide_patches, decoder_width
    )
    grad_canvas_narrow = grad_canvas[wide_patch_rows:].reshape(
        narrow_count, narrow_patches, decoder_width
    )
    grad_filler = masked_sum(grad_canvas_wide, visible_wide) + masked_sum(
        grad_canvas_narrow, visible_narrow
    )
    grad_embedded = jnp.concatenate(
        [
            pick_rows(grad_canvas_wide, visible_wide).reshape(-1, decoder_width),
            pick_rows(grad_canvas_narrow, visible_narrow).reshape(-1, decoder_width),
        ],
        0,
    ).astype(jnp.bfloat16)
    enc_back = enc_full
    grad_proj = matmul_tn(encoded_low, grad_embedded)
    grad_encoded = matmul_nt(grad_embedded, enc_back[6])
    grad_input, enc_grads = block_backward(
        grad_encoded, enc_saved, enc_back[:6], enc_layouts, HEADS
    )
    low = jnp.bfloat16
    grads = [
        enc_grads[1], enc_grads[2], enc_grads[4], enc_grads[5], grad_proj,
        dec_grads[1], dec_grads[2], dec_grads[4], dec_grads[5],
    ]
    gains = [enc_grads[0], enc_grads[3], grad_filler, dec_grads[0], dec_grads[3]]
    m, v = reduce_all([g.astype(low) for g in grads], gains, devices)
    totals = (
        v[0], m[0], m[1], v[1], m[2], m[3], m[4], v[2], v[3], m[5], m[6], v[4], m[7], m[8],
    )
    encoded_wide = encoded_low[:wide_rows].reshape(wide_count, wide_visible, model_width)
    encoded_narrow = encoded_low[wide_rows:].reshape(narrow_count, narrow_visible, model_width)
    decoded_wide = decoded_low[:wide_patch_rows].reshape(wide_count, wide_patches, decoder_width)
    decoded_narrow = decoded_low[wide_patch_rows:].reshape(
        narrow_count, narrow_patches, decoder_width
    )
    grad_wide = grad_input[:wide_rows].reshape(wide_count, wide_visible, model_width)
    grad_narrow = grad_input[wide_rows:].reshape(narrow_count, narrow_visible, model_width)
    return (
        encoded_wide,
        encoded_narrow,
        decoded_wide,
        decoded_narrow,
        grad_wide,
        grad_narrow,
        totals[0],
        totals[1],
        totals[2],
        totals[3],
        totals[4],
        totals[5],
        totals[6],
        totals[7],
        totals[8],
        totals[9],
        totals[10],
        totals[11],
        totals[12],
        totals[13],
    )


def solution(mesh):
    return jax.shard_map(
        local,
        mesh=mesh,
        in_specs=(
            P(("fsdp", "dp"), None, None),
            P(("fsdp", "dp"), None, None),
            P(("fsdp", "dp"), None),
            P(("fsdp", "dp"), None),
            P(("fsdp", "dp"), None),
            P(("fsdp", "dp")),
            P("fsdp"),
            P("fsdp", None),
            P("fsdp", None),
            P("fsdp"),
            P("fsdp", None),
            P("fsdp", None),
            P("fsdp", None),
            P("fsdp"),
            P("fsdp"),
            P("fsdp", None),
            P("fsdp", None),
            P("fsdp"),
            P("fsdp", None),
            P("fsdp", None),
            P(("fsdp", "dp"), None, None),
            P(("fsdp", "dp"), None, None),
        ),
        out_specs=(
            P(("fsdp", "dp"), None, None),
            P(("fsdp", "dp"), None, None),
            P(("fsdp", "dp"), None, None),
            P(("fsdp", "dp"), None, None),
            P(("fsdp", "dp"), None, None),
            P(("fsdp", "dp"), None, None),
            P("fsdp"),
            P("fsdp", None),
            P("fsdp", None),
            P("fsdp"),
            P("fsdp", None),
            P("fsdp", None),
            P("fsdp", None),
            P("fsdp"),
            P("fsdp"),
            P("fsdp", None),
            P("fsdp", None),
            P("fsdp"),
            P("fsdp", None),
            P("fsdp", None),
        ),
        check_vma=False,
    )
```

```python
import functools

import jax
import jax.numpy as jnp
from jax import lax
from jax.experimental import pallas as pl
from jax.experimental.pallas import tpu as pltpu
from jax.sharding import PartitionSpec as P

MESH = pl.DeviceIdType.MESH


def slots():
    out=[]
    for bx in (0,1):
        for by in (0,1):
            for sgn in (0,1,-1):
                if (bx,by,sgn)!=(0,0,0): out.append((bx,by,sgn))
    return out

def forwards(order,bx,by,sgn):
    differs={'x':bx,'y':by,'z':int(sgn!=0)}
    last=max([j for j,d in enumerate(order) if differs[d]],default=-1)
    dirs=[]
    for j,d in enumerate(order):
        if j>last:
            dirs += ['u','d'] if d=='z' else [d]
    if last>=0 and order[last]=='z':
        dirs.append('u' if sgn<0 else 'd')
    return dirs

def ag_kernel(nz, pieces, nw, *refs):
    ins=refs[:nw]; outs=refs[nw:2*nw]
    send, recv, sib_send, sib_recv, loc = refs[2*nw:]
    f=lax.axis_index("fsdp"); c=lax.axis_index("dp")
    z=f//4; y=(f//2)%2; x=f%2
    xn=(f+1-2*x, c); yn=(f+2-4*y, c); up=(f+4,c); dn=(f-4,c); sib=(f,1-c)
    bar=pltpu.get_barrier_semaphore()
    def sig(dev): pl.semaphore_signal(bar,inc=1,device_id=dev,device_id_type=MESH)
    sig(xn); sig(yn); sig(sib)
    @pl.when(z<nz-1)
    def _(): sig(up)
    @pl.when(z>0)
    def _(): sig(dn)
    pl.semaphore_wait(bar, 3+(z<nz-1).astype(jnp.int32)+(z>0).astype(jnp.int32))
    dest={'x':xn,'y':yn,'u':up,'d':dn}
    ok={'x':None,'y':None,'u':z<nz-1,'d':z>0}
    code={'x':0,'y':1,'u':2,'d':3}
    def rows(w): return ins[w].shape[0]
    def region(i, s, half):
        w,c0,cols,order,share=pieces[i]
        r=rows(w)
        n=ins[w].shape[1]
        col=c0 if not share else pl.multiple_of(half*(n//2)+c0,128)
        return outs[w].at[pl.ds(pl.multiple_of(s*r,r),r), pl.ds(col,cols)]
    def own(i):
        w,c0,cols,order,share=pieces[i]
        n=ins[w].shape[1]
        col=c0 if not share else pl.multiple_of(c*(n//2)+c0,128)
        return ins[w].at[:, pl.ds(col,cols)]
    def remote(i,s,src,d):
        return pltpu.make_async_remote_copy(src_ref=src,dst_ref=region(i,s,c),send_sem=send.at[i,s,code[d]],recv_sem=recv.at[i,s],device_id=dest[d],device_id_type=MESH)
    def sibling(i,s):
        return pltpu.make_async_remote_copy(src_ref=region(i,s,c),dst_ref=region(i,s,c),send_sem=sib_send.at[i,s],recv_sem=sib_recv.at[i,s],device_id=sib,device_id_type=MESH)
    def go(i,s,src,dirs):
        for d in dirs:
            if ok[d] is None: remote(i,s,src,d).start()
            else:
                pl.when(ok[d])(lambda d=d: remote(i,s,src,d).start())
    def wait_sends(i,s,src,dirs):
        for d in dirs:
            if ok[d] is None: remote(i,s,src,d).wait_send()
            else:
                pl.when(ok[d])(lambda d=d: remote(i,s,src,d).wait_send())
    locals_=[]
    for i in range(len(pieces)):
        go(i,f,own(i),forwards(pieces[i][3],0,0,0))
    for w in range(nw):
        r=rows(w)
        cp=pltpu.make_async_copy(ins[w],outs[w].at[pl.ds(pl.multiple_of(f*r,r),r)],loc.at[w]); cp.start(); locals_.append(cp)
    def each(h, i, action):
        for bx,by,sgn in slots():
            k=h-bx-by
            zs=z+sgn*k
            if sgn==0: valid=k==0
            else: valid=(k>=1)&(zs>=0)&(zs<nz)
            s=zs*4+(y+by-2*by*y)*2+(x+bx-2*bx*x)
            pl.when(valid)(lambda s=s,bx=bx,by=by,sgn=sgn: action(i,s,forwards(pieces[i][3],bx,by,sgn)))
    def step(i,s,dirs):
        remote(i,s,region(i,s,c),'x').wait_recv()
        go(i,s,region(i,s,c),dirs)
        if pieces[i][4]: sibling(i,s).start()
    def fin(i,s,dirs):
        wait_sends(i,s,region(i,s,c),dirs)
        if pieces[i][4]:
            sibling(i,s).wait_send()
            pltpu.make_async_remote_copy(src_ref=region(i,s,1-c),dst_ref=region(i,s,1-c),send_sem=sib_send.at[i,s],recv_sem=sib_recv.at[i,s],device_id=sib,device_id_type=MESH).wait_recv()
    @pl.loop(1,nz+2)
    def _(h):
        for i in range(len(pieces)):
            each(h,i,step)
    for i in range(len(pieces)):
        wait_sends(i,f,own(i),forwards(pieces[i][3],0,0,0))
    for cp in locals_: cp.wait()
    @pl.loop(1,nz+2)
    def _(h):
        for i in range(len(pieces)):
            each(h,i,fin)

def all_gather(shards, pieces, nz, cid=1):
    nw=len(shards); npc=len(pieces); n=nz*4
    return pl.pallas_call(functools.partial(ag_kernel,nz,pieces,nw),
        out_shape=[jax.ShapeDtypeStruct((s.shape[0]*n,s.shape[1]),s.dtype) for s in shards],
        in_specs=[pl.BlockSpec(memory_space=pl.ANY)]*nw,
        out_specs=[pl.BlockSpec(memory_space=pl.ANY)]*nw,
        scratch_shapes=[pltpu.SemaphoreType.DMA((npc,n,4)),pltpu.SemaphoreType.DMA((npc,n)),pltpu.SemaphoreType.DMA((npc,n)),pltpu.SemaphoreType.DMA((npc,n)),pltpu.SemaphoreType.DMA((nw,))],
        compiler_params=pltpu.CompilerParams(collective_id=cid,has_side_effects=True),
        name="gather_weights")(*shards)

def slot_count(order, d, nz):
    size={'x':2,'y':2,'z':nz}
    j=order.index('z' if d in 'ud' else d)
    k=1
    for e in order[:j]: k*=size[e]
    return k*(nz+1) if d in 'ud' else k

def slot_index(order, d, nz, pos):
    size={'x':2,'y':2,'z':nz}
    j=order.index('z' if d in 'ud' else d)
    k=0
    for e in order[:j]: k=k*size[e]+pos[e]
    if d in 'ud': k=k*(nz+1)+pos['z']+(1 if d=='d' else 0)
    return k

LEAD = 0
def rs_kernel(nz, pieces, nw, *refs):
    ins=refs[:nw]; vec=refs[nw]; outs=refs[nw+1:2*nw+1]; vout=refs[2*nw+1]
    rest=list(refs[2*nw+2:])
    npc=len(pieces)
    own=[rest.pop(0) for _ in range(npc)]
    sibb=[rest.pop(0) for _ in range(npc)]
    rbuf=[[rest.pop(0) for _ in range(3)] for _ in range(npc)]
    res=[rest.pop(0) for _ in range(npc)]
    vbuf, own_sem, sib_send, sib_recv, send, recv, res_sem, res_send, res_recv, vsend, vrecv = rest
    f=lax.axis_index("fsdp"); c=lax.axis_index("dp")
    z=f//4; y=(f//2)%2; x=f%2
    bits=(nz*4).bit_length()-1
    def flip(b): return f+(1<<b)*(1-2*((f//(1<<b))%2))
    xn=(flip(0), c); yn=(flip(1), c); up=(f+4,c); dn=(f-4,c); sib=(f,1-c)
    bar=pltpu.get_barrier_semaphore()
    def sig(dev): pl.semaphore_signal(bar,inc=1,device_id=dev,device_id_type=MESH)
    sig(xn); sig(yn); sig(sib)
    @pl.when(z<nz-1)
    def _(): sig(up)
    @pl.when(z>0)
    def _(): sig(dn)
    extra=[b for b in range(3,bits)]
    for b in extra: sig((flip(b),c))
    pl.semaphore_wait(bar, 3+len(extra)+(z<nz-1).astype(jnp.int32)+(z>0).astype(jnp.int32))
    dest={'x':xn,'y':yn,'u':up,'d':dn}
    there={'u':z<nz-1,'d':z>0}
    opposite={'u':'d','d':'u','x':'x','y':'y'}
    bufof={'x':0,'y':1,'u':2,'d':2}
    def rws(i): return ins[pieces[i][0]].shape[0]//(nz*4)
    def half(i,h):
        w,c0,cols,order=pieces[i]
        n=ins[w].shape[1]
        return pl.ds(pl.multiple_of(h*(n//2)+c0,128),cols)
    def own_copy(i): return pltpu.make_async_copy(ins[pieces[i][0]].at[:,half(i,c)],own[i],own_sem.at[i])
    def sib_copy(i): return pltpu.make_async_remote_copy(src_ref=ins[pieces[i][0]].at[:,half(i,1-c)],dst_ref=sibb[i],send_sem=sib_send.at[i],recv_sem=sib_recv.at[i],device_id=sib,device_id_type=MESH)
    def vcopy(k):
        dev = sib if k==0 else (flip(k-1),c)
        return pltpu.make_async_remote_copy(src_ref=vbuf.at[0,k],dst_ref=vbuf.at[1,k],send_sem=vsend.at[k],recv_sem=vrecv.at[k],device_id=dev,device_id_type=MESH)
    for i in range(npc):
        sib_copy(i).start(); own_copy(i).start()
    vbuf[0,0]=vec[...]
    vcopy(0).start()
    def blk(i,s): r=rws(i); return pl.ds(pl.multiple_of(s*r,r),r)
    def message(i,s,pos,d):
        order=pieces[i][3]
        b=bufof[d]
        return pltpu.make_async_remote_copy(src_ref=own[i].at[blk(i,s)],dst_ref=rbuf[i][b].at[slot_index(order,opposite[d],nz,pos)],send_sem=send.at[i,s],recv_sem=recv.at[i,b,slot_index(order,opposite[d],nz,pos)],device_id=dest[d],device_id_type=MESH)
    def arrival(i,pos,d):
        order=pieces[i][3]; b=bufof[d]; k=slot_index(order,d,nz,pos)
        return pltpu.make_async_remote_copy(src_ref=rbuf[i][b].at[k],dst_ref=rbuf[i][b].at[k],send_sem=send.at[i,0],recv_sem=recv.at[i,b,k],device_id=sib,device_id_type=MESH)
    def add(i,s,pos,children,final):
        order=pieces[i][3]; r=rws(i)
        ks=[(bufof[d],slot_index(order,d,nz,pos)) for d in children]
        @pl.loop(0,r//16)
        def _(k):
            rr=pl.ds(pl.multiple_of(k*16,16),16)
            gr=pl.ds(pl.multiple_of(s*r+k*16,16),16)
            t=own[i][gr].astype(jnp.float32)+sibb[i][gr].astype(jnp.float32)
            for b,q in ks: t=t+rbuf[i][b][q,rr].astype(jnp.float32)
            if final: res[i][rr]=t
            else: own[i][gr]=t.astype(jnp.bfloat16)
    def parent(order,bx,by,sgn):
        differs={'x':bx,'y':by,'z':int(sgn!=0)}
        last=max(j for j,d in enumerate(order) if differs[d])
        if order[last]=='z': return 'd' if sgn<0 else 'u'
        return order[last]
    def with_children(i,s,pos,children,final):
        sure=[d for d in children if d in 'xy']; maybe=[d for d in children if d in 'ud']
        for d in sure: arrival(i,pos,d).wait_recv()
        for d in maybe: pl.when(there[d])(lambda d=d: arrival(i,pos,d).wait_recv())
        if not maybe: add(i,s,pos,sure,final)
        elif len(maybe)==1:
            pl.when(there[maybe[0]])(lambda: add(i,s,pos,sure+maybe,final))
            pl.when(jnp.logical_not(there[maybe[0]]))(lambda: add(i,s,pos,sure,final))
        else:
            u,d=there['u'],there['d']
            pl.when(u&d)(lambda: add(i,s,pos,sure+['u','d'],final))
            pl.when(u&jnp.logical_not(d))(lambda: add(i,s,pos,sure+['u'],final))
            pl.when(jnp.logical_not(u)&d)(lambda: add(i,s,pos,sure+['d'],final))
            if nz==1: add(i,s,pos,sure,final)
    def each(h,i,leaf,action):
        order=pieces[i][3]
        for bx,by,sgn in slots():
            ch=forwards(order,bx,by,sgn)
            if leaf is not None and (len(ch)==0)!=leaf: continue
            k=h-bx-by
            zs=z+sgn*k
            if sgn==0: valid=k==0
            else: valid=(k>=1)&(zs>=0)&(zs<nz)
            pos={'x':x+bx-2*bx*x,'y':y+by-2*by*y,'z':zs}
            s=zs*4+pos['y']*2+pos['x']
            pl.when(valid)(lambda s=s,pos=pos,ch=ch,p=parent(order,bx,by,sgn): action(i,s,pos,ch,p))
    def work(i,s,pos,ch,p):
        with_children(i,s,pos,ch,False)
        message(i,s,pos,p).start()
    def done(i,s,pos,ch,p):
        message(i,s,pos,p).wait_send()
    top=nz+1
    for i in range(npc):
        own_copy(i).wait(); sib_copy(i).wait_recv()
        for q in range(LEAD+1): each(jnp.int32(top-q),i,True,work)
    @pl.loop(0,top)
    def _(q):
        h=top-q
        for i in range(npc):
            each(h,i,False,work)
        for i in range(npc):
            each(h-LEAD-1,i,True,work)
        for k in range(bits+1):
            @pl.when(q==k)
            def _(k=k):
                vcopy(k).wait()
                vbuf[0,k+1]=vbuf[0,k]+vbuf[1,k]
                if k<bits: vcopy(k+1).start()
    for k in range(top,bits+1):
        vcopy(k).wait()
        vbuf[0,k+1]=vbuf[0,k]+vbuf[1,k]
        if k<bits: vcopy(k+1).start()
    def out_copy(i): return pltpu.make_async_copy(res[i],outs[pieces[i][0]].at[:,half(i,c)],res_sem.at[i])
    def out_sib(i,h): return pltpu.make_async_remote_copy(src_ref=res[i],dst_ref=outs[pieces[i][0]].at[:,half(i,h)],send_sem=res_send.at[i],recv_sem=res_recv.at[i],device_id=sib,device_id_type=MESH)
    for i in range(npc):
        with_children(i,f,{'x':x,'y':y,'z':z},forwards(pieces[i][3],0,0,0),True)
        out_sib(i,c).start(); out_copy(i).start()
    vout[...]=vbuf[0,bits+1]
    for i in range(npc): sib_copy(i).wait_send()
    @pl.loop(0,top)
    def _(q):
        for i in range(npc): each(top-q,i,None,done)
    for i in range(npc):
        out_copy(i).wait(); out_sib(i,c).wait_send(); out_sib(i,1-c).wait_recv()

def reduce_scatter(grads, vec, pieces, nz, cid=2):
    nw=len(grads); npc=len(pieces); n=nz*4; bits=n.bit_length()-1
    shards=[(g.shape[0]//n,g.shape[1]) for g in grads]
    sc=[]
    B=jnp.bfloat16
    for w,c0,cols,o in pieces: sc.append(pltpu.VMEM((shards[w][0]*n,cols),B))
    for w,c0,cols,o in pieces: sc.append(pltpu.VMEM((shards[w][0]*n,cols),B))
    most=1
    for w,c0,cols,o in pieces:
        ns=[slot_count(o,'x',nz),slot_count(o,'y',nz),slot_count(o,'u',nz)]
        most=max(most,*ns)
        for k in ns: sc.append(pltpu.VMEM((k,shards[w][0],cols),B))
    for w,c0,cols,o in pieces: sc.append(pltpu.VMEM((shards[w][0],cols),jnp.float32))
    D=pltpu.SemaphoreType.DMA
    sc += [pltpu.VMEM((2,bits+2)+vec.shape,jnp.float32),D((npc,)),D((npc,)),D((npc,)),D((npc,n)),D((npc,3,most)),D((npc,)),D((npc,)),D((npc,)),D((bits+1,)),D((bits+1,))]
    return pl.pallas_call(functools.partial(rs_kernel,nz,pieces,nw),
        out_shape=[jax.ShapeDtypeStruct(s,jnp.float32) for s in shards]+[jax.ShapeDtypeStruct(vec.shape,jnp.float32)],
        in_specs=[pl.BlockSpec(memory_space=pl.ANY)]*nw+[pl.BlockSpec(memory_space=pltpu.VMEM)],
        out_specs=[pl.BlockSpec(memory_space=pl.ANY)]*nw+[pl.BlockSpec(memory_space=pltpu.VMEM)],
        scratch_shapes=sc,
        compiler_params=pltpu.CompilerParams(collective_id=cid,has_side_effects=True,vmem_limit_bytes=58*2**20),
        name="reduce_gradients")(*grads,vec)


TIME = 64
WIN = 4
EPS = 1e-6
F = jnp.float32
B = jnp.bfloat16
VMEM_LIMIT = 60 * 2**20


def dot(a, b):
    return lax.dot_general(a, b, (((1,), (0,)), ((), ())), preferred_element_type=F)


def dot_nt(a, b):
    return lax.dot_general(a, b, (((1,), (1,)), ((), ())), preferred_element_type=F)


def dot_tn(a, b):
    return lax.dot_general(a, b, (((0,), (0,)), ((), ())), preferred_element_type=F)


def iota(shape, dim):
    return lax.broadcasted_iota(jnp.int32, shape, dim)


def norm_stats(x):
    center = jnp.mean(x, axis=-1, keepdims=True)
    shifted = x - center
    spread = jnp.mean(shifted * shifted, axis=-1, keepdims=True)
    scale = lax.rsqrt(spread + EPS)
    return shifted * scale, scale


def norm_back(x, gain, grad):
    unit, scale = norm_stats(x)
    by_gain = grad * unit
    by_unit = grad * gain
    mean_one = jnp.mean(by_unit, axis=-1, keepdims=True)
    mean_two = jnp.mean(by_unit * unit, axis=-1, keepdims=True)
    by_input = scale * (by_unit - mean_one - unit * mean_two)
    return by_input, jnp.sum(by_gain.reshape(-1, 8, x.shape[1]), axis=0)


def gelu_both(u):
    t = 1.0 / (1.0 + (0.3275911 * 0.7071067811865476) * jnp.abs(u))
    bell = jnp.exp(-0.5 * u * u)
    poly = t * (0.127414796 + t * (-0.142248368 + t * (0.7107068705 + t * (-0.7265760135 + t * 0.5307027145))))
    tail = poly * bell
    phi = jnp.where(u < 0, tail, 1.0 - tail)
    return u * phi, phi + u * (bell * 0.3989422804014327)


def spread_vector(tiles, lane, size, devices):
    part = size // devices
    pick = (iota((128, size), 1) % part == iota((128, size), 0)).astype(B)
    wide = dot(tiles, pick)
    rows = iota((tiles.shape[0], size), 0)
    keep = rows == (iota((tiles.shape[0], size), 1) // part) * 16 + lane
    return jnp.sum(jnp.where(keep, wide, 0.0), axis=0, keepdims=True)


def lane_groups(x, op):
    lanes = iota(x.shape, 1)
    width = x.shape[1]
    for d in (1, 2, 4, 8):
        other = jnp.where((lanes & d) != 0, pltpu.roll(x, d, 1), pltpu.roll(x, width - d, 1))
        x = op(x, other)
    return x


HEAD = 32
AREA = WIN * WIN


def stack8(block, mask):
    return jnp.concatenate([block] * 8, axis=0) * mask


def dec_kernel(wc, nc, devices, shw, shn, vis, tiles, m_ref, cotw, cotn, wq_h, wo_h, wu_h, wd_h,
               outw, outn, dm_ref, gq, go, gu, gd, vec_ref,
               wq, wo, wu, wd, perm, sel, mhi, mlo, dz, r_ref, a_ref, qkv, p_ref, o_ref, x1_ref,
               b_ref, h_ref, du, dx1, do_ref, dqkv, dec, dm_acc, acc, sems):
    D = wo.shape[0]
    wide_rows = cotw.shape[1]
    narrow_rows = cotn.shape[1]
    rows = wc * wide_rows + nc * narrow_rows
    T = 256
    nt = rows // T
    wide_tiles = wc * wide_rows // T
    cps = []
    for k, (src, dst) in enumerate(((wq_h, wq), (wo_h, wo), (wu_h, wu), (wd_h, wd))):
        cp = pltpu.make_async_copy(src, dst, sems.at[k])
        cp.start()
        cps.append(cp)
    gain1 = spread_vector(tiles[...], 3, D, devices)
    gain2 = spread_vector(tiles[...], 4, D, devices)
    filler = spread_vector(tiles[...], 2, D, devices)
    mhi[...] = m_ref[...].astype(B)
    mlo[...] = (m_ref[...] - mhi[...].astype(F)).astype(B)
    dm_acc[...] = jnp.zeros_like(dm_acc)
    acc[...] = jnp.zeros_like(acc)
    clips = [(i * wide_rows, wide_rows, 8, shw[i, 0], shw[i, 1], cotw, i, i) for i in range(wc)]
    clips += [(wc * wide_rows + i * narrow_rows, narrow_rows, 4, shn[i], 0, cotn, i, wc + i) for i in range(nc)]
    for base, n, cols, s, r, cot, i, v in clips:
        for k in range(0, n, T):
            j = iota((T, 1), 0) + k
            w, q = j >> 4, j & 15
            wf = cols // WIN
            t = ((w // wf) * WIN + (q >> 2) + s) & (TIME - 1)
            f = ((w % wf) * WIN + (q & 3) + r) & (cols - 1)
            patch = t * cols + f
            where = pl.ds(base + k, T)
            hot = jnp.where(iota((T, n), 1) == patch, 1.0, 0.0).astype(B)
            perm[where, 0:n] = hot
            sel[where] = jnp.where(vis[v:v + 1, :] == patch, 1.0, 0.0).astype(B)
            dz[where] = dot(hot, cot[i]).astype(B)

    def group_rows(t):
        g = jnp.where(t < wide_tiles, t * T // wide_rows, wc + (t - wide_tiles) // 2)
        return pl.ds(pl.multiple_of(g * 128, 128), 128)

    cps[0].wait()

    @pl.loop(0, nt)
    def _(t):
        rr = pl.ds(pl.multiple_of(t * T, T), T)
        g = group_rows(t)
        s = sel[rr]
        seen = jnp.sum(s.astype(F), axis=1, keepdims=True)
        x = dot(s, mhi[g]) + dot(s, mlo[g]) + (1.0 - seen) * filler
        r_ref[rr] = x
        a = (norm_stats(x)[0] * gain1).astype(B)
        a_ref[rr] = a
        qkv[rr] = dot(a, wq[...]).astype(B)

    mask = (iota((128, 256), 0) // AREA == iota((128, 256), 1) // HEAD).astype(B)
    scale = HEAD ** -0.5
    nw = 8

    @pl.loop(0, rows // (nw * AREA))
    def _(g):
        base = pl.multiple_of(g * nw * AREA, nw * AREA)
        rr = pl.ds(base, nw * AREA)
        for a in range(D // 256):
            cq = pl.ds(a * 256, 256)
            q, k, v = qkv[rr, cq], qkv[rr, pl.ds(D + a * 256, 256)], qkv[rr, pl.ds(2 * D + a * 256, 256)]
            w16 = [slice(AREA * j, AREA * j + AREA) for j in range(nw)]
            s = jnp.concatenate([dot_nt(q[w], stack8(k[w], mask)) for w in w16], axis=0) * scale
            e = jnp.exp(s - lane_groups(s, jnp.maximum))
            p = e / lane_groups(e, jnp.add)
            p_ref[rr, pl.ds(a * 128, 128)] = p
            low = p.astype(B)
            o_ref[rr, cq] = jnp.concatenate([dot(low[w], stack8(v[w], mask)) for w in w16], axis=0).astype(B)

    for cp in cps[1:]:
        cp.wait()

    @pl.loop(0, nt)
    def _(t):
        rr = pl.ds(pl.multiple_of(t * T, T), T)
        x1 = r_ref[rr] + dot(o_ref[rr], wo[...])
        x1_ref[rr] = x1
        b = (norm_stats(x1)[0] * gain2).astype(B)
        b_ref[rr] = b
        z = dz[rr]
        out = x1
        back = jnp.zeros((T, D), F)
        C = 512
        for k in range(0, wu.shape[1], C):
            u = dot(b, wu[:, k:k + C])
            h, slope = gelu_both(u)
            h = h.astype(B)
            h_ref[rr, k:k + C] = h
            out = out + dot(h, wd[k:k + C, :])
            d = (slope * dot_nt(z, wd[k:k + C, :])).astype(B)
            du[rr, k:k + C] = d
            back = back + dot_nt(d, wu[:, k:k + C])
        dec[rr] = out.astype(B)
        by_input, by_gain = norm_back(x1, gain2, back)
        acc[1] += by_gain
        dx = z.astype(F) + by_input
        dx1[rr] = dx
        do_ref[rr] = dot_nt(dx.astype(B), wo[...]).astype(B)

    for base, n, cols, s, r, cot, i, v in clips:
        res = dot_tn(perm[base:base + n, 0:n], dec[base:base + n]).astype(B)
        if cols == 8:
            outw[i] = res
        else:
            outn[i] = res

    @pl.loop(0, rows // (nw * AREA))
    def _(g):
        base = pl.multiple_of(g * nw * AREA, nw * AREA)
        rr = pl.ds(base, nw * AREA)
        w16 = [slice(AREA * j, AREA * j + AREA) for j in range(nw)]
        for a in range(D // 256):
            cq = pl.ds(a * 256, 256)
            q, k, v = qkv[rr, cq], qkv[rr, pl.ds(D + a * 256, 256)], qkv[rr, pl.ds(2 * D + a * 256, 256)]
            go_ = do_ref[rr, cq]
            ks = [stack8(k[w], mask) for w in w16]
            qs = [stack8(q[w], mask) for w in w16]
            gs = [stack8(go_[w], mask) for w in w16]
            p = p_ref[rr, pl.ds(a * 128, 128)]
            dp = jnp.concatenate([dot_nt(go_[w], stack8(v[w], mask)) for w in w16], axis=0)
            ds = (p * (dp - lane_groups(dp * p, jnp.add))).astype(B)
            dqkv[rr, cq] = (jnp.concatenate([dot(ds[w], m) for w, m in zip(w16, ks)], axis=0) * scale).astype(B)
            s = jnp.concatenate([dot_nt(k[w], m) for w, m in zip(w16, qs)], axis=0) * scale
            s = s.reshape(nw, AREA, 128)
            e = jnp.exp(s - jnp.max(s, axis=1, keepdims=True))
            p = e / jnp.sum(e, axis=1, keepdims=True)
            dp = jnp.concatenate([dot_nt(v[w], m) for w, m in zip(w16, gs)], axis=0).reshape(nw, AREA, 128)
            ds = (p * (dp - jnp.sum(dp * p, axis=1, keepdims=True))).reshape(nw * AREA, 128).astype(B)
            p = p.reshape(nw * AREA, 128).astype(B)
            dqkv[rr, pl.ds(D + a * 256, 256)] = (jnp.concatenate([dot(ds[w], m) for w, m in zip(w16, qs)], axis=0) * scale).astype(B)
            dqkv[rr, pl.ds(2 * D + a * 256, 256)] = jnp.concatenate([dot(p[w], m) for w, m in zip(w16, gs)], axis=0).astype(B)

    @pl.loop(0, nt)
    def _(t):
        rr = pl.ds(pl.multiple_of(t * T, T), T)
        g = group_rows(t)
        by_input, by_gain = norm_back(r_ref[rr], gain1, dot_nt(dqkv[rr], wq[...]))
        acc[0] += by_gain
        dr = dx1[rr] + by_input
        s = sel[rr]
        hidden = 1.0 - jnp.sum(s.astype(F), axis=1, keepdims=True)
        acc[2] += jnp.sum((dr * hidden).reshape(-1, 8, D), axis=0)
        dm_acc[g] += dot_tn(s, dr.astype(B))

    dm_ref[...] = dm_acc[...].astype(B)
    for k in range(3):
        vec_ref[k:k + 1, :] = jnp.sum(acc[k], axis=0, keepdims=True)
    vec_ref[3:, :] = jnp.zeros((5, D), F)
    gd_step = 512

    @pl.loop(0, wd.shape[0] // gd_step)
    def _(k):
        kk = pl.ds(pl.multiple_of(k * gd_step, gd_step), gd_step)
        gd[kk, :] = dot_tn(h_ref[:, kk], dz[...]).astype(B)
        gu[:, kk] = dot_tn(b_ref[...], du[:, kk]).astype(B)

    @pl.loop(0, wq.shape[1] // 512)
    def _(k):
        kk = pl.ds(pl.multiple_of(k * 512, 512), 512)
        gq[:, kk] = dot_tn(a_ref[...], dqkv[:, kk]).astype(B)

    go[...] = dot_tn(o_ref[...], dx1[...].astype(B)).astype(B)


def decoder(m, vis, shw, shn, tiles, cotw, cotn, wq, wo, wu, wd, devices):
    wc, nc = cotw.shape[0], cotn.shape[0]
    D = cotw.shape[2]
    FFD = wu.shape[1]
    rows = wc * cotw.shape[1] + nc * cotn.shape[1]
    V = pl.BlockSpec(memory_space=pltpu.VMEM)
    S = pl.BlockSpec(memory_space=pltpu.SMEM)
    A = pl.BlockSpec(memory_space=pl.ANY)
    sds = jax.ShapeDtypeStruct
    return pl.pallas_call(
        functools.partial(dec_kernel, wc, nc, devices),
        out_shape=[sds(cotw.shape, B), sds(cotn.shape, B), sds(m.shape, B), sds(wq.shape, B), sds(wo.shape, B),
                   sds(wu.shape, B), sds(wd.shape, B), sds((8, D), F)],
        in_specs=[S, S, V, V, V, V, V, A, A, A, A],
        out_specs=[V] * 8,
        scratch_shapes=[
            pltpu.VMEM(wq.shape, B), pltpu.VMEM(wo.shape, B), pltpu.VMEM(wu.shape, B), pltpu.VMEM(wd.shape, B),
            pltpu.VMEM((rows, cotw.shape[1]), B), pltpu.VMEM((rows, 128), B),
            pltpu.VMEM(m.shape, B), pltpu.VMEM(m.shape, B),
            pltpu.VMEM((rows, D), B), pltpu.VMEM((rows, D), F), pltpu.VMEM((rows, D), B), pltpu.VMEM((rows, 3 * D), B),
            pltpu.VMEM((rows, D // 2), F), pltpu.VMEM((rows, D), B), pltpu.VMEM((rows, D), F),
            pltpu.VMEM((rows, D), B), pltpu.VMEM((rows, FFD), B), pltpu.VMEM((rows, FFD), B), pltpu.VMEM((rows, D), F),
            pltpu.VMEM((rows, D), B), pltpu.VMEM((rows, 3 * D), B), pltpu.VMEM((rows, D), B),
            pltpu.VMEM(m.shape, F), pltpu.VMEM((3, 8, D), F), pltpu.SemaphoreType.DMA((4,)),
        ],
        compiler_params=pltpu.CompilerParams(vmem_limit_bytes=VMEM_LIMIT),
        name="decoder_block",
    )(shw, shn, vis, tiles, m, cotw, cotn, wq, wo, wu, wd)


ENC_HEAD = 64


def valid_keys(kind, wide_seen, narrow_seen):
    q, k = iota((128, 128), 0), iota((128, 128), 1)
    if kind == 0:
        return k < wide_seen
    return ((q // 64) == (k // 64)) & (k % 64 < narrow_seen)


def pair_mask():
    return (iota((256, 128), 0) // 128 == iota((256, 128), 1) // ENC_HEAD).astype(B)


def pair_shares(q, k2, valid):
    s2 = dot_nt(q, k2) * (ENC_HEAD ** -0.5)
    shares = []
    for h in range(2):
        s = jnp.where(valid, s2[:, 128 * h:128 * h + 128], -1e30)
        e = jnp.exp(s - jnp.max(s, axis=1, keepdims=True))
        shares.append(e / jnp.sum(e, axis=1, keepdims=True))
    return shares


def load_rows(dst, wide, narrow, wc, nc):
    dst[...] = jnp.zeros_like(dst)
    for i in range(wc):
        dst[128 * i:128 * i + wide.shape[1], :] = wide[i].astype(F)
    for i in range(nc):
        o = 128 * wc + 64 * i
        dst[o:o + narrow.shape[1], :] = narrow[i].astype(F)


def store_rows(src, wide, narrow, wc, nc):
    for i in range(wc):
        wide[i] = src[128 * i:128 * i + wide.shape[1], :]
    for i in range(nc):
        o = 128 * wc + 64 * i
        narrow[i] = src[o:o + narrow.shape[1], :]


def enc_forward_kernel(wc, nc, devices, tiles, cw, cn, wq_h, wo_h, wu_h, wd_h, we_h,
                       encw, encn, m_ref, a_ref, qkv, o_ref, x1_ref, b_ref, h_ref, slope_ref, e_ref,
                       wq, wo, wu, wd, we, x_ref, sems):
    D = wo.shape[0]
    cps = []
    for k, (src, dst) in enumerate(((wq_h, wq), (wo_h, wo), (wu_h, wu), (wd_h, wd), (we_h, we))):
        cp = pltpu.make_async_copy(src, dst, sems.at[k])
        cp.start()
        cps.append(cp)
    load_rows(x_ref, cw, cn, wc, nc)
    gain1 = spread_vector(tiles[...], 0, D, devices)
    gain2 = spread_vector(tiles[...], 1, D, devices)
    x = x_ref[...]
    a = (norm_stats(x)[0] * gain1).astype(B)
    a_ref[...] = a
    cps[0].wait()
    for k in range(0, 3 * D, D):
        qkv[:, k:k + D] = dot(a, wq[:, k:k + D]).astype(B)
    mask = pair_mask()
    groups = x_ref.shape[0] // 128
    for g in range(groups):
        rr = slice(128 * g, 128 * g + 128)
        valid = valid_keys(0 if g < wc else 1, cw.shape[1], cn.shape[1])
        for j in range(D // 128):
            q, k, v = (qkv[rr, o + 128 * j:o + 128 * j + 128] for o in (0, D, 2 * D))
            k2 = jnp.concatenate([k, k], axis=0) * mask
            v2 = jnp.concatenate([v, v], axis=0) * mask
            p2 = jnp.concatenate(pair_shares(q, k2, valid), axis=1).astype(B)
            o_ref[rr, 128 * j:128 * j + 128] = dot(p2, v2).astype(B)
    cps[1].wait()
    x1 = x_ref[...] + dot(o_ref[...], wo[...])
    x1_ref[...] = x1
    b = (norm_stats(x1)[0] * gain2).astype(B)
    b_ref[...] = b
    cps[2].wait()
    cps[3].wait()
    out = x1
    C = 512
    for k in range(0, wu.shape[1], C):
        h, slope = gelu_both(dot(b, wu[:, k:k + C]))
        h = h.astype(B)
        h_ref[:, k:k + C] = h
        slope_ref[:, k:k + C] = slope
        out = out + dot(h, wd[k:k + C, :])
    e_ref[...] = out.astype(B)
    store_rows(e_ref, encw, encn, wc, nc)
    cps[4].wait()
    m_ref[...] = dot(e_ref[...], we[...])


def encoder_forward(tiles, cw, cn, wq, wo, wu, wd, we, devices):
    wc, nc = cw.shape[0], cn.shape[0]
    D = cw.shape[2]
    FFD = wu.shape[1]
    R = 128 * wc + 128 * ((nc + 1) // 2)
    V = pl.BlockSpec(memory_space=pltpu.VMEM)
    A = pl.BlockSpec(memory_space=pl.ANY)
    sds = jax.ShapeDtypeStruct
    return pl.pallas_call(
        functools.partial(enc_forward_kernel, wc, nc, devices),
        out_shape=[sds(cw.shape, B), sds(cn.shape, B), sds((R, we.shape[1]), F), sds((R, D), B), sds((R, 3 * D), B),
                   sds((R, D), B), sds((R, D), F), sds((R, D), B), sds((R, FFD), B), sds((R, FFD), F), sds((R, D), B)],
        in_specs=[V, V, V, A, A, A, A, A],
        out_specs=[V] * 11,
        scratch_shapes=[pltpu.VMEM(w.shape, B) for w in (wq, wo, wu, wd, we)]
        + [pltpu.VMEM((R, D), F), pltpu.SemaphoreType.DMA((5,))],
        compiler_params=pltpu.CompilerParams(vmem_limit_bytes=VMEM_LIMIT),
        name="encoder_forward",
    )(tiles, cw, cn, wq, wo, wu, wd, we)


def enc_backward_kernel(wc, nc, devices, tiles, cw, cn, dm, dec_vec, a_ref, qkv, o_ref, x1_ref, b_ref, h_ref, slope_ref, e_ref,
                        wq_h, wo_h, wu_h, wd_h, we_h,
                        gradw, gradn, gq, go, gu, gd, ge, vec_ref,
                        wq, wo, wu, wd, we, x_ref, do_ref, dqkv, du, sems):
    D = wo.shape[0]
    cps = []
    for k, (src, dst) in enumerate(((we_h, we), (wd_h, wd), (wu_h, wu), (wo_h, wo), (wq_h, wq))):
        cp = pltpu.make_async_copy(src, dst, sems.at[k])
        cp.start()
        cps.append(cp)
    load_rows(x_ref, cw, cn, wc, nc)
    gain1 = spread_vector(tiles[...], 0, D, devices)
    gain2 = spread_vector(tiles[...], 1, D, devices)
    cps[0].wait()
    grad = dot_nt(dm[...], we[...])
    z = grad.astype(B)
    ge[...] = dot_tn(e_ref[...], dm[...]).astype(B)
    cps[1].wait()
    cps[2].wait()
    back = jnp.zeros_like(grad)
    C = 512
    for k in range(0, wu.shape[1], C):
        d = (slope_ref[:, k:k + C] * dot_nt(z, wd[k:k + C, :])).astype(B)
        du[:, k:k + C] = d
        back = back + dot_nt(d, wu[:, k:k + C])
        gd[k:k + C, :] = dot_tn(h_ref[:, k:k + C], z).astype(B)
        gu[:, k:k + C] = dot_tn(b_ref[...], d).astype(B)
    by_input, by_gain = norm_back(x1_ref[...], gain2, back)
    vec_ref[...] = jnp.zeros_like(vec_ref)
    vec_ref[1:2, :] = jnp.sum(by_gain, axis=0, keepdims=True)
    dx1 = grad + by_input
    y = dx1.astype(B)
    cps[3].wait()
    do_ref[...] = dot_nt(y, wo[...]).astype(B)
    go[...] = dot_tn(o_ref[...], y).astype(B)
    mask = pair_mask()
    groups = x_ref.shape[0] // 128
    scale = ENC_HEAD ** -0.5
    lane = iota((128, 128), 1)
    for g in range(groups):
        rr = slice(128 * g, 128 * g + 128)
        valid = valid_keys(0 if g < wc else 1, cw.shape[1], cn.shape[1])
        for j in range(D // 128):
            q, k, v = (qkv[rr, o + 128 * j:o + 128 * j + 128] for o in (0, D, 2 * D))
            g_o = do_ref[rr, 128 * j:128 * j + 128]
            k2 = jnp.concatenate([k, k], axis=0) * mask
            v2 = jnp.concatenate([v, v], axis=0) * mask
            shares = pair_shares(q, k2, valid)
            dp2 = dot_nt(g_o, v2)
            ds, low = [], []
            for h in range(2):
                dp = dp2[:, 128 * h:128 * h + 128]
                p = shares[h]
                ds.append((p * (dp - jnp.sum(dp * p, axis=1, keepdims=True))).astype(B))
                low.append(p.astype(B))
            dq = dot(jnp.concatenate(ds, axis=1), k2) * scale
            dk = jnp.where(lane < ENC_HEAD, dot_tn(ds[0], q), dot_tn(ds[1], q)) * scale
            dv = jnp.where(lane < ENC_HEAD, dot_tn(low[0], g_o), dot_tn(low[1], g_o))
            for o, d in ((0, dq), (D, dk), (2 * D, dv)):
                dqkv[rr, o + 128 * j:o + 128 * j + 128] = d.astype(B)
    cps[4].wait()
    for k in range(0, 3 * D, D):
        gq[:, k:k + D] = dot_tn(a_ref[...], dqkv[:, k:k + D]).astype(B)
    by_input, by_gain = norm_back(x_ref[...], gain1, dot_nt(dqkv[...], wq[...]))
    vec_ref[0:1, :] = jnp.sum(by_gain, axis=0, keepdims=True)
    DD = dec_vec.shape[1]
    vec_ref[2:3, 0:DD] = dec_vec[2:3, :]
    vec_ref[3:5, 0:DD] = dec_vec[0:2, :]
    x_ref[...] = dx1 + by_input
    store_rows(x_ref, gradw, gradn, wc, nc)


def encoder_backward(tiles, cw, cn, dm, dec_vec, saved, wq, wo, wu, wd, we, devices):
    wc, nc = cw.shape[0], cn.shape[0]
    D = cw.shape[2]
    FFD = wu.shape[1]
    R = dm.shape[0]
    V = pl.BlockSpec(memory_space=pltpu.VMEM)
    A = pl.BlockSpec(memory_space=pl.ANY)
    sds = jax.ShapeDtypeStruct
    return pl.pallas_call(
        functools.partial(enc_backward_kernel, wc, nc, devices),
        out_shape=[sds(cw.shape, F), sds(cn.shape, F)] + [sds(w.shape, B) for w in (wq, wo, wu, wd, we)] + [sds((8, D), F)],
        in_specs=[V] * 13 + [A] * 5,
        out_specs=[V] * 8,
        scratch_shapes=[pltpu.VMEM(w.shape, B) for w in (wq, wo, wu, wd, we)]
        + [pltpu.VMEM((R, D), F), pltpu.VMEM((R, D), B), pltpu.VMEM((R, 3 * D), B), pltpu.VMEM((R, FFD), B),
           pltpu.SemaphoreType.DMA((5,))],
        compiler_params=pltpu.CompilerParams(vmem_limit_bytes=VMEM_LIMIT),
        name="encoder_backward",
    )(tiles, cw, cn, dm, dec_vec, *saved, wq, wo, wu, wd, we)


ZXY = ("z", "x", "y")
ZYX = ("z", "y", "x")
XYZ = ("x", "y", "z")
YXZ = ("y", "x", "z")
ROUTES = (
    (7, XYZ), (8, YXZ), (0, ZXY), (3, ZYX), (2, ZXY), (1, ZYX), (5, ZYX), (4, ZYX), (6, ZXY),
)


def whole_tiles(shapes, devices):
    return devices % 4 == 0 and all(r % 16 == 0 and n % 256 == 0 for r, n in shapes)


def gather_all(matrices, vectors, devices):
    rows = [jnp.pad(v, (0, 128 - v.shape[0])) for v in vectors]
    packed = jnp.pad(jnp.stack(rows), ((0, 16 - len(rows)), (0, 0)))
    if not whole_tiles([m.shape for m in matrices], devices):
        got = [lax.all_gather(m, "fsdp", axis=0, tiled=True) for m in (*matrices, packed)]
        return got[:-1], got[-1]
    pieces = [(len(matrices), 0, 128, ZXY, False)]
    pieces += [(w, 0, matrices[w].shape[1] // 2, order, True) for w, order in ROUTES]
    got = all_gather(list(matrices) + [packed], pieces, devices // 4)
    return got[:-1], got[-1]


def reduce_all(grads, packed, sizes, devices):
    if not whole_tiles([(g.shape[0] // devices, g.shape[1]) for g in grads], devices):
        total = lax.psum(packed, ("fsdp", "dp"))
        shares = [
            lax.psum_scatter(lax.psum(g.astype(jnp.float32), "dp"), "fsdp", scatter_dimension=0, tiled=True)
            for g in grads
        ]
    else:
        pieces = [(w, 0, grads[w].shape[1] // 2, order) for w, order in ROUTES]
        *shares, total = reduce_scatter(grads, packed, pieces, devices // 4)
    me = lax.axis_index("fsdp")
    vectors = [lax.dynamic_slice(total[k], (me * (n // devices),), (n // devices,)) for k, n in enumerate(sizes)]
    return shares, vectors


def local(
    clips_wide, clips_narrow, visible_wide, visible_narrow, shift_wide, shift_narrow,
    enc_norm1, enc_qkv, enc_out, enc_norm2, enc_up, enc_down, embed_proj, mask_token,
    dec_norm1, dec_qkv, dec_out, dec_norm2, dec_up, dec_down, cotan_wide, cotan_narrow,
):
    devices = lax.axis_size("fsdp")
    matrices = (enc_qkv, enc_out, enc_up, enc_down, embed_proj, dec_qkv, dec_out, dec_up, dec_down)
    vectors = (enc_norm1, enc_norm2, mask_token, dec_norm1, dec_norm2)
    whole, tiles = gather_all(matrices, vectors, devices)
    enc, dec = whole[:5], whole[5:]
    shown = [jnp.pad(visible_wide, ((0, 0), (0, 128 - visible_wide.shape[1])), constant_values=-1)]
    for i in range(visible_narrow.shape[0]):
        o = 64 * (i % 2)
        shown.append(
            jnp.pad(visible_narrow[i:i + 1], ((0, 0), (o, 128 - o - visible_narrow.shape[1])), constant_values=-1)
        )
    shown = jnp.concatenate(shown, 0)
    encoded_wide, encoded_narrow, embedded, *saved = encoder_forward(tiles, clips_wide, clips_narrow, *enc, devices)
    decoded_wide, decoded_narrow, grad_embedded, *dec_grads, dec_gains = decoder(
        embedded, shown, shift_wide, shift_narrow, tiles, cotan_wide, cotan_narrow, *dec, devices
    )
    grad_wide, grad_narrow, *enc_grads, gains = encoder_backward(
        tiles, clips_wide, clips_narrow, grad_embedded, dec_gains, saved, *enc, devices
    )
    m, v = reduce_all(enc_grads + dec_grads, gains, [n.shape[0] * devices for n in vectors], devices)
    return (
        encoded_wide, encoded_narrow, decoded_wide, decoded_narrow, grad_wide, grad_narrow,
        v[0], m[0], m[1], v[1], m[2], m[3], m[4], v[2], v[3], m[5], m[6], v[4], m[7], m[8],
    )


def solution(mesh):
    clips = ("fsdp", "dp")
    matrix, vector = P("fsdp", None), P("fsdp")
    weights = (
        vector, matrix, matrix, vector, matrix, matrix, matrix, vector,
        vector, matrix, matrix, vector, matrix, matrix,
    )
    rows, pairs = P(clips, None, None), P(clips, None)
    return jax.shard_map(
        local,
        mesh=mesh,
        in_specs=(rows, rows, pairs, pairs, pairs, P(clips), *weights, rows, rows),
        out_specs=(rows,) * 6 + weights,
        check_vma=False,
    )
```

```python
import functools

import jax
import jax.numpy as jnp
from jax import lax
from jax.experimental import pallas as pl
from jax.experimental.pallas import tpu as pltpu
from jax.sharding import PartitionSpec as P

MESH = pl.DeviceIdType.MESH


def slots():
    out=[]
    for bx in (0,1):
        for by in (0,1):
            for sgn in (0,1,-1):
                if (bx,by,sgn)!=(0,0,0): out.append((bx,by,sgn))
    return out

def forwards(order,bx,by,sgn):
    differs={'x':bx,'y':by,'z':int(sgn!=0)}
    last=max([j for j,d in enumerate(order) if differs[d]],default=-1)
    dirs=[]
    for j,d in enumerate(order):
        if j>last:
            dirs += ['u','d'] if d=='z' else [d]
    if last>=0 and order[last]=='z':
        dirs.append('u' if sgn<0 else 'd')
    return dirs


TIME = 64
WIN = 4
EPS = 1e-6
F = jnp.float32
B = jnp.bfloat16
VMEM_LIMIT = 60 * 2**20


def dot(a, b):
    return lax.dot_general(a, b, (((1,), (0,)), ((), ())), preferred_element_type=F)


def dot_nt(a, b):
    return lax.dot_general(a, b, (((1,), (1,)), ((), ())), preferred_element_type=F)


def dot_tn(a, b):
    return lax.dot_general(a, b, (((0,), (0,)), ((), ())), preferred_element_type=F)


def iota(shape, dim):
    return lax.broadcasted_iota(jnp.int32, shape, dim)


def norm_stats(x):
    center = jnp.mean(x, axis=-1, keepdims=True)
    shifted = x - center
    spread = jnp.mean(shifted * shifted, axis=-1, keepdims=True)
    scale = lax.rsqrt(spread + EPS)
    return shifted * scale, scale


def norm_back(x, gain, grad):
    unit, scale = norm_stats(x)
    by_gain = grad * unit
    by_unit = grad * gain
    mean_one = jnp.mean(by_unit, axis=-1, keepdims=True)
    mean_two = jnp.mean(by_unit * unit, axis=-1, keepdims=True)
    by_input = scale * (by_unit - mean_one - unit * mean_two)
    return by_input, jnp.sum(by_gain.reshape(-1, 8, x.shape[1]), axis=0)


def gelu_both(u):
    t = 1.0 / (1.0 + (0.3275911 * 0.7071067811865476) * jnp.abs(u))
    bell = jnp.exp(-0.5 * u * u)
    poly = t * (0.127414796 + t * (-0.142248368 + t * (0.7107068705 + t * (-0.7265760135 + t * 0.5307027145))))
    tail = poly * bell
    phi = jnp.where(u < 0, tail, 1.0 - tail)
    return u * phi, phi + u * (bell * 0.3989422804014327)


def spread_vector(tiles, lane, size, devices):
    part = size // devices
    pick = (iota((128, size), 1) % part == iota((128, size), 0)).astype(B)
    wide = dot(tiles, pick)
    rows = iota((tiles.shape[0], size), 0)
    keep = rows == (iota((tiles.shape[0], size), 1) // part) * 16 + lane
    return jnp.sum(jnp.where(keep, wide, 0.0), axis=0, keepdims=True)


def lane_groups(x, op):
    lanes = iota(x.shape, 1)
    width = x.shape[1]
    for d in (1, 2, 4, 8):
        other = jnp.where((lanes & d) != 0, pltpu.roll(x, d, 1), pltpu.roll(x, width - d, 1))
        x = op(x, other)
    return x


HEAD = 32
AREA = WIN * WIN


def stack8(block, mask):
    return jnp.concatenate([block] * 8, axis=0) * mask


def dec_kernel(wc, nc, devices, shw, shn, vis, tiles, m_ref, cotw, cotn, wq_h, wo_h, wu_h, wd_h,
               outw, outn, dm_ref, gq, go, gu, gd, vec_ref,
               wq, wo, wu, wd, perm, sel, mhi, mlo, dz, r_ref, a_ref, qkv, p_ref, o_ref, x1_ref,
               b_ref, h_ref, du, dx1, do_ref, dqkv, dec, dm_acc, acc, sems):
    D = wo.shape[0]
    wide_rows = cotw.shape[1]
    narrow_rows = cotn.shape[1]
    rows = wc * wide_rows + nc * narrow_rows
    T = 256
    nt = rows // T
    wide_tiles = wc * wide_rows // T
    cps = []
    for k, (src, dst) in enumerate(((wq_h, wq), (wo_h, wo), (wu_h, wu), (wd_h, wd))):
        cp = pltpu.make_async_copy(src, dst, sems.at[k])
        cp.start()
        cps.append(cp)
    gain1 = spread_vector(tiles[...], 3, D, devices)
    gain2 = spread_vector(tiles[...], 4, D, devices)
    filler = spread_vector(tiles[...], 2, D, devices)
    mhi[...] = m_ref[...].astype(B)
    mlo[...] = (m_ref[...] - mhi[...].astype(F)).astype(B)
    dm_acc[...] = jnp.zeros_like(dm_acc)
    acc[...] = jnp.zeros_like(acc)
    clips = [(i * wide_rows, wide_rows, 8, shw[i, 0], shw[i, 1], cotw, i, i) for i in range(wc)]
    clips += [(wc * wide_rows + i * narrow_rows, narrow_rows, 4, shn[i], 0, cotn, i, wc + i) for i in range(nc)]
    for base, n, cols, s, r, cot, i, v in clips:
        for k in range(0, n, T):
            j = iota((T, 1), 0) + k
            w, q = j >> 4, j & 15
            wf = cols // WIN
            t = ((w // wf) * WIN + (q >> 2) + s) & (TIME - 1)
            f = ((w % wf) * WIN + (q & 3) + r) & (cols - 1)
            patch = t * cols + f
            where = pl.ds(base + k, T)
            hot = jnp.where(iota((T, n), 1) == patch, 1.0, 0.0).astype(B)
            perm[where, 0:n] = hot
            sel[where] = jnp.where(vis[v:v + 1, :] == patch, 1.0, 0.0).astype(B)
            dz[where] = dot(hot, cot[i]).astype(B)

    def group_rows(t):
        g = jnp.where(t < wide_tiles, t * T // wide_rows, wc + (t - wide_tiles) // 2)
        return pl.ds(pl.multiple_of(g * 128, 128), 128)

    cps[0].wait()

    @pl.loop(0, nt)
    def _(t):
        rr = pl.ds(pl.multiple_of(t * T, T), T)
        g = group_rows(t)
        s = sel[rr]
        seen = jnp.sum(s.astype(F), axis=1, keepdims=True)
        x = dot(s, mhi[g]) + dot(s, mlo[g]) + (1.0 - seen) * filler
        r_ref[rr] = x
        a = (norm_stats(x)[0] * gain1).astype(B)
        a_ref[rr] = a
        qkv[rr] = dot(a, wq[...]).astype(B)

    mask = (iota((128, 256), 0) // AREA == iota((128, 256), 1) // HEAD).astype(B)
    scale = HEAD ** -0.5
    nw = 8

    @pl.loop(0, rows // (nw * AREA))
    def _(g):
        base = pl.multiple_of(g * nw * AREA, nw * AREA)
        rr = pl.ds(base, nw * AREA)
        for a in range(D // 256):
            cq = pl.ds(a * 256, 256)
            q, k, v = qkv[rr, cq], qkv[rr, pl.ds(D + a * 256, 256)], qkv[rr, pl.ds(2 * D + a * 256, 256)]
            w16 = [slice(AREA * j, AREA * j + AREA) for j in range(nw)]
            s = jnp.concatenate([dot_nt(q[w], stack8(k[w], mask)) for w in w16], axis=0) * scale
            e = jnp.exp(s - lane_groups(s, jnp.maximum))
            p = e / lane_groups(e, jnp.add)
            p_ref[rr, pl.ds(a * 128, 128)] = p
            low = p.astype(B)
            o_ref[rr, cq] = jnp.concatenate([dot(low[w], stack8(v[w], mask)) for w in w16], axis=0).astype(B)

    for cp in cps[1:]:
        cp.wait()

    @pl.loop(0, nt)
    def _(t):
        rr = pl.ds(pl.multiple_of(t * T, T), T)
        x1 = r_ref[rr] + dot(o_ref[rr], wo[...])
        x1_ref[rr] = x1
        b = (norm_stats(x1)[0] * gain2).astype(B)
        b_ref[rr] = b
        z = dz[rr]
        out = x1
        back = jnp.zeros((T, D), F)
        C = 512
        for k in range(0, wu.shape[1], C):
            u = dot(b, wu[:, k:k + C])
            h, slope = gelu_both(u)
            h = h.astype(B)
            h_ref[rr, k:k + C] = h
            out = out + dot(h, wd[k:k + C, :])
            d = (slope * dot_nt(z, wd[k:k + C, :])).astype(B)
            du[rr, k:k + C] = d
            back = back + dot_nt(d, wu[:, k:k + C])
        dec[rr] = out.astype(B)
        by_input, by_gain = norm_back(x1, gain2, back)
        acc[1] += by_gain
        dx = z.astype(F) + by_input
        dx1[rr] = dx
        do_ref[rr] = dot_nt(dx.astype(B), wo[...]).astype(B)

    for base, n, cols, s, r, cot, i, v in clips:
        res = dot_tn(perm[base:base + n, 0:n], dec[base:base + n]).astype(B)
        if cols == 8:
            outw[i] = res
        else:
            outn[i] = res

    @pl.loop(0, rows // (nw * AREA))
    def _(g):
        base = pl.multiple_of(g * nw * AREA, nw * AREA)
        rr = pl.ds(base, nw * AREA)
        w16 = [slice(AREA * j, AREA * j + AREA) for j in range(nw)]
        for a in range(D // 256):
            cq = pl.ds(a * 256, 256)
            q, k, v = qkv[rr, cq], qkv[rr, pl.ds(D + a * 256, 256)], qkv[rr, pl.ds(2 * D + a * 256, 256)]
            go_ = do_ref[rr, cq]
            ks = [stack8(k[w], mask) for w in w16]
            qs = [stack8(q[w], mask) for w in w16]
            gs = [stack8(go_[w], mask) for w in w16]
            p = p_ref[rr, pl.ds(a * 128, 128)]
            dp = jnp.concatenate([dot_nt(go_[w], stack8(v[w], mask)) for w in w16], axis=0)
            ds = (p * (dp - lane_groups(dp * p, jnp.add))).astype(B)
            dqkv[rr, cq] = (jnp.concatenate([dot(ds[w], m) for w, m in zip(w16, ks)], axis=0) * scale).astype(B)
            s = jnp.concatenate([dot_nt(k[w], m) for w, m in zip(w16, qs)], axis=0) * scale
            s = s.reshape(nw, AREA, 128)
            e = jnp.exp(s - jnp.max(s, axis=1, keepdims=True))
            p = e / jnp.sum(e, axis=1, keepdims=True)
            dp = jnp.concatenate([dot_nt(v[w], m) for w, m in zip(w16, gs)], axis=0).reshape(nw, AREA, 128)
            ds = (p * (dp - jnp.sum(dp * p, axis=1, keepdims=True))).reshape(nw * AREA, 128).astype(B)
            p = p.reshape(nw * AREA, 128).astype(B)
            dqkv[rr, pl.ds(D + a * 256, 256)] = (jnp.concatenate([dot(ds[w], m) for w, m in zip(w16, qs)], axis=0) * scale).astype(B)
            dqkv[rr, pl.ds(2 * D + a * 256, 256)] = jnp.concatenate([dot(p[w], m) for w, m in zip(w16, gs)], axis=0).astype(B)

    @pl.loop(0, nt)
    def _(t):
        rr = pl.ds(pl.multiple_of(t * T, T), T)
        g = group_rows(t)
        by_input, by_gain = norm_back(r_ref[rr], gain1, dot_nt(dqkv[rr], wq[...]))
        acc[0] += by_gain
        dr = dx1[rr] + by_input
        s = sel[rr]
        hidden = 1.0 - jnp.sum(s.astype(F), axis=1, keepdims=True)
        acc[2] += jnp.sum((dr * hidden).reshape(-1, 8, D), axis=0)
        dm_acc[g] += dot_tn(s, dr.astype(B))

    dm_ref[...] = dm_acc[...].astype(B)
    for k in range(3):
        vec_ref[k:k + 1, :] = jnp.sum(acc[k], axis=0, keepdims=True)
    vec_ref[3:, :] = jnp.zeros((5, D), F)
    gd_step = 512

    @pl.loop(0, wd.shape[0] // gd_step)
    def _(k):
        kk = pl.ds(pl.multiple_of(k * gd_step, gd_step), gd_step)
        gd[kk, :] = dot_tn(h_ref[:, kk], dz[...]).astype(B)
        gu[:, kk] = dot_tn(b_ref[...], du[:, kk]).astype(B)

    @pl.loop(0, wq.shape[1] // 512)
    def _(k):
        kk = pl.ds(pl.multiple_of(k * 512, 512), 512)
        gq[:, kk] = dot_tn(a_ref[...], dqkv[:, kk]).astype(B)

    go[...] = dot_tn(o_ref[...], dx1[...].astype(B)).astype(B)


def decoder(m, vis, shw, shn, tiles, cotw, cotn, wq, wo, wu, wd, devices):
    wc, nc = cotw.shape[0], cotn.shape[0]
    D = cotw.shape[2]
    FFD = wu.shape[1]
    rows = wc * cotw.shape[1] + nc * cotn.shape[1]
    V = pl.BlockSpec(memory_space=pltpu.VMEM)
    S = pl.BlockSpec(memory_space=pltpu.SMEM)
    A = pl.BlockSpec(memory_space=pl.ANY)
    sds = jax.ShapeDtypeStruct
    return pl.pallas_call(
        functools.partial(dec_kernel, wc, nc, devices),
        out_shape=[sds(cotw.shape, B), sds(cotn.shape, B), sds(m.shape, B), sds(wq.shape, B), sds(wo.shape, B),
                   sds(wu.shape, B), sds(wd.shape, B), sds((8, D), F)],
        in_specs=[S, S, V, V, V, V, V, A, A, A, A],
        out_specs=[V] * 8,
        scratch_shapes=[
            pltpu.VMEM(wq.shape, B), pltpu.VMEM(wo.shape, B), pltpu.VMEM(wu.shape, B), pltpu.VMEM(wd.shape, B),
            pltpu.VMEM((rows, cotw.shape[1]), B), pltpu.VMEM((rows, 128), B),
            pltpu.VMEM(m.shape, B), pltpu.VMEM(m.shape, B),
            pltpu.VMEM((rows, D), B), pltpu.VMEM((rows, D), F), pltpu.VMEM((rows, D), B), pltpu.VMEM((rows, 3 * D), B),
            pltpu.VMEM((rows, D // 2), F), pltpu.VMEM((rows, D), B), pltpu.VMEM((rows, D), F),
            pltpu.VMEM((rows, D), B), pltpu.VMEM((rows, FFD), B), pltpu.VMEM((rows, FFD), B), pltpu.VMEM((rows, D), F),
            pltpu.VMEM((rows, D), B), pltpu.VMEM((rows, 3 * D), B), pltpu.VMEM((rows, D), B),
            pltpu.VMEM(m.shape, F), pltpu.VMEM((3, 8, D), F), pltpu.SemaphoreType.DMA((4,)),
        ],
        compiler_params=pltpu.CompilerParams(vmem_limit_bytes=VMEM_LIMIT),
        name="decoder_block",
    )(shw, shn, vis, tiles, m, cotw, cotn, wq, wo, wu, wd)


ENC_HEAD = 64


def valid_keys(kind, wide_seen, narrow_seen):
    q, k = iota((128, 128), 0), iota((128, 128), 1)
    if kind == 0:
        return k < wide_seen
    return ((q // 64) == (k // 64)) & (k % 64 < narrow_seen)


def pair_mask():
    return (iota((256, 128), 0) // 128 == iota((256, 128), 1) // ENC_HEAD).astype(B)


def pair_shares(q, k2, valid):
    s2 = dot_nt(q, k2) * (ENC_HEAD ** -0.5)
    shares = []
    for h in range(2):
        s = jnp.where(valid, s2[:, 128 * h:128 * h + 128], -1e30)
        e = jnp.exp(s - jnp.max(s, axis=1, keepdims=True))
        shares.append(e / jnp.sum(e, axis=1, keepdims=True))
    return shares


def load_rows(dst, pair, wide, narrow, wc, nc):
    dst[...] = jnp.zeros_like(dst)
    for i in range(wc):
        dst[128 * i:128 * i + wide.shape[1], :] = wide[i].astype(F)
    pair[...] = narrow[...].astype(F)
    for i in range(nc):
        o = 128 * wc + 64 * i
        dst[o:o + narrow.shape[0], :] = pair[:, i, :]


def enc_forward_kernel(wc, nc, devices, tiles, cw, cn, wq_h, wo_h, wu_h, wd_h, we_h,
                       m_ref, x_ref, a_ref, qkv, o_ref, x1_ref, b_ref, h_ref, slope_ref, e_ref,
                       wq, wo, wu, wd, we, pair, sems):
    D = wo.shape[0]
    cps = []
    for k, (src, dst) in enumerate(((wq_h, wq), (wo_h, wo), (wu_h, wu), (wd_h, wd), (we_h, we))):
        cp = pltpu.make_async_copy(src, dst, sems.at[k])
        cp.start()
        cps.append(cp)
    load_rows(x_ref, pair, cw, cn, wc, nc)
    gain1 = spread_vector(tiles[...], 0, D, devices)
    gain2 = spread_vector(tiles[...], 1, D, devices)
    x = x_ref[...]
    a = (norm_stats(x)[0] * gain1).astype(B)
    a_ref[...] = a
    cps[0].wait()
    for k in range(0, 3 * D, D):
        qkv[:, k:k + D] = dot(a, wq[:, k:k + D]).astype(B)
    mask = pair_mask()
    groups = x_ref.shape[0] // 128
    for g in range(groups):
        rr = slice(128 * g, 128 * g + 128)
        valid = valid_keys(0 if g < wc else 1, cw.shape[1], cn.shape[0])
        for j in range(D // 128):
            q, k, v = (qkv[rr, o + 128 * j:o + 128 * j + 128] for o in (0, D, 2 * D))
            k2 = jnp.concatenate([k, k], axis=0) * mask
            v2 = jnp.concatenate([v, v], axis=0) * mask
            p2 = jnp.concatenate(pair_shares(q, k2, valid), axis=1).astype(B)
            o_ref[rr, 128 * j:128 * j + 128] = dot(p2, v2).astype(B)
    cps[1].wait()
    x1 = x_ref[...] + dot(o_ref[...], wo[...])
    x1_ref[...] = x1
    b = (norm_stats(x1)[0] * gain2).astype(B)
    b_ref[...] = b
    cps[2].wait()
    cps[3].wait()
    out = x1
    C = 512
    for k in range(0, wu.shape[1], C):
        h, slope = gelu_both(dot(b, wu[:, k:k + C]))
        h = h.astype(B)
        h_ref[:, k:k + C] = h
        slope_ref[:, k:k + C] = slope
        out = out + dot(h, wd[k:k + C, :])
    e_ref[...] = out.astype(B)
    cps[4].wait()
    m_ref[...] = dot(e_ref[...], we[...])


def encoder_forward(tiles, cw, cn, wq, wo, wu, wd, we, devices):
    wc, nc = cw.shape[0], cn.shape[1]
    D = cw.shape[2]
    FFD = wu.shape[1]
    R = 128 * wc + 128 * ((nc + 1) // 2)
    V = pl.BlockSpec(memory_space=pltpu.VMEM)
    A = pl.BlockSpec(memory_space=pl.ANY)
    sds = jax.ShapeDtypeStruct
    return pl.pallas_call(
        functools.partial(enc_forward_kernel, wc, nc, devices),
        out_shape=[sds((R, we.shape[1]), F), sds((R, D), F), sds((R, D), B), sds((R, 3 * D), B),
                   sds((R, D), B), sds((R, D), F), sds((R, D), B), sds((R, FFD), B), sds((R, FFD), F), sds((R, D), B)],
        in_specs=[V, V, V, A, A, A, A, A],
        out_specs=[V] * 10,
        scratch_shapes=[pltpu.VMEM(w.shape, B) for w in (wq, wo, wu, wd, we)]
        + [pltpu.VMEM(cn.shape, F), pltpu.SemaphoreType.DMA((5,))],
        compiler_params=pltpu.CompilerParams(vmem_limit_bytes=VMEM_LIMIT),
        name="encoder_forward",
    )(tiles, cw, cn, wq, wo, wu, wd, we)


def enc_backward_kernel(wc, wide_seen, narrow_seen, devices, tiles, dm, dec_vec, x_in, a_ref, qkv, o_ref, x1_ref, b_ref, h_ref, slope_ref, e_ref,
                        wq_h, wo_h, wu_h, wd_h, we_h,
                        dx_ref, gq, go, gu, gd, ge, vec_ref,
                        wq, wo, wu, wd, we, do_ref, dqkv, du, sems):
    D = wo.shape[0]
    cps = []
    for k, (src, dst) in enumerate(((we_h, we), (wd_h, wd), (wu_h, wu), (wo_h, wo), (wq_h, wq))):
        cp = pltpu.make_async_copy(src, dst, sems.at[k])
        cp.start()
        cps.append(cp)
    gain1 = spread_vector(tiles[...], 0, D, devices)
    gain2 = spread_vector(tiles[...], 1, D, devices)
    cps[0].wait()
    grad = dot_nt(dm[...], we[...])
    z = grad.astype(B)
    ge[...] = dot_tn(e_ref[...], dm[...]).astype(B)
    cps[1].wait()
    cps[2].wait()
    back = jnp.zeros_like(grad)
    C = 512
    for k in range(0, wu.shape[1], C):
        d = (slope_ref[:, k:k + C] * dot_nt(z, wd[k:k + C, :])).astype(B)
        du[:, k:k + C] = d
        back = back + dot_nt(d, wu[:, k:k + C])
        gd[k:k + C, :] = dot_tn(h_ref[:, k:k + C], z).astype(B)
        gu[:, k:k + C] = dot_tn(b_ref[...], d).astype(B)
    by_input, by_gain = norm_back(x1_ref[...], gain2, back)
    vec_ref[...] = jnp.zeros_like(vec_ref)
    vec_ref[1:2, :] = jnp.sum(by_gain, axis=0, keepdims=True)
    dx1 = grad + by_input
    y = dx1.astype(B)
    cps[3].wait()
    do_ref[...] = dot_nt(y, wo[...]).astype(B)
    go[...] = dot_tn(o_ref[...], y).astype(B)
    mask = pair_mask()
    groups = x_in.shape[0] // 128
    scale = ENC_HEAD ** -0.5
    lane = iota((128, 128), 1)
    for g in range(groups):
        rr = slice(128 * g, 128 * g + 128)
        valid = valid_keys(0 if g < wc else 1, wide_seen, narrow_seen)
        for j in range(D // 128):
            q, k, v = (qkv[rr, o + 128 * j:o + 128 * j + 128] for o in (0, D, 2 * D))
            g_o = do_ref[rr, 128 * j:128 * j + 128]
            k2 = jnp.concatenate([k, k], axis=0) * mask
            v2 = jnp.concatenate([v, v], axis=0) * mask
            shares = pair_shares(q, k2, valid)
            dp2 = dot_nt(g_o, v2)
            ds, low = [], []
            for h in range(2):
                dp = dp2[:, 128 * h:128 * h + 128]
                p = shares[h]
                ds.append((p * (dp - jnp.sum(dp * p, axis=1, keepdims=True))).astype(B))
                low.append(p.astype(B))
            dq = dot(jnp.concatenate(ds, axis=1), k2) * scale
            dk = jnp.where(lane < ENC_HEAD, dot_tn(ds[0], q), dot_tn(ds[1], q)) * scale
            dv = jnp.where(lane < ENC_HEAD, dot_tn(low[0], g_o), dot_tn(low[1], g_o))
            for o, d in ((0, dq), (D, dk), (2 * D, dv)):
                dqkv[rr, o + 128 * j:o + 128 * j + 128] = d.astype(B)
    cps[4].wait()
    for k in range(0, 3 * D, D):
        gq[:, k:k + D] = dot_tn(a_ref[...], dqkv[:, k:k + D]).astype(B)
    by_input, by_gain = norm_back(x_in[...], gain1, dot_nt(dqkv[...], wq[...]))
    vec_ref[0:1, :] = jnp.sum(by_gain, axis=0, keepdims=True)
    DD = dec_vec.shape[1]
    vec_ref[2:3, 0:DD] = dec_vec[2:3, :]
    vec_ref[3:5, 0:DD] = dec_vec[0:2, :]
    dx_ref[...] = dx1 + by_input


def encoder_backward(tiles, counts, dm, dec_vec, saved, wq, wo, wu, wd, we, devices):
    D = wq.shape[0]
    FFD = wu.shape[1]
    R = dm.shape[0]
    V = pl.BlockSpec(memory_space=pltpu.VMEM)
    A = pl.BlockSpec(memory_space=pl.ANY)
    sds = jax.ShapeDtypeStruct
    return pl.pallas_call(
        functools.partial(enc_backward_kernel, *counts, devices),
        out_shape=[sds((R, D), F)] + [sds(w.shape, B) for w in (wq, wo, wu, wd, we)] + [sds((8, D), F)],
        in_specs=[V] * 12 + [A] * 5,
        out_specs=[V] * 7,
        scratch_shapes=[pltpu.VMEM(w.shape, B) for w in (wq, wo, wu, wd, we)]
        + [pltpu.VMEM((R, D), B), pltpu.VMEM((R, 3 * D), B), pltpu.VMEM((R, FFD), B), pltpu.SemaphoreType.DMA((5,))],
        compiler_params=pltpu.CompilerParams(vmem_limit_bytes=VMEM_LIMIT),
        name="encoder_backward",
    )(tiles, dm, dec_vec, *saved, wq, wo, wu, wd, we)


def results_kernel(wc, nc, sizes, *refs):
    me, e, dx, vec, *refs = refs
    shares, refs = refs[:9], refs[9:]
    encw, encn, gradw, gradn, *refs = refs
    outs, refs = refs[:9], refs[9:]
    vectors, (pair,) = refs[:len(sizes)], refs[len(sizes):]
    for src, wide, narrow in ((e, encw, encn), (dx, gradw, gradn)):
        for i in range(wc):
            rows = src[128 * i:128 * i + encw.shape[1], :]
            if wide is encw:
                wide[i] = rows
            else:
                wide[:, i, :] = rows
        for i in range(nc):
            o = 128 * wc + 64 * i
            pair[:, i, :] = src[o:o + narrow.shape[0], :].astype(F)
        narrow[...] = pair[...].astype(narrow.dtype)
    for src, dst in zip(shares, outs):
        dst[...] = src[...]
    width = vec.shape[1]
    for k, (n, ref) in enumerate(zip(sizes, vectors)):
        ref[...] = pltpu.roll(vec[k:k + 1, :], lax.rem(width - me[0] * n, width), 1)[:, 0:n]


def results(me, e, dx, vec, shares, sizes, wide_shape, narrow_shape):
    wc, nw, D = wide_shape
    nc, nn, _ = narrow_shape
    V = pl.BlockSpec(memory_space=pltpu.VMEM)
    S = pl.BlockSpec(memory_space=pltpu.SMEM)
    sds = jax.ShapeDtypeStruct
    out = pl.pallas_call(
        functools.partial(results_kernel, wc, nc, sizes),
        out_shape=[sds(wide_shape, B), sds((nn, nc, D), B), sds((nw, wc, D), F), sds((nn, nc, D), F)]
        + [sds(s.shape, F) for s in shares] + [sds((1, n), F) for n in sizes],
        in_specs=[S] + [V] * 12,
        out_specs=[V] * (13 + len(sizes)),
        scratch_shapes=[pltpu.VMEM((nn, nc, D), F)],
        compiler_params=pltpu.CompilerParams(vmem_limit_bytes=VMEM_LIMIT),
        name="results",
    )(me.reshape(1), e, dx, vec, *shares)
    swap = functools.partial(jnp.transpose, axes=(1, 0, 2))
    return out[0], swap(out[1]), swap(out[2]), swap(out[3]), out[4:13], [v.reshape(-1) for v in out[13:]]


def gather_ops(nz, pieces, ins, outs, send, recv, sib_send, sib_recv):
    f, c = lax.axis_index("fsdp"), lax.axis_index("dp")
    z, y, x = f // 4, (f // 2) % 2, f % 2
    xn, yn, up, dn, sib = (f + 1 - 2 * x, c), (f + 2 - 4 * y, c), (f + 4, c), (f - 4, c), (f, 1 - c)
    bar = pltpu.get_barrier_semaphore()

    def greet(dev):
        pl.semaphore_signal(bar, inc=1, device_id=dev, device_id_type=MESH)

    greet(xn)
    greet(yn)
    greet(sib)
    pl.when(z < nz - 1)(lambda: greet(up))
    pl.when(z > 0)(lambda: greet(dn))
    pl.semaphore_wait(bar, 3 + (z < nz - 1).astype(jnp.int32) + (z > 0).astype(jnp.int32))
    dest = {"x": xn, "y": yn, "u": up, "d": dn}
    there = {"x": None, "y": None, "u": z < nz - 1, "d": z > 0}
    code = {"x": 0, "y": 1, "u": 2, "d": 3}

    def columns(i, half):
        w, c0, cols, order, share = pieces[i]
        return pl.ds(pl.multiple_of(half * (ins[w].shape[1] // 2) + c0, 128) if share else c0, cols)

    def region(i, s, half):
        w = pieces[i][0]
        r = ins[w].shape[0]
        return outs[w].at[pl.ds(pl.multiple_of(s * r, r), r), columns(i, half)]

    def own(i):
        return ins[pieces[i][0]].at[:, columns(i, c)]

    def remote(i, s, src, d):
        return pltpu.make_async_remote_copy(
            src_ref=src, dst_ref=region(i, s, c), send_sem=send.at[i, s, code[d]], recv_sem=recv.at[i, s],
            device_id=dest[d], device_id_type=MESH)

    def sibling(i, s, half):
        return pltpu.make_async_remote_copy(
            src_ref=region(i, s, half), dst_ref=region(i, s, half), send_sem=sib_send.at[i, s],
            recv_sem=sib_recv.at[i, s], device_id=sib, device_id_type=MESH)

    def along(dirs, act):
        for d in dirs:
            if there[d] is None:
                act(d)
            else:
                pl.when(there[d])(lambda d=d: act(d))

    def each(h, i, act):
        for bx, by, sgn in slots():
            k = h - bx - by
            if isinstance(h, int) and not ((k == 0) if sgn == 0 else (1 <= k < nz)):
                continue
            zs = z + sgn * k
            valid = (k == 0) if sgn == 0 else (k >= 1) & (zs >= 0) & (zs < nz)
            s = zs * 4 + (y + by - 2 * by * y) * 2 + (x + bx - 2 * bx * x)
            dirs = forwards(pieces[i][3], bx, by, sgn)
            if isinstance(valid, bool):
                act(i, s, dirs)
            else:
                pl.when(valid)(lambda s=s, dirs=dirs: act(i, s, dirs))

    def start(i):
        along(forwards(pieces[i][3], 0, 0, 0), lambda d: remote(i, f, own(i), d).start())

    def step(i, s, dirs):
        remote(i, s, region(i, s, c), "x").wait_recv()
        along(dirs, lambda d: remote(i, s, region(i, s, c), d).start())
        if pieces[i][4]:
            sibling(i, s, c).start()

    def got(i, s, dirs):
        if pieces[i][4]:
            sibling(i, s, 1 - c).wait_recv()

    def sent(i, s, dirs):
        along(dirs, lambda d: remote(i, s, region(i, s, c), d).wait_send())
        if pieces[i][4]:
            sibling(i, s, c).wait_send()

    def over(act):
        def run(indices):
            @pl.loop(1, nz + 2)
            def _(h):
                for i in indices:
                    each(h, i, act)
        return run

    def finish(indices):
        for i in indices:
            along(forwards(pieces[i][3], 0, 0, 0), lambda d: remote(i, f, own(i), d).wait_send())
        over(sent)(indices)

    def level(h, indices):
        for i in indices:
            each(h, i, step)

    return start, level, over(got), finish


def gather_encode_kernel(wc, nc, nz, pieces, early, late, nw, *refs):
    devices = 4 * nz
    ins, (cw, cn), refs = refs[:nw], refs[nw:nw + 2], refs[nw + 2:]
    outs, refs = refs[:nw], refs[nw:]
    m_ref, x_ref, a_ref, qkv, o_ref, x1_ref, b_ref, h_ref, slope_ref, e_ref, *refs = refs
    wq, wo, wu, wd, we, tiles, sum_ref, pair, send, recv, sib_send, sib_recv, loc, sems = refs
    D = wo.shape[0]
    start, level, arrived, finish = gather_ops(nz, pieces, ins, outs, send, recv, sib_send, sib_recv)
    for i in early:
        start(i)
    locals_ = []
    for w in range(nw):
        r = ins[w].shape[0]
        cp = pltpu.make_async_copy(ins[w], outs[w].at[pl.ds(pl.multiple_of(lax.axis_index("fsdp") * r, r), r)], loc.at[w])
        cp.start()
        locals_.append(cp)
    load_rows(x_ref, pair, cw, cn, wc, nc)
    last = nz + 1

    for h in range(1, last + 1):
        level(h, early)
        if h == last - 2:
            for i in late:
                start(i)
        if h == last - 1:
            level(1, late)
    for cp in locals_:
        cp.wait()
    loads = []
    for k, (w, dst) in enumerate(((nw - 1, tiles), (0, wq), (1, wo), (2, wu), (3, wd), (4, we))):
        arrived([i for i in early if pieces[i][0] == w])
        cp = pltpu.make_async_copy(outs[w], dst, sems.at[k])
        cp.start()
        loads.append(cp)
    rest = [(h, i) for h in range(2, last + 1) for i in late]
    parts = 3 + 2 + 1 + wu.shape[1] // 512
    done = [0, 0]

    def turn():
        done[0] += 1
        upto = min(len(rest), -(-len(rest) * done[0] // parts))
        for h, i in rest[done[1]:upto]:
            level(h, [i])
        done[1] = upto

    loads[0].wait()
    gain1 = spread_vector(tiles[...], 0, D, devices)
    gain2 = spread_vector(tiles[...], 1, D, devices)
    x = x_ref[...]
    a = (norm_stats(x)[0] * gain1).astype(B)
    a_ref[...] = a
    loads[1].wait()
    for k in range(0, 3 * D, D):
        qkv[:, k:k + D] = dot(a, wq[:, k:k + D]).astype(B)
        turn()
    mask = pair_mask()
    groups = x_ref.shape[0] // 128
    for g in range(groups):
        rr = slice(128 * g, 128 * g + 128)
        valid = valid_keys(0 if g < wc else 1, cw.shape[1], cn.shape[0])
        for j in range(D // 128):
            q, k, v = (qkv[rr, o + 128 * j:o + 128 * j + 128] for o in (0, D, 2 * D))
            k2 = jnp.concatenate([k, k], axis=0) * mask
            v2 = jnp.concatenate([v, v], axis=0) * mask
            p2 = jnp.concatenate(pair_shares(q, k2, valid), axis=1).astype(B)
            o_ref[rr, 128 * j:128 * j + 128] = dot(p2, v2).astype(B)
        turn()
    loads[2].wait()
    x1 = x_ref[...] + dot(o_ref[...], wo[...])
    x1_ref[...] = x1
    b = (norm_stats(x1)[0] * gain2).astype(B)
    b_ref[...] = b
    turn()
    loads[3].wait()
    loads[4].wait()
    sum_ref[...] = x1
    C = 512
    for k in range(0, wu.shape[1], C):
        h, slope = gelu_both(dot(b_ref[...], wu[:, k:k + C]))
        h = h.astype(B)
        h_ref[:, k:k + C] = h
        slope_ref[:, k:k + C] = slope
        sum_ref[...] += dot(h, wd[k:k + C, :])
        turn()
    e_ref[...] = sum_ref[...].astype(B)
    loads[5].wait()
    m_ref[...] = dot(e_ref[...], we[...])
    for h, i in rest[done[1]:]:
        level(h, [i])
    arrived(late)
    finish(early + late)


def gather_encode(shards, pieces, early, late, cw, cn, nz, cid=1):
    nw, npc, n = len(shards), len(pieces), 4 * nz
    wc, nc, D = cw.shape[0], cn.shape[1], cw.shape[2]
    R = 128 * wc + 128 * ((nc + 1) // 2)
    V = pl.BlockSpec(memory_space=pltpu.VMEM)
    A = pl.BlockSpec(memory_space=pl.ANY)
    sds = jax.ShapeDtypeStruct
    whole = [sds((s.shape[0] * n, s.shape[1]), s.dtype) for s in shards]
    FFD, DD = shards[2].shape[1], shards[4].shape[1]
    dma = pltpu.SemaphoreType.DMA
    out = pl.pallas_call(
        functools.partial(gather_encode_kernel, wc, nc, nz, pieces, early, late, nw),
        out_shape=whole + [sds((R, DD), F), sds((R, D), F), sds((R, D), B), sds((R, 3 * D), B), sds((R, D), B), sds((R, D), F),
                           sds((R, D), B), sds((R, FFD), B), sds((R, FFD), F), sds((R, D), B)],
        in_specs=[A] * nw + [V, V],
        out_specs=[A] * nw + [V] * 10,
        scratch_shapes=[pltpu.VMEM(w.shape, B) for w in whole[:5]] + [
            pltpu.VMEM(whole[-1].shape, B), pltpu.VMEM((R, D), F), pltpu.VMEM(cn.shape, F),
            dma((npc, n, 4)), dma((npc, n)), dma((npc, n)), dma((npc, n)), dma((nw,)), dma((6,))],
        compiler_params=pltpu.CompilerParams(collective_id=cid, has_side_effects=True, vmem_limit_bytes=VMEM_LIMIT),
        name="gather_and_encode",
    )(*shards, cw, cn)
    return out[:nw], out[nw:]


def slot_count(order, d, nz):
    size = {"x": 2, "y": 2, "z": nz}
    k = 1
    for e in order[:order.index("z" if d in "ud" else d)]:
        k *= size[e]
    return k * (nz + 1) if d in "ud" else k


def slot_index(order, d, nz, pos):
    size = {"x": 2, "y": 2, "z": nz}
    k = 0
    for e in order[:order.index("z" if d in "ud" else d)]:
        k = k * size[e] + pos[e]
    return k * (nz + 1) + pos["z"] + (1 if d == "d" else 0) if d in "ud" else k


def parent(order, bx, by, sgn):
    differs = {"x": bx, "y": by, "z": int(sgn != 0)}
    last = max(j for j, d in enumerate(order) if differs[d])
    if order[last] == "z":
        return "d" if sgn < 0 else "u"
    return order[last]


def reduce_ops(nz, pieces, rows, mine, other, sibb, rbuf, res, outs, sib_send, sib_recv, send, recv, res_sem, res_send, res_recv):
    f, c = lax.axis_index("fsdp"), lax.axis_index("dp")
    z, y, x = f // 4, (f // 2) % 2, f % 2
    bits = (nz * 4).bit_length() - 1

    def flip(b):
        return f + (1 << b) * (1 - 2 * ((f // (1 << b)) % 2))

    xn, yn, up, dn, sib = (flip(0), c), (flip(1), c), (f + 4, c), (f - 4, c), (f, 1 - c)
    bar = pltpu.get_barrier_semaphore()

    def greet(dev):
        pl.semaphore_signal(bar, inc=1, device_id=dev, device_id_type=MESH)

    greet(xn)
    greet(yn)
    greet(sib)
    pl.when(z < nz - 1)(lambda: greet(up))
    pl.when(z > 0)(lambda: greet(dn))
    far = range(3, bits)
    for b in far:
        greet((flip(b), c))
    pl.semaphore_wait(bar, 3 + len(far) + (z < nz - 1).astype(jnp.int32) + (z > 0).astype(jnp.int32))
    dest = {"x": xn, "y": yn, "u": up, "d": dn}
    there = {"u": z < nz - 1, "d": z > 0}
    opposite = {"u": "d", "d": "u", "x": "x", "y": "y"}
    kind = {"x": 0, "y": 1, "u": 2, "d": 2}

    def give(w):
        return pltpu.make_async_remote_copy(
            src_ref=other[w], dst_ref=sibb[w], send_sem=sib_send.at[w], recv_sem=sib_recv.at[w],
            device_id=sib, device_id_type=MESH)

    def cols(i):
        return pl.ds(pieces[i][1], pieces[i][2])

    def message(i, s, pos, d):
        w, order, b = pieces[i][0], pieces[i][3], kind[d]
        r = rows[w]
        q = slot_index(order, opposite[d], nz, pos)
        return pltpu.make_async_remote_copy(
            src_ref=mine[w].at[pl.ds(pl.multiple_of(s * r, r), r), cols(i)], dst_ref=rbuf[i][b].at[q],
            send_sem=send.at[i, s], recv_sem=recv.at[i, b, q], device_id=dest[d], device_id_type=MESH)

    def arrival(i, pos, d):
        b = kind[d]
        q = slot_index(pieces[i][3], d, nz, pos)
        return pltpu.make_async_remote_copy(
            src_ref=rbuf[i][b].at[q], dst_ref=rbuf[i][b].at[q], send_sem=send.at[i, 0],
            recv_sem=recv.at[i, b, q], device_id=sib, device_id_type=MESH)

    def add(i, s, pos, children, final):
        w, order = pieces[i][0], pieces[i][3]
        r = rows[w]
        ks = [(kind[d], slot_index(order, d, nz, pos)) for d in children]

        @pl.loop(0, r // 16)
        def _(k):
            rr = pl.ds(pl.multiple_of(k * 16, 16), 16)
            gr = pl.ds(pl.multiple_of(s * r + k * 16, 16), 16)
            t = mine[w][gr, cols(i)].astype(F) + sibb[w][gr, cols(i)].astype(F)
            for b, q in ks:
                t = t + rbuf[i][b][q, rr].astype(F)
            if final:
                res[w][rr, cols(i)] = t
            else:
                mine[w][gr, cols(i)] = t.astype(B)

    def gather_children(i, s, pos, children, final):
        sure = [d for d in children if d in "xy"]
        maybe = [d for d in children if d in "ud"]
        for d in sure:
            arrival(i, pos, d).wait_recv()
        for d in maybe:
            pl.when(there[d])(lambda d=d: arrival(i, pos, d).wait_recv())
        if not maybe:
            add(i, s, pos, sure, final)
        elif len(maybe) == 1:
            pl.when(there[maybe[0]])(lambda: add(i, s, pos, sure + maybe, final))
            pl.when(jnp.logical_not(there[maybe[0]]))(lambda: add(i, s, pos, sure, final))
        else:
            u, d = there["u"], there["d"]
            pl.when(u & d)(lambda: add(i, s, pos, sure + ["u", "d"], final))
            pl.when(u & jnp.logical_not(d))(lambda: add(i, s, pos, sure + ["u"], final))
            pl.when(jnp.logical_not(u) & d)(lambda: add(i, s, pos, sure + ["d"], final))
            if nz == 1:
                add(i, s, pos, sure, final)

    def each(h, i, leaf, act):
        order = pieces[i][3]
        for bx, by, sgn in slots():
            children = forwards(order, bx, by, sgn)
            if leaf is not None and (len(children) == 0) != leaf:
                continue
            k = h - bx - by
            if isinstance(h, int) and not ((k == 0) if sgn == 0 else (1 <= k < nz)):
                continue
            zs = z + sgn * k
            valid = (k == 0) if sgn == 0 else (k >= 1) & (zs >= 0) & (zs < nz)
            pos = {"x": x + bx - 2 * bx * x, "y": y + by - 2 * by * y, "z": zs}
            s = zs * 4 + pos["y"] * 2 + pos["x"]
            p = parent(order, bx, by, sgn)
            if isinstance(valid, bool):
                act(i, s, pos, children, p)
            else:
                pl.when(valid)(lambda s=s, pos=pos, children=children, p=p: act(i, s, pos, children, p))

    def work(i, s, pos, children, p):
        gather_children(i, s, pos, children, False)
        message(i, s, pos, p).start()

    def leaves(h, indices):
        for i in indices:
            each(h, i, True, work)

    def nodes(h, indices):
        for i in indices:
            each(h, i, False, work)

    def out_copy(w):
        n = outs[w].shape[1] // 2
        return pltpu.make_async_copy(res[w], outs[w].at[:, pl.ds(pl.multiple_of(c * n, 128), n)], res_sem.at[w])

    def out_sib(w, half):
        n = outs[w].shape[1] // 2
        return pltpu.make_async_remote_copy(
            src_ref=res[w], dst_ref=outs[w].at[:, pl.ds(pl.multiple_of(half * n, 128), n)], send_sem=res_send.at[w],
            recv_sem=res_recv.at[w], device_id=sib, device_id_type=MESH)

    def total(w):
        for i, piece in enumerate(pieces):
            if piece[0] == w:
                gather_children(i, f, {"x": x, "y": y, "z": z}, forwards(piece[3], 0, 0, 0), True)
        out_sib(w, c).start()
        out_copy(w).start()

    def sent(indices):
        def act(i, s, pos, children, p):
            message(i, s, pos, p).wait_send()

        @pl.loop(0, nz + 1)
        def _(q):
            for i in indices:
                each(nz + 1 - q, i, None, act)

    def finish(ws):
        for w in ws:
            give(w).wait_send()
            out_copy(w).wait()
            out_sib(w, c).wait_send()
            out_sib(w, 1 - c).wait_recv()

    return flip, give, leaves, nodes, total, sent, finish


def encode_back_reduce_kernel(wc, wide_seen, narrow_seen, nz, routes, *refs):
    devices = 4 * nz
    (tiles, x_ref, dm, dec_vec, e_ref, b_ref, x1_ref, o_ref, qkv, a_ref, *refs) = refs
    h_h, slope_h, we_h, wd_h, wu_h, wo_h, wq_h, *refs = refs
    dec_g, refs = refs[:4], refs[4:]
    (dx_ref, vec_out, *refs) = refs
    outs, refs = refs[:9], refs[9:]
    (we, wo, wq, wd2, wu2, h2, slope2, dx1_ref, z_ref, do_ref, dqkv, *refs) = refs
    mine, refs = refs[:9], refs[9:]
    enc_other, refs = refs[:5], refs[5:]
    sibb, refs = refs[:9], refs[9:]
    res, refs = refs[:9], refs[9:]
    npc = len(routes)
    rbuf, refs = [refs[3 * i:3 * i + 3] for i in range(npc)], refs[3 * npc:]
    (vbuf, wsem, dsem, sib_send, sib_recv, send, recv, res_sem, res_send, res_recv, vsend, vrecv) = refs
    c = lax.axis_index("dp")
    D = wo.shape[0]
    n_up = mine[2].shape[1]
    rows = [m.shape[0] // devices for m in mine]

    def half(ref, h):
        n = ref.shape[1] // 2
        return ref.at[:, pl.ds(pl.multiple_of(h * n, 128), n)]

    other = list(enc_other) + [half(g, 1 - c) for g in dec_g]
    flip, give, leaves, nodes, total, sent, finish = reduce_ops(
        nz, routes, rows, mine, other, sibb, rbuf, res, outs, sib_send, sib_recv, send, recv, res_sem, res_send, res_recv)
    dec_ws = [5, 6, 7, 8]
    for w in dec_ws:
        give(w).start()
    takes = [pltpu.make_async_copy(half(dec_g[w - 5], c), mine[w], dsem.at[w - 5]) for w in dec_ws]
    for t in takes:
        t.start()
    loads = [pltpu.make_async_copy(s, d, wsem.at[k]) for k, (s, d) in enumerate(((we_h, we), (wo_h, wo), (wq_h, wq)))]
    C = 512
    chunks = 2 * n_up // C

    def chunk(j):
        h = (1 - c) if j < chunks // 2 else c
        return pl.multiple_of(h * n_up + (j % (chunks // 2)) * C, 128)

    def feed(j):
        k = chunk(j)
        return (pltpu.make_async_copy(wd_h.at[pl.ds(k, C)], wd2.at[j % 2], wsem.at[3 + j % 2]),
                pltpu.make_async_copy(wu_h.at[:, pl.ds(k, C)], wu2.at[j % 2], wsem.at[5 + j % 2]),
                pltpu.make_async_copy(h_h.at[:, pl.ds(k, C)], h2.at[j % 2], wsem.at[7 + j % 2]),
                pltpu.make_async_copy(slope_h.at[:, pl.ds(k, C)], slope2.at[j % 2], wsem.at[9 + j % 2]))

    loads[0].start()
    for j in (0, 1):
        for cp in feed(j):
            cp.start()
    loads[1].start()
    loads[2].start()
    gain1 = spread_vector(tiles[...], 0, D, devices)
    gain2 = spread_vector(tiles[...], 1, D, devices)
    def own_cols(w):
        n = mine[w].shape[1]
        return pl.ds(pl.multiple_of(c * n, 128), n), pl.ds(pl.multiple_of((1 - c) * n, 128), n)

    sets = {"D": dec_ws, "F": [3, 2, 4], "O": [1], "Q": [0]}
    members = {s: [i for i, p in enumerate(routes) if p[0] in ws] for s, ws in sets.items()}
    kept = {}

    def first():
        loads[0].wait()
        grad = dot_nt(dm[...], we[...])
        dx1_ref[...] = grad
        z_ref[...] = grad.astype(B)
        own, rest = own_cols(4)
        enc_other[4][...] = dot_tn(e_ref[...], dm[:, rest]).astype(B)
        mine[4][...] = dot_tn(e_ref[...], dm[:, own]).astype(B)
        give(4).start()
        kept["back"] = jnp.zeros_like(grad)

    def feed_forward(j):
        own, rest = own_cols(3)
        for cp in feed(j):
            cp.wait()
        kk = pl.ds(chunk(j), C)
        d = (slope2[j % 2] * dot_nt(z_ref[...], wd2[j % 2])).astype(B)
        kept["back"] = kept["back"] + dot_nt(d, wu2[j % 2])
        hk = h2[j % 2]
        enc_other[3][kk, :] = dot_tn(hk, z_ref[:, rest]).astype(B)
        mine[3][kk, :] = dot_tn(hk, z_ref[:, own]).astype(B)
        g = dot_tn(b_ref[...], d).astype(B)
        at = (j % (chunks // 2)) * C
        if j < chunks // 2:
            enc_other[2][:, at:at + C] = g
        else:
            mine[2][:, at:at + C] = g
        if j == chunks // 2 - 1:
            give(2).start()
        if j == chunks - 1:
            give(3).start()
        if j + 2 < chunks:
            for cp in feed(j + 2):
                cp.start()

    def project():
        by_input, by_gain = norm_back(x1_ref[...], gain2, kept.pop("back"))
        vbuf[0, 0] = jnp.zeros_like(vbuf[0, 0])
        vbuf[0, 0, 1:2, :] = jnp.sum(by_gain, axis=0, keepdims=True)
        dx1_ref[...] += by_input
        z_ref[...] = dx1_ref[...].astype(B)
        loads[1].wait()
        do_ref[...] = dot_nt(z_ref[...], wo[...]).astype(B)
        own, rest = own_cols(1)
        enc_other[1][...] = dot_tn(o_ref[...], z_ref[:, rest]).astype(B)
        mine[1][...] = dot_tn(o_ref[...], z_ref[:, own]).astype(B)
        give(1).start()

    def attend(part):
        mask = pair_mask()
        groups = x_ref.shape[0] // 128
        scale = ENC_HEAD ** -0.5
        lane = iota((128, 128), 1)
        for g in range(groups):
            if g * 2 // groups != part:
                continue
            rr = slice(128 * g, 128 * g + 128)
            valid = valid_keys(0 if g < wc else 1, wide_seen, narrow_seen)
            for j in range(D // 128):
                q, k, v = (qkv[rr, o + 128 * j:o + 128 * j + 128] for o in (0, D, 2 * D))
                g_o = do_ref[rr, 128 * j:128 * j + 128]
                k2 = jnp.concatenate([k, k], axis=0) * mask
                v2 = jnp.concatenate([v, v], axis=0) * mask
                shares = pair_shares(q, k2, valid)
                dp2 = dot_nt(g_o, v2)
                ds, low = [], []
                for h in range(2):
                    dp = dp2[:, 128 * h:128 * h + 128]
                    p = shares[h]
                    ds.append((p * (dp - jnp.sum(dp * p, axis=1, keepdims=True))).astype(B))
                    low.append(p.astype(B))
                dq = dot(jnp.concatenate(ds, axis=1), k2) * scale
                dk = jnp.where(lane < ENC_HEAD, dot_tn(ds[0], q), dot_tn(ds[1], q)) * scale
                dv = jnp.where(lane < ENC_HEAD, dot_tn(low[0], g_o), dot_tn(low[1], g_o))
                for o, d in ((0, dq), (D, dk), (2 * D, dv)):
                    dqkv[rr, o + 128 * j:o + 128 * j + 128] = d.astype(B)

    def mix():
        own, rest = own_cols(0)
        enc_other[0][...] = dot_tn(a_ref[...], dqkv[:, rest]).astype(B)
        give(0).start()
        mine[0][...] = dot_tn(a_ref[...], dqkv[:, own]).astype(B)

    bits = devices.bit_length() - 1

    def vcopy(k):
        return pltpu.make_async_remote_copy(
            src_ref=vbuf.at[0, k], dst_ref=vbuf.at[1, k], send_sem=vsend.at[k], recv_sem=vrecv.at[k],
            device_id=(lax.axis_index("fsdp"), 1 - c) if k == 0 else (flip(k - 1), c), device_id_type=MESH)

    def vstep(k):
        vcopy(k).wait()
        vbuf[0, k + 1] = vbuf[0, k] + vbuf[1, k]
        if k < bits:
            vcopy(k + 1).start()

    def last():
        loads[2].wait()
        by_input, by_gain = norm_back(x_ref[...], gain1, dot_nt(dqkv[...], wq[...]))
        vbuf[0, 0, 0:1, :] = jnp.sum(by_gain, axis=0, keepdims=True)
        DD = dec_vec.shape[1]
        vbuf[0, 0, 2:3, 0:DD] = dec_vec[2:3, :]
        vbuf[0, 0, 3:5, 0:DD] = dec_vec[0:2, :]
        vcopy(0).start()
        dx_ref[...] = dx1_ref[...] + by_input

    compute = [first] + [functools.partial(feed_forward, j) for j in range(chunks)] + [project]
    compute += [functools.partial(attend, 0), functools.partial(attend, 1), mix, last]

    def ready(s):
        if s == "D":
            for t in takes:
                t.wait()
        for w in sets[s]:
            give(w).wait_recv()

    vectors = []
    for token in schedule(nz + 1, len(compute)):
        if token[0] == "C":
            compute[token[1]]()
            if token[1] == len(compute) - 1:
                vectors = list(range(bits + 1))
        elif token[0] == "R":
            ready(token[1])
        elif token[0] == "L":
            leaves(token[1], members[token[2]])
        elif token[0] == "N":
            nodes(token[1], members[token[2]])
        else:
            for w in sets[token[1]]:
                total(w)
        if vectors and token[0] == "N":
            vstep(vectors.pop(0))
    for k in vectors:
        vstep(k)
    vec_out[...] = vbuf[0, bits + 1]
    sent(range(npc))
    finish(range(9))


def schedule(top, steps):
    if (top, steps) == (5, 12):
        return list(SCHEDULE)
    tokens = [("C", k) for k in range(steps)] + [("R", s) for s in "DFOQ"]
    tokens += [("L", top, s) for s in "DFOQ"]
    for h in range(top, 0, -1):
        tokens += [("N", h, s) for s in "DFOQ"]
        tokens += [("L", h - 1, s) for s in "DFOQ"] if h > 1 else []
    return tokens + [("T", s) for s in "DFOQ"]


def encode_back_reduce(tiles, counts, dm, dec_vec, saved, enc, dec_grads, routes, nz, cid=2):
    R = dm.shape[0]
    n = 4 * nz
    bits = n.bit_length() - 1
    x, a, qkv, o, x1, b, h, slope, e = saved
    wq, wo, wu, wd, we = enc
    D = wq.shape[0]
    grads = [*enc, *dec_grads]
    shards = [(g.shape[0] // n, g.shape[1]) for g in grads]
    V = pl.BlockSpec(memory_space=pltpu.VMEM)
    A = pl.BlockSpec(memory_space=pl.ANY)
    sds = jax.ShapeDtypeStruct
    dma = pltpu.SemaphoreType.DMA
    most = 1
    rbuf = []
    for w, c0, cols, order in routes:
        for d in "xyu":
            k = slot_count(order, d, nz)
            most = max(most, k)
            rbuf.append(pltpu.VMEM((k, shards[w][0], cols), B))
    npc = len(routes)
    halves = [pltpu.VMEM((g.shape[0], g.shape[1] // 2), B) for g in grads]
    C = 512
    out = pl.pallas_call(
        functools.partial(encode_back_reduce_kernel, *counts, nz, routes),
        out_shape=[sds((R, D), F), sds((8, D), F)] + [sds(s, F) for s in shards],
        in_specs=[V] * 10 + [A] * 11,
        out_specs=[V] * 2 + [A] * 9,
        scratch_shapes=[
            pltpu.VMEM(we.shape, B), pltpu.VMEM(wo.shape, B), pltpu.VMEM(wq.shape, B),
            pltpu.VMEM((2, C, D), B), pltpu.VMEM((2, D, C), B), pltpu.VMEM((2, R, C), B), pltpu.VMEM((2, R, C), F),
            pltpu.VMEM((R, D), F), pltpu.VMEM((R, D), B), pltpu.VMEM((R, D), B),
            pltpu.VMEM((R, 3 * D), B),
        ] + halves + halves[:5] + halves + [pltpu.VMEM((s[0], s[1] // 2), F) for s in shards] + rbuf + [
            pltpu.VMEM((2, bits + 2, 8, D), F), dma((11,)), dma((4,)), dma((9,)), dma((9,)), dma((npc, n)),
            dma((npc, 3, most)), dma((9,)), dma((9,)), dma((9,)), dma((bits + 1,)), dma((bits + 1,))],
        compiler_params=pltpu.CompilerParams(collective_id=cid, has_side_effects=True, vmem_limit_bytes=63 * 2**20),
        name="encoder_backward_and_reduce",
    )(tiles, x, dm, dec_vec, e, b, x1, o, qkv, a, h, slope, we, wd, wu, wo, wq, *dec_grads)
    return out[0], out[1], out[2:]


ZXY = ("z", "x", "y")
ZYX = ("z", "y", "x")
XYZ = ("x", "y", "z")
YXZ = ("y", "x", "z")
GATHER_EARLY = ((0, XYZ), (2, ZXY), (3, ZYX), (1, ZYX), (4, ZXY))
GATHER_LATE = ((5, XYZ), (7, ZXY), (8, ZYX), (6, ZXY))
REDUCE = ((5, XYZ), (7, ZXY), (8, ZYX), (6, ZXY), (3, ZYX), (2, ZXY), (4, ZXY), (1, ZYX), (0, XYZ))
SCHEDULE = (
    ("C", 0), ("C", 1), ("C", 2), ("C", 3), ("R", "D"), ("L", 5, "D"), ("N", 5, "D"), ("L", 4, "D"), ("C", 4),
    ("N", 4, "D"), ("L", 3, "D"), ("C", 5), ("C", 6), ("N", 3, "D"), ("C", 7), ("L", 2, "D"), ("C", 8),
    ("N", 2, "D"), ("R", "F"), ("C", 9), ("L", 1, "D"), ("N", 5, "F"), ("C", 10), ("N", 1, "D"), ("R", "O"),
    ("L", 5, "O"), ("L", 5, "F"), ("L", 4, "O"), ("L", 4, "F"), ("L", 3, "F"), ("R", "Q"), ("L", 5, "Q"),
    ("N", 5, "Q"), ("N", 4, "Q"), ("N", 5, "O"), ("L", 4, "Q"), ("L", 3, "Q"), ("N", 4, "F"), ("L", 3, "O"),
    ("N", 4, "O"), ("L", 2, "F"), ("N", 3, "Q"), ("L", 2, "Q"), ("N", 2, "Q"), ("L", 2, "O"), ("L", 1, "O"),
    ("N", 3, "F"), ("N", 3, "O"), ("N", 1, "Q"), ("C", 11), ("T", "D"), ("L", 1, "Q"), ("N", 2, "F"),
    ("N", 2, "O"), ("L", 1, "F"), ("N", 1, "F"), ("N", 1, "O"), ("T", "Q"), ("T", "F"), ("T", "O"),
)


def whole_tiles(shards, devices):
    return devices % 4 == 0 and all(s.shape[0] % 16 == 0 and s.shape[1] % 256 == 0 for s in shards)


def local(
    clips_wide, clips_narrow, visible_wide, visible_narrow, shift_wide, shift_narrow,
    enc_norm1, enc_qkv, enc_out, enc_norm2, enc_up, enc_down, embed_proj, mask_token,
    dec_norm1, dec_qkv, dec_out, dec_norm2, dec_up, dec_down, cotan_wide, cotan_narrow,
):
    devices = lax.axis_size("fsdp")
    matrices = [enc_qkv, enc_out, enc_up, enc_down, embed_proj, dec_qkv, dec_out, dec_up, dec_down]
    vectors = [enc_norm1, enc_norm2, mask_token, dec_norm1, dec_norm2]
    packed = jnp.stack([jnp.pad(v, (0, 128 - v.shape[0])) for v in vectors])
    packed = jnp.pad(packed, ((0, 16 - len(vectors)), (0, 0)))
    shown = [jnp.pad(visible_wide, ((0, 0), (0, 128 - visible_wide.shape[1])), constant_values=-1)]
    for i in range(visible_narrow.shape[0]):
        o = 64 * (i % 2)
        shown.append(
            jnp.pad(visible_narrow[i:i + 1], ((0, 0), (o, 128 - o - visible_narrow.shape[1])), constant_values=-1)
        )
    shown = jnp.concatenate(shown, 0)
    narrow = jnp.transpose(clips_narrow, (1, 0, 2))
    counts = (clips_wide.shape[0], clips_wide.shape[1], clips_narrow.shape[1])
    direct = whole_tiles(matrices, devices)
    if direct:
        pieces = [(len(matrices), 0, 128, ZXY, False)]
        pieces += [(w, 0, matrices[w].shape[1] // 2, order, True) for w, order in GATHER_EARLY + GATHER_LATE]
        early = list(range(1 + len(GATHER_EARLY)))
        late = list(range(len(early), len(pieces)))
        whole, (embedded, *saved) = gather_encode(
            matrices + [packed], pieces, early, late, clips_wide, narrow, devices // 4
        )
    else:
        whole = [lax.all_gather(m, "fsdp", axis=0, tiled=True) for m in (*matrices, packed)]
        embedded, *saved = encoder_forward(whole[9], clips_wide, narrow, *whole[:5], devices)
    enc, dec, tiles = whole[:5], whole[5:9], whole[9]
    decoded_wide, decoded_narrow, grad_embedded, *dec_grads, gains = decoder(
        embedded, shown, shift_wide, shift_narrow, tiles, cotan_wide, cotan_narrow, *dec, devices
    )
    if direct:
        routes = [(w, 0, matrices[w].shape[1] // 2, order) for w, order in REDUCE]
        grad_rows, gains, shares = encode_back_reduce(
            tiles, counts, grad_embedded, gains, saved, enc, dec_grads, routes, devices // 4
        )
    else:
        grad_rows, *enc_grads, gains = encoder_backward(
            tiles, counts, grad_embedded, gains, saved, *enc, devices
        )
        gains = lax.psum(gains, ("fsdp", "dp"))
        shares = [
            lax.psum_scatter(lax.psum(g.astype(F), "dp"), "fsdp", scatter_dimension=0, tiled=True)
            for g in enc_grads + dec_grads
        ]
    encoded_wide, encoded_narrow, grad_wide, grad_narrow, m, v = results(
        lax.axis_index("fsdp"), saved[-1], grad_rows, gains, shares, [v.shape[0] for v in vectors],
        clips_wide.shape, clips_narrow.shape,
    )
    return (
        encoded_wide, encoded_narrow, decoded_wide, decoded_narrow, grad_wide, grad_narrow,
        v[0], m[0], m[1], v[1], m[2], m[3], m[4], v[2], v[3], m[5], m[6], v[4], m[7], m[8],
    )


def solution(mesh):
    clips = ("fsdp", "dp")
    matrix, vector = P("fsdp", None), P("fsdp")
    weights = (
        vector, matrix, matrix, vector, matrix, matrix, matrix, vector,
        vector, matrix, matrix, vector, matrix, matrix,
    )
    rows, pairs = P(clips, None, None), P(clips, None)
    return jax.shard_map(
        local,
        mesh=mesh,
        in_specs=(rows, rows, pairs, pairs, pairs, P(clips), *weights, rows, rows),
        out_specs=(rows,) * 6 + weights,
        check_vma=False,
    )
```

```python
import functools

import jax
import jax.numpy as jnp
from jax import lax
from jax.experimental import pallas as pl
from jax.experimental.pallas import tpu as pltpu
from jax.sharding import PartitionSpec as P

MESH = pl.DeviceIdType.MESH


def slots():
    out=[]
    for bx in (0,1):
        for by in (0,1):
            for sgn in (0,1,-1):
                if (bx,by,sgn)!=(0,0,0): out.append((bx,by,sgn))
    return out

def forwards(order,bx,by,sgn):
    differs={'x':bx,'y':by,'z':int(sgn!=0)}
    last=max([j for j,d in enumerate(order) if differs[d]],default=-1)
    dirs=[]
    for j,d in enumerate(order):
        if j>last:
            dirs += ['u','d'] if d=='z' else [d]
    if last>=0 and order[last]=='z':
        dirs.append('u' if sgn<0 else 'd')
    return dirs


TIME = 64
WIN = 4
EPS = 1e-6
F = jnp.float32
B = jnp.bfloat16
VMEM_LIMIT = 60 * 2**20


def dot(a, b):
    return lax.dot_general(a, b, (((1,), (0,)), ((), ())), preferred_element_type=F)


def dot_nt(a, b):
    return lax.dot_general(a, b, (((1,), (1,)), ((), ())), preferred_element_type=F)


def dot_tn(a, b):
    return lax.dot_general(a, b, (((0,), (0,)), ((), ())), preferred_element_type=F)


def iota(shape, dim):
    return lax.broadcasted_iota(jnp.int32, shape, dim)


def norm_stats(x):
    center = jnp.mean(x, axis=-1, keepdims=True)
    shifted = x - center
    spread = jnp.mean(shifted * shifted, axis=-1, keepdims=True)
    scale = lax.rsqrt(spread + EPS)
    return shifted * scale, scale


def norm_back(x, gain, grad):
    unit, scale = norm_stats(x)
    by_gain = grad * unit
    by_unit = grad * gain
    mean_one = jnp.mean(by_unit, axis=-1, keepdims=True)
    mean_two = jnp.mean(by_unit * unit, axis=-1, keepdims=True)
    by_input = scale * (by_unit - mean_one - unit * mean_two)
    return by_input, jnp.sum(by_gain.reshape(-1, 8, x.shape[1]), axis=0)


def gelu_both(u):
    t = 1.0 / (1.0 + (0.3275911 * 0.7071067811865476) * jnp.abs(u))
    bell = jnp.exp(-0.5 * u * u)
    poly = t * (0.127414796 + t * (-0.142248368 + t * (0.7107068705 + t * (-0.7265760135 + t * 0.5307027145))))
    tail = poly * bell
    phi = jnp.where(u < 0, tail, 1.0 - tail)
    return u * phi, phi + u * (bell * 0.3989422804014327)


def spread_vector(tiles, lane, size, devices):
    part = size // devices
    pick = (iota((128, size), 1) % part == iota((128, size), 0)).astype(B)
    wide = dot(tiles, pick)
    rows = iota((tiles.shape[0], size), 0)
    keep = rows == (iota((tiles.shape[0], size), 1) // part) * 16 + lane
    return jnp.sum(jnp.where(keep, wide, 0.0), axis=0, keepdims=True)


def group_sums(x, ones):
    high = x.astype(B)
    return dot(high, ones) + dot((x - high.astype(F)).astype(B), ones)


def lane_groups(x, op):
    lanes = iota(x.shape, 1)
    width = x.shape[1]
    for d in (1, 2, 4, 8):
        other = jnp.where((lanes & d) != 0, pltpu.roll(x, d, 1), pltpu.roll(x, width - d, 1))
        x = op(x, other)
    return x


HEAD = 32
AREA = WIN * WIN


def stack8(block, mask):
    return jnp.concatenate([block] * 8, axis=0) * mask


def dec_kernel(wc, nc, wide_rows, narrow_rows, devices, tiles, m_ref, perm, sel, dz, wq_h, wo_h, wu_h, wd_h,
               outw, outn, dm_ref, gq_h, go_h, gu_h, gd_h, vec_ref,
               wq, wo, wu, wd, mhi, mlo, r_ref, a_ref, qkv, p_ref, o_ref, x1_ref,
               b_ref, h_ref, du, dx1, do_ref, dqkv, dec, dm_acc, acc, gq, go, gu, gd, sems):
    D = wo.shape[0]
    rows = wc * wide_rows + nc * narrow_rows
    T = 256
    tall = 512 if rows % 512 == 0 else T
    nt = rows // T
    wide_tiles = wc * wide_rows // T
    cps = []
    for k, (src, dst) in enumerate(((wq_h, wq), (wo_h, wo), (wu_h, wu), (wd_h, wd))):
        cp = pltpu.make_async_copy(src, dst, sems.at[k])
        cp.start()
        cps.append(cp)
    gain1 = spread_vector(tiles[...], 3, D, devices)
    gain2 = spread_vector(tiles[...], 4, D, devices)
    filler = spread_vector(tiles[...], 2, D, devices)
    mhi[...] = m_ref[...].astype(B)
    mlo[...] = (m_ref[...] - mhi[...].astype(F)).astype(B)
    dm_acc[...] = jnp.zeros_like(dm_acc)
    acc[...] = jnp.zeros_like(acc)
    def group_rows(t):
        g = jnp.where(t < wide_tiles, t * T // wide_rows, wc + (t - wide_tiles) // 2)
        return pl.ds(pl.multiple_of(g * 128, 128), 128)

    cps[0].wait()

    @pl.loop(0, nt)
    def _(t):
        rr = pl.ds(pl.multiple_of(t * T, T), T)
        g = group_rows(t)
        s = sel[rr]
        seen = jnp.sum(s.astype(F), axis=1, keepdims=True)
        x = dot(s, mhi[g]) + dot(s, mlo[g]) + (1.0 - seen) * filler
        r_ref[rr] = x
        a = (norm_stats(x)[0] * gain1).astype(B)
        a_ref[rr] = a
        qkv[rr] = dot(a, wq[...]).astype(B)

    mask = (iota((128, 256), 0) // AREA == iota((128, 256), 1) // HEAD).astype(B)
    scale = HEAD ** -0.5
    nw = 32
    while rows % (nw * AREA):
        nw //= 2
    ones = (iota((128, 128), 0) // AREA == iota((128, 128), 1) // AREA).astype(B)

    @pl.loop(0, rows // (nw * AREA))
    def _(g):
        base = pl.multiple_of(g * nw * AREA, nw * AREA)
        rr = pl.ds(base, nw * AREA)
        for a in range(D // 256):
            cq = pl.ds(a * 256, 256)
            q, k, v = qkv[rr, cq], qkv[rr, pl.ds(D + a * 256, 256)], qkv[rr, pl.ds(2 * D + a * 256, 256)]
            w16 = [slice(AREA * j, AREA * j + AREA) for j in range(nw)]
            s = jnp.concatenate([dot_nt(q[w], stack8(k[w], mask)) for w in w16], axis=0) * scale
            e = jnp.exp(s - lane_groups(s, jnp.maximum))
            p = e / group_sums(e, ones)
            p_ref[rr, pl.ds(a * 128, 128)] = p
            low = p.astype(B)
            o_ref[rr, cq] = jnp.concatenate([dot(low[w], stack8(v[w], mask)) for w in w16], axis=0).astype(B)

    for cp in cps[1:]:
        cp.wait()

    @pl.loop(0, rows // tall)
    def _(t):
        rr = pl.ds(pl.multiple_of(t * tall, tall), tall)
        x1 = r_ref[rr] + dot(o_ref[rr], wo[...])
        x1_ref[rr] = x1
        b = (norm_stats(x1)[0] * gain2).astype(B)
        b_ref[rr] = b
        z = dz[rr]
        out = x1
        back = jnp.zeros((tall, D), F)
        C = 512
        for k in range(0, wu.shape[1], C):
            u = dot(b, wu[:, k:k + C])
            h, slope = gelu_both(u)
            h = h.astype(B)
            h_ref[rr, k:k + C] = h
            out = out + dot(h, wd[k:k + C, :])
            d = (slope * dot_nt(z, wd[k:k + C, :])).astype(B)
            du[rr, k:k + C] = d
            back = back + dot_nt(d, wu[:, k:k + C])
        dec[rr] = out.astype(B)
        by_input, by_gain = norm_back(x1, gain2, back)
        acc[1] += by_gain
        dx = z.astype(F) + by_input
        dx1[rr] = dx
        do_ref[rr] = dot_nt(dx.astype(B), wo[...]).astype(B)

    for i in range(wc + nc):
        base, n, out = (i * wide_rows, wide_rows, outw) if i < wc else (
            wc * wide_rows + (i - wc) * narrow_rows, narrow_rows, outn)
        out[i if i < wc else i - wc] = dot_tn(perm[base:base + n, 0:n], dec[base:base + n]).astype(B)

    @pl.loop(0, rows // (nw * AREA))
    def _(g):
        base = pl.multiple_of(g * nw * AREA, nw * AREA)
        rr = pl.ds(base, nw * AREA)
        w16 = [slice(AREA * j, AREA * j + AREA) for j in range(nw)]
        for a in range(D // 256):
            cq = pl.ds(a * 256, 256)
            q, k, v = qkv[rr, cq], qkv[rr, pl.ds(D + a * 256, 256)], qkv[rr, pl.ds(2 * D + a * 256, 256)]
            go_ = do_ref[rr, cq]
            ks = [stack8(k[w], mask) for w in w16]
            qs = [stack8(q[w], mask) for w in w16]
            gs = [stack8(go_[w], mask) for w in w16]
            p = p_ref[rr, pl.ds(a * 128, 128)]
            dp = jnp.concatenate([dot_nt(go_[w], stack8(v[w], mask)) for w in w16], axis=0)
            ds = (p * (dp - group_sums(dp * p, ones))).astype(B)
            dqkv[rr, cq] = (jnp.concatenate([dot(ds[w], m) for w, m in zip(w16, ks)], axis=0) * scale).astype(B)
            s = jnp.concatenate([dot_nt(k[w], m) for w, m in zip(w16, qs)], axis=0) * scale
            s = s.reshape(nw, AREA, 128)
            e = jnp.exp(s - jnp.max(s, axis=1, keepdims=True))
            p = e / jnp.sum(e, axis=1, keepdims=True)
            dp = jnp.concatenate([dot_nt(v[w], m) for w, m in zip(w16, gs)], axis=0).reshape(nw, AREA, 128)
            ds = (p * (dp - jnp.sum(dp * p, axis=1, keepdims=True))).reshape(nw * AREA, 128).astype(B)
            p = p.reshape(nw * AREA, 128).astype(B)
            dqkv[rr, pl.ds(D + a * 256, 256)] = (jnp.concatenate([dot(ds[w], m) for w, m in zip(w16, qs)], axis=0) * scale).astype(B)
            dqkv[rr, pl.ds(2 * D + a * 256, 256)] = jnp.concatenate([dot(p[w], m) for w, m in zip(w16, gs)], axis=0).astype(B)

    @pl.loop(0, nt)
    def _(t):
        rr = pl.ds(pl.multiple_of(t * T, T), T)
        g = group_rows(t)
        by_input, by_gain = norm_back(r_ref[rr], gain1, dot_nt(dqkv[rr], wq[...]))
        acc[0] += by_gain
        dr = dx1[rr] + by_input
        s = sel[rr]
        hidden = 1.0 - jnp.sum(s.astype(F), axis=1, keepdims=True)
        acc[2] += jnp.sum((dr * hidden).reshape(-1, 8, D), axis=0)
        dm_acc[g] += dot_tn(s, dr.astype(B))

    dm_ref[...] = dm_acc[...].astype(B)
    for k in range(3):
        vec_ref[k:k + 1, :] = jnp.sum(acc[k], axis=0, keepdims=True)
    vec_ref[3:, :] = jnp.zeros((5, D), F)
    step = 512
    copies = []

    def leave(k, src, dst):
        cp = pltpu.make_async_copy(src, dst, sems.at[4 + k])
        cp.start()
        copies.append(cp)

    @pl.loop(0, wd.shape[0] // step)
    def _(k):
        kk = pl.ds(pl.multiple_of(k * step, step), step)
        gd[kk, :] = dot_tn(h_ref[:, kk], dz[...]).astype(B)

    leave(0, gd, gd_h)

    @pl.loop(0, wd.shape[0] // step)
    def _(k):
        kk = pl.ds(pl.multiple_of(k * step, step), step)
        gu[:, kk] = dot_tn(b_ref[...], du[:, kk]).astype(B)

    leave(1, gu, gu_h)

    @pl.loop(0, wq.shape[1] // step)
    def _(k):
        kk = pl.ds(pl.multiple_of(k * step, step), step)
        gq[:, kk] = dot_tn(a_ref[...], dqkv[:, kk]).astype(B)

    leave(2, gq, gq_h)
    go[...] = dot_tn(o_ref[...], dx1[...].astype(B)).astype(B)
    leave(3, go, go_h)
    for cp in copies:
        cp.wait()


def decoder(m, tiles, placed, wide_shape, narrow_shape, wq, wo, wu, wd, devices):
    wc, wide_rows, D = wide_shape
    nc, narrow_rows, _ = narrow_shape
    FFD = wu.shape[1]
    rows = wc * wide_rows + nc * narrow_rows
    V = pl.BlockSpec(memory_space=pltpu.VMEM)
    A = pl.BlockSpec(memory_space=pl.ANY)
    sds = jax.ShapeDtypeStruct
    weights = [pltpu.VMEM(w.shape, B) for w in (wq, wo, wu, wd)]
    return pl.pallas_call(
        functools.partial(dec_kernel, wc, nc, wide_rows, narrow_rows, devices),
        out_shape=[sds(wide_shape, B), sds(narrow_shape, B), sds(m.shape, B), sds(wq.shape, B), sds(wo.shape, B),
                   sds(wu.shape, B), sds(wd.shape, B), sds((8, D), F)],
        in_specs=[V] * 5 + [A] * 4,
        out_specs=[V] * 3 + [A] * 4 + [V],
        scratch_shapes=weights + [
            pltpu.VMEM(m.shape, B), pltpu.VMEM(m.shape, B),
            pltpu.VMEM((rows, D), F), pltpu.VMEM((rows, D), B), pltpu.VMEM((rows, 3 * D), B),
            pltpu.VMEM((rows, D // 2), F), pltpu.VMEM((rows, D), B), pltpu.VMEM((rows, D), F),
            pltpu.VMEM((rows, D), B), pltpu.VMEM((rows, FFD), B), pltpu.VMEM((rows, FFD), B), pltpu.VMEM((rows, D), F),
            pltpu.VMEM((rows, D), B), pltpu.VMEM((rows, 3 * D), B), pltpu.VMEM((rows, D), B),
            pltpu.VMEM(m.shape, F), pltpu.VMEM((3, 8, D), F)] + weights + [pltpu.SemaphoreType.DMA((8,))],
        compiler_params=pltpu.CompilerParams(vmem_limit_bytes=VMEM_LIMIT),
        name="decoder_block",
    )(tiles, m, *placed, wq, wo, wu, wd)


def placement(wc, nc, shw, shn, visw, visn, cotw, cotn, perm, sel, dz):
    T = 256
    wide_rows, narrow_rows = cotw.shape[1], cotn.shape[1]
    clips = [(i * wide_rows, wide_rows, 8, shw[i, 0], shw[i, 1], cotw, i, visw, 0) for i in range(wc)]
    clips += [(wc * wide_rows + i * narrow_rows, narrow_rows, 4, shn[i], 0, cotn, i, visn, 64 * (i % 2)) for i in range(nc)]
    for base, n, cols, s, r, cot, i, vis, o in clips:
        seen = vis.shape[1]
        parts = [jnp.full((1, o), -1, jnp.int32)] if o else []
        parts += [vis[i:i + 1, :], jnp.full((1, 128 - o - seen), -1, jnp.int32)]
        shown = jnp.concatenate(parts, axis=1)
        for k in range(0, n, T):
            j = iota((T, 1), 0) + k
            w, q = j >> 4, j & 15
            wf = cols // WIN
            t = ((w // wf) * WIN + (q >> 2) + s) & (TIME - 1)
            f = ((w % wf) * WIN + (q & 3) + r) & (cols - 1)
            patch = t * cols + f
            where = pl.ds(base + k, T)
            hot = jnp.where(iota((T, n), 1) == patch, 1.0, 0.0).astype(B)
            perm[where, 0:n] = hot
            if n < perm.shape[1]:
                perm[where, n:] = jnp.zeros((T, perm.shape[1] - n), B)
            sel[where] = jnp.where(shown == patch, 1.0, 0.0).astype(B)
            dz[where] = dot(hot, cot[i]).astype(B)


def placed_shapes(cotw, cotn):
    rows = cotw.shape[0] * cotw.shape[1] + cotn.shape[0] * cotn.shape[1]
    return [jax.ShapeDtypeStruct((rows, n), B) for n in (cotw.shape[1], 128, cotw.shape[2])]


ENC_HEAD = 64


def valid_keys(kind, wide_seen, narrow_seen):
    q, k = iota((128, 128), 0), iota((128, 128), 1)
    if kind == 0:
        return k < wide_seen
    return ((q // 64) == (k // 64)) & (k % 64 < narrow_seen)


def pair_mask():
    return (iota((256, 128), 0) // 128 == iota((256, 128), 1) // ENC_HEAD).astype(B)


def pair_shares(q, k2, valid):
    s2 = dot_nt(q, k2) * (ENC_HEAD ** -0.5)
    shares = []
    for h in range(2):
        s = jnp.where(valid, s2[:, 128 * h:128 * h + 128], -1e30)
        e = jnp.exp(s - jnp.max(s, axis=1, keepdims=True))
        shares.append(e / jnp.sum(e, axis=1, keepdims=True))
    return shares


def load_rows(dst, pair, wide, narrow, wc, nc):
    dst[...] = jnp.zeros_like(dst)
    for i in range(wc):
        dst[128 * i:128 * i + wide.shape[1], :] = wide[i].astype(F)
    pair[...] = narrow[...].astype(F)
    for i in range(nc):
        o = 128 * wc + 64 * i
        dst[o:o + narrow.shape[0], :] = pair[:, i, :]


def enc_forward_kernel(wc, nc, devices, shw, shn, visw, visn, cotw, cotn, tiles, cw, cn, wq_h, wo_h, wu_h, wd_h, we_h,
                       perm, sel, dz, m_ref, x_ref, a_ref, qkv, o_ref, x1_ref, b_ref, h_ref, slope_ref, e_ref,
                       wq, wo, wu, wd, we, pair, sems):
    D = wo.shape[0]
    cps = []
    for k, (src, dst) in enumerate(((wq_h, wq), (wo_h, wo), (wu_h, wu), (wd_h, wd), (we_h, we))):
        cp = pltpu.make_async_copy(src, dst, sems.at[k])
        cp.start()
        cps.append(cp)
    placement(wc, nc, shw, shn, visw, visn, cotw, cotn, perm, sel, dz)
    load_rows(x_ref, pair, cw, cn, wc, nc)
    gain1 = spread_vector(tiles[...], 0, D, devices)
    gain2 = spread_vector(tiles[...], 1, D, devices)
    x = x_ref[...]
    a = (norm_stats(x)[0] * gain1).astype(B)
    a_ref[...] = a
    cps[0].wait()
    for k in range(0, 3 * D, D):
        qkv[:, k:k + D] = dot(a, wq[:, k:k + D]).astype(B)
    mask = pair_mask()
    groups = x_ref.shape[0] // 128
    for g in range(groups):
        rr = slice(128 * g, 128 * g + 128)
        valid = valid_keys(0 if g < wc else 1, cw.shape[1], cn.shape[0])
        for j in range(D // 128):
            q, k, v = (qkv[rr, o + 128 * j:o + 128 * j + 128] for o in (0, D, 2 * D))
            k2 = jnp.concatenate([k, k], axis=0) * mask
            v2 = jnp.concatenate([v, v], axis=0) * mask
            p2 = jnp.concatenate(pair_shares(q, k2, valid), axis=1).astype(B)
            o_ref[rr, 128 * j:128 * j + 128] = dot(p2, v2).astype(B)
    cps[1].wait()
    x1 = x_ref[...] + dot(o_ref[...], wo[...])
    x1_ref[...] = x1
    b = (norm_stats(x1)[0] * gain2).astype(B)
    b_ref[...] = b
    cps[2].wait()
    cps[3].wait()
    out = x1
    C = 512
    for k in range(0, wu.shape[1], C):
        h, slope = gelu_both(dot(b, wu[:, k:k + C]))
        h = h.astype(B)
        h_ref[:, k:k + C] = h
        slope_ref[:, k:k + C] = slope
        out = out + dot(h, wd[k:k + C, :])
    e_ref[...] = out.astype(B)
    cps[4].wait()
    m_ref[...] = dot(e_ref[...], we[...])


def encoder_forward(place, tiles, cw, cn, wq, wo, wu, wd, we, devices):
    wc, nc = cw.shape[0], cn.shape[1]
    D = cw.shape[2]
    FFD = wu.shape[1]
    R = 128 * wc + 128 * ((nc + 1) // 2)
    V = pl.BlockSpec(memory_space=pltpu.VMEM)
    S = pl.BlockSpec(memory_space=pltpu.SMEM)
    A = pl.BlockSpec(memory_space=pl.ANY)
    sds = jax.ShapeDtypeStruct
    return pl.pallas_call(
        functools.partial(enc_forward_kernel, wc, nc, devices),
        out_shape=placed_shapes(*place[4:]) + [sds((R, we.shape[1]), F), sds((R, D), F), sds((R, D), B), sds((R, 3 * D), B),
                   sds((R, D), B), sds((R, D), F), sds((R, D), B), sds((R, FFD), B), sds((R, FFD), F), sds((R, D), B)],
        in_specs=[S, S] + [V] * 7 + [A] * 5,
        out_specs=[V] * 13,
        scratch_shapes=[pltpu.VMEM(w.shape, B) for w in (wq, wo, wu, wd, we)]
        + [pltpu.VMEM(cn.shape, F), pltpu.SemaphoreType.DMA((5,))],
        compiler_params=pltpu.CompilerParams(vmem_limit_bytes=VMEM_LIMIT),
        name="encoder_forward",
    )(*place, tiles, cw, cn, wq, wo, wu, wd, we)


def enc_backward_kernel(wc, wide_seen, narrow_seen, devices, tiles, dm, dec_vec, x_in, a_ref, qkv, o_ref, x1_ref, b_ref, h_ref, slope_ref, e_ref,
                        wq_h, wo_h, wu_h, wd_h, we_h,
                        dx_ref, gq, go, gu, gd, ge, vec_ref,
                        wq, wo, wu, wd, we, do_ref, dqkv, du, sems):
    D = wo.shape[0]
    cps = []
    for k, (src, dst) in enumerate(((we_h, we), (wd_h, wd), (wu_h, wu), (wo_h, wo), (wq_h, wq))):
        cp = pltpu.make_async_copy(src, dst, sems.at[k])
        cp.start()
        cps.append(cp)
    gain1 = spread_vector(tiles[...], 0, D, devices)
    gain2 = spread_vector(tiles[...], 1, D, devices)
    cps[0].wait()
    grad = dot_nt(dm[...], we[...])
    z = grad.astype(B)
    ge[...] = dot_tn(e_ref[...], dm[...]).astype(B)
    cps[1].wait()
    cps[2].wait()
    back = jnp.zeros_like(grad)
    C = 512
    for k in range(0, wu.shape[1], C):
        d = (slope_ref[:, k:k + C] * dot_nt(z, wd[k:k + C, :])).astype(B)
        du[:, k:k + C] = d
        back = back + dot_nt(d, wu[:, k:k + C])
        gd[k:k + C, :] = dot_tn(h_ref[:, k:k + C], z).astype(B)
        gu[:, k:k + C] = dot_tn(b_ref[...], d).astype(B)
    by_input, by_gain = norm_back(x1_ref[...], gain2, back)
    vec_ref[...] = jnp.zeros_like(vec_ref)
    vec_ref[1:2, :] = jnp.sum(by_gain, axis=0, keepdims=True)
    dx1 = grad + by_input
    y = dx1.astype(B)
    cps[3].wait()
    do_ref[...] = dot_nt(y, wo[...]).astype(B)
    go[...] = dot_tn(o_ref[...], y).astype(B)
    mask = pair_mask()
    groups = x_in.shape[0] // 128
    scale = ENC_HEAD ** -0.5
    lane = iota((128, 128), 1)
    for g in range(groups):
        rr = slice(128 * g, 128 * g + 128)
        valid = valid_keys(0 if g < wc else 1, wide_seen, narrow_seen)
        for j in range(D // 128):
            q, k, v = (qkv[rr, o + 128 * j:o + 128 * j + 128] for o in (0, D, 2 * D))
            g_o = do_ref[rr, 128 * j:128 * j + 128]
            k2 = jnp.concatenate([k, k], axis=0) * mask
            v2 = jnp.concatenate([v, v], axis=0) * mask
            shares = pair_shares(q, k2, valid)
            dp2 = dot_nt(g_o, v2)
            ds, low = [], []
            for h in range(2):
                dp = dp2[:, 128 * h:128 * h + 128]
                p = shares[h]
                ds.append((p * (dp - jnp.sum(dp * p, axis=1, keepdims=True))).astype(B))
                low.append(p.astype(B))
            dq = dot(jnp.concatenate(ds, axis=1), k2) * scale
            dk = jnp.where(lane < ENC_HEAD, dot_tn(ds[0], q), dot_tn(ds[1], q)) * scale
            dv = jnp.where(lane < ENC_HEAD, dot_tn(low[0], g_o), dot_tn(low[1], g_o))
            for o, d in ((0, dq), (D, dk), (2 * D, dv)):
                dqkv[rr, o + 128 * j:o + 128 * j + 128] = d.astype(B)
    cps[4].wait()
    for k in range(0, 3 * D, D):
        gq[:, k:k + D] = dot_tn(a_ref[...], dqkv[:, k:k + D]).astype(B)
    by_input, by_gain = norm_back(x_in[...], gain1, dot_nt(dqkv[...], wq[...]))
    vec_ref[0:1, :] = jnp.sum(by_gain, axis=0, keepdims=True)
    DD = dec_vec.shape[1]
    vec_ref[2:3, 0:DD] = dec_vec[2:3, :]
    vec_ref[3:5, 0:DD] = dec_vec[0:2, :]
    dx_ref[...] = dx1 + by_input


def encoder_backward(tiles, counts, dm, dec_vec, saved, wq, wo, wu, wd, we, devices):
    D = wq.shape[0]
    FFD = wu.shape[1]
    R = dm.shape[0]
    V = pl.BlockSpec(memory_space=pltpu.VMEM)
    A = pl.BlockSpec(memory_space=pl.ANY)
    sds = jax.ShapeDtypeStruct
    return pl.pallas_call(
        functools.partial(enc_backward_kernel, *counts, devices),
        out_shape=[sds((R, D), F)] + [sds(w.shape, B) for w in (wq, wo, wu, wd, we)] + [sds((8, D), F)],
        in_specs=[V] * 12 + [A] * 5,
        out_specs=[V] * 7,
        scratch_shapes=[pltpu.VMEM(w.shape, B) for w in (wq, wo, wu, wd, we)]
        + [pltpu.VMEM((R, D), B), pltpu.VMEM((R, 3 * D), B), pltpu.VMEM((R, FFD), B), pltpu.SemaphoreType.DMA((5,))],
        compiler_params=pltpu.CompilerParams(vmem_limit_bytes=VMEM_LIMIT),
        name="encoder_backward",
    )(tiles, dm, dec_vec, *saved, wq, wo, wu, wd, we)


def results_kernel(wc, nc, sizes, *refs):
    me, e, dx, vec, *refs = refs
    shares, refs = refs[:9], refs[9:]
    encw, encn, gradw, gradn, *refs = refs
    outs, refs = refs[:9], refs[9:]
    vectors, (pair,) = refs[:len(sizes)], refs[len(sizes):]
    for src, wide, narrow in ((e, encw, encn), (dx, gradw, gradn)):
        for i in range(wc):
            rows = src[128 * i:128 * i + encw.shape[1], :]
            if wide is encw:
                wide[i] = rows
            else:
                wide[:, i, :] = rows
        for i in range(nc):
            o = 128 * wc + 64 * i
            pair[:, i, :] = src[o:o + narrow.shape[0], :].astype(F)
        narrow[...] = pair[...].astype(narrow.dtype)
    for src, dst in zip(shares, outs):
        dst[...] = src[...]
    width = vec.shape[1]
    for k, (n, ref) in enumerate(zip(sizes, vectors)):
        ref[...] = pltpu.roll(vec[k:k + 1, :], lax.rem(width - me[0] * n, width), 1)[:, 0:n]


def results(me, e, dx, vec, shares, sizes, wide_shape, narrow_shape):
    wc, nw, D = wide_shape
    nc, nn, _ = narrow_shape
    V = pl.BlockSpec(memory_space=pltpu.VMEM)
    S = pl.BlockSpec(memory_space=pltpu.SMEM)
    sds = jax.ShapeDtypeStruct
    out = pl.pallas_call(
        functools.partial(results_kernel, wc, nc, sizes),
        out_shape=[sds(wide_shape, B), sds((nn, nc, D), B), sds((nw, wc, D), F), sds((nn, nc, D), F)]
        + [sds(s.shape, F) for s in shares] + [sds((1, n), F) for n in sizes],
        in_specs=[S] + [V] * 12,
        out_specs=[V] * (13 + len(sizes)),
        scratch_shapes=[pltpu.VMEM((nn, nc, D), F)],
        compiler_params=pltpu.CompilerParams(vmem_limit_bytes=VMEM_LIMIT),
        name="results",
    )(me.reshape(1), e, dx, vec, *shares)
    swap = functools.partial(jnp.transpose, axes=(1, 0, 2))
    return out[0], swap(out[1]), swap(out[2]), swap(out[3]), out[4:13], [v.reshape(-1) for v in out[13:]]


def gather_ops(nz, pieces, ins, outs, send, recv, sib_send, sib_recv):
    f, c = lax.axis_index("fsdp"), lax.axis_index("dp")
    z, y, x = f // 4, (f // 2) % 2, f % 2
    xn, yn, up, dn, sib = (f + 1 - 2 * x, c), (f + 2 - 4 * y, c), (f + 4, c), (f - 4, c), (f, 1 - c)
    bar = pltpu.get_barrier_semaphore()

    def greet(dev):
        pl.semaphore_signal(bar, inc=1, device_id=dev, device_id_type=MESH)

    greet(xn)
    greet(yn)
    greet(sib)
    pl.when(z < nz - 1)(lambda: greet(up))
    pl.when(z > 0)(lambda: greet(dn))
    pl.semaphore_wait(bar, 3 + (z < nz - 1).astype(jnp.int32) + (z > 0).astype(jnp.int32))
    dest = {"x": xn, "y": yn, "u": up, "d": dn}
    there = {"x": None, "y": None, "u": z < nz - 1, "d": z > 0}
    code = {"x": 0, "y": 0, "u": 1, "d": 2}

    def columns(i, half):
        w, c0, cols, order, share = pieces[i]
        return pl.ds(pl.multiple_of(half * (ins[w].shape[1] // 2) + c0, 128) if share else c0, cols)

    def region(i, s, half):
        w = pieces[i][0]
        r = ins[w].shape[0]
        return outs[w].at[pl.ds(pl.multiple_of(s * r, r), r), columns(i, half)]

    def own(i):
        return ins[pieces[i][0]].at[:, columns(i, c)]

    def remote(i, s, src, d):
        return pltpu.make_async_remote_copy(
            src_ref=src, dst_ref=region(i, s, c), send_sem=send.at[i, code[d]], recv_sem=recv.at[i, s],
            device_id=dest[d], device_id_type=MESH)

    def sibling(i, s, half):
        return pltpu.make_async_remote_copy(
            src_ref=region(i, s, half), dst_ref=region(i, s, half), send_sem=sib_send.at[i],
            recv_sem=sib_recv.at[i], device_id=sib, device_id_type=MESH)

    def some(i, half, count):
        w = pieces[i][0]
        part = outs[w].at[pl.ds(0, count * ins[w].shape[0]), columns(i, half)]
        return lambda a, b: pltpu.make_async_remote_copy(
            src_ref=part, dst_ref=part, send_sem=a, recv_sem=b, device_id=sib, device_id_type=MESH)

    def along(dirs, act):
        for d in dirs:
            if there[d] is None:
                act(d)
            else:
                pl.when(there[d])(lambda d=d: act(d))

    def each(h, i, act):
        for bx, by, sgn in slots():
            k = h - bx - by
            if isinstance(h, int) and not ((k == 0) if sgn == 0 else (1 <= k < nz)):
                continue
            zs = z + sgn * k
            valid = (k == 0) if sgn == 0 else (k >= 1) & (zs >= 0) & (zs < nz)
            s = zs * 4 + (y + by - 2 * by * y) * 2 + (x + bx - 2 * bx * x)
            dirs = forwards(pieces[i][3], bx, by, sgn)
            if isinstance(valid, bool):
                act(i, s, dirs)
            else:
                pl.when(valid)(lambda s=s, dirs=dirs: act(i, s, dirs))

    def start(i):
        along(forwards(pieces[i][3], 0, 0, 0), lambda d: remote(i, f, own(i), d).start())

    def step(i, s, dirs):
        remote(i, s, region(i, s, c), "x").wait_recv()
        along(dirs, lambda d: remote(i, s, region(i, s, c), d).start())
        if pieces[i][4]:
            sibling(i, s, c).start()

    def arrived(i):
        if pieces[i][4]:
            some(i, 1 - c, 4 * nz - 1)(sib_send.at[i], sib_recv.at[i]).wait_recv()

    def finish(i):
        order = pieces[i][3]
        before = {d: order[:order.index(d)] for d in "xyz"}
        size = {"x": 2, "y": 2, "z": nz}

        def blocks(d):
            n = 1
            for e in before[d]:
                n *= size[e]
            return n

        some(i, c, blocks("x") + blocks("y"))(send.at[i, 0], recv.at[i, 0]).wait_send()
        for p in range(nz):
            if p < nz - 1:
                pl.when(z == p)(lambda p=p: some(i, c, blocks("z") * (p + 1))(send.at[i, 1], recv.at[i, 0]).wait_send())
            if p > 0:
                pl.when(z == p)(lambda p=p: some(i, c, blocks("z") * (nz - p))(send.at[i, 2], recv.at[i, 0]).wait_send())
        if pieces[i][4]:
            some(i, c, 4 * nz - 1)(sib_send.at[i], sib_recv.at[i]).wait_send()

    def level(h, indices):
        for i in indices:
            each(h, i, step)

    return start, level, arrived, finish


def gather_encode_kernel(wc, nc, nz, pieces, nw, shw, shn, visw, visn, cotw, cotn, cw, cn, *refs):
    devices = 4 * nz
    ins, refs = refs[:nw], refs[nw:]
    outs, refs = refs[:nw], refs[nw:]
    perm, sel, dz, m_ref, x_ref, a_ref, qkv, o_ref, x1_ref, b_ref, h_ref, slope_ref, e_ref, *refs = refs
    wq, wo, wu, wd, we, tiles, sum_ref, pair, send, recv, sib_send, sib_recv, loc, sems = refs
    D = wo.shape[0]
    start, level, arrived, finish = gather_ops(nz, pieces, ins, outs, send, recv, sib_send, sib_recv)
    sets = {"q": [nw - 1, 0], "u": [2], "d": [3], "o": [1], "e": [4], "D": [5, 6], "X": [7, 8]}
    members = {s: [i for w in ws for i, p in enumerate(pieces) if p[0] == w] for s, ws in sets.items()}
    into = [wq, wo, wu, wd, we, None, None, None, None, tiles]
    loads = {}
    gains = []
    locals_ = []
    C = 512
    chunks = wu.shape[1] // C

    def prepare():
        for w in range(nw):
            r = ins[w].shape[0]
            cp = pltpu.make_async_copy(
                ins[w], outs[w].at[pl.ds(pl.multiple_of(lax.axis_index("fsdp") * r, r), r)], loc.at[w])
            cp.start()
            locals_.append(cp)
        placement(wc, nc, shw, shn, visw, visn, cotw, cotn, perm, sel, dz)
        load_rows(x_ref, pair, cw, cn, wc, nc)

    def ready(s):
        for w, i in zip(sets[s], members[s]):
            arrived(i)
            locals_[w].wait()
            loads[w] = pltpu.make_async_copy(outs[w], into[w], sems.at[w])
            loads[w].start()

    def project():
        loads[nw - 1].wait()
        gains.append(spread_vector(tiles[...], 0, D, devices))
        gains.append(spread_vector(tiles[...], 1, D, devices))
        a = (norm_stats(x_ref[...])[0] * gains[0]).astype(B)
        a_ref[...] = a
        loads[0].wait()
        for k in range(0, 3 * D, D):
            qkv[:, k:k + D] = dot(a, wq[:, k:k + D]).astype(B)

    def attend(part):
        mask = pair_mask()
        groups = x_ref.shape[0] // 128
        for g in range(groups):
            if g * 2 // groups != part:
                continue
            rr = slice(128 * g, 128 * g + 128)
            valid = valid_keys(0 if g < wc else 1, cw.shape[1], cn.shape[0])
            for j in range(D // 128):
                q, k, v = (qkv[rr, o + 128 * j:o + 128 * j + 128] for o in (0, D, 2 * D))
                k2 = jnp.concatenate([k, k], axis=0) * mask
                v2 = jnp.concatenate([v, v], axis=0) * mask
                p2 = jnp.concatenate(pair_shares(q, k2, valid), axis=1).astype(B)
                o_ref[rr, 128 * j:128 * j + 128] = dot(p2, v2).astype(B)

    def middle():
        loads[1].wait()
        x1 = x_ref[...] + dot(o_ref[...], wo[...])
        x1_ref[...] = x1
        sum_ref[...] = x1
        b_ref[...] = (norm_stats(x1)[0] * gains[1]).astype(B)

    def feed_forward(j):
        if j == 0:
            loads[2].wait()
            loads[3].wait()
        k = j * C
        h, slope = gelu_both(dot(b_ref[...], wu[:, k:k + C]))
        h = h.astype(B)
        h_ref[:, k:k + C] = h
        slope_ref[:, k:k + C] = slope
        sum_ref[...] += dot(h, wd[k:k + C, :])

    def embed():
        e_ref[...] = sum_ref[...].astype(B)
        loads[4].wait()
        m_ref[...] = dot(e_ref[...], we[...])

    compute = [project, functools.partial(attend, 0), functools.partial(attend, 1), middle]
    compute += [functools.partial(feed_forward, j) for j in range(chunks)] + [embed]
    for token in gather_schedule(nz + 1, len(compute)):
        if token[0] == "S":
            for i in members[token[1]]:
                start(i)
        elif token[0] == "V":
            level(token[1], members[token[2]])
        elif token[0] == "R":
            ready(token[1])
        elif token[0] == "P":
            prepare()
        else:
            compute[token[1]]()
    for w in sets["D"] + sets["X"]:
        locals_[w].wait()
    for s in "DX":
        for i in members[s]:
            arrived(i)
    for i in range(len(pieces)):
        finish(i)


def gather_schedule(top, steps):
    if (top, steps) == (5, 11):
        return list(GATHER_SCHEDULE)
    tokens = [("S", s) for s in "qudoe"] + [("P",), ("S", "D"), ("S", "X")]
    tokens += [("V", h, s) for h in range(1, top + 1) for s in "qudoeDX"]
    return tokens + [("R", s) for s in "qoude"] + [("C", k) for k in range(steps)]


def gather_encode(shards, pieces, place, cw, cn, nz, cid=1):
    nw, npc, n = len(shards), len(pieces), 4 * nz
    wc, nc, D = cw.shape[0], cn.shape[1], cw.shape[2]
    R = 128 * wc + 128 * ((nc + 1) // 2)
    V = pl.BlockSpec(memory_space=pltpu.VMEM)
    S = pl.BlockSpec(memory_space=pltpu.SMEM)
    A = pl.BlockSpec(memory_space=pl.ANY)
    sds = jax.ShapeDtypeStruct
    whole = [sds((s.shape[0] * n, s.shape[1]), s.dtype) for s in shards]
    FFD, DD = shards[2].shape[1], shards[4].shape[1]
    dma = pltpu.SemaphoreType.DMA
    out = pl.pallas_call(
        functools.partial(gather_encode_kernel, wc, nc, nz, pieces, nw),
        out_shape=whole + placed_shapes(*place[4:]) + [
            sds((R, DD), F), sds((R, D), F), sds((R, D), B), sds((R, 3 * D), B), sds((R, D), B), sds((R, D), F),
            sds((R, D), B), sds((R, FFD), B), sds((R, FFD), F), sds((R, D), B)],
        in_specs=[S, S] + [V] * 6 + [A] * nw,
        out_specs=[A] * nw + [V] * 13,
        scratch_shapes=[pltpu.VMEM(w.shape, B) for w in whole[:5]] + [
            pltpu.VMEM(whole[-1].shape, B), pltpu.VMEM((R, D), F), pltpu.VMEM(cn.shape, F),
            dma((npc, 3)), dma((npc, n)), dma((npc,)), dma((npc,)), dma((nw,)), dma((nw,))],
        compiler_params=pltpu.CompilerParams(collective_id=cid, has_side_effects=True, vmem_limit_bytes=VMEM_LIMIT),
        name="gather_and_encode",
    )(*place, cw, cn, *shards)
    return out[:nw], out[nw:nw + 3], out[nw + 3:]


def slot_count(order, d, nz):
    size = {"x": 2, "y": 2, "z": nz}
    k = 1
    for e in order[:order.index("z" if d in "ud" else d)]:
        k *= size[e]
    return k * (nz + 1) if d in "ud" else k


def slot_index(order, d, nz, pos):
    size = {"x": 2, "y": 2, "z": nz}
    k = 0
    for e in order[:order.index("z" if d in "ud" else d)]:
        k = k * size[e] + pos[e]
    return k * (nz + 1) + pos["z"] + (1 if d == "d" else 0) if d in "ud" else k


def parent(order, bx, by, sgn):
    differs = {"x": bx, "y": by, "z": int(sgn != 0)}
    last = max(j for j, d in enumerate(order) if differs[d])
    if order[last] == "z":
        return "d" if sgn < 0 else "u"
    return order[last]


def reduce_ops(nz, pieces, rows, mine, other, sibb, rbuf, res, outs, sib_send, sib_recv, send, recv, res_sem, res_send, res_recv):
    f, c = lax.axis_index("fsdp"), lax.axis_index("dp")
    z, y, x = f // 4, (f // 2) % 2, f % 2
    bits = (nz * 4).bit_length() - 1

    def flip(b):
        return f + (1 << b) * (1 - 2 * ((f // (1 << b)) % 2))

    xn, yn, up, dn, sib = (flip(0), c), (flip(1), c), (f + 4, c), (f - 4, c), (f, 1 - c)
    bar = pltpu.get_barrier_semaphore()

    def greet(dev):
        pl.semaphore_signal(bar, inc=1, device_id=dev, device_id_type=MESH)

    greet(xn)
    greet(yn)
    greet(sib)
    pl.when(z < nz - 1)(lambda: greet(up))
    pl.when(z > 0)(lambda: greet(dn))
    far = range(3, bits)
    for b in far:
        greet((flip(b), c))
    pl.semaphore_wait(bar, 3 + len(far) + (z < nz - 1).astype(jnp.int32) + (z > 0).astype(jnp.int32))
    dest = {"x": xn, "y": yn, "u": up, "d": dn}
    there = {"u": z < nz - 1, "d": z > 0}
    opposite = {"u": "d", "d": "u", "x": "x", "y": "y"}
    kind = {"x": 0, "y": 1, "u": 2, "d": 2}

    def give(w):
        return pltpu.make_async_remote_copy(
            src_ref=other[w], dst_ref=sibb[w], send_sem=sib_send.at[w], recv_sem=sib_recv.at[w],
            device_id=sib, device_id_type=MESH)

    def cols(i):
        return pl.ds(pieces[i][1], pieces[i][2])

    def message(i, s, pos, d):
        w, order, b = pieces[i][0], pieces[i][3], kind[d]
        r = rows[w]
        q = slot_index(order, opposite[d], nz, pos)
        return pltpu.make_async_remote_copy(
            src_ref=mine[w].at[pl.ds(pl.multiple_of(s * r, r), r), cols(i)], dst_ref=rbuf[i][b].at[q],
            send_sem=send.at[i], recv_sem=recv.at[i, b, q], device_id=dest[d], device_id_type=MESH)

    def arrival(i, pos, d):
        b = kind[d]
        q = slot_index(pieces[i][3], d, nz, pos)
        return pltpu.make_async_remote_copy(
            src_ref=rbuf[i][b].at[q], dst_ref=rbuf[i][b].at[q], send_sem=send.at[i],
            recv_sem=recv.at[i, b, q], device_id=sib, device_id_type=MESH)

    def add(i, s, pos, children, final):
        w, order = pieces[i][0], pieces[i][3]
        r = rows[w]
        ks = [(kind[d], slot_index(order, d, nz, pos)) for d in children]

        @pl.loop(0, r // 16)
        def _(k):
            rr = pl.ds(pl.multiple_of(k * 16, 16), 16)
            gr = pl.ds(pl.multiple_of(s * r + k * 16, 16), 16)
            t = mine[w][gr, cols(i)].astype(F) + sibb[w][gr, cols(i)].astype(F)
            for b, q in ks:
                t = t + rbuf[i][b][q, rr].astype(F)
            if final:
                res[w][rr, cols(i)] = t
            else:
                mine[w][gr, cols(i)] = t.astype(B)

    def gather_children(i, s, pos, children, final):
        sure = [d for d in children if d in "xy"]
        maybe = [d for d in children if d in "ud"]
        for d in sure:
            arrival(i, pos, d).wait_recv()
        for d in maybe:
            pl.when(there[d])(lambda d=d: arrival(i, pos, d).wait_recv())
        if not maybe:
            add(i, s, pos, sure, final)
        elif len(maybe) == 1:
            pl.when(there[maybe[0]])(lambda: add(i, s, pos, sure + maybe, final))
            pl.when(jnp.logical_not(there[maybe[0]]))(lambda: add(i, s, pos, sure, final))
        else:
            u, d = there["u"], there["d"]
            pl.when(u & d)(lambda: add(i, s, pos, sure + ["u", "d"], final))
            pl.when(u & jnp.logical_not(d))(lambda: add(i, s, pos, sure + ["u"], final))
            pl.when(jnp.logical_not(u) & d)(lambda: add(i, s, pos, sure + ["d"], final))
            if nz == 1:
                add(i, s, pos, sure, final)

    def each(h, i, leaf, act):
        order = pieces[i][3]
        for bx, by, sgn in slots():
            children = forwards(order, bx, by, sgn)
            if leaf is not None and (len(children) == 0) != leaf:
                continue
            k = h - bx - by
            if isinstance(h, int) and not ((k == 0) if sgn == 0 else (1 <= k < nz)):
                continue
            zs = z + sgn * k
            valid = (k == 0) if sgn == 0 else (k >= 1) & (zs >= 0) & (zs < nz)
            pos = {"x": x + bx - 2 * bx * x, "y": y + by - 2 * by * y, "z": zs}
            s = zs * 4 + pos["y"] * 2 + pos["x"]
            p = parent(order, bx, by, sgn)
            if isinstance(valid, bool):
                act(i, s, pos, children, p)
            else:
                pl.when(valid)(lambda s=s, pos=pos, children=children, p=p: act(i, s, pos, children, p))

    def work(i, s, pos, children, p):
        gather_children(i, s, pos, children, False)
        message(i, s, pos, p).start()

    def leaves(h, indices):
        for i in indices:
            each(h, i, True, work)

    def nodes(h, indices):
        for i in indices:
            each(h, i, False, work)

    def out_copy(w):
        n = outs[w].shape[1] // 2
        return pltpu.make_async_copy(res[w], outs[w].at[:, pl.ds(pl.multiple_of(c * n, 128), n)], res_sem.at[w])

    def out_sib(w, half):
        n = outs[w].shape[1] // 2
        return pltpu.make_async_remote_copy(
            src_ref=res[w], dst_ref=outs[w].at[:, pl.ds(pl.multiple_of(half * n, 128), n)], send_sem=res_send.at[w],
            recv_sem=res_recv.at[w], device_id=sib, device_id_type=MESH)

    def total(w):
        for i, piece in enumerate(pieces):
            if piece[0] == w:
                gather_children(i, f, {"x": x, "y": y, "z": z}, forwards(piece[3], 0, 0, 0), True)
        out_sib(w, c).start()
        out_copy(w).start()

    def sent(indices):
        for i in indices:
            w = pieces[i][0]
            part = mine[w].at[pl.ds(0, (4 * nz - 1) * rows[w]), cols(i)]
            pltpu.make_async_remote_copy(
                src_ref=part, dst_ref=part, send_sem=send.at[i], recv_sem=recv.at[i, 0, 0], device_id=sib,
                device_id_type=MESH).wait_send()

    def finish(ws):
        for w in ws:
            give(w).wait_send()
            out_copy(w).wait()
            out_sib(w, c).wait_send()
            out_sib(w, 1 - c).wait_recv()

    return flip, give, leaves, nodes, total, sent, finish


def encode_back_reduce_kernel(wc, wide_seen, narrow_seen, nz, routes, *refs):
    devices = 4 * nz
    (tiles, x_ref, dm, dec_vec, e_ref, b_ref, x1_ref, o_ref, qkv, a_ref, *refs) = refs
    h_h, slope_h, we_h, wd_h, wu_h, wo_h, wq_h, *refs = refs
    dec_g, refs = refs[:4], refs[4:]
    (dx_ref, vec_out, *refs) = refs
    outs, refs = refs[:9], refs[9:]
    (we, wo, wq, wd2, wu2, h2, slope2, dx1_ref, z_ref, do_ref, dqkv, *refs) = refs
    mine, refs = refs[:9], refs[9:]
    enc_other, refs = refs[:5], refs[5:]
    sibb, refs = refs[:9], refs[9:]
    res, refs = refs[:9], refs[9:]
    npc = len(routes)
    rbuf, refs = [refs[3 * i:3 * i + 3] for i in range(npc)], refs[3 * npc:]
    (vbuf, wsem, dsem, sib_send, sib_recv, send, recv, res_sem, res_send, res_recv, vsend, vrecv) = refs
    c = lax.axis_index("dp")
    D = wo.shape[0]
    n_up = mine[2].shape[1]
    rows = [m.shape[0] // devices for m in mine]

    def half(ref, h):
        n = ref.shape[1] // 2
        return ref.at[:, pl.ds(pl.multiple_of(h * n, 128), n)]

    other = list(enc_other) + [half(g, 1 - c) for g in dec_g]
    flip, give, leaves, nodes, total, sent, finish = reduce_ops(
        nz, routes, rows, mine, other, sibb, rbuf, res, outs, sib_send, sib_recv, send, recv, res_sem, res_send, res_recv)
    dec_ws = [5, 6, 7, 8]
    for w in dec_ws:
        give(w).start()
    takes = [pltpu.make_async_copy(half(dec_g[w - 5], c), mine[w], dsem.at[w - 5]) for w in dec_ws]
    for t in takes:
        t.start()
    loads = [pltpu.make_async_copy(s, d, wsem.at[k]) for k, (s, d) in enumerate(((we_h, we), (wo_h, wo), (wq_h, wq)))]
    C = 512
    chunks = 2 * n_up // C

    def chunk(j):
        h = (1 - c) if j < chunks // 2 else c
        return pl.multiple_of(h * n_up + (j % (chunks // 2)) * C, 128)

    def feed(j):
        k = chunk(j)
        return (pltpu.make_async_copy(wd_h.at[pl.ds(k, C)], wd2.at[j % 2], wsem.at[3 + j % 2]),
                pltpu.make_async_copy(wu_h.at[:, pl.ds(k, C)], wu2.at[j % 2], wsem.at[5 + j % 2]),
                pltpu.make_async_copy(h_h.at[:, pl.ds(k, C)], h2.at[j % 2], wsem.at[7 + j % 2]),
                pltpu.make_async_copy(slope_h.at[:, pl.ds(k, C)], slope2.at[j % 2], wsem.at[9 + j % 2]))

    loads[0].start()
    for j in (0, 1):
        for cp in feed(j):
            cp.start()
    loads[1].start()
    loads[2].start()
    gain1 = spread_vector(tiles[...], 0, D, devices)
    gain2 = spread_vector(tiles[...], 1, D, devices)
    def own_cols(w):
        n = mine[w].shape[1]
        return pl.ds(pl.multiple_of(c * n, 128), n), pl.ds(pl.multiple_of((1 - c) * n, 128), n)

    sets = {"A": [5, 6], "B": [7, 8], "d": [3], "u": [2], "e": [4], "O": [1], "Q": [0]}
    members = {s: [i for i, p in enumerate(routes) if p[0] in ws] for s, ws in sets.items()}
    kept = {}

    def first():
        loads[0].wait()
        grad = dot_nt(dm[...], we[...])
        dx1_ref[...] = grad
        z_ref[...] = grad.astype(B)
        own, rest = own_cols(4)
        enc_other[4][...] = dot_tn(e_ref[...], dm[:, rest]).astype(B)
        mine[4][...] = dot_tn(e_ref[...], dm[:, own]).astype(B)
        give(4).start()
        kept["back"] = jnp.zeros_like(grad)

    def feed_forward(j):
        own, rest = own_cols(3)
        for cp in feed(j):
            cp.wait()
        kk = pl.ds(chunk(j), C)
        d = (slope2[j % 2] * dot_nt(z_ref[...], wd2[j % 2])).astype(B)
        kept["back"] = kept["back"] + dot_nt(d, wu2[j % 2])
        hk = h2[j % 2]
        enc_other[3][kk, :] = dot_tn(hk, z_ref[:, rest]).astype(B)
        mine[3][kk, :] = dot_tn(hk, z_ref[:, own]).astype(B)
        g = dot_tn(b_ref[...], d).astype(B)
        at = (j % (chunks // 2)) * C
        if j < chunks // 2:
            enc_other[2][:, at:at + C] = g
        else:
            mine[2][:, at:at + C] = g
        if j == chunks // 2 - 1:
            give(2).start()
        if j == chunks - 1:
            give(3).start()
        if j + 2 < chunks:
            for cp in feed(j + 2):
                cp.start()

    def project():
        by_input, by_gain = norm_back(x1_ref[...], gain2, kept.pop("back"))
        vbuf[0, 0] = jnp.zeros_like(vbuf[0, 0])
        vbuf[0, 0, 1:2, :] = jnp.sum(by_gain, axis=0, keepdims=True)
        dx1_ref[...] += by_input
        z_ref[...] = dx1_ref[...].astype(B)
        loads[1].wait()
        do_ref[...] = dot_nt(z_ref[...], wo[...]).astype(B)
        own, rest = own_cols(1)
        enc_other[1][...] = dot_tn(o_ref[...], z_ref[:, rest]).astype(B)
        mine[1][...] = dot_tn(o_ref[...], z_ref[:, own]).astype(B)
        give(1).start()

    def attend(part):
        mask = pair_mask()
        groups = x_ref.shape[0] // 128
        scale = ENC_HEAD ** -0.5
        lane = iota((128, 128), 1)
        for g in range(groups):
            if g * 2 // groups != part:
                continue
            rr = slice(128 * g, 128 * g + 128)
            valid = valid_keys(0 if g < wc else 1, wide_seen, narrow_seen)
            for j in range(D // 128):
                q, k, v = (qkv[rr, o + 128 * j:o + 128 * j + 128] for o in (0, D, 2 * D))
                g_o = do_ref[rr, 128 * j:128 * j + 128]
                k2 = jnp.concatenate([k, k], axis=0) * mask
                v2 = jnp.concatenate([v, v], axis=0) * mask
                shares = pair_shares(q, k2, valid)
                dp2 = dot_nt(g_o, v2)
                ds, low = [], []
                for h in range(2):
                    dp = dp2[:, 128 * h:128 * h + 128]
                    p = shares[h]
                    ds.append((p * (dp - jnp.sum(dp * p, axis=1, keepdims=True))).astype(B))
                    low.append(p.astype(B))
                dq = dot(jnp.concatenate(ds, axis=1), k2) * scale
                dk = jnp.where(lane < ENC_HEAD, dot_tn(ds[0], q), dot_tn(ds[1], q)) * scale
                dv = jnp.where(lane < ENC_HEAD, dot_tn(low[0], g_o), dot_tn(low[1], g_o))
                for o, d in ((0, dq), (D, dk), (2 * D, dv)):
                    dqkv[rr, o + 128 * j:o + 128 * j + 128] = d.astype(B)

    def mix():
        own, rest = own_cols(0)
        enc_other[0][...] = dot_tn(a_ref[...], dqkv[:, rest]).astype(B)
        give(0).start()
        mine[0][...] = dot_tn(a_ref[...], dqkv[:, own]).astype(B)

    bits = devices.bit_length() - 1

    def vcopy(k):
        return pltpu.make_async_remote_copy(
            src_ref=vbuf.at[0, k], dst_ref=vbuf.at[1, k], send_sem=vsend.at[k], recv_sem=vrecv.at[k],
            device_id=(lax.axis_index("fsdp"), 1 - c) if k == 0 else (flip(k - 1), c), device_id_type=MESH)

    def vstep(k):
        vcopy(k).wait()
        vbuf[0, k + 1] = vbuf[0, k] + vbuf[1, k]
        if k < bits:
            vcopy(k + 1).start()

    def last():
        loads[2].wait()
        by_input, by_gain = norm_back(x_ref[...], gain1, dot_nt(dqkv[...], wq[...]))
        vbuf[0, 0, 0:1, :] = jnp.sum(by_gain, axis=0, keepdims=True)
        DD = dec_vec.shape[1]
        vbuf[0, 0, 2:3, 0:DD] = dec_vec[2:3, :]
        vbuf[0, 0, 3:5, 0:DD] = dec_vec[0:2, :]
        vcopy(0).start()
        dx_ref[...] = dx1_ref[...] + by_input

    compute = [first] + [functools.partial(feed_forward, j) for j in range(chunks)] + [project]
    compute += [functools.partial(attend, 0), functools.partial(attend, 1), mix, last]

    def ready(s):
        if s in "AB":
            for w in sets[s]:
                takes[w - 5].wait()
        for w in sets[s]:
            give(w).wait_recv()

    vectors = []
    for token in schedule(nz + 1, len(compute)):
        if token[0] == "C":
            compute[token[1]]()
            if token[1] == len(compute) - 1:
                vectors = list(range(bits + 1))
        elif token[0] == "R":
            ready(token[1])
        elif token[0] == "L":
            leaves(token[1], members[token[2]])
        elif token[0] == "N":
            nodes(token[1], members[token[2]])
        else:
            for w in sets[token[1]]:
                total(w)
        if vectors and token[0] == "N":
            vstep(vectors.pop(0))
    for k in vectors:
        vstep(k)
    vec_out[...] = vbuf[0, bits + 1]
    sent(range(npc))
    finish(range(9))


def schedule(top, steps):
    if (top, steps) == (5, 12):
        return list(SCHEDULE)
    tokens = [("C", k) for k in range(steps)] + [("R", s) for s in "ABdueOQ"]
    tokens += [("L", top, s) for s in "ABdueOQ"]
    for h in range(top, 0, -1):
        tokens += [("N", h, s) for s in "ABdueOQ"]
        tokens += [("L", h - 1, s) for s in "ABdueOQ"] if h > 1 else []
    return tokens + [("T", s) for s in "ABdueOQ"]


def encode_back_reduce(tiles, counts, dm, dec_vec, saved, enc, dec_grads, routes, nz, cid=2):
    R = dm.shape[0]
    n = 4 * nz
    bits = n.bit_length() - 1
    x, a, qkv, o, x1, b, h, slope, e = saved
    wq, wo, wu, wd, we = enc
    D = wq.shape[0]
    grads = [*enc, *dec_grads]
    shards = [(g.shape[0] // n, g.shape[1]) for g in grads]
    V = pl.BlockSpec(memory_space=pltpu.VMEM)
    A = pl.BlockSpec(memory_space=pl.ANY)
    sds = jax.ShapeDtypeStruct
    dma = pltpu.SemaphoreType.DMA
    most = 1
    rbuf = []
    for w, c0, cols, order in routes:
        for d in "xyu":
            k = slot_count(order, d, nz)
            most = max(most, k)
            rbuf.append(pltpu.VMEM((k, shards[w][0], cols), B))
    npc = len(routes)
    halves = [pltpu.VMEM((g.shape[0], g.shape[1] // 2), B) for g in grads]
    C = 512
    out = pl.pallas_call(
        functools.partial(encode_back_reduce_kernel, *counts, nz, routes),
        out_shape=[sds((R, D), F), sds((8, D), F)] + [sds(s, F) for s in shards],
        in_specs=[V] * 10 + [A] * 11,
        out_specs=[V] * 2 + [A] * 9,
        scratch_shapes=[
            pltpu.VMEM(we.shape, B), pltpu.VMEM(wo.shape, B), pltpu.VMEM(wq.shape, B),
            pltpu.VMEM((2, C, D), B), pltpu.VMEM((2, D, C), B), pltpu.VMEM((2, R, C), B), pltpu.VMEM((2, R, C), F),
            pltpu.VMEM((R, D), F), pltpu.VMEM((R, D), B), pltpu.VMEM((R, D), B),
            pltpu.VMEM((R, 3 * D), B),
        ] + halves + halves[:5] + halves + [pltpu.VMEM((s[0], s[1] // 2), F) for s in shards] + rbuf + [
            pltpu.VMEM((2, bits + 2, 8, D), F), dma((11,)), dma((4,)), dma((9,)), dma((9,)), dma((npc,)),
            dma((npc, 3, most)), dma((9,)), dma((9,)), dma((9,)), dma((bits + 1,)), dma((bits + 1,))],
        compiler_params=pltpu.CompilerParams(collective_id=cid, has_side_effects=True, vmem_limit_bytes=63 * 2**20),
        name="encoder_backward_and_reduce",
    )(tiles, x, dm, dec_vec, e, b, x1, o, qkv, a, h, slope, we, wd, wu, wo, wq, *dec_grads)
    return out[0], out[1], out[2:]


ZXY = ("z", "x", "y")
ZYX = ("z", "y", "x")
XYZ = ("x", "y", "z")
YXZ = ("y", "x", "z")
XZY = ("x", "z", "y")
YZX = ("y", "z", "x")
GATHER = ((0, YXZ), (2, ZXY), (3, ZYX), (1, ZXY), (4, ZYX), (5, XZY), (7, YZX), (8, ZXY), (6, ZYX))
GATHER_SCHEDULE = (
    ("S", "e"), ("S", "o"), ("S", "u"), ("S", "d"), ("S", "q"), ("P",), ("V", 1, "d"), ("V", 1, "o"),
    ("V", 1, "q"), ("V", 1, "u"), ("V", 2, "q"), ("V", 2, "d"), ("V", 2, "u"), ("V", 2, "o"), ("S", "D"),
    ("V", 3, "q"), ("V", 3, "d"), ("V", 3, "u"), ("V", 3, "o"), ("V", 1, "e"), ("V", 4, "d"), ("V", 4, "u"),
    ("V", 4, "q"), ("V", 4, "o"), ("S", "X"), ("V", 2, "e"), ("V", 1, "D"), ("V", 5, "q"), ("V", 5, "o"),
    ("R", "q"), ("V", 5, "u"), ("V", 1, "X"), ("V", 5, "d"), ("V", 3, "e"), ("C", 0), ("V", 2, "D"), ("R", "u"),
    ("C", 1), ("V", 2, "X"), ("R", "d"), ("R", "o"), ("C", 2), ("V", 4, "e"), ("C", 3), ("V", 3, "D"), ("C", 4),
    ("V", 3, "X"), ("C", 5), ("V", 4, "D"), ("C", 6), ("V", 5, "e"), ("V", 4, "X"), ("C", 7), ("C", 8),
    ("R", "e"), ("C", 9), ("V", 5, "D"), ("V", 5, "X"), ("C", 10),
)
REDUCE = ((5, YXZ), (7, ZXY), (8, ZYX), (6, YXZ), (3, ZYX), (2, ZXY), (4, ZXY), (1, ZYX), (0, XYZ))
SCHEDULE = (
    ("C", 0), ("C", 1), ("C", 2), ("R", "A"), ("N", 5, "A"), ("L", 5, "A"), ("C", 3), ("N", 4, "A"), ("R", "B"),
    ("L", 5, "B"), ("L", 4, "A"), ("C", 4), ("L", 4, "B"), ("N", 5, "B"), ("L", 3, "A"), ("C", 5), ("N", 4, "B"),
    ("N", 3, "A"), ("C", 6), ("R", "u"), ("L", 3, "B"), ("C", 7), ("R", "e"), ("L", 5, "e"), ("N", 3, "B"),
    ("N", 2, "A"), ("L", 5, "u"), ("L", 2, "A"), ("N", 5, "u"), ("L", 2, "B"), ("R", "d"), ("C", 8),
    ("N", 2, "B"), ("L", 5, "d"), ("C", 9), ("R", "O"), ("C", 10), ("L", 1, "B"), ("N", 5, "O"), ("N", 1, "A"),
    ("L", 4, "e"), ("N", 1, "B"), ("L", 5, "O"), ("R", "Q"), ("L", 5, "Q"), ("L", 4, "Q"), ("N", 5, "d"),
    ("N", 5, "Q"), ("L", 4, "u"), ("N", 4, "u"), ("L", 4, "d"), ("N", 4, "d"), ("N", 5, "e"), ("L", 3, "Q"),
    ("L", 1, "A"), ("N", 4, "Q"), ("L", 3, "d"), ("L", 3, "u"), ("N", 3, "u"), ("N", 3, "d"), ("L", 2, "u"),
    ("L", 2, "Q"), ("L", 4, "O"), ("N", 3, "Q"), ("T", "B"), ("L", 3, "O"), ("N", 4, "O"), ("N", 4, "e"),
    ("L", 2, "O"), ("C", 11), ("N", 2, "d"), ("L", 2, "d"), ("N", 2, "u"), ("L", 1, "Q"), ("L", 3, "e"),
    ("N", 3, "e"), ("N", 2, "Q"), ("N", 3, "O"), ("N", 1, "d"), ("L", 1, "d"), ("L", 2, "e"), ("N", 2, "e"),
    ("L", 1, "e"), ("N", 2, "O"), ("N", 1, "Q"), ("T", "A"), ("T", "d"), ("L", 1, "u"), ("L", 1, "O"),
    ("N", 1, "e"), ("N", 1, "u"), ("T", "Q"), ("N", 1, "O"), ("T", "u"), ("T", "e"), ("T", "O"),
)


def whole_tiles(shards, devices):
    return devices % 4 == 0 and all(s.shape[0] % 16 == 0 and s.shape[1] % 256 == 0 for s in shards)


def local(
    clips_wide, clips_narrow, visible_wide, visible_narrow, shift_wide, shift_narrow,
    enc_norm1, enc_qkv, enc_out, enc_norm2, enc_up, enc_down, embed_proj, mask_token,
    dec_norm1, dec_qkv, dec_out, dec_norm2, dec_up, dec_down, cotan_wide, cotan_narrow,
):
    devices = lax.axis_size("fsdp")
    matrices = [enc_qkv, enc_out, enc_up, enc_down, embed_proj, dec_qkv, dec_out, dec_up, dec_down]
    vectors = [enc_norm1, enc_norm2, mask_token, dec_norm1, dec_norm2]
    packed = jnp.stack([jnp.pad(v, (0, 128 - v.shape[0])) for v in vectors])
    packed = jnp.pad(packed, ((0, 16 - len(vectors)), (0, 0)))
    narrow = jnp.transpose(clips_narrow, (1, 0, 2))
    place = (shift_wide, shift_narrow, visible_wide, visible_narrow, cotan_wide, cotan_narrow)
    counts = (clips_wide.shape[0], clips_wide.shape[1], clips_narrow.shape[1])
    direct = whole_tiles(matrices, devices)
    if direct:
        pieces = [(len(matrices), 0, 128, ZXY, False)]
        pieces += [(w, 0, matrices[w].shape[1] // 2, order, True) for w, order in GATHER]
        whole, placed, (embedded, *saved) = gather_encode(
            matrices + [packed], pieces, place, clips_wide, narrow, devices // 4
        )
    else:
        whole = [lax.all_gather(m, "fsdp", axis=0, tiled=True) for m in (*matrices, packed)]
        got = encoder_forward(place, whole[9], clips_wide, narrow, *whole[:5], devices)
        placed, embedded, saved = got[:3], got[3], got[4:]
    enc, dec, tiles = whole[:5], whole[5:9], whole[9]
    decoded_wide, decoded_narrow, grad_embedded, *dec_grads, gains = decoder(
        embedded, tiles, placed, cotan_wide.shape, cotan_narrow.shape, *dec, devices
    )
    if direct:
        routes = [(w, 0, matrices[w].shape[1] // 2, order) for w, order in REDUCE]
        grad_rows, gains, shares = encode_back_reduce(
            tiles, counts, grad_embedded, gains, saved, enc, dec_grads, routes, devices // 4
        )
    else:
        grad_rows, *enc_grads, gains = encoder_backward(
            tiles, counts, grad_embedded, gains, saved, *enc, devices
        )
        gains = lax.psum(gains, ("fsdp", "dp"))
        shares = [
            lax.psum_scatter(lax.psum(g.astype(F), "dp"), "fsdp", scatter_dimension=0, tiled=True)
            for g in enc_grads + dec_grads
        ]
    encoded_wide, encoded_narrow, grad_wide, grad_narrow, m, v = results(
        lax.axis_index("fsdp"), saved[-1], grad_rows, gains, shares, [v.shape[0] for v in vectors],
        clips_wide.shape, clips_narrow.shape,
    )
    return (
        encoded_wide, encoded_narrow, decoded_wide, decoded_narrow, grad_wide, grad_narrow,
        v[0], m[0], m[1], v[1], m[2], m[3], m[4], v[2], v[3], m[5], m[6], v[4], m[7], m[8],
    )


def solution(mesh):
    clips = ("fsdp", "dp")
    matrix, vector = P("fsdp", None), P("fsdp")
    weights = (
        vector, matrix, matrix, vector, matrix, matrix, matrix, vector,
        vector, matrix, matrix, vector, matrix, matrix,
    )
    rows, pairs = P(clips, None, None), P(clips, None)
    return jax.shard_map(
        local,
        mesh=mesh,
        in_specs=(rows, rows, pairs, pairs, pairs, P(clips), *weights, rows, rows),
        out_specs=(rows,) * 6 + weights,
        check_vma=False,
    )
```

```python
import functools

import jax
import jax.numpy as jnp
from jax import lax
from jax.experimental import pallas as pl
from jax.experimental.pallas import tpu as pltpu
from jax.sharding import PartitionSpec as P

MESH = pl.DeviceIdType.MESH


def slots():
    out=[]
    for bx in (0,1):
        for by in (0,1):
            for sgn in (0,1,-1):
                if (bx,by,sgn)!=(0,0,0): out.append((bx,by,sgn))
    return out

def forwards(order,bx,by,sgn):
    differs={'x':bx,'y':by,'z':int(sgn!=0)}
    last=max([j for j,d in enumerate(order) if differs[d]],default=-1)
    dirs=[]
    for j,d in enumerate(order):
        if j>last:
            dirs += ['u','d'] if d=='z' else [d]
    if last>=0 and order[last]=='z':
        dirs.append('u' if sgn<0 else 'd')
    return dirs


TIME = 64
WIN = 4
EPS = 1e-6
F = jnp.float32
B = jnp.bfloat16
VMEM_LIMIT = 60 * 2**20


def dot(a, b):
    return lax.dot_general(a, b, (((1,), (0,)), ((), ())), preferred_element_type=F)


def dot_nt(a, b):
    return lax.dot_general(a, b, (((1,), (1,)), ((), ())), preferred_element_type=F)


def dot_tn(a, b):
    return lax.dot_general(a, b, (((0,), (0,)), ((), ())), preferred_element_type=F)


def iota(shape, dim):
    return lax.broadcasted_iota(jnp.int32, shape, dim)


def norm_stats(x):
    center = jnp.mean(x, axis=-1, keepdims=True)
    shifted = x - center
    spread = jnp.mean(shifted * shifted, axis=-1, keepdims=True)
    scale = lax.rsqrt(spread + EPS)
    return shifted * scale, scale


def norm_back(x, gain, grad):
    unit, scale = norm_stats(x)
    by_gain = grad * unit
    by_unit = grad * gain
    mean_one = jnp.mean(by_unit, axis=-1, keepdims=True)
    mean_two = jnp.mean(by_unit * unit, axis=-1, keepdims=True)
    by_input = scale * (by_unit - mean_one - unit * mean_two)
    return by_input, jnp.sum(by_gain.reshape(-1, 8, x.shape[1]), axis=0)


def gelu_both(u):
    t = 1.0 / (1.0 + (0.3275911 * 0.7071067811865476) * jnp.abs(u))
    bell = jnp.exp(-0.5 * u * u)
    poly = t * (0.127414796 + t * (-0.142248368 + t * (0.7107068705 + t * (-0.7265760135 + t * 0.5307027145))))
    tail = poly * bell
    phi = jnp.where(u < 0, tail, 1.0 - tail)
    return u * phi, phi + u * (bell * 0.3989422804014327)


def spread_vector(tiles, lane, size, devices):
    part = size // devices
    pick = (iota((128, size), 1) % part == iota((128, size), 0)).astype(B)
    wide = dot(tiles, pick)
    rows = iota((tiles.shape[0], size), 0)
    keep = rows == (iota((tiles.shape[0], size), 1) // part) * 16 + lane
    return jnp.sum(jnp.where(keep, wide, 0.0), axis=0, keepdims=True)


def group_sums(x, ones):
    high = x.astype(B)
    return dot(high, ones) + dot((x - high.astype(F)).astype(B), ones)


def lane_groups(x, op):
    lanes = iota(x.shape, 1)
    width = x.shape[1]
    for d in (1, 2, 4, 8):
        other = jnp.where((lanes & d) != 0, pltpu.roll(x, d, 1), pltpu.roll(x, width - d, 1))
        x = op(x, other)
    return x


HEAD = 32
AREA = WIN * WIN


def stack8(block, mask):
    return jnp.concatenate([block] * 8, axis=0) * mask


def dec_kernel(wc, nc, wide_rows, narrow_rows, devices, tiles, m_ref, sel, perm_h, dz_h, wq_h, wo_h, wu_h, wd_h,
               outw, outn, dm_ref, gq_h, go_h, gu_h, gd_h, vec_ref,
               wq, wo, wu, wd, mhi, mlo, r_ref, a_ref, qkv, p_ref, o_ref,
               b_ref, h_ref, du, dx1, do_ref, dqkv, dec, dm_acc, acc, gq, go, gu, gd, perm, dz, sems):
    D = wo.shape[0]
    rows = wc * wide_rows + nc * narrow_rows
    T = 256
    tall = 512 if rows % 512 == 0 else T
    nt = rows // T
    wide_tiles = wc * wide_rows // T
    cps = []
    for k, (src, dst) in enumerate(((wq_h, wq), (wo_h, wo), (wu_h, wu), (wd_h, wd), (dz_h, dz), (perm_h, perm))):
        cp = pltpu.make_async_copy(src, dst, sems.at[k])
        cp.start()
        cps.append(cp)
    gain1 = spread_vector(tiles[...], 3, D, devices)
    gain2 = spread_vector(tiles[...], 4, D, devices)
    filler = spread_vector(tiles[...], 2, D, devices)
    mhi[...] = m_ref[...].astype(B)
    mlo[...] = (m_ref[...] - mhi[...].astype(F)).astype(B)
    dm_acc[...] = jnp.zeros_like(dm_acc)
    acc[...] = jnp.zeros_like(acc)
    def group_rows(t):
        g = jnp.where(t < wide_tiles, t * T // wide_rows, wc + (t - wide_tiles) // 2)
        return pl.ds(pl.multiple_of(g * 128, 128), 128)

    cps[0].wait()

    @pl.loop(0, nt)
    def _(t):
        rr = pl.ds(pl.multiple_of(t * T, T), T)
        g = group_rows(t)
        s = sel[rr]
        seen = jnp.sum(s.astype(F), axis=1, keepdims=True)
        x = dot(s, mhi[g]) + dot(s, mlo[g]) + (1.0 - seen) * filler
        r_ref[rr] = x
        a = (norm_stats(x)[0] * gain1).astype(B)
        a_ref[rr] = a
        qkv[rr] = dot(a, wq[...]).astype(B)

    mask = (iota((128, 256), 0) // AREA == iota((128, 256), 1) // HEAD).astype(B)
    scale = HEAD ** -0.5
    nw = 32
    while rows % (nw * AREA):
        nw //= 2
    ones = (iota((128, 128), 0) // AREA == iota((128, 128), 1) // AREA).astype(B)

    @pl.loop(0, rows // (nw * AREA))
    def _(g):
        base = pl.multiple_of(g * nw * AREA, nw * AREA)
        rr = pl.ds(base, nw * AREA)
        for a in range(D // 256):
            cq = pl.ds(a * 256, 256)
            q, k, v = qkv[rr, cq], qkv[rr, pl.ds(D + a * 256, 256)], qkv[rr, pl.ds(2 * D + a * 256, 256)]
            w16 = [slice(AREA * j, AREA * j + AREA) for j in range(nw)]
            s = jnp.concatenate([dot_nt(q[w], stack8(k[w], mask)) for w in w16], axis=0) * scale
            e = jnp.exp(s - lane_groups(s, jnp.maximum))
            p = e / group_sums(e, ones)
            p_ref[rr, pl.ds(a * 128, 128)] = p
            low = p.astype(B)
            o_ref[rr, cq] = jnp.concatenate([dot(low[w], stack8(v[w], mask)) for w in w16], axis=0).astype(B)

    for cp in cps[1:]:
        cp.wait()

    @pl.loop(0, rows // tall)
    def _(t):
        rr = pl.ds(pl.multiple_of(t * tall, tall), tall)
        x1 = r_ref[rr] + dot(o_ref[rr], wo[...])
        b = (norm_stats(x1)[0] * gain2).astype(B)
        b_ref[rr] = b
        z = dz[rr]
        out = x1
        back = jnp.zeros((tall, D), F)
        C = 512
        for k in range(0, wu.shape[1], C):
            u = dot(b, wu[:, k:k + C])
            h, slope = gelu_both(u)
            h = h.astype(B)
            h_ref[rr, k:k + C] = h
            out = out + dot(h, wd[k:k + C, :])
            d = (slope * dot_nt(z, wd[k:k + C, :])).astype(B)
            du[rr, k:k + C] = d
            back = back + dot_nt(d, wu[:, k:k + C])
        dec[rr] = out.astype(B)
        by_input, by_gain = norm_back(x1, gain2, back)
        acc[1] += by_gain
        dx = z.astype(F) + by_input
        dx1[rr] = dx
        do_ref[rr] = dot_nt(dx.astype(B), wo[...]).astype(B)

    for i in range(wc + nc):
        base, n, out = (i * wide_rows, wide_rows, outw) if i < wc else (
            wc * wide_rows + (i - wc) * narrow_rows, narrow_rows, outn)
        out[i if i < wc else i - wc] = dot_tn(perm[base:base + n, 0:n], dec[base:base + n]).astype(B)

    @pl.loop(0, rows // (nw * AREA))
    def _(g):
        base = pl.multiple_of(g * nw * AREA, nw * AREA)
        rr = pl.ds(base, nw * AREA)
        w16 = [slice(AREA * j, AREA * j + AREA) for j in range(nw)]
        for a in range(D // 256):
            cq = pl.ds(a * 256, 256)
            q, k, v = qkv[rr, cq], qkv[rr, pl.ds(D + a * 256, 256)], qkv[rr, pl.ds(2 * D + a * 256, 256)]
            go_ = do_ref[rr, cq]
            ks = [stack8(k[w], mask) for w in w16]
            qs = [stack8(q[w], mask) for w in w16]
            gs = [stack8(go_[w], mask) for w in w16]
            p = p_ref[rr, pl.ds(a * 128, 128)]
            dp = jnp.concatenate([dot_nt(go_[w], stack8(v[w], mask)) for w in w16], axis=0)
            ds = (p * (dp - group_sums(dp * p, ones))).astype(B)
            dqkv[rr, cq] = (jnp.concatenate([dot(ds[w], m) for w, m in zip(w16, ks)], axis=0) * scale).astype(B)
            s = jnp.concatenate([dot_nt(k[w], m) for w, m in zip(w16, qs)], axis=0) * scale
            s = s.reshape(nw, AREA, 128)
            e = jnp.exp(s - jnp.max(s, axis=1, keepdims=True))
            p = e / jnp.sum(e, axis=1, keepdims=True)
            dp = jnp.concatenate([dot_nt(v[w], m) for w, m in zip(w16, gs)], axis=0).reshape(nw, AREA, 128)
            ds = (p * (dp - jnp.sum(dp * p, axis=1, keepdims=True))).reshape(nw * AREA, 128).astype(B)
            p = p.reshape(nw * AREA, 128).astype(B)
            dqkv[rr, pl.ds(D + a * 256, 256)] = (jnp.concatenate([dot(ds[w], m) for w, m in zip(w16, qs)], axis=0) * scale).astype(B)
            dqkv[rr, pl.ds(2 * D + a * 256, 256)] = jnp.concatenate([dot(p[w], m) for w, m in zip(w16, gs)], axis=0).astype(B)

    @pl.loop(0, nt)
    def _(t):
        rr = pl.ds(pl.multiple_of(t * T, T), T)
        g = group_rows(t)
        by_input, by_gain = norm_back(r_ref[rr], gain1, dot_nt(dqkv[rr], wq[...]))
        acc[0] += by_gain
        dr = dx1[rr] + by_input
        s = sel[rr]
        hidden = 1.0 - jnp.sum(s.astype(F), axis=1, keepdims=True)
        acc[2] += jnp.sum((dr * hidden).reshape(-1, 8, D), axis=0)
        dm_acc[g] += dot_tn(s, dr.astype(B))

    dm_ref[...] = dm_acc[...].astype(B)
    for k in range(3):
        vec_ref[k:k + 1, :] = jnp.sum(acc[k], axis=0, keepdims=True)
    vec_ref[3:, :] = jnp.zeros((5, D), F)
    step = 512
    copies = []

    def leave(k, src, dst):
        cp = pltpu.make_async_copy(src, dst, sems.at[6 + k])
        cp.start()
        copies.append(cp)

    @pl.loop(0, wd.shape[0] // step)
    def _(k):
        kk = pl.ds(pl.multiple_of(k * step, step), step)
        gd[kk, :] = dot_tn(h_ref[:, kk], dz[...]).astype(B)

    leave(0, gd, gd_h)

    @pl.loop(0, wd.shape[0] // step)
    def _(k):
        kk = pl.ds(pl.multiple_of(k * step, step), step)
        gu[:, kk] = dot_tn(b_ref[...], du[:, kk]).astype(B)

    leave(1, gu, gu_h)

    @pl.loop(0, wq.shape[1] // step)
    def _(k):
        kk = pl.ds(pl.multiple_of(k * step, step), step)
        gq[:, kk] = dot_tn(a_ref[...], dqkv[:, kk]).astype(B)

    leave(2, gq, gq_h)
    go[...] = dot_tn(o_ref[...], dx1[...].astype(B)).astype(B)
    leave(3, go, go_h)
    for cp in copies:
        cp.wait()


def decoder(m, tiles, placed, wide_shape, narrow_shape, wq, wo, wu, wd, devices):
    wc, wide_rows, D = wide_shape
    nc, narrow_rows, _ = narrow_shape
    FFD = wu.shape[1]
    rows = wc * wide_rows + nc * narrow_rows
    V = pl.BlockSpec(memory_space=pltpu.VMEM)
    A = pl.BlockSpec(memory_space=pl.ANY)
    sds = jax.ShapeDtypeStruct
    weights = [pltpu.VMEM(w.shape, B) for w in (wq, wo, wu, wd)]
    return pl.pallas_call(
        functools.partial(dec_kernel, wc, nc, wide_rows, narrow_rows, devices),
        out_shape=[sds(wide_shape, B), sds(narrow_shape, B), sds(m.shape, B), sds(wq.shape, B), sds(wo.shape, B),
                   sds(wu.shape, B), sds(wd.shape, B), sds((8, D), F)],
        in_specs=[V] * 3 + [A] * 6,
        out_specs=[V] * 3 + [A] * 4 + [V],
        scratch_shapes=weights + [
            pltpu.VMEM(m.shape, B), pltpu.VMEM(m.shape, B),
            pltpu.VMEM((rows, D), F), pltpu.VMEM((rows, D), B), pltpu.VMEM((rows, 3 * D), B),
            pltpu.VMEM((rows, D // 2), F), pltpu.VMEM((rows, D), B),
            pltpu.VMEM((rows, D), B), pltpu.VMEM((rows, FFD), B), pltpu.VMEM((rows, FFD), B), pltpu.VMEM((rows, D), F),
            pltpu.VMEM((rows, D), B), pltpu.VMEM((rows, 3 * D), B), pltpu.VMEM((rows, D), B),
            pltpu.VMEM(m.shape, F), pltpu.VMEM((3, 8, D), F)] + weights + [
            pltpu.VMEM(placed[0].shape, B), pltpu.VMEM(placed[2].shape, B), pltpu.SemaphoreType.DMA((10,))],
        compiler_params=pltpu.CompilerParams(vmem_limit_bytes=VMEM_LIMIT),
        name="decoder_block",
    )(tiles, m, placed[1], placed[0], placed[2], wq, wo, wu, wd)


def placement(wc, nc, shw, shn, visw, visn, cotw, cotn, perm, sel, dz):
    T = 256
    wide_rows, narrow_rows = cotw.shape[1], cotn.shape[1]
    clips = [(i * wide_rows, wide_rows, 8, shw[i, 0], shw[i, 1], cotw, i, visw, 0) for i in range(wc)]
    clips += [(wc * wide_rows + i * narrow_rows, narrow_rows, 4, shn[i], 0, cotn, i, visn, 64 * (i % 2)) for i in range(nc)]
    for base, n, cols, s, r, cot, i, vis, o in clips:
        seen = vis.shape[1]
        parts = [jnp.full((1, o), -1, jnp.int32)] if o else []
        parts += [vis[i:i + 1, :], jnp.full((1, 128 - o - seen), -1, jnp.int32)]
        shown = jnp.concatenate(parts, axis=1)
        for k in range(0, n, T):
            j = iota((T, 1), 0) + k
            w, q = j >> 4, j & 15
            wf = cols // WIN
            t = ((w // wf) * WIN + (q >> 2) + s) & (TIME - 1)
            f = ((w % wf) * WIN + (q & 3) + r) & (cols - 1)
            patch = t * cols + f
            where = pl.ds(base + k, T)
            hot = jnp.where(iota((T, n), 1) == patch, 1.0, 0.0).astype(B)
            perm[where, 0:n] = hot
            if n < perm.shape[1]:
                perm[where, n:] = jnp.zeros((T, perm.shape[1] - n), B)
            sel[where] = jnp.where(shown == patch, 1.0, 0.0).astype(B)
            dz[where] = dot(hot, cot[i]).astype(B)


def placed_shapes(cotw, cotn):
    rows = cotw.shape[0] * cotw.shape[1] + cotn.shape[0] * cotn.shape[1]
    return [jax.ShapeDtypeStruct((rows, n), B) for n in (cotw.shape[1], 128, cotw.shape[2])]


ENC_HEAD = 64


def valid_keys(kind, wide_seen, narrow_seen):
    q, k = iota((128, 128), 0), iota((128, 128), 1)
    if kind == 0:
        return k < wide_seen
    return ((q // 64) == (k // 64)) & (k % 64 < narrow_seen)


def pair_mask():
    return (iota((256, 128), 0) // 128 == iota((256, 128), 1) // ENC_HEAD).astype(B)


def pair_shares(q, k2, valid):
    s2 = dot_nt(q, k2) * (ENC_HEAD ** -0.5)
    shares = []
    for h in range(2):
        s = jnp.where(valid, s2[:, 128 * h:128 * h + 128], -1e30)
        e = jnp.exp(s - jnp.max(s, axis=1, keepdims=True))
        shares.append(e / jnp.sum(e, axis=1, keepdims=True))
    return shares


def load_rows(dst, pair, wide, narrow, wc, nc):
    dst[...] = jnp.zeros_like(dst)
    for i in range(wc):
        dst[128 * i:128 * i + wide.shape[1], :] = wide[i].astype(F)
    pair[...] = narrow[...].astype(F)
    for i in range(nc):
        o = 128 * wc + 64 * i
        dst[o:o + narrow.shape[0], :] = pair[:, i, :]


def enc_forward_kernel(wc, nc, devices, shw, shn, visw, visn, cotw, cotn, tiles, cw, cn, wq_h, wo_h, wu_h, wd_h, we_h,
                       perm, sel, dz, m_ref, x_ref, a_ref, qkv, o_ref, x1_ref, b_ref, h_ref, slope_ref, e_ref,
                       wq, wo, wu, wd, we, pair, sems):
    D = wo.shape[0]
    cps = []
    for k, (src, dst) in enumerate(((wq_h, wq), (wo_h, wo), (wu_h, wu), (wd_h, wd), (we_h, we))):
        cp = pltpu.make_async_copy(src, dst, sems.at[k])
        cp.start()
        cps.append(cp)
    placement(wc, nc, shw, shn, visw, visn, cotw, cotn, perm, sel, dz)
    load_rows(x_ref, pair, cw, cn, wc, nc)
    gain1 = spread_vector(tiles[...], 0, D, devices)
    gain2 = spread_vector(tiles[...], 1, D, devices)
    x = x_ref[...]
    a = (norm_stats(x)[0] * gain1).astype(B)
    a_ref[...] = a
    cps[0].wait()
    for k in range(0, 3 * D, D):
        qkv[:, k:k + D] = dot(a, wq[:, k:k + D]).astype(B)
    mask = pair_mask()
    groups = x_ref.shape[0] // 128
    for g in range(groups):
        rr = slice(128 * g, 128 * g + 128)
        valid = valid_keys(0 if g < wc else 1, cw.shape[1], cn.shape[0])
        for j in range(D // 128):
            q, k, v = (qkv[rr, o + 128 * j:o + 128 * j + 128] for o in (0, D, 2 * D))
            k2 = jnp.concatenate([k, k], axis=0) * mask
            v2 = jnp.concatenate([v, v], axis=0) * mask
            p2 = jnp.concatenate(pair_shares(q, k2, valid), axis=1).astype(B)
            o_ref[rr, 128 * j:128 * j + 128] = dot(p2, v2).astype(B)
    cps[1].wait()
    x1 = x_ref[...] + dot(o_ref[...], wo[...])
    x1_ref[...] = x1
    b = (norm_stats(x1)[0] * gain2).astype(B)
    b_ref[...] = b
    cps[2].wait()
    cps[3].wait()
    out = x1
    C = 512
    for k in range(0, wu.shape[1], C):
        h, slope = gelu_both(dot(b, wu[:, k:k + C]))
        h = h.astype(B)
        h_ref[:, k:k + C] = h
        slope_ref[:, k:k + C] = slope
        out = out + dot(h, wd[k:k + C, :])
    e_ref[...] = out.astype(B)
    cps[4].wait()
    m_ref[...] = dot(e_ref[...], we[...])


def encoder_forward(place, tiles, cw, cn, wq, wo, wu, wd, we, devices):
    wc, nc = cw.shape[0], cn.shape[1]
    D = cw.shape[2]
    FFD = wu.shape[1]
    R = 128 * wc + 128 * ((nc + 1) // 2)
    V = pl.BlockSpec(memory_space=pltpu.VMEM)
    S = pl.BlockSpec(memory_space=pltpu.SMEM)
    A = pl.BlockSpec(memory_space=pl.ANY)
    sds = jax.ShapeDtypeStruct
    return pl.pallas_call(
        functools.partial(enc_forward_kernel, wc, nc, devices),
        out_shape=placed_shapes(*place[4:]) + [sds((R, we.shape[1]), F), sds((R, D), F), sds((R, D), B), sds((R, 3 * D), B),
                   sds((R, D), B), sds((R, D), F), sds((R, D), B), sds((R, FFD), B), sds((R, FFD), F), sds((R, D), B)],
        in_specs=[S, S] + [V] * 7 + [A] * 5,
        out_specs=[V] * 13,
        scratch_shapes=[pltpu.VMEM(w.shape, B) for w in (wq, wo, wu, wd, we)]
        + [pltpu.VMEM(cn.shape, F), pltpu.SemaphoreType.DMA((5,))],
        compiler_params=pltpu.CompilerParams(vmem_limit_bytes=VMEM_LIMIT),
        name="encoder_forward",
    )(*place, tiles, cw, cn, wq, wo, wu, wd, we)


def enc_backward_kernel(wc, wide_seen, narrow_seen, devices, tiles, dm, dec_vec, x_in, a_ref, qkv, o_ref, x1_ref, b_ref, h_ref, slope_ref, e_ref,
                        wq_h, wo_h, wu_h, wd_h, we_h,
                        dx_ref, gq, go, gu, gd, ge, vec_ref,
                        wq, wo, wu, wd, we, do_ref, dqkv, du, sems):
    D = wo.shape[0]
    cps = []
    for k, (src, dst) in enumerate(((we_h, we), (wd_h, wd), (wu_h, wu), (wo_h, wo), (wq_h, wq))):
        cp = pltpu.make_async_copy(src, dst, sems.at[k])
        cp.start()
        cps.append(cp)
    gain1 = spread_vector(tiles[...], 0, D, devices)
    gain2 = spread_vector(tiles[...], 1, D, devices)
    cps[0].wait()
    grad = dot_nt(dm[...], we[...])
    z = grad.astype(B)
    ge[...] = dot_tn(e_ref[...], dm[...]).astype(B)
    cps[1].wait()
    cps[2].wait()
    back = jnp.zeros_like(grad)
    C = 512
    for k in range(0, wu.shape[1], C):
        d = (slope_ref[:, k:k + C] * dot_nt(z, wd[k:k + C, :])).astype(B)
        du[:, k:k + C] = d
        back = back + dot_nt(d, wu[:, k:k + C])
        gd[k:k + C, :] = dot_tn(h_ref[:, k:k + C], z).astype(B)
        gu[:, k:k + C] = dot_tn(b_ref[...], d).astype(B)
    by_input, by_gain = norm_back(x1_ref[...], gain2, back)
    vec_ref[...] = jnp.zeros_like(vec_ref)
    vec_ref[1:2, :] = jnp.sum(by_gain, axis=0, keepdims=True)
    dx1 = grad + by_input
    y = dx1.astype(B)
    cps[3].wait()
    do_ref[...] = dot_nt(y, wo[...]).astype(B)
    go[...] = dot_tn(o_ref[...], y).astype(B)
    mask = pair_mask()
    groups = x_in.shape[0] // 128
    scale = ENC_HEAD ** -0.5
    lane = iota((128, 128), 1)
    for g in range(groups):
        rr = slice(128 * g, 128 * g + 128)
        valid = valid_keys(0 if g < wc else 1, wide_seen, narrow_seen)
        for j in range(D // 128):
            q, k, v = (qkv[rr, o + 128 * j:o + 128 * j + 128] for o in (0, D, 2 * D))
            g_o = do_ref[rr, 128 * j:128 * j + 128]
            k2 = jnp.concatenate([k, k], axis=0) * mask
            v2 = jnp.concatenate([v, v], axis=0) * mask
            shares = pair_shares(q, k2, valid)
            dp2 = dot_nt(g_o, v2)
            ds, low = [], []
            for h in range(2):
                dp = dp2[:, 128 * h:128 * h + 128]
                p = shares[h]
                ds.append((p * (dp - jnp.sum(dp * p, axis=1, keepdims=True))).astype(B))
                low.append(p.astype(B))
            dq = dot(jnp.concatenate(ds, axis=1), k2) * scale
            dk = jnp.where(lane < ENC_HEAD, dot_tn(ds[0], q), dot_tn(ds[1], q)) * scale
            dv = jnp.where(lane < ENC_HEAD, dot_tn(low[0], g_o), dot_tn(low[1], g_o))
            for o, d in ((0, dq), (D, dk), (2 * D, dv)):
                dqkv[rr, o + 128 * j:o + 128 * j + 128] = d.astype(B)
    cps[4].wait()
    for k in range(0, 3 * D, D):
        gq[:, k:k + D] = dot_tn(a_ref[...], dqkv[:, k:k + D]).astype(B)
    by_input, by_gain = norm_back(x_in[...], gain1, dot_nt(dqkv[...], wq[...]))
    vec_ref[0:1, :] = jnp.sum(by_gain, axis=0, keepdims=True)
    DD = dec_vec.shape[1]
    vec_ref[2:3, 0:DD] = dec_vec[2:3, :]
    vec_ref[3:5, 0:DD] = dec_vec[0:2, :]
    dx_ref[...] = dx1 + by_input


def encoder_backward(tiles, counts, dm, dec_vec, saved, wq, wo, wu, wd, we, devices):
    D = wq.shape[0]
    FFD = wu.shape[1]
    R = dm.shape[0]
    V = pl.BlockSpec(memory_space=pltpu.VMEM)
    A = pl.BlockSpec(memory_space=pl.ANY)
    sds = jax.ShapeDtypeStruct
    return pl.pallas_call(
        functools.partial(enc_backward_kernel, *counts, devices),
        out_shape=[sds((R, D), F)] + [sds(w.shape, B) for w in (wq, wo, wu, wd, we)] + [sds((8, D), F)],
        in_specs=[V] * 12 + [A] * 5,
        out_specs=[V] * 7,
        scratch_shapes=[pltpu.VMEM(w.shape, B) for w in (wq, wo, wu, wd, we)]
        + [pltpu.VMEM((R, D), B), pltpu.VMEM((R, 3 * D), B), pltpu.VMEM((R, FFD), B), pltpu.SemaphoreType.DMA((5,))],
        compiler_params=pltpu.CompilerParams(vmem_limit_bytes=VMEM_LIMIT),
        name="encoder_backward",
    )(tiles, dm, dec_vec, *saved, wq, wo, wu, wd, we)


def results_kernel(wc, nc, sizes, *refs):
    me, e, dx, vec, *refs = refs
    shares, refs = refs[:9], refs[9:]
    encw, encn, gradw, gradn, *refs = refs
    outs, refs = refs[:9], refs[9:]
    vectors, (pair,) = refs[:len(sizes)], refs[len(sizes):]
    for src, wide, narrow in ((e, encw, encn), (dx, gradw, gradn)):
        for i in range(wc):
            rows = src[128 * i:128 * i + encw.shape[1], :]
            if wide is encw:
                wide[i] = rows
            else:
                wide[:, i, :] = rows
        for i in range(nc):
            o = 128 * wc + 64 * i
            pair[:, i, :] = src[o:o + narrow.shape[0], :].astype(F)
        narrow[...] = pair[...].astype(narrow.dtype)
    for src, dst in zip(shares, outs):
        dst[...] = src[...]
    width = vec.shape[1]
    for k, (n, ref) in enumerate(zip(sizes, vectors)):
        ref[...] = pltpu.roll(vec[k:k + 1, :], lax.rem(width - me[0] * n, width), 1)[:, 0:n]


def results(me, e, dx, vec, shares, sizes, wide_shape, narrow_shape):
    wc, nw, D = wide_shape
    nc, nn, _ = narrow_shape
    V = pl.BlockSpec(memory_space=pltpu.VMEM)
    S = pl.BlockSpec(memory_space=pltpu.SMEM)
    sds = jax.ShapeDtypeStruct
    out = pl.pallas_call(
        functools.partial(results_kernel, wc, nc, sizes),
        out_shape=[sds(wide_shape, B), sds((nn, nc, D), B), sds((nw, wc, D), F), sds((nn, nc, D), F)]
        + [sds(s.shape, F) for s in shares] + [sds((1, n), F) for n in sizes],
        in_specs=[S] + [V] * 12,
        out_specs=[V] * (13 + len(sizes)),
        scratch_shapes=[pltpu.VMEM((nn, nc, D), F)],
        compiler_params=pltpu.CompilerParams(vmem_limit_bytes=VMEM_LIMIT),
        name="results",
    )(me.reshape(1), e, dx, vec, *shares)
    swap = functools.partial(jnp.transpose, axes=(1, 0, 2))
    return out[0], swap(out[1]), swap(out[2]), swap(out[3]), out[4:13], [v.reshape(-1) for v in out[13:]]


def gather_ops(nz, pieces, ins, outs, send, recv, sib_send, sib_recv):
    f, c = lax.axis_index("fsdp"), lax.axis_index("dp")
    z, y, x = f // 4, (f // 2) % 2, f % 2
    xn, yn, up, dn, sib = (f + 1 - 2 * x, c), (f + 2 - 4 * y, c), (f + 4, c), (f - 4, c), (f, 1 - c)
    bar = pltpu.get_barrier_semaphore()

    def greet(dev):
        pl.semaphore_signal(bar, inc=1, device_id=dev, device_id_type=MESH)

    greet(xn)
    greet(yn)
    greet(sib)
    pl.when(z < nz - 1)(lambda: greet(up))
    pl.when(z > 0)(lambda: greet(dn))
    pl.semaphore_wait(bar, 3 + (z < nz - 1).astype(jnp.int32) + (z > 0).astype(jnp.int32))
    dest = {"x": xn, "y": yn, "u": up, "d": dn}
    there = {"x": None, "y": None, "u": z < nz - 1, "d": z > 0}
    code = {"x": 0, "y": 0, "u": 1, "d": 2}

    def columns(i, half):
        w, c0, cols, order, share = pieces[i]
        return pl.ds(pl.multiple_of(half * (ins[w].shape[1] // 2) + c0, 128) if share else c0, cols)

    def region(i, s, half):
        w = pieces[i][0]
        r = ins[w].shape[0]
        return outs[w].at[pl.ds(pl.multiple_of(s * r, r), r), columns(i, half)]

    def own(i):
        return ins[pieces[i][0]].at[:, columns(i, c)]

    def remote(i, s, src, d):
        return pltpu.make_async_remote_copy(
            src_ref=src, dst_ref=region(i, s, c), send_sem=send.at[i, code[d]], recv_sem=recv.at[i, s],
            device_id=dest[d], device_id_type=MESH)

    def sibling(i, s, half):
        return pltpu.make_async_remote_copy(
            src_ref=region(i, s, half), dst_ref=region(i, s, half), send_sem=sib_send.at[i],
            recv_sem=sib_recv.at[i], device_id=sib, device_id_type=MESH)

    def some(i, half, count):
        w = pieces[i][0]
        part = outs[w].at[pl.ds(0, count * ins[w].shape[0]), columns(i, half)]
        return lambda a, b: pltpu.make_async_remote_copy(
            src_ref=part, dst_ref=part, send_sem=a, recv_sem=b, device_id=sib, device_id_type=MESH)

    def along(dirs, act):
        for d in dirs:
            if there[d] is None:
                act(d)
            else:
                pl.when(there[d])(lambda d=d: act(d))

    def each(h, i, act):
        for bx, by, sgn in slots():
            k = h - bx - by
            if isinstance(h, int) and not ((k == 0) if sgn == 0 else (1 <= k < nz)):
                continue
            zs = z + sgn * k
            valid = (k == 0) if sgn == 0 else (k >= 1) & (zs >= 0) & (zs < nz)
            s = zs * 4 + (y + by - 2 * by * y) * 2 + (x + bx - 2 * bx * x)
            dirs = forwards(pieces[i][3], bx, by, sgn)
            if isinstance(valid, bool):
                act(i, s, dirs)
            else:
                pl.when(valid)(lambda s=s, dirs=dirs: act(i, s, dirs))

    def start(i):
        along(forwards(pieces[i][3], 0, 0, 0), lambda d: remote(i, f, own(i), d).start())

    def step(i, s, dirs):
        remote(i, s, region(i, s, c), "x").wait_recv()
        along(dirs, lambda d: remote(i, s, region(i, s, c), d).start())
        if pieces[i][4]:
            sibling(i, s, c).start()

    def arrived(i):
        if pieces[i][4]:
            some(i, 1 - c, 4 * nz - 1)(sib_send.at[i], sib_recv.at[i]).wait_recv()

    def finish(i):
        order = pieces[i][3]
        before = {d: order[:order.index(d)] for d in "xyz"}
        size = {"x": 2, "y": 2, "z": nz}

        def blocks(d):
            n = 1
            for e in before[d]:
                n *= size[e]
            return n

        some(i, c, blocks("x") + blocks("y"))(send.at[i, 0], recv.at[i, 0]).wait_send()
        for p in range(nz):
            if p < nz - 1:
                pl.when(z == p)(lambda p=p: some(i, c, blocks("z") * (p + 1))(send.at[i, 1], recv.at[i, 0]).wait_send())
            if p > 0:
                pl.when(z == p)(lambda p=p: some(i, c, blocks("z") * (nz - p))(send.at[i, 2], recv.at[i, 0]).wait_send())
        if pieces[i][4]:
            some(i, c, 4 * nz - 1)(sib_send.at[i], sib_recv.at[i]).wait_send()

    def level(h, indices):
        for i in indices:
            each(h, i, step)

    return start, level, arrived, finish


def gather_encode_kernel(wc, nc, nz, pieces, nw, shw, shn, visw, visn, cotw, cotn, cw, cn, *refs):
    devices = 4 * nz
    vectors, refs = refs[:5], refs[5:]
    ins, refs = list(refs[:nw - 1]), refs[nw - 1:]
    outs, refs = refs[:nw], refs[nw:]
    results_, refs = refs[:13], refs[13:]
    buffers, refs = refs[:13], refs[13:]
    perm, sel, dz, m_ref, x_ref, a_ref, qkv, o_ref, x1_ref, b_ref, h_ref, slope_ref, e_ref = buffers
    wq, wo, wu, wd, we, tiles, sum_ref, pair, tile, send, recv, sib_send, sib_recv, loc, sems, out_sems = refs
    row = iota((16, 128), 0)
    shares = jnp.zeros((16, 128), F)
    for k, v in enumerate(vectors):
        n = v.shape[-1]
        wide = jnp.concatenate([v[...].astype(F).reshape(1, n), jnp.zeros((1, 128 - n), F)], axis=1)
        shares = jnp.where(row == k, wide, shares)
    tile[...] = shares.astype(B)
    ins.append(tile)

    def leave(*which):
        for k in which:
            pltpu.make_async_copy(buffers[k], results_[k], out_sems.at[k]).start()

    D = wo.shape[0]
    start, level, arrived, finish = gather_ops(nz, pieces, ins, outs, send, recv, sib_send, sib_recv)
    sets = {"q": [nw - 1, 0], "u": [2], "d": [3], "o": [1], "e": [4], "D": [5, 6], "X": [7, 8]}
    members = {s: [i for w in ws for i, p in enumerate(pieces) if p[0] == w] for s, ws in sets.items()}
    into = [wq, wo, wu, wd, we, None, None, None, None, tiles]
    loads = {}
    gains = []
    locals_ = []
    C = 512
    chunks = wu.shape[1] // C

    def prepare():
        for w in range(nw):
            r = ins[w].shape[0]
            cp = pltpu.make_async_copy(
                ins[w], outs[w].at[pl.ds(pl.multiple_of(lax.axis_index("fsdp") * r, r), r)], loc.at[w])
            cp.start()
            locals_.append(cp)
        placement(wc, nc, shw, shn, visw, visn, cotw, cotn, perm, sel, dz)
        load_rows(x_ref, pair, cw, cn, wc, nc)
        leave(0, 1, 2, 4)

    def ready(s):
        for w, i in zip(sets[s], members[s]):
            arrived(i)
            locals_[w].wait()
            loads[w] = pltpu.make_async_copy(outs[w], into[w], sems.at[w])
            loads[w].start()

    def project():
        loads[nw - 1].wait()
        gains.append(spread_vector(tiles[...], 0, D, devices))
        gains.append(spread_vector(tiles[...], 1, D, devices))
        a = (norm_stats(x_ref[...])[0] * gains[0]).astype(B)
        a_ref[...] = a
        loads[0].wait()
        for k in range(0, 3 * D, D):
            qkv[:, k:k + D] = dot(a, wq[:, k:k + D]).astype(B)
        leave(5, 6)

    def attend(part):
        mask = pair_mask()
        groups = x_ref.shape[0] // 128
        for g in range(groups):
            if g * 2 // groups != part:
                continue
            rr = slice(128 * g, 128 * g + 128)
            valid = valid_keys(0 if g < wc else 1, cw.shape[1], cn.shape[0])
            for j in range(D // 128):
                q, k, v = (qkv[rr, o + 128 * j:o + 128 * j + 128] for o in (0, D, 2 * D))
                k2 = jnp.concatenate([k, k], axis=0) * mask
                v2 = jnp.concatenate([v, v], axis=0) * mask
                p2 = jnp.concatenate(pair_shares(q, k2, valid), axis=1).astype(B)
                o_ref[rr, 128 * j:128 * j + 128] = dot(p2, v2).astype(B)

    def middle():
        loads[1].wait()
        x1 = x_ref[...] + dot(o_ref[...], wo[...])
        x1_ref[...] = x1
        sum_ref[...] = x1
        b_ref[...] = (norm_stats(x1)[0] * gains[1]).astype(B)
        leave(7, 8, 9)

    def feed_forward(j):
        if j == 0:
            loads[2].wait()
            loads[3].wait()
        k = j * C
        h, slope = gelu_both(dot(b_ref[...], wu[:, k:k + C]))
        h = h.astype(B)
        h_ref[:, k:k + C] = h
        slope_ref[:, k:k + C] = slope
        sum_ref[...] += dot(h, wd[k:k + C, :])
        for n in (10, 11):
            pltpu.make_async_copy(buffers[n].at[:, k:k + C], results_[n].at[:, k:k + C], out_sems.at[n]).start()

    def embed():
        e_ref[...] = sum_ref[...].astype(B)
        leave(12)
        loads[4].wait()
        m_ref[...] = dot(e_ref[...], we[...])
        leave(3)

    compute = [project, functools.partial(attend, 0), functools.partial(attend, 1), middle]
    compute += [functools.partial(feed_forward, j) for j in range(chunks)] + [embed]
    for token in gather_schedule(nz + 1, len(compute)):
        if token[0] == "S":
            for i in members[token[1]]:
                start(i)
        elif token[0] == "V":
            level(token[1], members[token[2]])
        elif token[0] == "R":
            ready(token[1])
        elif token[0] == "P":
            prepare()
        else:
            compute[token[1]]()
    for w in sets["D"] + sets["X"]:
        locals_[w].wait()
    for s in "DX":
        for i in members[s]:
            arrived(i)
    for i in range(len(pieces)):
        finish(i)
    for n in range(13):
        pltpu.make_async_copy(buffers[n], results_[n], out_sems.at[n]).wait()


def gather_schedule(top, steps):
    if (top, steps) == (5, 11):
        return list(GATHER_SCHEDULE)
    tokens = [("S", s) for s in "qudoe"] + [("P",), ("S", "D"), ("S", "X")]
    tokens += [("V", h, s) for h in range(1, top + 1) for s in "qudoeDX"]
    return tokens + [("R", s) for s in "qoude"] + [("C", k) for k in range(steps)]


def gather_encode(shards, vectors, pieces, place, cw, cn, nz, cid=1):
    nw, npc, n = len(shards) + 1, len(pieces), 4 * nz
    wc, nc, D = cw.shape[0], cn.shape[1], cw.shape[2]
    R = 128 * wc + 128 * ((nc + 1) // 2)
    V = pl.BlockSpec(memory_space=pltpu.VMEM)
    S = pl.BlockSpec(memory_space=pltpu.SMEM)
    A = pl.BlockSpec(memory_space=pl.ANY)
    sds = jax.ShapeDtypeStruct
    whole = [sds((s.shape[0] * n, s.shape[1]), s.dtype) for s in shards] + [sds((16 * n, 128), B)]
    FFD, DD = shards[2].shape[1], shards[4].shape[1]
    dma = pltpu.SemaphoreType.DMA
    kept = placed_shapes(*place[4:]) + [
        sds((R, DD), F), sds((R, D), F), sds((R, D), B), sds((R, 3 * D), B), sds((R, D), B), sds((R, D), F),
        sds((R, D), B), sds((R, FFD), B), sds((R, FFD), F), sds((R, D), B)]
    out = pl.pallas_call(
        functools.partial(gather_encode_kernel, wc, nc, nz, pieces, nw),
        out_shape=whole + kept,
        in_specs=[S, S] + [V] * 11 + [A] * (nw - 1),
        out_specs=[A] * (nw + 13),
        scratch_shapes=[pltpu.VMEM(s.shape, s.dtype) for s in kept] + [pltpu.VMEM(w.shape, B) for w in whole[:5]] + [
            pltpu.VMEM(whole[-1].shape, B), pltpu.VMEM((R, D), F), pltpu.VMEM(cn.shape, F), pltpu.VMEM((16, 128), B),
            dma((npc, 3)), dma((npc, n)), dma((npc,)), dma((npc,)), dma((nw,)), dma((nw,)), dma((13,))],
        compiler_params=pltpu.CompilerParams(collective_id=cid, has_side_effects=True, vmem_limit_bytes=VMEM_LIMIT),
        name="gather_and_encode",
    )(*place, cw, cn, *vectors, *shards)
    return out[:nw], out[nw:nw + 3], out[nw + 3:]


def slot_count(order, d, nz):
    size = {"x": 2, "y": 2, "z": nz}
    k = 1
    for e in order[:order.index("z" if d in "ud" else d)]:
        k *= size[e]
    return k * (nz + 1) if d in "ud" else k


def slot_index(order, d, nz, pos):
    size = {"x": 2, "y": 2, "z": nz}
    k = 0
    for e in order[:order.index("z" if d in "ud" else d)]:
        k = k * size[e] + pos[e]
    return k * (nz + 1) + pos["z"] + (1 if d == "d" else 0) if d in "ud" else k


def parent(order, bx, by, sgn):
    differs = {"x": bx, "y": by, "z": int(sgn != 0)}
    last = max(j for j, d in enumerate(order) if differs[d])
    if order[last] == "z":
        return "d" if sgn < 0 else "u"
    return order[last]


def reduce_ops(nz, pieces, rows, mine, other, sibb, rbuf, res, outs, sib_send, sib_recv, send, recv, res_sem, res_send, res_recv):
    f, c = lax.axis_index("fsdp"), lax.axis_index("dp")
    z, y, x = f // 4, (f // 2) % 2, f % 2
    bits = (nz * 4).bit_length() - 1

    def flip(b):
        return f + (1 << b) * (1 - 2 * ((f // (1 << b)) % 2))

    xn, yn, up, dn, sib = (flip(0), c), (flip(1), c), (f + 4, c), (f - 4, c), (f, 1 - c)
    bar = pltpu.get_barrier_semaphore()

    def greet(dev):
        pl.semaphore_signal(bar, inc=1, device_id=dev, device_id_type=MESH)

    greet(xn)
    greet(yn)
    greet(sib)
    pl.when(z < nz - 1)(lambda: greet(up))
    pl.when(z > 0)(lambda: greet(dn))
    far = range(3, bits)
    for b in far:
        greet((flip(b), c))
    pl.semaphore_wait(bar, 3 + len(far) + (z < nz - 1).astype(jnp.int32) + (z > 0).astype(jnp.int32))
    dest = {"x": xn, "y": yn, "u": up, "d": dn}
    there = {"u": z < nz - 1, "d": z > 0}
    opposite = {"u": "d", "d": "u", "x": "x", "y": "y"}
    kind = {"x": 0, "y": 1, "u": 2, "d": 2}

    def give(w):
        return pltpu.make_async_remote_copy(
            src_ref=other[w], dst_ref=sibb[w], send_sem=sib_send.at[w], recv_sem=sib_recv.at[w],
            device_id=sib, device_id_type=MESH)

    def cols(i):
        return pl.ds(pieces[i][1], pieces[i][2])

    def message(i, s, pos, d):
        w, order, b = pieces[i][0], pieces[i][3], kind[d]
        r = rows[w]
        q = slot_index(order, opposite[d], nz, pos)
        return pltpu.make_async_remote_copy(
            src_ref=mine[w].at[pl.ds(pl.multiple_of(s * r, r), r), cols(i)], dst_ref=rbuf[i][b].at[q],
            send_sem=send.at[i], recv_sem=recv.at[i, b, q], device_id=dest[d], device_id_type=MESH)

    def arrival(i, pos, d):
        b = kind[d]
        q = slot_index(pieces[i][3], d, nz, pos)
        return pltpu.make_async_remote_copy(
            src_ref=rbuf[i][b].at[q], dst_ref=rbuf[i][b].at[q], send_sem=send.at[i],
            recv_sem=recv.at[i, b, q], device_id=sib, device_id_type=MESH)

    def add(i, s, pos, children, final):
        w, order = pieces[i][0], pieces[i][3]
        r = rows[w]
        ks = [(kind[d], slot_index(order, d, nz, pos)) for d in children]

        tall = 16
        while r % (2 * tall) == 0 and 2 * tall * pieces[i][2] <= 24 * 16 * 128:
            tall *= 2
        if r % 48 == 0 and 48 * pieces[i][2] <= 27 * 16 * 128:
            tall = max(tall, 48)

        @pl.loop(0, r // tall)
        def _(k):
            rr = pl.ds(pl.multiple_of(k * tall, 16), tall)
            gr = pl.ds(pl.multiple_of(s * r + k * tall, 16), tall)
            t = mine[w][gr, cols(i)].astype(F) + sibb[w][gr, cols(i)].astype(F)
            for b, q in ks:
                t = t + rbuf[i][b][q, rr].astype(F)
            if final:
                res[w][rr, cols(i)] = t
            else:
                mine[w][gr, cols(i)] = t.astype(B)

    def gather_children(i, s, pos, children, final):
        sure = [d for d in children if d in "xy"]
        maybe = [d for d in children if d in "ud"]
        for d in sure:
            arrival(i, pos, d).wait_recv()
        for d in maybe:
            pl.when(there[d])(lambda d=d: arrival(i, pos, d).wait_recv())
        if not maybe:
            add(i, s, pos, sure, final)
        elif len(maybe) == 1:
            pl.when(there[maybe[0]])(lambda: add(i, s, pos, sure + maybe, final))
            pl.when(jnp.logical_not(there[maybe[0]]))(lambda: add(i, s, pos, sure, final))
        else:
            u, d = there["u"], there["d"]
            pl.when(u & d)(lambda: add(i, s, pos, sure + ["u", "d"], final))
            pl.when(u & jnp.logical_not(d))(lambda: add(i, s, pos, sure + ["u"], final))
            pl.when(jnp.logical_not(u) & d)(lambda: add(i, s, pos, sure + ["d"], final))
            if nz == 1:
                add(i, s, pos, sure, final)

    def each(h, i, leaf, act):
        order = pieces[i][3]
        for bx, by, sgn in slots():
            children = forwards(order, bx, by, sgn)
            if leaf is not None and (len(children) == 0) != leaf:
                continue
            k = h - bx - by
            if isinstance(h, int) and not ((k == 0) if sgn == 0 else (1 <= k < nz)):
                continue
            zs = z + sgn * k
            valid = (k == 0) if sgn == 0 else (k >= 1) & (zs >= 0) & (zs < nz)
            pos = {"x": x + bx - 2 * bx * x, "y": y + by - 2 * by * y, "z": zs}
            s = zs * 4 + pos["y"] * 2 + pos["x"]
            p = parent(order, bx, by, sgn)
            if isinstance(valid, bool):
                act(i, s, pos, children, p)
            else:
                pl.when(valid)(lambda s=s, pos=pos, children=children, p=p: act(i, s, pos, children, p))

    def work(i, s, pos, children, p):
        gather_children(i, s, pos, children, False)
        message(i, s, pos, p).start()

    def leaves(h, indices):
        for i in indices:
            each(h, i, True, work)

    def nodes(h, indices):
        for i in indices:
            each(h, i, False, work)

    def out_copy(w):
        n = outs[w].shape[1] // 2
        return pltpu.make_async_copy(res[w], outs[w].at[:, pl.ds(pl.multiple_of(c * n, 128), n)], res_sem.at[w])

    def out_sib(w, half):
        n = outs[w].shape[1] // 2
        return pltpu.make_async_remote_copy(
            src_ref=res[w], dst_ref=outs[w].at[:, pl.ds(pl.multiple_of(half * n, 128), n)], send_sem=res_send.at[w],
            recv_sem=res_recv.at[w], device_id=sib, device_id_type=MESH)

    def total(w):
        for i, piece in enumerate(pieces):
            if piece[0] == w:
                gather_children(i, f, {"x": x, "y": y, "z": z}, forwards(piece[3], 0, 0, 0), True)
        out_sib(w, c).start()
        out_copy(w).start()

    def sent(indices):
        for i in indices:
            w = pieces[i][0]
            part = mine[w].at[pl.ds(0, (4 * nz - 1) * rows[w]), cols(i)]
            pltpu.make_async_remote_copy(
                src_ref=part, dst_ref=part, send_sem=send.at[i], recv_sem=recv.at[i, 0, 0], device_id=sib,
                device_id_type=MESH).wait_send()

    def finish(ws):
        for w in ws:
            give(w).wait_send()
            out_copy(w).wait()
            out_sib(w, c).wait_send()
            out_sib(w, 1 - c).wait_recv()

    return flip, give, leaves, nodes, total, sent, finish


def encode_back_reduce_kernel(wc, wide_seen, narrow_seen, nz, routes, *refs):
    devices = 4 * nz
    dec_vec, *refs = refs
    given, refs = refs[:9], refs[9:]
    h_h, slope_h, we_h, wd_h, wu_h, wo_h, wq_h, *refs = refs
    dec_g, refs = refs[:4], refs[4:]
    (dx_ref, vec_out, *refs) = refs
    outs, refs = refs[:9], refs[9:]
    (we, wo, wq, wd2, wu2, h2, slope2, dx1_ref, z_ref, do_ref, dqkv, *refs) = refs
    tiles, dm, e_ref, b_ref, x1_ref, o_ref, qkv, a_ref, x_ref = refs[:9]
    refs = refs[9:]
    mine, refs = refs[:9], refs[9:]
    enc_other, refs = refs[:5], refs[5:]
    sibb, refs = refs[:9], refs[9:]
    res, refs = refs[:9], refs[9:]
    npc = len(routes)
    rbuf, refs = [refs[3 * i:3 * i + 3] for i in range(npc)], refs[3 * npc:]
    (vbuf, wsem, gsem, dsem, sib_send, sib_recv, send, recv, res_sem, res_send, res_recv, vsend, vrecv) = refs
    c = lax.axis_index("dp")
    held = [tiles, dm, e_ref, b_ref, x1_ref, o_ref, qkv, a_ref, x_ref]
    takes_in = [pltpu.make_async_copy(s, d, gsem.at[k]) for k, (s, d) in enumerate(zip(given, held))]
    for cp in takes_in:
        cp.start()
    D = wo.shape[0]
    n_up = mine[2].shape[1]
    rows = [m.shape[0] // devices for m in mine]

    def half(ref, h):
        n = ref.shape[1] // 2
        return ref.at[:, pl.ds(pl.multiple_of(h * n, 128), n)]

    other = list(enc_other) + [half(g, 1 - c) for g in dec_g]
    flip, give, leaves, nodes, total, sent, finish = reduce_ops(
        nz, routes, rows, mine, other, sibb, rbuf, res, outs, sib_send, sib_recv, send, recv, res_sem, res_send, res_recv)
    dec_ws = [5, 6, 7, 8]
    for w in dec_ws:
        give(w).start()
    takes = [pltpu.make_async_copy(half(dec_g[w - 5], c), mine[w], dsem.at[w - 5]) for w in dec_ws]
    for t in takes:
        t.start()
    loads = [pltpu.make_async_copy(s, d, wsem.at[k]) for k, (s, d) in enumerate(((we_h, we), (wo_h, wo), (wq_h, wq)))]
    C = 512
    chunks = 2 * n_up // C

    def chunk(j):
        h = (1 - c) if j < chunks // 2 else c
        return pl.multiple_of(h * n_up + (j % (chunks // 2)) * C, 128)

    def feed(j):
        k = chunk(j)
        return (pltpu.make_async_copy(wd_h.at[pl.ds(k, C)], wd2.at[j % 2], wsem.at[3 + j % 2]),
                pltpu.make_async_copy(wu_h.at[:, pl.ds(k, C)], wu2.at[j % 2], wsem.at[5 + j % 2]),
                pltpu.make_async_copy(h_h.at[:, pl.ds(k, C)], h2.at[j % 2], wsem.at[7 + j % 2]),
                pltpu.make_async_copy(slope_h.at[:, pl.ds(k, C)], slope2.at[j % 2], wsem.at[9 + j % 2]))

    loads[0].start()
    for j in (0, 1):
        for cp in feed(j):
            cp.start()
    loads[1].start()
    loads[2].start()
    takes_in[0].wait()
    gain1 = spread_vector(tiles[...], 0, D, devices)
    gain2 = spread_vector(tiles[...], 1, D, devices)
    def own_cols(w):
        n = mine[w].shape[1]
        return pl.ds(pl.multiple_of(c * n, 128), n), pl.ds(pl.multiple_of((1 - c) * n, 128), n)

    sets = {"A": [5, 6], "B": [7, 8], "d": [3], "u": [2], "e": [4], "O": [1], "Q": [0]}
    members = {s: [i for i, p in enumerate(routes) if p[0] in ws] for s, ws in sets.items()}
    kept = {}

    def first():
        for cp in takes_in[1:4]:
            cp.wait()
        loads[0].wait()
        grad = dot_nt(dm[...], we[...])
        dx1_ref[...] = grad
        z_ref[...] = grad.astype(B)
        own, rest = own_cols(4)
        enc_other[4][...] = dot_tn(e_ref[...], dm[:, rest]).astype(B)
        mine[4][...] = dot_tn(e_ref[...], dm[:, own]).astype(B)
        give(4).start()
        kept["back"] = jnp.zeros_like(grad)

    def feed_forward(j):
        own, rest = own_cols(3)
        for cp in feed(j):
            cp.wait()
        kk = pl.ds(chunk(j), C)
        d = (slope2[j % 2] * dot_nt(z_ref[...], wd2[j % 2])).astype(B)
        kept["back"] = kept["back"] + dot_nt(d, wu2[j % 2])
        hk = h2[j % 2]
        enc_other[3][kk, :] = dot_tn(hk, z_ref[:, rest]).astype(B)
        mine[3][kk, :] = dot_tn(hk, z_ref[:, own]).astype(B)
        g = dot_tn(b_ref[...], d).astype(B)
        at = (j % (chunks // 2)) * C
        if j < chunks // 2:
            enc_other[2][:, at:at + C] = g
        else:
            mine[2][:, at:at + C] = g
        if j == chunks // 2 - 1:
            give(2).start()
        if j == chunks - 1:
            give(3).start()
        if j + 2 < chunks:
            for cp in feed(j + 2):
                cp.start()

    def project():
        takes_in[4].wait()
        takes_in[5].wait()
        by_input, by_gain = norm_back(x1_ref[...], gain2, kept.pop("back"))
        vbuf[0, 0] = jnp.zeros_like(vbuf[0, 0])
        vbuf[0, 0, 1:2, :] = jnp.sum(by_gain, axis=0, keepdims=True)
        dx1_ref[...] += by_input
        z_ref[...] = dx1_ref[...].astype(B)
        loads[1].wait()
        do_ref[...] = dot_nt(z_ref[...], wo[...]).astype(B)
        own, rest = own_cols(1)
        enc_other[1][...] = dot_tn(o_ref[...], z_ref[:, rest]).astype(B)
        mine[1][...] = dot_tn(o_ref[...], z_ref[:, own]).astype(B)
        give(1).start()

    def attend(part):
        if part == 0:
            takes_in[6].wait()
        mask = pair_mask()
        groups = x_ref.shape[0] // 128
        scale = ENC_HEAD ** -0.5
        lane = iota((128, 128), 1)
        for g in range(groups):
            if g * 2 // groups != part:
                continue
            rr = slice(128 * g, 128 * g + 128)
            valid = valid_keys(0 if g < wc else 1, wide_seen, narrow_seen)
            for j in range(D // 128):
                q, k, v = (qkv[rr, o + 128 * j:o + 128 * j + 128] for o in (0, D, 2 * D))
                g_o = do_ref[rr, 128 * j:128 * j + 128]
                k2 = jnp.concatenate([k, k], axis=0) * mask
                v2 = jnp.concatenate([v, v], axis=0) * mask
                shares = pair_shares(q, k2, valid)
                dp2 = dot_nt(g_o, v2)
                ds, low = [], []
                for h in range(2):
                    dp = dp2[:, 128 * h:128 * h + 128]
                    p = shares[h]
                    ds.append((p * (dp - jnp.sum(dp * p, axis=1, keepdims=True))).astype(B))
                    low.append(p.astype(B))
                dq = dot(jnp.concatenate(ds, axis=1), k2) * scale
                dk = jnp.where(lane < ENC_HEAD, dot_tn(ds[0], q), dot_tn(ds[1], q)) * scale
                dv = jnp.where(lane < ENC_HEAD, dot_tn(low[0], g_o), dot_tn(low[1], g_o))
                for o, d in ((0, dq), (D, dk), (2 * D, dv)):
                    dqkv[rr, o + 128 * j:o + 128 * j + 128] = d.astype(B)

    def mix():
        takes_in[7].wait()
        own, rest = own_cols(0)
        enc_other[0][...] = dot_tn(a_ref[...], dqkv[:, rest]).astype(B)
        give(0).start()
        mine[0][...] = dot_tn(a_ref[...], dqkv[:, own]).astype(B)

    bits = devices.bit_length() - 1

    def vcopy(k):
        return pltpu.make_async_remote_copy(
            src_ref=vbuf.at[0, k], dst_ref=vbuf.at[1, k], send_sem=vsend.at[k], recv_sem=vrecv.at[k],
            device_id=(lax.axis_index("fsdp"), 1 - c) if k == 0 else (flip(k - 1), c), device_id_type=MESH)

    def vstep(k):
        vcopy(k).wait()
        vbuf[0, k + 1] = vbuf[0, k] + vbuf[1, k]
        if k < bits:
            vcopy(k + 1).start()

    def last():
        takes_in[8].wait()
        loads[2].wait()
        by_input, by_gain = norm_back(x_ref[...], gain1, dot_nt(dqkv[...], wq[...]))
        vbuf[0, 0, 0:1, :] = jnp.sum(by_gain, axis=0, keepdims=True)
        DD = dec_vec.shape[1]
        vbuf[0, 0, 2:3, 0:DD] = dec_vec[2:3, :]
        vbuf[0, 0, 3:5, 0:DD] = dec_vec[0:2, :]
        vcopy(0).start()
        dx_ref[...] = dx1_ref[...] + by_input

    compute = [first] + [functools.partial(feed_forward, j) for j in range(chunks)] + [project]
    compute += [functools.partial(attend, 0), functools.partial(attend, 1), mix, last]

    def ready(s):
        if s in "AB":
            for w in sets[s]:
                takes[w - 5].wait()
        for w in sets[s]:
            give(w).wait_recv()

    vectors = []
    for token in schedule(nz + 1, len(compute)):
        if token[0] == "C":
            compute[token[1]]()
            if token[1] == len(compute) - 1:
                vectors = list(range(bits + 1))
        elif token[0] == "R":
            ready(token[1])
        elif token[0] == "L":
            leaves(token[1], members[token[2]])
        elif token[0] == "N":
            nodes(token[1], members[token[2]])
        else:
            for w in sets[token[1]]:
                total(w)
        if vectors and token[0] == "N":
            vstep(vectors.pop(0))
    for k in vectors:
        vstep(k)
    vec_out[...] = vbuf[0, bits + 1]
    sent(range(npc))
    finish(range(9))


def schedule(top, steps):
    if (top, steps) == (5, 12):
        return list(SCHEDULE)
    tokens = [("C", k) for k in range(steps)] + [("R", s) for s in "ABdueOQ"]
    tokens += [("L", top, s) for s in "ABdueOQ"]
    for h in range(top, 0, -1):
        tokens += [("N", h, s) for s in "ABdueOQ"]
        tokens += [("L", h - 1, s) for s in "ABdueOQ"] if h > 1 else []
    return tokens + [("T", s) for s in "ABdueOQ"]


def encode_back_reduce(tiles, counts, dm, dec_vec, saved, enc, dec_grads, routes, nz, cid=2):
    R = dm.shape[0]
    n = 4 * nz
    bits = n.bit_length() - 1
    x, a, qkv, o, x1, b, h, slope, e = saved
    wq, wo, wu, wd, we = enc
    D = wq.shape[0]
    grads = [*enc, *dec_grads]
    shards = [(g.shape[0] // n, g.shape[1]) for g in grads]
    V = pl.BlockSpec(memory_space=pltpu.VMEM)
    A = pl.BlockSpec(memory_space=pl.ANY)
    sds = jax.ShapeDtypeStruct
    dma = pltpu.SemaphoreType.DMA
    most = 1
    rbuf = []
    for w, c0, cols, order in routes:
        for d in "xyu":
            k = slot_count(order, d, nz)
            most = max(most, k)
            rbuf.append(pltpu.VMEM((k, shards[w][0], cols), B))
    npc = len(routes)
    halves = [pltpu.VMEM((g.shape[0], g.shape[1] // 2), B) for g in grads]
    C = 512
    given = [tiles, dm, e, b, x1, o, qkv, a, x]
    out = pl.pallas_call(
        functools.partial(encode_back_reduce_kernel, *counts, nz, routes),
        out_shape=[sds((R, D), F), sds((8, D), F)] + [sds(s, F) for s in shards],
        in_specs=[V] + [A] * 20,
        out_specs=[V] * 2 + [A] * 9,
        scratch_shapes=[
            pltpu.VMEM(we.shape, B), pltpu.VMEM(wo.shape, B), pltpu.VMEM(wq.shape, B),
            pltpu.VMEM((2, C, D), B), pltpu.VMEM((2, D, C), B), pltpu.VMEM((2, R, C), B), pltpu.VMEM((2, R, C), F),
            pltpu.VMEM((R, D), F), pltpu.VMEM((R, D), B), pltpu.VMEM((R, D), B),
            pltpu.VMEM((R, 3 * D), B),
        ] + [pltpu.VMEM(g.shape, g.dtype) for g in given] + halves + halves[:5] + halves + [pltpu.VMEM((s[0], s[1] // 2), F) for s in shards] + rbuf + [
            pltpu.VMEM((2, bits + 2, 8, D), F), dma((11,)), dma((9,)), dma((4,)), dma((9,)), dma((9,)), dma((npc,)),
            dma((npc, 3, most)), dma((9,)), dma((9,)), dma((9,)), dma((bits + 1,)), dma((bits + 1,))],
        compiler_params=pltpu.CompilerParams(collective_id=cid, has_side_effects=True, vmem_limit_bytes=63 * 2**20),
        name="encoder_backward_and_reduce",
    )(dec_vec, *given, h, slope, we, wd, wu, wo, wq, *dec_grads)
    return out[0], out[1], out[2:]


ZXY = ("z", "x", "y")
ZYX = ("z", "y", "x")
XYZ = ("x", "y", "z")
YXZ = ("y", "x", "z")
XZY = ("x", "z", "y")
YZX = ("y", "z", "x")
GATHER = ((0, YXZ), (2, ZXY), (3, ZYX), (1, ZXY), (4, ZYX), (5, XZY), (7, YZX), (8, ZXY), (6, ZYX))
GATHER_SCHEDULE = (
    ("S", "e"), ("S", "o"), ("S", "u"), ("S", "d"), ("S", "q"), ("P",), ("V", 1, "d"), ("V", 1, "o"),
    ("V", 1, "q"), ("V", 1, "u"), ("V", 2, "q"), ("V", 2, "d"), ("V", 2, "u"), ("V", 2, "o"), ("S", "D"),
    ("V", 3, "q"), ("V", 3, "d"), ("V", 3, "u"), ("V", 3, "o"), ("V", 1, "e"), ("V", 4, "d"), ("V", 4, "u"),
    ("V", 4, "q"), ("V", 4, "o"), ("S", "X"), ("V", 2, "e"), ("V", 1, "D"), ("V", 5, "q"), ("V", 5, "o"),
    ("R", "q"), ("V", 5, "u"), ("V", 1, "X"), ("V", 5, "d"), ("V", 3, "e"), ("C", 0), ("V", 2, "D"), ("R", "u"),
    ("C", 1), ("V", 2, "X"), ("R", "d"), ("R", "o"), ("C", 2), ("V", 4, "e"), ("C", 3), ("V", 3, "D"), ("C", 4),
    ("V", 3, "X"), ("C", 5), ("V", 4, "D"), ("C", 6), ("V", 5, "e"), ("V", 4, "X"), ("C", 7), ("C", 8),
    ("R", "e"), ("C", 9), ("V", 5, "D"), ("V", 5, "X"), ("C", 10),
)
REDUCE = ((5, YXZ), (7, ZXY), (8, ZYX), (6, YXZ), (3, ZYX), (2, ZXY), (4, ZXY), (1, ZYX), (0, XYZ))
SCHEDULE = (
    ("C", 0), ("C", 1), ("C", 2), ("R", "A"), ("N", 5, "A"), ("L", 5, "A"), ("C", 3), ("N", 4, "A"), ("R", "B"),
    ("L", 5, "B"), ("L", 4, "A"), ("C", 4), ("L", 4, "B"), ("N", 5, "B"), ("L", 3, "A"), ("C", 5), ("N", 4, "B"),
    ("N", 3, "A"), ("C", 6), ("R", "u"), ("L", 3, "B"), ("C", 7), ("R", "e"), ("L", 5, "e"), ("N", 3, "B"),
    ("N", 2, "A"), ("L", 5, "u"), ("L", 2, "A"), ("N", 5, "u"), ("L", 2, "B"), ("R", "d"), ("C", 8),
    ("N", 2, "B"), ("L", 5, "d"), ("C", 9), ("R", "O"), ("C", 10), ("L", 1, "B"), ("N", 5, "O"), ("N", 1, "A"),
    ("L", 4, "e"), ("N", 1, "B"), ("L", 5, "O"), ("R", "Q"), ("L", 5, "Q"), ("L", 4, "Q"), ("N", 5, "d"),
    ("N", 5, "Q"), ("L", 4, "u"), ("N", 4, "u"), ("L", 4, "d"), ("N", 4, "d"), ("N", 5, "e"), ("L", 3, "Q"),
    ("L", 1, "A"), ("N", 4, "Q"), ("L", 3, "d"), ("L", 3, "u"), ("N", 3, "u"), ("N", 3, "d"), ("L", 2, "u"),
    ("L", 2, "Q"), ("L", 4, "O"), ("N", 3, "Q"), ("T", "B"), ("L", 3, "O"), ("N", 4, "O"), ("N", 4, "e"),
    ("L", 2, "O"), ("C", 11), ("N", 2, "d"), ("L", 2, "d"), ("N", 2, "u"), ("L", 1, "Q"), ("L", 3, "e"),
    ("N", 3, "e"), ("N", 2, "Q"), ("N", 3, "O"), ("N", 1, "d"), ("L", 1, "d"), ("L", 2, "e"), ("N", 2, "e"),
    ("L", 1, "e"), ("N", 2, "O"), ("N", 1, "Q"), ("T", "A"), ("T", "d"), ("L", 1, "u"), ("L", 1, "O"),
    ("N", 1, "e"), ("N", 1, "u"), ("T", "Q"), ("N", 1, "O"), ("T", "u"), ("T", "e"), ("T", "O"),
)


def whole_tiles(shards, devices):
    return devices % 4 == 0 and all(s.shape[0] % 16 == 0 and s.shape[1] % 256 == 0 for s in shards)


def local(
    clips_wide, clips_narrow, visible_wide, visible_narrow, shift_wide, shift_narrow,
    enc_norm1, enc_qkv, enc_out, enc_norm2, enc_up, enc_down, embed_proj, mask_token,
    dec_norm1, dec_qkv, dec_out, dec_norm2, dec_up, dec_down, cotan_wide, cotan_narrow,
):
    devices = lax.axis_size("fsdp")
    matrices = [enc_qkv, enc_out, enc_up, enc_down, embed_proj, dec_qkv, dec_out, dec_up, dec_down]
    vectors = [enc_norm1, enc_norm2, mask_token, dec_norm1, dec_norm2]
    narrow = jnp.transpose(clips_narrow, (1, 0, 2))
    place = (shift_wide, shift_narrow, visible_wide, visible_narrow, cotan_wide, cotan_narrow)
    counts = (clips_wide.shape[0], clips_wide.shape[1], clips_narrow.shape[1])
    direct = whole_tiles(matrices, devices)
    if direct:
        pieces = [(len(matrices), 0, 128, ZXY, False)]
        pieces += [(w, 0, matrices[w].shape[1] // 2, order, True) for w, order in GATHER]
        whole, placed, (embedded, *saved) = gather_encode(
            matrices, vectors, pieces, place, clips_wide, narrow, devices // 4
        )
    else:
        packed = jnp.stack([jnp.pad(v, (0, 128 - v.shape[0])) for v in vectors])
        packed = jnp.pad(packed, ((0, 16 - len(vectors)), (0, 0)))
        whole = [lax.all_gather(m, "fsdp", axis=0, tiled=True) for m in (*matrices, packed)]
        got = encoder_forward(place, whole[9], clips_wide, narrow, *whole[:5], devices)
        placed, embedded, saved = got[:3], got[3], got[4:]
    enc, dec, tiles = whole[:5], whole[5:9], whole[9]
    decoded_wide, decoded_narrow, grad_embedded, *dec_grads, gains = decoder(
        embedded, tiles, placed, cotan_wide.shape, cotan_narrow.shape, *dec, devices
    )
    if direct:
        routes = [(w, 0, matrices[w].shape[1] // 2, order) for w, order in REDUCE]
        grad_rows, gains, shares = encode_back_reduce(
            tiles, counts, grad_embedded, gains, saved, enc, dec_grads, routes, devices // 4
        )
    else:
        grad_rows, *enc_grads, gains = encoder_backward(
            tiles, counts, grad_embedded, gains, saved, *enc, devices
        )
        gains = lax.psum(gains, ("fsdp", "dp"))
        shares = [
            lax.psum_scatter(lax.psum(g.astype(F), "dp"), "fsdp", scatter_dimension=0, tiled=True)
            for g in enc_grads + dec_grads
        ]
    encoded_wide, encoded_narrow, grad_wide, grad_narrow, m, v = results(
        lax.axis_index("fsdp"), saved[-1], grad_rows, gains, shares, [v.shape[0] for v in vectors],
        clips_wide.shape, clips_narrow.shape,
    )
    return (
        encoded_wide, encoded_narrow, decoded_wide, decoded_narrow, grad_wide, grad_narrow,
        v[0], m[0], m[1], v[1], m[2], m[3], m[4], v[2], v[3], m[5], m[6], v[4], m[7], m[8],
    )


def solution(mesh):
    clips = ("fsdp", "dp")
    matrix, vector = P("fsdp", None), P("fsdp")
    weights = (
        vector, matrix, matrix, vector, matrix, matrix, matrix, vector,
        vector, matrix, matrix, vector, matrix, matrix,
    )
    rows, pairs = P(clips, None, None), P(clips, None)
    return jax.shard_map(
        local,
        mesh=mesh,
        in_specs=(rows, rows, pairs, pairs, pairs, P(clips), *weights, rows, rows),
        out_specs=(rows,) * 6 + weights,
        check_vma=False,
    )
```

```python
import functools

import jax
import jax.numpy as jnp
from jax import lax
from jax.experimental import pallas as pl
from jax.experimental.pallas import tpu as pltpu
from jax.sharding import PartitionSpec as P

MESH = pl.DeviceIdType.MESH


def slots():
    out=[]
    for bx in (0,1):
        for by in (0,1):
            for sgn in (0,1,-1):
                if (bx,by,sgn)!=(0,0,0): out.append((bx,by,sgn))
    return out

def forwards(order,bx,by,sgn):
    differs={'x':bx,'y':by,'z':int(sgn!=0)}
    last=max([j for j,d in enumerate(order) if differs[d]],default=-1)
    dirs=[]
    for j,d in enumerate(order):
        if j>last:
            dirs += ['u','d'] if d=='z' else [d]
    if last>=0 and order[last]=='z':
        dirs.append('u' if sgn<0 else 'd')
    return dirs


TIME = 64
WIN = 4
EPS = 1e-6
F = jnp.float32
B = jnp.bfloat16
VMEM_LIMIT = 60 * 2**20


def dot(a, b):
    return lax.dot_general(a, b, (((1,), (0,)), ((), ())), preferred_element_type=F)


def dot_nt(a, b):
    return lax.dot_general(a, b, (((1,), (1,)), ((), ())), preferred_element_type=F)


def dot_tn(a, b):
    return lax.dot_general(a, b, (((0,), (0,)), ((), ())), preferred_element_type=F)


def iota(shape, dim):
    return lax.broadcasted_iota(jnp.int32, shape, dim)


def norm_stats(x):
    center = jnp.mean(x, axis=-1, keepdims=True)
    shifted = x - center
    spread = jnp.mean(shifted * shifted, axis=-1, keepdims=True)
    scale = lax.rsqrt(spread + EPS)
    return shifted * scale, scale


def norm_back(x, gain, grad):
    unit, scale = norm_stats(x)
    by_gain = grad * unit
    by_unit = grad * gain
    mean_one = jnp.mean(by_unit, axis=-1, keepdims=True)
    mean_two = jnp.mean(by_unit * unit, axis=-1, keepdims=True)
    by_input = scale * (by_unit - mean_one - unit * mean_two)
    return by_input, jnp.sum(by_gain.reshape(-1, 8, x.shape[1]), axis=0)


def gelu_both(u):
    t = 1.0 / (1.0 + (0.3275911 * 0.7071067811865476) * jnp.abs(u))
    bell = jnp.exp(-0.5 * u * u)
    poly = t * (0.127414796 + t * (-0.142248368 + t * (0.7107068705 + t * (-0.7265760135 + t * 0.5307027145))))
    tail = poly * bell
    phi = jnp.where(u < 0, tail, 1.0 - tail)
    return u * phi, phi + u * (bell * 0.3989422804014327)


def spread_vector(tiles, lane, size, devices):
    part = size // devices
    pick = (iota((128, size), 1) % part == iota((128, size), 0)).astype(B)
    wide = dot(tiles, pick)
    rows = iota((tiles.shape[0], size), 0)
    keep = rows == (iota((tiles.shape[0], size), 1) // part) * 16 + lane
    return jnp.sum(jnp.where(keep, wide, 0.0), axis=0, keepdims=True)


def group_sums(x, ones):
    high = x.astype(B)
    return dot(high, ones) + dot((x - high.astype(F)).astype(B), ones)


def lane_groups(x, op):
    lanes = iota(x.shape, 1)
    width = x.shape[1]
    for d in (1, 2, 4, 8):
        other = jnp.where((lanes & d) != 0, pltpu.roll(x, d, 1), pltpu.roll(x, width - d, 1))
        x = op(x, other)
    return x


HEAD = 32
AREA = WIN * WIN


def stack8(block, mask):
    return jnp.concatenate([block] * 8, axis=0) * mask


def dec_kernel(wc, nc, wide_rows, narrow_rows, devices, tiles, m_ref, sel, perm_h, dz_h, wq_h, wo_h, wu_h, wd_h,
               outw, outn, dm_ref, gq_h, go_h, gu_h, gd_h, vec_ref,
               wq, wo, wu, wd, mhi, mlo, r_ref, a_ref, qkv, p_ref, o_ref,
               b_ref, h_ref, du, dx1, do_ref, dqkv, dec, dm_acc, acc, gq, go, gu, gd, perm, dz, sems):
    D = wo.shape[0]
    rows = wc * wide_rows + nc * narrow_rows
    T = 256
    tall = 512 if rows % 512 == 0 else T
    nt = rows // T
    wide_tiles = wc * wide_rows // T
    cps = []
    for k, (src, dst) in enumerate(((wq_h, wq), (wo_h, wo), (wu_h, wu), (wd_h, wd), (dz_h, dz), (perm_h, perm))):
        cp = pltpu.make_async_copy(src, dst, sems.at[k])
        cp.start()
        cps.append(cp)
    gain1 = spread_vector(tiles[...], 3, D, devices)
    gain2 = spread_vector(tiles[...], 4, D, devices)
    filler = spread_vector(tiles[...], 2, D, devices)
    mhi[...] = m_ref[...].astype(B)
    mlo[...] = (m_ref[...] - mhi[...].astype(F)).astype(B)
    dm_acc[...] = jnp.zeros_like(dm_acc)
    acc[...] = jnp.zeros_like(acc)
    def group_rows(t):
        g = jnp.where(t < wide_tiles, t * T // wide_rows, wc + (t - wide_tiles) // 2)
        return pl.ds(pl.multiple_of(g * 128, 128), 128)

    cps[0].wait()

    @pl.loop(0, nt)
    def _(t):
        rr = pl.ds(pl.multiple_of(t * T, T), T)
        g = group_rows(t)
        s = sel[rr]
        seen = jnp.sum(s.astype(F), axis=1, keepdims=True)
        x = dot(s, mhi[g]) + dot(s, mlo[g]) + (1.0 - seen) * filler
        r_ref[rr] = x
        a = (norm_stats(x)[0] * gain1).astype(B)
        a_ref[rr] = a
        qkv[rr] = dot(a, wq[...]).astype(B)

    mask = (iota((128, 256), 0) // AREA == iota((128, 256), 1) // HEAD).astype(B)
    scale = HEAD ** -0.5
    nw = 32
    while rows % (nw * AREA):
        nw //= 2
    ones = (iota((128, 128), 0) // AREA == iota((128, 128), 1) // AREA).astype(B)

    @pl.loop(0, rows // (nw * AREA))
    def _(g):
        base = pl.multiple_of(g * nw * AREA, nw * AREA)
        rr = pl.ds(base, nw * AREA)
        for a in range(D // 256):
            cq = pl.ds(a * 256, 256)
            q, k, v = qkv[rr, cq], qkv[rr, pl.ds(D + a * 256, 256)], qkv[rr, pl.ds(2 * D + a * 256, 256)]
            w16 = [slice(AREA * j, AREA * j + AREA) for j in range(nw)]
            s = jnp.concatenate([dot_nt(q[w], stack8(k[w], mask)) for w in w16], axis=0) * scale
            e = jnp.exp(s - lane_groups(s, jnp.maximum))
            p = e / group_sums(e, ones)
            p_ref[rr, pl.ds(a * 128, 128)] = p
            low = p.astype(B)
            o_ref[rr, cq] = jnp.concatenate([dot(low[w], stack8(v[w], mask)) for w in w16], axis=0).astype(B)

    for cp in cps[1:]:
        cp.wait()

    @pl.loop(0, rows // tall)
    def _(t):
        rr = pl.ds(pl.multiple_of(t * tall, tall), tall)
        x1 = r_ref[rr] + dot(o_ref[rr], wo[...])
        b = (norm_stats(x1)[0] * gain2).astype(B)
        b_ref[rr] = b
        z = dz[rr]
        out = x1
        back = jnp.zeros((tall, D), F)
        C = 512
        for k in range(0, wu.shape[1], C):
            u = dot(b, wu[:, k:k + C])
            h, slope = gelu_both(u)
            h = h.astype(B)
            h_ref[rr, k:k + C] = h
            out = out + dot(h, wd[k:k + C, :])
            d = (slope * dot_nt(z, wd[k:k + C, :])).astype(B)
            du[rr, k:k + C] = d
            back = back + dot_nt(d, wu[:, k:k + C])
        dec[rr] = out.astype(B)
        by_input, by_gain = norm_back(x1, gain2, back)
        acc[1] += by_gain
        dx = z.astype(F) + by_input
        dx1[rr] = dx
        do_ref[rr] = dot_nt(dx.astype(B), wo[...]).astype(B)

    for i in range(wc + nc):
        base, n, out = (i * wide_rows, wide_rows, outw) if i < wc else (
            wc * wide_rows + (i - wc) * narrow_rows, narrow_rows, outn)
        out[i if i < wc else i - wc] = dot_tn(perm[base:base + n, 0:n], dec[base:base + n]).astype(B)

    @pl.loop(0, rows // (nw * AREA))
    def _(g):
        base = pl.multiple_of(g * nw * AREA, nw * AREA)
        rr = pl.ds(base, nw * AREA)
        w16 = [slice(AREA * j, AREA * j + AREA) for j in range(nw)]
        for a in range(D // 256):
            cq = pl.ds(a * 256, 256)
            q, k, v = qkv[rr, cq], qkv[rr, pl.ds(D + a * 256, 256)], qkv[rr, pl.ds(2 * D + a * 256, 256)]
            go_ = do_ref[rr, cq]
            ks = [stack8(k[w], mask) for w in w16]
            qs = [stack8(q[w], mask) for w in w16]
            gs = [stack8(go_[w], mask) for w in w16]
            p = p_ref[rr, pl.ds(a * 128, 128)]
            dp = jnp.concatenate([dot_nt(go_[w], stack8(v[w], mask)) for w in w16], axis=0)
            ds = (p * (dp - group_sums(dp * p, ones))).astype(B)
            dqkv[rr, cq] = (jnp.concatenate([dot(ds[w], m) for w, m in zip(w16, ks)], axis=0) * scale).astype(B)
            s = jnp.concatenate([dot_nt(k[w], m) for w, m in zip(w16, qs)], axis=0) * scale
            s = s.reshape(nw, AREA, 128)
            e = jnp.exp(s - jnp.max(s, axis=1, keepdims=True))
            p = e / jnp.sum(e, axis=1, keepdims=True)
            dp = jnp.concatenate([dot_nt(v[w], m) for w, m in zip(w16, gs)], axis=0).reshape(nw, AREA, 128)
            ds = (p * (dp - jnp.sum(dp * p, axis=1, keepdims=True))).reshape(nw * AREA, 128).astype(B)
            p = p.reshape(nw * AREA, 128).astype(B)
            dqkv[rr, pl.ds(D + a * 256, 256)] = (jnp.concatenate([dot(ds[w], m) for w, m in zip(w16, qs)], axis=0) * scale).astype(B)
            dqkv[rr, pl.ds(2 * D + a * 256, 256)] = jnp.concatenate([dot(p[w], m) for w, m in zip(w16, gs)], axis=0).astype(B)

    @pl.loop(0, nt)
    def _(t):
        rr = pl.ds(pl.multiple_of(t * T, T), T)
        g = group_rows(t)
        by_input, by_gain = norm_back(r_ref[rr], gain1, dot_nt(dqkv[rr], wq[...]))
        acc[0] += by_gain
        dr = dx1[rr] + by_input
        s = sel[rr]
        hidden = 1.0 - jnp.sum(s.astype(F), axis=1, keepdims=True)
        acc[2] += jnp.sum((dr * hidden).reshape(-1, 8, D), axis=0)
        dm_acc[g] += dot_tn(s, dr.astype(B))

    dm_ref[...] = dm_acc[...].astype(B)
    for k in range(3):
        vec_ref[k:k + 1, :] = jnp.sum(acc[k], axis=0, keepdims=True)
    vec_ref[3:, :] = jnp.zeros((5, D), F)
    step = 512
    copies = []

    def leave(k, src, dst):
        cp = pltpu.make_async_copy(src, dst, sems.at[6 + k])
        cp.start()
        copies.append(cp)

    @pl.loop(0, wd.shape[0] // step)
    def _(k):
        kk = pl.ds(pl.multiple_of(k * step, step), step)
        gd[kk, :] = dot_tn(h_ref[:, kk], dz[...]).astype(B)

    leave(0, gd, gd_h)

    @pl.loop(0, wd.shape[0] // step)
    def _(k):
        kk = pl.ds(pl.multiple_of(k * step, step), step)
        gu[:, kk] = dot_tn(b_ref[...], du[:, kk]).astype(B)

    leave(1, gu, gu_h)

    @pl.loop(0, wq.shape[1] // step)
    def _(k):
        kk = pl.ds(pl.multiple_of(k * step, step), step)
        gq[:, kk] = dot_tn(a_ref[...], dqkv[:, kk]).astype(B)

    leave(2, gq, gq_h)
    go[...] = dot_tn(o_ref[...], dx1[...].astype(B)).astype(B)
    leave(3, go, go_h)
    for cp in copies:
        cp.wait()


def decoder(m, tiles, placed, wide_shape, narrow_shape, wq, wo, wu, wd, devices):
    wc, wide_rows, D = wide_shape
    nc, narrow_rows, _ = narrow_shape
    FFD = wu.shape[1]
    rows = wc * wide_rows + nc * narrow_rows
    V = pl.BlockSpec(memory_space=pltpu.VMEM)
    A = pl.BlockSpec(memory_space=pl.ANY)
    sds = jax.ShapeDtypeStruct
    weights = [pltpu.VMEM(w.shape, B) for w in (wq, wo, wu, wd)]
    return pl.pallas_call(
        functools.partial(dec_kernel, wc, nc, wide_rows, narrow_rows, devices),
        out_shape=[sds(wide_shape, B), sds(narrow_shape, B), sds(m.shape, B), sds(wq.shape, B), sds(wo.shape, B),
                   sds(wu.shape, B), sds(wd.shape, B), sds((8, D), F)],
        in_specs=[V] * 3 + [A] * 6,
        out_specs=[V] * 3 + [A] * 4 + [V],
        scratch_shapes=weights + [
            pltpu.VMEM(m.shape, B), pltpu.VMEM(m.shape, B),
            pltpu.VMEM((rows, D), F), pltpu.VMEM((rows, D), B), pltpu.VMEM((rows, 3 * D), B),
            pltpu.VMEM((rows, D // 2), F), pltpu.VMEM((rows, D), B),
            pltpu.VMEM((rows, D), B), pltpu.VMEM((rows, FFD), B), pltpu.VMEM((rows, FFD), B), pltpu.VMEM((rows, D), F),
            pltpu.VMEM((rows, D), B), pltpu.VMEM((rows, 3 * D), B), pltpu.VMEM((rows, D), B),
            pltpu.VMEM(m.shape, F), pltpu.VMEM((3, 8, D), F)] + weights + [
            pltpu.VMEM(placed[0].shape, B), pltpu.VMEM(placed[2].shape, B), pltpu.SemaphoreType.DMA((10,))],
        compiler_params=pltpu.CompilerParams(vmem_limit_bytes=VMEM_LIMIT),
        name="decoder_block",
    )(tiles, m, placed[1], placed[0], placed[2], wq, wo, wu, wd)


def placement(wc, nc, shw, shn, visw, visn, cotw, cotn, perm, sel, dz):
    T = 256
    wide_rows, narrow_rows = cotw.shape[1], cotn.shape[1]
    clips = [(i * wide_rows, wide_rows, 8, shw[i, 0], shw[i, 1], cotw, i, visw, 0) for i in range(wc)]
    clips += [(wc * wide_rows + i * narrow_rows, narrow_rows, 4, shn[i], 0, cotn, i, visn, 64 * (i % 2)) for i in range(nc)]
    for base, n, cols, s, r, cot, i, vis, o in clips:
        seen = vis.shape[1]
        parts = [jnp.full((1, o), -1, jnp.int32)] if o else []
        parts += [vis[i:i + 1, :], jnp.full((1, 128 - o - seen), -1, jnp.int32)]
        shown = jnp.concatenate(parts, axis=1)
        for k in range(0, n, T):
            j = iota((T, 1), 0) + k
            w, q = j >> 4, j & 15
            wf = cols // WIN
            t = ((w // wf) * WIN + (q >> 2) + s) & (TIME - 1)
            f = ((w % wf) * WIN + (q & 3) + r) & (cols - 1)
            patch = t * cols + f
            where = pl.ds(base + k, T)
            hot = jnp.where(iota((T, n), 1) == patch, 1.0, 0.0).astype(B)
            perm[where, 0:n] = hot
            if n < perm.shape[1]:
                perm[where, n:] = jnp.zeros((T, perm.shape[1] - n), B)
            sel[where] = jnp.where(shown == patch, 1.0, 0.0).astype(B)
            dz[where] = dot(hot, cot[i]).astype(B)


def placed_shapes(cotw, cotn):
    rows = cotw.shape[0] * cotw.shape[1] + cotn.shape[0] * cotn.shape[1]
    return [jax.ShapeDtypeStruct((rows, n), B) for n in (cotw.shape[1], 128, cotw.shape[2])]


ENC_HEAD = 64


def valid_keys(kind, wide_seen, narrow_seen):
    q, k = iota((128, 128), 0), iota((128, 128), 1)
    if kind == 0:
        return k < wide_seen
    return ((q // 64) == (k // 64)) & (k % 64 < narrow_seen)


def pair_mask():
    return (iota((256, 128), 0) // 128 == iota((256, 128), 1) // ENC_HEAD).astype(B)


def pair_shares(q, k2, valid):
    s2 = dot_nt(q, k2) * (ENC_HEAD ** -0.5)
    shares = []
    for h in range(2):
        s = jnp.where(valid, s2[:, 128 * h:128 * h + 128], -1e30)
        e = jnp.exp(s - jnp.max(s, axis=1, keepdims=True))
        shares.append(e / jnp.sum(e, axis=1, keepdims=True))
    return shares


def load_rows(dst, pair, wide, narrow, wc, nc):
    dst[...] = jnp.zeros_like(dst)
    for i in range(wc):
        dst[128 * i:128 * i + wide.shape[1], :] = wide[i].astype(F)
    pair[...] = narrow[...].astype(F)
    for i in range(nc):
        o = 128 * wc + 64 * i
        dst[o:o + narrow.shape[0], :] = pair[:, i, :]


def enc_forward_kernel(wc, nc, devices, shw, shn, visw, visn, cotw, cotn, tiles, cw, cn, wq_h, wo_h, wu_h, wd_h, we_h,
                       perm, sel, dz, m_ref, x_ref, a_ref, qkv, o_ref, x1_ref, b_ref, h_ref, slope_ref, e_ref,
                       wq, wo, wu, wd, we, pair, sems):
    D = wo.shape[0]
    cps = []
    for k, (src, dst) in enumerate(((wq_h, wq), (wo_h, wo), (wu_h, wu), (wd_h, wd), (we_h, we))):
        cp = pltpu.make_async_copy(src, dst, sems.at[k])
        cp.start()
        cps.append(cp)
    placement(wc, nc, shw, shn, visw, visn, cotw, cotn, perm, sel, dz)
    load_rows(x_ref, pair, cw, cn, wc, nc)
    gain1 = spread_vector(tiles[...], 0, D, devices)
    gain2 = spread_vector(tiles[...], 1, D, devices)
    x = x_ref[...]
    a = (norm_stats(x)[0] * gain1).astype(B)
    a_ref[...] = a
    cps[0].wait()
    for k in range(0, 3 * D, D):
        qkv[:, k:k + D] = dot(a, wq[:, k:k + D]).astype(B)
    mask = pair_mask()
    groups = x_ref.shape[0] // 128
    for g in range(groups):
        rr = slice(128 * g, 128 * g + 128)
        valid = valid_keys(0 if g < wc else 1, cw.shape[1], cn.shape[0])
        for j in range(D // 128):
            q, k, v = (qkv[rr, o + 128 * j:o + 128 * j + 128] for o in (0, D, 2 * D))
            k2 = jnp.concatenate([k, k], axis=0) * mask
            v2 = jnp.concatenate([v, v], axis=0) * mask
            p2 = jnp.concatenate(pair_shares(q, k2, valid), axis=1).astype(B)
            o_ref[rr, 128 * j:128 * j + 128] = dot(p2, v2).astype(B)
    cps[1].wait()
    x1 = x_ref[...] + dot(o_ref[...], wo[...])
    x1_ref[...] = x1
    b = (norm_stats(x1)[0] * gain2).astype(B)
    b_ref[...] = b
    cps[2].wait()
    cps[3].wait()
    out = x1
    C = 512
    for k in range(0, wu.shape[1], C):
        h, slope = gelu_both(dot(b, wu[:, k:k + C]))
        h = h.astype(B)
        h_ref[:, k:k + C] = h
        slope_ref[:, k:k + C] = slope
        out = out + dot(h, wd[k:k + C, :])
    e_ref[...] = out.astype(B)
    cps[4].wait()
    m_ref[...] = dot(e_ref[...], we[...])


def encoder_forward(place, tiles, cw, cn, wq, wo, wu, wd, we, devices):
    wc, nc = cw.shape[0], cn.shape[1]
    D = cw.shape[2]
    FFD = wu.shape[1]
    R = 128 * wc + 128 * ((nc + 1) // 2)
    V = pl.BlockSpec(memory_space=pltpu.VMEM)
    S = pl.BlockSpec(memory_space=pltpu.SMEM)
    A = pl.BlockSpec(memory_space=pl.ANY)
    sds = jax.ShapeDtypeStruct
    return pl.pallas_call(
        functools.partial(enc_forward_kernel, wc, nc, devices),
        out_shape=placed_shapes(*place[4:]) + [sds((R, we.shape[1]), F), sds((R, D), F), sds((R, D), B), sds((R, 3 * D), B),
                   sds((R, D), B), sds((R, D), F), sds((R, D), B), sds((R, FFD), B), sds((R, FFD), F), sds((R, D), B)],
        in_specs=[S, S] + [V] * 7 + [A] * 5,
        out_specs=[V] * 13,
        scratch_shapes=[pltpu.VMEM(w.shape, B) for w in (wq, wo, wu, wd, we)]
        + [pltpu.VMEM(cn.shape, F), pltpu.SemaphoreType.DMA((5,))],
        compiler_params=pltpu.CompilerParams(vmem_limit_bytes=VMEM_LIMIT),
        name="encoder_forward",
    )(*place, tiles, cw, cn, wq, wo, wu, wd, we)


def enc_backward_kernel(wc, wide_seen, narrow_seen, devices, tiles, dm, dec_vec, x_in, a_ref, qkv, o_ref, x1_ref, b_ref, h_ref, slope_ref, e_ref,
                        wq_h, wo_h, wu_h, wd_h, we_h,
                        dx_ref, gq, go, gu, gd, ge, vec_ref,
                        wq, wo, wu, wd, we, do_ref, dqkv, du, sems):
    D = wo.shape[0]
    cps = []
    for k, (src, dst) in enumerate(((we_h, we), (wd_h, wd), (wu_h, wu), (wo_h, wo), (wq_h, wq))):
        cp = pltpu.make_async_copy(src, dst, sems.at[k])
        cp.start()
        cps.append(cp)
    gain1 = spread_vector(tiles[...], 0, D, devices)
    gain2 = spread_vector(tiles[...], 1, D, devices)
    cps[0].wait()
    grad = dot_nt(dm[...], we[...])
    z = grad.astype(B)
    ge[...] = dot_tn(e_ref[...], dm[...]).astype(B)
    cps[1].wait()
    cps[2].wait()
    back = jnp.zeros_like(grad)
    C = 512
    for k in range(0, wu.shape[1], C):
        d = (slope_ref[:, k:k + C] * dot_nt(z, wd[k:k + C, :])).astype(B)
        du[:, k:k + C] = d
        back = back + dot_nt(d, wu[:, k:k + C])
        gd[k:k + C, :] = dot_tn(h_ref[:, k:k + C], z).astype(B)
        gu[:, k:k + C] = dot_tn(b_ref[...], d).astype(B)
    by_input, by_gain = norm_back(x1_ref[...], gain2, back)
    vec_ref[...] = jnp.zeros_like(vec_ref)
    vec_ref[1:2, :] = jnp.sum(by_gain, axis=0, keepdims=True)
    dx1 = grad + by_input
    y = dx1.astype(B)
    cps[3].wait()
    do_ref[...] = dot_nt(y, wo[...]).astype(B)
    go[...] = dot_tn(o_ref[...], y).astype(B)
    mask = pair_mask()
    groups = x_in.shape[0] // 128
    scale = ENC_HEAD ** -0.5
    lane = iota((128, 128), 1)
    for g in range(groups):
        rr = slice(128 * g, 128 * g + 128)
        valid = valid_keys(0 if g < wc else 1, wide_seen, narrow_seen)
        for j in range(D // 128):
            q, k, v = (qkv[rr, o + 128 * j:o + 128 * j + 128] for o in (0, D, 2 * D))
            g_o = do_ref[rr, 128 * j:128 * j + 128]
            k2 = jnp.concatenate([k, k], axis=0) * mask
            v2 = jnp.concatenate([v, v], axis=0) * mask
            shares = pair_shares(q, k2, valid)
            dp2 = dot_nt(g_o, v2)
            ds, low = [], []
            for h in range(2):
                dp = dp2[:, 128 * h:128 * h + 128]
                p = shares[h]
                ds.append((p * (dp - jnp.sum(dp * p, axis=1, keepdims=True))).astype(B))
                low.append(p.astype(B))
            dq = dot(jnp.concatenate(ds, axis=1), k2) * scale
            dk = jnp.where(lane < ENC_HEAD, dot_tn(ds[0], q), dot_tn(ds[1], q)) * scale
            dv = jnp.where(lane < ENC_HEAD, dot_tn(low[0], g_o), dot_tn(low[1], g_o))
            for o, d in ((0, dq), (D, dk), (2 * D, dv)):
                dqkv[rr, o + 128 * j:o + 128 * j + 128] = d.astype(B)
    cps[4].wait()
    for k in range(0, 3 * D, D):
        gq[:, k:k + D] = dot_tn(a_ref[...], dqkv[:, k:k + D]).astype(B)
    by_input, by_gain = norm_back(x_in[...], gain1, dot_nt(dqkv[...], wq[...]))
    vec_ref[0:1, :] = jnp.sum(by_gain, axis=0, keepdims=True)
    DD = dec_vec.shape[1]
    vec_ref[2:3, 0:DD] = dec_vec[2:3, :]
    vec_ref[3:5, 0:DD] = dec_vec[0:2, :]
    dx_ref[...] = dx1 + by_input


def encoder_backward(tiles, counts, dm, dec_vec, saved, wq, wo, wu, wd, we, devices):
    D = wq.shape[0]
    FFD = wu.shape[1]
    R = dm.shape[0]
    V = pl.BlockSpec(memory_space=pltpu.VMEM)
    A = pl.BlockSpec(memory_space=pl.ANY)
    sds = jax.ShapeDtypeStruct
    return pl.pallas_call(
        functools.partial(enc_backward_kernel, *counts, devices),
        out_shape=[sds((R, D), F)] + [sds(w.shape, B) for w in (wq, wo, wu, wd, we)] + [sds((8, D), F)],
        in_specs=[V] * 12 + [A] * 5,
        out_specs=[V] * 7,
        scratch_shapes=[pltpu.VMEM(w.shape, B) for w in (wq, wo, wu, wd, we)]
        + [pltpu.VMEM((R, D), B), pltpu.VMEM((R, 3 * D), B), pltpu.VMEM((R, FFD), B), pltpu.SemaphoreType.DMA((5,))],
        compiler_params=pltpu.CompilerParams(vmem_limit_bytes=VMEM_LIMIT),
        name="encoder_backward",
    )(tiles, dm, dec_vec, *saved, wq, wo, wu, wd, we)


def results_kernel(wc, nc, sizes, *refs):
    me, e, dx, vec, *refs = refs
    shares, refs = refs[:9], refs[9:]
    encw, encn, gradw, gradn, *refs = refs
    outs, refs = refs[:9], refs[9:]
    vectors, (pair,) = refs[:len(sizes)], refs[len(sizes):]
    for src, wide, narrow in ((e, encw, encn), (dx, gradw, gradn)):
        for i in range(wc):
            rows = src[128 * i:128 * i + encw.shape[1], :]
            if wide is encw:
                wide[i] = rows
            else:
                wide[:, i, :] = rows
        for i in range(nc):
            o = 128 * wc + 64 * i
            pair[:, i, :] = src[o:o + narrow.shape[0], :].astype(F)
        narrow[...] = pair[...].astype(narrow.dtype)
    for src, dst in zip(shares, outs):
        dst[...] = src[...]
    width = vec.shape[1]
    for k, (n, ref) in enumerate(zip(sizes, vectors)):
        ref[...] = pltpu.roll(vec[k:k + 1, :], lax.rem(width - me[0] * n, width), 1)[:, 0:n]


def results(me, e, dx, vec, shares, sizes, wide_shape, narrow_shape):
    wc, nw, D = wide_shape
    nc, nn, _ = narrow_shape
    V = pl.BlockSpec(memory_space=pltpu.VMEM)
    S = pl.BlockSpec(memory_space=pltpu.SMEM)
    sds = jax.ShapeDtypeStruct
    out = pl.pallas_call(
        functools.partial(results_kernel, wc, nc, sizes),
        out_shape=[sds(wide_shape, B), sds((nn, nc, D), B), sds((nw, wc, D), F), sds((nn, nc, D), F)]
        + [sds(s.shape, F) for s in shares] + [sds((1, n), F) for n in sizes],
        in_specs=[S] + [V] * 12,
        out_specs=[V] * (13 + len(sizes)),
        scratch_shapes=[pltpu.VMEM((nn, nc, D), F)],
        compiler_params=pltpu.CompilerParams(vmem_limit_bytes=VMEM_LIMIT),
        name="results",
    )(me.reshape(1), e, dx, vec, *shares)
    swap = functools.partial(jnp.transpose, axes=(1, 0, 2))
    return out[0], swap(out[1]), swap(out[2]), swap(out[3]), out[4:13], [v.reshape(-1) for v in out[13:]]


def gather_ops(nz, pieces, ins, outs, send, recv, sib_send, sib_recv):
    f, c = lax.axis_index("fsdp"), lax.axis_index("dp")
    z, y, x = f // 4, (f // 2) % 2, f % 2
    xn, yn, up, dn, sib = (f + 1 - 2 * x, c), (f + 2 - 4 * y, c), (f + 4, c), (f - 4, c), (f, 1 - c)
    bar = pltpu.get_barrier_semaphore()

    def greet(dev):
        pl.semaphore_signal(bar, inc=1, device_id=dev, device_id_type=MESH)

    greet(xn)
    greet(yn)
    greet(sib)
    pl.when(z < nz - 1)(lambda: greet(up))
    pl.when(z > 0)(lambda: greet(dn))
    pl.semaphore_wait(bar, 3 + (z < nz - 1).astype(jnp.int32) + (z > 0).astype(jnp.int32))
    dest = {"x": xn, "y": yn, "u": up, "d": dn}
    there = {"x": None, "y": None, "u": z < nz - 1, "d": z > 0}
    code = {"x": 0, "y": 0, "u": 1, "d": 2}

    def columns(i, half):
        w, c0, cols, order, share = pieces[i]
        return pl.ds(pl.multiple_of(half * (ins[w].shape[1] // 2) + c0, 128) if share else c0, cols)

    def region(i, s, half):
        w = pieces[i][0]
        r = ins[w].shape[0]
        return outs[w].at[pl.ds(pl.multiple_of(s * r, r), r), columns(i, half)]

    def own(i):
        return ins[pieces[i][0]].at[:, columns(i, c)]

    def remote(i, s, src, d):
        return pltpu.make_async_remote_copy(
            src_ref=src, dst_ref=region(i, s, c), send_sem=send.at[i, code[d]], recv_sem=recv.at[i, s],
            device_id=dest[d], device_id_type=MESH)

    def sibling(i, s, half):
        return pltpu.make_async_remote_copy(
            src_ref=region(i, s, half), dst_ref=region(i, s, half), send_sem=sib_send.at[i],
            recv_sem=sib_recv.at[i], device_id=sib, device_id_type=MESH)

    def some(i, half, count):
        w = pieces[i][0]
        part = outs[w].at[pl.ds(0, count * ins[w].shape[0]), columns(i, half)]
        return lambda a, b: pltpu.make_async_remote_copy(
            src_ref=part, dst_ref=part, send_sem=a, recv_sem=b, device_id=sib, device_id_type=MESH)

    def along(dirs, act):
        for d in dirs:
            if there[d] is None:
                act(d)
            else:
                pl.when(there[d])(lambda d=d: act(d))

    def each(h, i, act):
        for bx, by, sgn in slots():
            k = h - bx - by
            if isinstance(h, int) and not ((k == 0) if sgn == 0 else (1 <= k < nz)):
                continue
            zs = z + sgn * k
            valid = (k == 0) if sgn == 0 else (k >= 1) & (zs >= 0) & (zs < nz)
            s = zs * 4 + (y + by - 2 * by * y) * 2 + (x + bx - 2 * bx * x)
            dirs = forwards(pieces[i][3], bx, by, sgn)
            if isinstance(valid, bool):
                act(i, s, dirs)
            else:
                pl.when(valid)(lambda s=s, dirs=dirs: act(i, s, dirs))

    def start(i):
        along(forwards(pieces[i][3], 0, 0, 0), lambda d: remote(i, f, own(i), d).start())

    def step(i, s, dirs):
        remote(i, s, region(i, s, c), "x").wait_recv()
        along(dirs, lambda d: remote(i, s, region(i, s, c), d).start())
        if pieces[i][4]:
            sibling(i, s, c).start()

    def arrived(i):
        if pieces[i][4]:
            some(i, 1 - c, 4 * nz - 1)(sib_send.at[i], sib_recv.at[i]).wait_recv()

    def finish(i):
        order = pieces[i][3]
        before = {d: order[:order.index(d)] for d in "xyz"}
        size = {"x": 2, "y": 2, "z": nz}

        def blocks(d):
            n = 1
            for e in before[d]:
                n *= size[e]
            return n

        some(i, c, blocks("x") + blocks("y"))(send.at[i, 0], recv.at[i, 0]).wait_send()
        for p in range(nz):
            if p < nz - 1:
                pl.when(z == p)(lambda p=p: some(i, c, blocks("z") * (p + 1))(send.at[i, 1], recv.at[i, 0]).wait_send())
            if p > 0:
                pl.when(z == p)(lambda p=p: some(i, c, blocks("z") * (nz - p))(send.at[i, 2], recv.at[i, 0]).wait_send())
        if pieces[i][4]:
            some(i, c, 4 * nz - 1)(sib_send.at[i], sib_recv.at[i]).wait_send()

    def level(h, indices):
        for i in indices:
            each(h, i, step)

    return start, level, arrived, finish


def gather_encode_kernel(wc, nc, nz, pieces, nw, shw, shn, visw, visn, cotw, cotn, cw, cn, *refs):
    devices = 4 * nz
    vectors, refs = refs[:5], refs[5:]
    ins, refs = list(refs[:nw - 1]), refs[nw - 1:]
    outs, refs = refs[:nw], refs[nw:]
    results_, refs = refs[:13], refs[13:]
    buffers, refs = refs[:13], refs[13:]
    perm, sel, dz, m_ref, x_ref, a_ref, qkv, o_ref, x1_ref, b_ref, h_ref, slope_ref, e_ref = buffers
    wq, wo, wu, wd, we, tiles, sum_ref, pair, tile, send, recv, sib_send, sib_recv, loc, sems, out_sems = refs
    row = iota((16, 128), 0)
    shares = jnp.zeros((16, 128), F)
    for k, v in enumerate(vectors):
        n = v.shape[-1]
        wide = jnp.concatenate([v[...].astype(F).reshape(1, n), jnp.zeros((1, 128 - n), F)], axis=1)
        shares = jnp.where(row == k, wide, shares)
    tile[...] = shares.astype(B)
    ins.append(tile)

    def leave(*which):
        for k in which:
            pltpu.make_async_copy(buffers[k], results_[k], out_sems.at[k]).start()

    D = wo.shape[0]
    start, level, arrived, finish = gather_ops(nz, pieces, ins, outs, send, recv, sib_send, sib_recv)
    sets = {"q": [nw - 1, 0], "u": [2], "d": [3], "o": [1], "e": [4], "5": [5], "6": [6], "7": [7], "8": [8]}
    members = {s: [i for w in ws for i, p in enumerate(pieces) if p[0] == w] for s, ws in sets.items()}
    into = [wq, wo, wu, wd, we, None, None, None, None, tiles]
    loads = {}
    gains = []
    locals_ = []
    C = 512
    chunks = wu.shape[1] // C

    def prepare():
        for w in range(nw):
            r = ins[w].shape[0]
            cp = pltpu.make_async_copy(
                ins[w], outs[w].at[pl.ds(pl.multiple_of(lax.axis_index("fsdp") * r, r), r)], loc.at[w])
            cp.start()
            locals_.append(cp)
        placement(wc, nc, shw, shn, visw, visn, cotw, cotn, perm, sel, dz)
        load_rows(x_ref, pair, cw, cn, wc, nc)
        leave(0, 1, 2, 4)

    def ready(s):
        for w, i in zip(sets[s], members[s]):
            arrived(i)
            locals_[w].wait()
            loads[w] = pltpu.make_async_copy(outs[w], into[w], sems.at[w])
            loads[w].start()

    def project():
        loads[nw - 1].wait()
        gains.append(spread_vector(tiles[...], 0, D, devices))
        gains.append(spread_vector(tiles[...], 1, D, devices))
        a = (norm_stats(x_ref[...])[0] * gains[0]).astype(B)
        a_ref[...] = a
        loads[0].wait()
        for k in range(0, 3 * D, D):
            qkv[:, k:k + D] = dot(a, wq[:, k:k + D]).astype(B)
        leave(5, 6)

    def attend(part):
        mask = pair_mask()
        groups = x_ref.shape[0] // 128
        for g in range(groups):
            if g * 2 // groups != part:
                continue
            rr = slice(128 * g, 128 * g + 128)
            valid = valid_keys(0 if g < wc else 1, cw.shape[1], cn.shape[0])
            for j in range(D // 128):
                q, k, v = (qkv[rr, o + 128 * j:o + 128 * j + 128] for o in (0, D, 2 * D))
                k2 = jnp.concatenate([k, k], axis=0) * mask
                v2 = jnp.concatenate([v, v], axis=0) * mask
                p2 = jnp.concatenate(pair_shares(q, k2, valid), axis=1).astype(B)
                o_ref[rr, 128 * j:128 * j + 128] = dot(p2, v2).astype(B)

    def middle():
        loads[1].wait()
        x1 = x_ref[...] + dot(o_ref[...], wo[...])
        x1_ref[...] = x1
        sum_ref[...] = x1
        b_ref[...] = (norm_stats(x1)[0] * gains[1]).astype(B)
        leave(7, 8, 9)

    def feed_forward(j):
        if j == 0:
            loads[2].wait()
            loads[3].wait()
        k = j * C
        h, slope = gelu_both(dot(b_ref[...], wu[:, k:k + C]))
        h = h.astype(B)
        h_ref[:, k:k + C] = h
        slope_ref[:, k:k + C] = slope
        sum_ref[...] += dot(h, wd[k:k + C, :])
        for n in (10, 11):
            pltpu.make_async_copy(buffers[n].at[:, k:k + C], results_[n].at[:, k:k + C], out_sems.at[n]).start()

    def embed():
        e_ref[...] = sum_ref[...].astype(B)
        leave(12)
        loads[4].wait()
        m_ref[...] = dot(e_ref[...], we[...])
        leave(3)

    compute = [project, functools.partial(attend, 0), functools.partial(attend, 1), middle]
    compute += [functools.partial(feed_forward, j) for j in range(chunks)] + [embed]
    for token in gather_schedule(nz + 1, len(compute)):
        if token[0] == "S":
            for i in members[token[1]]:
                start(i)
        elif token[0] == "V":
            level(token[1], members[token[2]])
        elif token[0] == "R":
            ready(token[1])
        elif token[0] == "P":
            prepare()
        else:
            compute[token[1]]()
    for w in (5, 6, 7, 8):
        locals_[w].wait()
    for s in "5678":
        for i in members[s]:
            arrived(i)
    for i in range(len(pieces)):
        finish(i)
    for n in range(13):
        pltpu.make_async_copy(buffers[n], results_[n], out_sems.at[n]).wait()


def gather_schedule(top, steps):
    if (top, steps) == (5, 11):
        return list(GATHER_SCHEDULE)
    tokens = [("S", s) for s in "qudoe"] + [("P",)] + [("S", s) for s in "5678"]
    tokens += [("V", h, s) for h in range(1, top + 1) for s in "qudoe5678"]
    return tokens + [("R", s) for s in "qoude"] + [("C", k) for k in range(steps)]


def gather_encode(shards, vectors, pieces, place, cw, cn, nz, cid=1):
    nw, npc, n = len(shards) + 1, len(pieces), 4 * nz
    wc, nc, D = cw.shape[0], cn.shape[1], cw.shape[2]
    R = 128 * wc + 128 * ((nc + 1) // 2)
    V = pl.BlockSpec(memory_space=pltpu.VMEM)
    S = pl.BlockSpec(memory_space=pltpu.SMEM)
    A = pl.BlockSpec(memory_space=pl.ANY)
    sds = jax.ShapeDtypeStruct
    whole = [sds((s.shape[0] * n, s.shape[1]), s.dtype) for s in shards] + [sds((16 * n, 128), B)]
    FFD, DD = shards[2].shape[1], shards[4].shape[1]
    dma = pltpu.SemaphoreType.DMA
    kept = placed_shapes(*place[4:]) + [
        sds((R, DD), F), sds((R, D), F), sds((R, D), B), sds((R, 3 * D), B), sds((R, D), B), sds((R, D), F),
        sds((R, D), B), sds((R, FFD), B), sds((R, FFD), F), sds((R, D), B)]
    out = pl.pallas_call(
        functools.partial(gather_encode_kernel, wc, nc, nz, pieces, nw),
        out_shape=whole + kept,
        in_specs=[S, S] + [V] * 11 + [A] * (nw - 1),
        out_specs=[A] * (nw + 13),
        scratch_shapes=[pltpu.VMEM(s.shape, s.dtype) for s in kept] + [pltpu.VMEM(w.shape, B) for w in whole[:5]] + [
            pltpu.VMEM(whole[-1].shape, B), pltpu.VMEM((R, D), F), pltpu.VMEM(cn.shape, F), pltpu.VMEM((16, 128), B),
            dma((npc, 3)), dma((npc, n)), dma((npc,)), dma((npc,)), dma((nw,)), dma((nw,)), dma((13,))],
        compiler_params=pltpu.CompilerParams(collective_id=cid, has_side_effects=True, vmem_limit_bytes=VMEM_LIMIT),
        name="gather_and_encode",
    )(*place, cw, cn, *vectors, *shards)
    return out[:nw], out[nw:nw + 3], out[nw + 3:]


def slot_count(order, d, nz):
    size = {"x": 2, "y": 2, "z": nz}
    k = 1
    for e in order[:order.index("z" if d in "ud" else d)]:
        k *= size[e]
    return k * (nz + 1) if d in "ud" else k


def slot_index(order, d, nz, pos):
    size = {"x": 2, "y": 2, "z": nz}
    k = 0
    for e in order[:order.index("z" if d in "ud" else d)]:
        k = k * size[e] + pos[e]
    return k * (nz + 1) + pos["z"] + (1 if d == "d" else 0) if d in "ud" else k


def parent(order, bx, by, sgn):
    differs = {"x": bx, "y": by, "z": int(sgn != 0)}
    last = max(j for j, d in enumerate(order) if differs[d])
    if order[last] == "z":
        return "d" if sgn < 0 else "u"
    return order[last]


def reduce_ops(nz, pieces, rows, mine, other, sibb, rbuf, res, outs, sib_send, sib_recv, send, recv, res_sem, res_send, res_recv):
    f, c = lax.axis_index("fsdp"), lax.axis_index("dp")
    z, y, x = f // 4, (f // 2) % 2, f % 2
    bits = (nz * 4).bit_length() - 1

    def flip(b):
        return f + (1 << b) * (1 - 2 * ((f // (1 << b)) % 2))

    xn, yn, up, dn, sib = (flip(0), c), (flip(1), c), (f + 4, c), (f - 4, c), (f, 1 - c)
    bar = pltpu.get_barrier_semaphore()

    def greet(dev):
        pl.semaphore_signal(bar, inc=1, device_id=dev, device_id_type=MESH)

    greet(xn)
    greet(yn)
    greet(sib)
    pl.when(z < nz - 1)(lambda: greet(up))
    pl.when(z > 0)(lambda: greet(dn))
    far = range(3, bits)
    for b in far:
        greet((flip(b), c))
    pl.semaphore_wait(bar, 3 + len(far) + (z < nz - 1).astype(jnp.int32) + (z > 0).astype(jnp.int32))
    dest = {"x": xn, "y": yn, "u": up, "d": dn}
    there = {"u": z < nz - 1, "d": z > 0}
    opposite = {"u": "d", "d": "u", "x": "x", "y": "y"}
    kind = {"x": 0, "y": 1, "u": 2, "d": 2}

    def give(w):
        return pltpu.make_async_remote_copy(
            src_ref=other[w], dst_ref=sibb[w], send_sem=sib_send.at[w], recv_sem=sib_recv.at[w],
            device_id=sib, device_id_type=MESH)

    def cols(i):
        return pl.ds(pieces[i][1], pieces[i][2])

    def message(i, s, pos, d):
        w, order, b = pieces[i][0], pieces[i][3], kind[d]
        r = rows[w]
        q = slot_index(order, opposite[d], nz, pos)
        return pltpu.make_async_remote_copy(
            src_ref=mine[w].at[pl.ds(pl.multiple_of(s * r, r), r), cols(i)], dst_ref=rbuf[i][b].at[q],
            send_sem=send.at[i], recv_sem=recv.at[i, b, q], device_id=dest[d], device_id_type=MESH)

    def arrival(i, pos, d):
        b = kind[d]
        q = slot_index(pieces[i][3], d, nz, pos)
        return pltpu.make_async_remote_copy(
            src_ref=rbuf[i][b].at[q], dst_ref=rbuf[i][b].at[q], send_sem=send.at[i],
            recv_sem=recv.at[i, b, q], device_id=sib, device_id_type=MESH)

    def add(i, s, pos, children, final):
        w, order = pieces[i][0], pieces[i][3]
        r = rows[w]
        ks = [(kind[d], slot_index(order, d, nz, pos)) for d in children]

        tall = 16
        while r % (2 * tall) == 0 and 2 * tall * pieces[i][2] <= 24 * 16 * 128:
            tall *= 2
        if r % 48 == 0 and 48 * pieces[i][2] <= 27 * 16 * 128:
            tall = max(tall, 48)

        @pl.loop(0, r // tall)
        def _(k):
            rr = pl.ds(pl.multiple_of(k * tall, 16), tall)
            gr = pl.ds(pl.multiple_of(s * r + k * tall, 16), tall)
            t = mine[w][gr, cols(i)].astype(F) + sibb[w][gr, cols(i)].astype(F)
            for b, q in ks:
                t = t + rbuf[i][b][q, rr].astype(F)
            if final:
                res[w][rr, cols(i)] = t
            else:
                mine[w][gr, cols(i)] = t.astype(B)

    def gather_children(i, s, pos, children, final):
        sure = [d for d in children if d in "xy"]
        maybe = [d for d in children if d in "ud"]
        for d in sure:
            arrival(i, pos, d).wait_recv()
        for d in maybe:
            pl.when(there[d])(lambda d=d: arrival(i, pos, d).wait_recv())
        if not maybe:
            add(i, s, pos, sure, final)
        elif len(maybe) == 1:
            pl.when(there[maybe[0]])(lambda: add(i, s, pos, sure + maybe, final))
            pl.when(jnp.logical_not(there[maybe[0]]))(lambda: add(i, s, pos, sure, final))
        else:
            u, d = there["u"], there["d"]
            pl.when(u & d)(lambda: add(i, s, pos, sure + ["u", "d"], final))
            pl.when(u & jnp.logical_not(d))(lambda: add(i, s, pos, sure + ["u"], final))
            pl.when(jnp.logical_not(u) & d)(lambda: add(i, s, pos, sure + ["d"], final))
            if nz == 1:
                add(i, s, pos, sure, final)

    def each(h, i, leaf, act):
        order = pieces[i][3]
        for bx, by, sgn in slots():
            children = forwards(order, bx, by, sgn)
            if leaf is not None and (len(children) == 0) != leaf:
                continue
            k = h - bx - by
            if isinstance(h, int) and not ((k == 0) if sgn == 0 else (1 <= k < nz)):
                continue
            zs = z + sgn * k
            valid = (k == 0) if sgn == 0 else (k >= 1) & (zs >= 0) & (zs < nz)
            pos = {"x": x + bx - 2 * bx * x, "y": y + by - 2 * by * y, "z": zs}
            s = zs * 4 + pos["y"] * 2 + pos["x"]
            p = parent(order, bx, by, sgn)
            if isinstance(valid, bool):
                act(i, s, pos, children, p)
            else:
                pl.when(valid)(lambda s=s, pos=pos, children=children, p=p: act(i, s, pos, children, p))

    def work(i, s, pos, children, p):
        gather_children(i, s, pos, children, False)
        message(i, s, pos, p).start()

    def leaves(h, indices):
        for i in indices:
            each(h, i, True, work)

    def nodes(h, indices):
        for i in indices:
            each(h, i, False, work)

    def out_copy(w):
        n = outs[w].shape[1] // 2
        return pltpu.make_async_copy(res[w], outs[w].at[:, pl.ds(pl.multiple_of(c * n, 128), n)], res_sem.at[w])

    def out_sib(w, half):
        n = outs[w].shape[1] // 2
        return pltpu.make_async_remote_copy(
            src_ref=res[w], dst_ref=outs[w].at[:, pl.ds(pl.multiple_of(half * n, 128), n)], send_sem=res_send.at[w],
            recv_sem=res_recv.at[w], device_id=sib, device_id_type=MESH)

    def total(w):
        for i, piece in enumerate(pieces):
            if piece[0] == w:
                gather_children(i, f, {"x": x, "y": y, "z": z}, forwards(piece[3], 0, 0, 0), True)
        out_sib(w, c).start()
        out_copy(w).start()

    def sent(indices):
        for i in indices:
            w = pieces[i][0]
            part = mine[w].at[pl.ds(0, (4 * nz - 1) * rows[w]), cols(i)]
            pltpu.make_async_remote_copy(
                src_ref=part, dst_ref=part, send_sem=send.at[i], recv_sem=recv.at[i, 0, 0], device_id=sib,
                device_id_type=MESH).wait_send()

    def finish(ws):
        for w in ws:
            give(w).wait_send()
            out_copy(w).wait()
            out_sib(w, c).wait_send()
            out_sib(w, 1 - c).wait_recv()

    return flip, give, leaves, nodes, total, sent, finish


def encode_back_reduce_kernel(wc, wide_seen, narrow_seen, nz, routes, *refs):
    devices = 4 * nz
    dec_vec, *refs = refs
    given, refs = refs[:9], refs[9:]
    h_h, slope_h, we_h, wd_h, wu_h, wo_h, wq_h, *refs = refs
    dec_g, refs = refs[:4], refs[4:]
    (dx_ref, vec_out, *refs) = refs
    outs, refs = refs[:9], refs[9:]
    (we, wo, wq, wd2, wu2, h2, slope2, dx1_ref, z_ref, do_ref, dqkv, *refs) = refs
    tiles, dm, e_ref, b_ref, x1_ref, o_ref, qkv, a_ref, x_ref = refs[:9]
    refs = refs[9:]
    mine, refs = refs[:9], refs[9:]
    enc_other, refs = refs[:5], refs[5:]
    sibb, refs = refs[:9], refs[9:]
    res, refs = refs[:9], refs[9:]
    npc = len(routes)
    rbuf, refs = [refs[3 * i:3 * i + 3] for i in range(npc)], refs[3 * npc:]
    (vbuf, wsem, gsem, dsem, sib_send, sib_recv, send, recv, res_sem, res_send, res_recv, vsend, vrecv) = refs
    c = lax.axis_index("dp")
    held = [tiles, dm, e_ref, b_ref, x1_ref, o_ref, qkv, a_ref, x_ref]
    takes_in = [pltpu.make_async_copy(s, d, gsem.at[k]) for k, (s, d) in enumerate(zip(given, held))]
    for cp in takes_in:
        cp.start()
    D = wo.shape[0]
    n_up = mine[2].shape[1]
    rows = [m.shape[0] // devices for m in mine]

    def half(ref, h):
        n = ref.shape[1] // 2
        return ref.at[:, pl.ds(pl.multiple_of(h * n, 128), n)]

    other = list(enc_other) + [half(g, 1 - c) for g in dec_g]
    flip, give, leaves, nodes, total, sent, finish = reduce_ops(
        nz, routes, rows, mine, other, sibb, rbuf, res, outs, sib_send, sib_recv, send, recv, res_sem, res_send, res_recv)
    dec_ws = [5, 6, 7, 8]
    for w in dec_ws:
        give(w).start()
    takes = [pltpu.make_async_copy(half(dec_g[w - 5], c), mine[w], dsem.at[w - 5]) for w in dec_ws]
    for t in takes:
        t.start()
    loads = [pltpu.make_async_copy(s, d, wsem.at[k]) for k, (s, d) in enumerate(((we_h, we), (wo_h, wo), (wq_h, wq)))]
    C = 512
    chunks = 2 * n_up // C

    def chunk(j):
        h = (1 - c) if j < chunks // 2 else c
        return pl.multiple_of(h * n_up + (j % (chunks // 2)) * C, 128)

    def feed(j):
        k = chunk(j)
        return (pltpu.make_async_copy(wd_h.at[pl.ds(k, C)], wd2.at[j % 2], wsem.at[3 + j % 2]),
                pltpu.make_async_copy(wu_h.at[:, pl.ds(k, C)], wu2.at[j % 2], wsem.at[5 + j % 2]),
                pltpu.make_async_copy(h_h.at[:, pl.ds(k, C)], h2.at[j % 2], wsem.at[7 + j % 2]),
                pltpu.make_async_copy(slope_h.at[:, pl.ds(k, C)], slope2.at[j % 2], wsem.at[9 + j % 2]))

    loads[0].start()
    for j in (0, 1):
        for cp in feed(j):
            cp.start()
    loads[1].start()
    loads[2].start()
    takes_in[0].wait()
    gain1 = spread_vector(tiles[...], 0, D, devices)
    gain2 = spread_vector(tiles[...], 1, D, devices)
    def own_cols(w):
        n = mine[w].shape[1]
        return pl.ds(pl.multiple_of(c * n, 128), n), pl.ds(pl.multiple_of((1 - c) * n, 128), n)

    sets = {"5": [5], "7": [7], "8": [8], "6": [6], "d": [3], "u": [2], "e": [4], "O": [1], "Q": [0]}
    members = {s: [i for i, p in enumerate(routes) if p[0] in ws] for s, ws in sets.items()}
    kept = {}

    def first():
        for cp in takes_in[1:4]:
            cp.wait()
        loads[0].wait()
        grad = dot_nt(dm[...], we[...])
        dx1_ref[...] = grad
        z_ref[...] = grad.astype(B)
        own, rest = own_cols(4)
        enc_other[4][...] = dot_tn(e_ref[...], dm[:, rest]).astype(B)
        mine[4][...] = dot_tn(e_ref[...], dm[:, own]).astype(B)
        give(4).start()
        kept["back"] = jnp.zeros_like(grad)

    def feed_forward(j):
        own, rest = own_cols(3)
        for cp in feed(j):
            cp.wait()
        kk = pl.ds(chunk(j), C)
        d = (slope2[j % 2] * dot_nt(z_ref[...], wd2[j % 2])).astype(B)
        kept["back"] = kept["back"] + dot_nt(d, wu2[j % 2])
        hk = h2[j % 2]
        enc_other[3][kk, :] = dot_tn(hk, z_ref[:, rest]).astype(B)
        mine[3][kk, :] = dot_tn(hk, z_ref[:, own]).astype(B)
        g = dot_tn(b_ref[...], d).astype(B)
        at = (j % (chunks // 2)) * C
        if j < chunks // 2:
            enc_other[2][:, at:at + C] = g
        else:
            mine[2][:, at:at + C] = g
        if j == chunks // 2 - 1:
            give(2).start()
        if j == chunks - 1:
            give(3).start()
        if j + 2 < chunks:
            for cp in feed(j + 2):
                cp.start()

    def project():
        takes_in[4].wait()
        takes_in[5].wait()
        by_input, by_gain = norm_back(x1_ref[...], gain2, kept.pop("back"))
        vbuf[0, 0] = jnp.zeros_like(vbuf[0, 0])
        vbuf[0, 0, 1:2, :] = jnp.sum(by_gain, axis=0, keepdims=True)
        dx1_ref[...] += by_input
        z_ref[...] = dx1_ref[...].astype(B)
        loads[1].wait()
        do_ref[...] = dot_nt(z_ref[...], wo[...]).astype(B)
        own, rest = own_cols(1)
        enc_other[1][...] = dot_tn(o_ref[...], z_ref[:, rest]).astype(B)
        mine[1][...] = dot_tn(o_ref[...], z_ref[:, own]).astype(B)
        give(1).start()

    def attend(part):
        if part == 0:
            takes_in[6].wait()
        mask = pair_mask()
        groups = x_ref.shape[0] // 128
        scale = ENC_HEAD ** -0.5
        lane = iota((128, 128), 1)
        for g in range(groups):
            if g * 2 // groups != part:
                continue
            rr = slice(128 * g, 128 * g + 128)
            valid = valid_keys(0 if g < wc else 1, wide_seen, narrow_seen)
            for j in range(D // 128):
                q, k, v = (qkv[rr, o + 128 * j:o + 128 * j + 128] for o in (0, D, 2 * D))
                g_o = do_ref[rr, 128 * j:128 * j + 128]
                k2 = jnp.concatenate([k, k], axis=0) * mask
                v2 = jnp.concatenate([v, v], axis=0) * mask
                shares = pair_shares(q, k2, valid)
                dp2 = dot_nt(g_o, v2)
                ds, low = [], []
                for h in range(2):
                    dp = dp2[:, 128 * h:128 * h + 128]
                    p = shares[h]
                    ds.append((p * (dp - jnp.sum(dp * p, axis=1, keepdims=True))).astype(B))
                    low.append(p.astype(B))
                dq = dot(jnp.concatenate(ds, axis=1), k2) * scale
                dk = jnp.where(lane < ENC_HEAD, dot_tn(ds[0], q), dot_tn(ds[1], q)) * scale
                dv = jnp.where(lane < ENC_HEAD, dot_tn(low[0], g_o), dot_tn(low[1], g_o))
                for o, d in ((0, dq), (D, dk), (2 * D, dv)):
                    dqkv[rr, o + 128 * j:o + 128 * j + 128] = d.astype(B)

    def mix():
        takes_in[7].wait()
        own, rest = own_cols(0)
        enc_other[0][...] = dot_tn(a_ref[...], dqkv[:, rest]).astype(B)
        give(0).start()
        mine[0][...] = dot_tn(a_ref[...], dqkv[:, own]).astype(B)

    bits = devices.bit_length() - 1

    def vcopy(k):
        return pltpu.make_async_remote_copy(
            src_ref=vbuf.at[0, k], dst_ref=vbuf.at[1, k], send_sem=vsend.at[k], recv_sem=vrecv.at[k],
            device_id=(lax.axis_index("fsdp"), 1 - c) if k == 0 else (flip(k - 1), c), device_id_type=MESH)

    def vstep(k):
        vcopy(k).wait()
        vbuf[0, k + 1] = vbuf[0, k] + vbuf[1, k]
        if k < bits:
            vcopy(k + 1).start()

    def last():
        takes_in[8].wait()
        loads[2].wait()
        by_input, by_gain = norm_back(x_ref[...], gain1, dot_nt(dqkv[...], wq[...]))
        vbuf[0, 0, 0:1, :] = jnp.sum(by_gain, axis=0, keepdims=True)
        DD = dec_vec.shape[1]
        vbuf[0, 0, 2:3, 0:DD] = dec_vec[2:3, :]
        vbuf[0, 0, 3:5, 0:DD] = dec_vec[0:2, :]
        vcopy(0).start()
        dx_ref[...] = dx1_ref[...] + by_input

    compute = [first] + [functools.partial(feed_forward, j) for j in range(chunks)] + [project]
    compute += [functools.partial(attend, 0), functools.partial(attend, 1), mix, last]

    def ready(s):
        if s in "5678":
            for w in sets[s]:
                takes[w - 5].wait()
        for w in sets[s]:
            give(w).wait_recv()

    vectors = []
    for token in schedule(nz + 1, len(compute)):
        if token[0] == "C":
            compute[token[1]]()
            if token[1] == len(compute) - 1:
                vectors = list(range(bits + 1))
        elif token[0] == "R":
            ready(token[1])
        elif token[0] == "L":
            leaves(token[1], members[token[2]])
        elif token[0] == "N":
            nodes(token[1], members[token[2]])
        else:
            for w in sets[token[1]]:
                total(w)
        if vectors and token[0] == "N":
            vstep(vectors.pop(0))
    for k in vectors:
        vstep(k)
    vec_out[...] = vbuf[0, bits + 1]
    sent(range(npc))
    finish(range(9))


def schedule(top, steps):
    if (top, steps) == (5, 12):
        return list(SCHEDULE)
    tokens = [("C", k) for k in range(steps)] + [("R", s) for s in "5786dueOQ"]
    tokens += [("L", top, s) for s in "5786dueOQ"]
    for h in range(top, 0, -1):
        tokens += [("N", h, s) for s in "5786dueOQ"]
        tokens += [("L", h - 1, s) for s in "5786dueOQ"] if h > 1 else []
    return tokens + [("T", s) for s in "5786dueOQ"]


def encode_back_reduce(tiles, counts, dm, dec_vec, saved, enc, dec_grads, routes, nz, cid=2):
    R = dm.shape[0]
    n = 4 * nz
    bits = n.bit_length() - 1
    x, a, qkv, o, x1, b, h, slope, e = saved
    wq, wo, wu, wd, we = enc
    D = wq.shape[0]
    grads = [*enc, *dec_grads]
    shards = [(g.shape[0] // n, g.shape[1]) for g in grads]
    V = pl.BlockSpec(memory_space=pltpu.VMEM)
    A = pl.BlockSpec(memory_space=pl.ANY)
    sds = jax.ShapeDtypeStruct
    dma = pltpu.SemaphoreType.DMA
    most = 1
    rbuf = []
    for w, c0, cols, order in routes:
        for d in "xyu":
            k = slot_count(order, d, nz)
            most = max(most, k)
            rbuf.append(pltpu.VMEM((k, shards[w][0], cols), B))
    npc = len(routes)
    halves = [pltpu.VMEM((g.shape[0], g.shape[1] // 2), B) for g in grads]
    C = 512
    given = [tiles, dm, e, b, x1, o, qkv, a, x]
    out = pl.pallas_call(
        functools.partial(encode_back_reduce_kernel, *counts, nz, routes),
        out_shape=[sds((R, D), F), sds((8, D), F)] + [sds(s, F) for s in shards],
        in_specs=[V] + [A] * 20,
        out_specs=[V] * 2 + [A] * 9,
        scratch_shapes=[
            pltpu.VMEM(we.shape, B), pltpu.VMEM(wo.shape, B), pltpu.VMEM(wq.shape, B),
            pltpu.VMEM((2, C, D), B), pltpu.VMEM((2, D, C), B), pltpu.VMEM((2, R, C), B), pltpu.VMEM((2, R, C), F),
            pltpu.VMEM((R, D), F), pltpu.VMEM((R, D), B), pltpu.VMEM((R, D), B),
            pltpu.VMEM((R, 3 * D), B),
        ] + [pltpu.VMEM(g.shape, g.dtype) for g in given] + halves + halves[:5] + halves + [pltpu.VMEM((s[0], s[1] // 2), F) for s in shards] + rbuf + [
            pltpu.VMEM((2, bits + 2, 8, D), F), dma((11,)), dma((9,)), dma((4,)), dma((9,)), dma((9,)), dma((npc,)),
            dma((npc, 3, most)), dma((9,)), dma((9,)), dma((9,)), dma((bits + 1,)), dma((bits + 1,))],
        compiler_params=pltpu.CompilerParams(collective_id=cid, has_side_effects=True, vmem_limit_bytes=63 * 2**20),
        name="encoder_backward_and_reduce",
    )(dec_vec, *given, h, slope, we, wd, wu, wo, wq, *dec_grads)
    return out[0], out[1], out[2:]


ZXY = ("z", "x", "y")
ZYX = ("z", "y", "x")
XYZ = ("x", "y", "z")
YXZ = ("y", "x", "z")
XZY = ("x", "z", "y")
YZX = ("y", "z", "x")
GATHER = ((0, ZYX), (2, ZYX), (3, XZY), (1, YXZ), (4, ZXY), (5, YZX), (7, ZYX), (8, XZY), (6, XYZ))
GATHER_SCHEDULE = (
    ("S", "q"), ("S", "6"), ("S", "o"), ("S", "8"), ("P",), ("V", 1, "q"), ("S", "e"), ("S", "d"), ("V", 1, "o"),
    ("V", 2, "q"), ("S", "u"), ("V", 1, "d"), ("V", 2, "o"), ("V", 3, "q"), ("V", 1, "u"), ("V", 1, "e"),
    ("V", 1, "6"), ("V", 4, "q"), ("V", 2, "d"), ("V", 2, "u"), ("V", 2, "e"), ("S", "5"), ("V", 3, "o"),
    ("V", 5, "q"), ("V", 2, "6"), ("S", "7"), ("R", "q"), ("V", 3, "d"), ("C", 0), ("V", 3, "u"), ("V", 4, "o"),
    ("V", 1, "5"), ("V", 3, "e"), ("C", 1), ("V", 1, "8"), ("V", 4, "d"), ("V", 4, "u"), ("V", 5, "o"),
    ("V", 1, "7"), ("V", 2, "5"), ("V", 4, "e"), ("C", 2), ("V", 5, "u"), ("R", "o"), ("V", 5, "d"),
    ("V", 2, "8"), ("C", 3), ("V", 5, "e"), ("V", 2, "7"), ("R", "d"), ("V", 3, "6"), ("R", "u"), ("V", 3, "5"),
    ("C", 4), ("V", 3, "8"), ("C", 5), ("V", 3, "7"), ("C", 6), ("V", 4, "6"), ("R", "e"), ("V", 4, "5"),
    ("C", 7), ("V", 4, "8"), ("V", 4, "7"), ("C", 8), ("V", 5, "6"), ("C", 9), ("C", 10), ("V", 5, "7"),
    ("V", 5, "5"), ("V", 5, "8"),
)
REDUCE = ((5, XYZ), (7, ZYX), (8, XZY), (6, ZYX), (3, ZYX), (2, XZY), (4, XYZ), (1, ZYX), (0, ZYX))
SCHEDULE = (
    ("C", 0), ("C", 1), ("R", "5"), ("C", 2), ("C", 3), ("R", "e"), ("L", 5, "5"), ("R", "8"), ("R", "7"),
    ("N", 5, "e"), ("L", 5, "e"), ("L", 5, "8"), ("L", 5, "7"), ("L", 4, "5"), ("L", 3, "5"), ("N", 5, "5"),
    ("L", 4, "8"), ("L", 4, "e"), ("L", 3, "8"), ("L", 4, "7"), ("R", "6"), ("N", 5, "7"), ("N", 4, "e"),
    ("L", 2, "5"), ("N", 5, "8"), ("L", 3, "7"), ("L", 2, "7"), ("N", 4, "8"), ("C", 4), ("N", 4, "5"),
    ("L", 2, "8"), ("L", 1, "8"), ("C", 5), ("N", 3, "8"), ("C", 6), ("R", "u"), ("L", 1, "7"), ("L", 5, "6"),
    ("L", 5, "u"), ("L", 3, "e"), ("N", 3, "e"), ("N", 5, "u"), ("L", 4, "u"), ("L", 4, "6"), ("N", 3, "5"),
    ("L", 3, "6"), ("N", 4, "7"), ("L", 2, "6"), ("L", 3, "u"), ("L", 1, "6"), ("R", "d"), ("L", 5, "d"),
    ("L", 4, "d"), ("L", 3, "d"), ("N", 4, "u"), ("N", 5, "6"), ("C", 7), ("N", 5, "d"), ("N", 2, "5"), ("C", 8),
    ("N", 4, "6"), ("N", 2, "e"), ("R", "O"), ("N", 5, "O"), ("N", 3, "7"), ("N", 4, "d"), ("L", 5, "O"),
    ("L", 2, "u"), ("L", 2, "d"), ("N", 3, "u"), ("L", 1, "5"), ("C", 9), ("C", 10), ("L", 2, "e"),
    ("N", 2, "7"), ("L", 4, "O"), ("N", 2, "u"), ("R", "Q"), ("N", 5, "Q"), ("N", 2, "8"), ("L", 3, "O"),
    ("N", 3, "6"), ("L", 1, "u"), ("L", 5, "Q"), ("L", 4, "Q"), ("N", 4, "O"), ("N", 3, "d"), ("N", 4, "Q"),
    ("L", 3, "Q"), ("N", 1, "5"), ("N", 1, "7"), ("N", 3, "O"), ("N", 1, "u"), ("L", 1, "e"), ("L", 2, "O"),
    ("N", 1, "8"), ("N", 2, "6"), ("N", 3, "Q"), ("N", 2, "d"), ("N", 2, "O"), ("N", 1, "e"), ("T", "5"),
    ("C", 11), ("L", 2, "Q"), ("N", 1, "6"), ("L", 1, "d"), ("N", 2, "Q"), ("N", 1, "d"), ("L", 1, "Q"),
    ("N", 1, "Q"), ("T", "e"), ("L", 1, "O"), ("T", "8"), ("T", "7"), ("N", 1, "O"), ("T", "u"), ("T", "d"),
    ("T", "6"), ("T", "Q"), ("T", "O"),
)


def whole_tiles(shards, devices):
    return devices % 4 == 0 and all(s.shape[0] % 16 == 0 and s.shape[1] % 256 == 0 for s in shards)


def local(
    clips_wide, clips_narrow, visible_wide, visible_narrow, shift_wide, shift_narrow,
    enc_norm1, enc_qkv, enc_out, enc_norm2, enc_up, enc_down, embed_proj, mask_token,
    dec_norm1, dec_qkv, dec_out, dec_norm2, dec_up, dec_down, cotan_wide, cotan_narrow,
):
    devices = lax.axis_size("fsdp")
    matrices = [enc_qkv, enc_out, enc_up, enc_down, embed_proj, dec_qkv, dec_out, dec_up, dec_down]
    vectors = [enc_norm1, enc_norm2, mask_token, dec_norm1, dec_norm2]
    narrow = jnp.transpose(clips_narrow, (1, 0, 2))
    place = (shift_wide, shift_narrow, visible_wide, visible_narrow, cotan_wide, cotan_narrow)
    counts = (clips_wide.shape[0], clips_wide.shape[1], clips_narrow.shape[1])
    direct = whole_tiles(matrices, devices)
    if direct:
        pieces = [(len(matrices), 0, 128, ZXY, False)]
        pieces += [(w, 0, matrices[w].shape[1] // 2, order, True) for w, order in GATHER]
        whole, placed, (embedded, *saved) = gather_encode(
            matrices, vectors, pieces, place, clips_wide, narrow, devices // 4
        )
    else:
        packed = jnp.stack([jnp.pad(v, (0, 128 - v.shape[0])) for v in vectors])
        packed = jnp.pad(packed, ((0, 16 - len(vectors)), (0, 0)))
        whole = [lax.all_gather(m, "fsdp", axis=0, tiled=True) for m in (*matrices, packed)]
        got = encoder_forward(place, whole[9], clips_wide, narrow, *whole[:5], devices)
        placed, embedded, saved = got[:3], got[3], got[4:]
    enc, dec, tiles = whole[:5], whole[5:9], whole[9]
    decoded_wide, decoded_narrow, grad_embedded, *dec_grads, gains = decoder(
        embedded, tiles, placed, cotan_wide.shape, cotan_narrow.shape, *dec, devices
    )
    if direct:
        routes = [(w, 0, matrices[w].shape[1] // 2, order) for w, order in REDUCE]
        grad_rows, gains, shares = encode_back_reduce(
            tiles, counts, grad_embedded, gains, saved, enc, dec_grads, routes, devices // 4
        )
    else:
        grad_rows, *enc_grads, gains = encoder_backward(
            tiles, counts, grad_embedded, gains, saved, *enc, devices
        )
        gains = lax.psum(gains, ("fsdp", "dp"))
        shares = [
            lax.psum_scatter(lax.psum(g.astype(F), "dp"), "fsdp", scatter_dimension=0, tiled=True)
            for g in enc_grads + dec_grads
        ]
    encoded_wide, encoded_narrow, grad_wide, grad_narrow, m, v = results(
        lax.axis_index("fsdp"), saved[-1], grad_rows, gains, shares, [v.shape[0] for v in vectors],
        clips_wide.shape, clips_narrow.shape,
    )
    return (
        encoded_wide, encoded_narrow, decoded_wide, decoded_narrow, grad_wide, grad_narrow,
        v[0], m[0], m[1], v[1], m[2], m[3], m[4], v[2], v[3], m[5], m[6], v[4], m[7], m[8],
    )


def solution(mesh):
    clips = ("fsdp", "dp")
    matrix, vector = P("fsdp", None), P("fsdp")
    weights = (
        vector, matrix, matrix, vector, matrix, matrix, matrix, vector,
        vector, matrix, matrix, vector, matrix, matrix,
    )
    rows, pairs = P(clips, None, None), P(clips, None)
    return jax.shard_map(
        local,
        mesh=mesh,
        in_specs=(rows, rows, pairs, pairs, pairs, P(clips), *weights, rows, rows),
        out_specs=(rows,) * 6 + weights,
        check_vma=False,
    )
```

```python
import functools

import jax
import jax.numpy as jnp
from jax import lax
from jax.experimental import pallas as pl
from jax.experimental.pallas import tpu as pltpu
from jax.sharding import PartitionSpec as P

MESH = pl.DeviceIdType.MESH


def slots():
    out=[]
    for bx in (0,1):
        for by in (0,1):
            for sgn in (0,1,-1):
                if (bx,by,sgn)!=(0,0,0): out.append((bx,by,sgn))
    return out

def forwards(order,bx,by,sgn):
    differs={'x':bx,'y':by,'z':int(sgn!=0)}
    last=max([j for j,d in enumerate(order) if differs[d]],default=-1)
    dirs=[]
    for j,d in enumerate(order):
        if j>last:
            dirs += ['u','d'] if d=='z' else [d]
    if last>=0 and order[last]=='z':
        dirs.append('u' if sgn<0 else 'd')
    return dirs


TIME = 64
WIN = 4
EPS = 1e-6
F = jnp.float32
B = jnp.bfloat16
VMEM_LIMIT = 60 * 2**20


def dot(a, b):
    return lax.dot_general(a, b, (((1,), (0,)), ((), ())), preferred_element_type=F)


def dot_nt(a, b):
    return lax.dot_general(a, b, (((1,), (1,)), ((), ())), preferred_element_type=F)


def dot_tn(a, b):
    return lax.dot_general(a, b, (((0,), (0,)), ((), ())), preferred_element_type=F)


def iota(shape, dim):
    return lax.broadcasted_iota(jnp.int32, shape, dim)


def norm_stats(x):
    center = jnp.mean(x, axis=-1, keepdims=True)
    shifted = x - center
    spread = jnp.mean(shifted * shifted, axis=-1, keepdims=True)
    scale = lax.rsqrt(spread + EPS)
    return shifted * scale, scale


def norm_back(x, gain, grad):
    unit, scale = norm_stats(x)
    by_gain = grad * unit
    by_unit = grad * gain
    mean_one = jnp.mean(by_unit, axis=-1, keepdims=True)
    mean_two = jnp.mean(by_unit * unit, axis=-1, keepdims=True)
    by_input = scale * (by_unit - mean_one - unit * mean_two)
    return by_input, jnp.sum(by_gain.reshape(-1, 8, x.shape[1]), axis=0)


def gelu_both(u):
    t = 1.0 / (1.0 + (0.3275911 * 0.7071067811865476) * jnp.abs(u))
    bell = jnp.exp(-0.5 * u * u)
    poly = t * (0.127414796 + t * (-0.142248368 + t * (0.7107068705 + t * (-0.7265760135 + t * 0.5307027145))))
    tail = poly * bell
    phi = jnp.where(u < 0, tail, 1.0 - tail)
    return u * phi, phi + u * (bell * 0.3989422804014327)


def spread_vector(tiles, lane, size, devices):
    part = size // devices
    pick = (iota((128, size), 1) % part == iota((128, size), 0)).astype(B)
    wide = dot(tiles, pick)
    rows = iota((tiles.shape[0], size), 0)
    keep = rows == (iota((tiles.shape[0], size), 1) // part) * 16 + lane
    return jnp.sum(jnp.where(keep, wide, 0.0), axis=0, keepdims=True)


def group_sums(x, ones):
    high = x.astype(B)
    return dot(high, ones) + dot((x - high.astype(F)).astype(B), ones)


def lane_groups(x, op):
    lanes = iota(x.shape, 1)
    width = x.shape[1]
    for d in (1, 2, 4, 8):
        other = jnp.where((lanes & d) != 0, pltpu.roll(x, d, 1), pltpu.roll(x, width - d, 1))
        x = op(x, other)
    return x


HEAD = 32
AREA = WIN * WIN


def stack8(block, mask):
    return jnp.concatenate([block] * 8, axis=0) * mask


def dec_kernel(wc, nc, wide_rows, narrow_rows, devices, tiles, sel, perm_h, dz_h, r_h, a_h, qkv_h, p_h, o_h, wq_h, wo_h, wu_h, wd_h,
               outw, outn, dm_ref, gq_h, go_h, gu_h, gd_h, vec_ref,
               wq, wo, wu, wd, r_ref, a_ref, qkv, p_ref, o_ref,
               b_ref, h_ref, du, dx1, do_ref, dqkv, dec, dm_acc, acc, gq, go, gu, gd, perm, dz, sems):
    D = wo.shape[0]
    rows = wc * wide_rows + nc * narrow_rows
    T = 256
    tall = 512 if rows % 512 == 0 else T
    nt = rows // T
    wide_tiles = wc * wide_rows // T
    cps = []
    for k, (src, dst) in enumerate((
            (o_h, o_ref), (r_h, r_ref), (wo_h, wo), (wu_h, wu), (dz_h, dz), (wd_h, wd), (perm_h, perm), (qkv_h, qkv),
            (p_h, p_ref), (wq_h, wq), (a_h, a_ref))):
        cp = pltpu.make_async_copy(src, dst, sems.at[k])
        cp.start()
        cps.append(cp)
    gain1 = spread_vector(tiles[...], 3, D, devices)
    gain2 = spread_vector(tiles[...], 4, D, devices)
    dm_acc[...] = jnp.zeros_like(dm_acc)
    acc[...] = jnp.zeros_like(acc)
    def group_rows(t):
        g = jnp.where(t < wide_tiles, t * T // wide_rows, wc + (t - wide_tiles) // 2)
        return pl.ds(pl.multiple_of(g * 128, 128), 128)

    mask = (iota((128, 256), 0) // AREA == iota((128, 256), 1) // HEAD).astype(B)
    scale = HEAD ** -0.5
    nw = 32
    while rows % (nw * AREA):
        nw //= 2
    ones = (iota((128, 128), 0) // AREA == iota((128, 128), 1) // AREA).astype(B)
    for cp in cps[:3]:
        cp.wait()

    @pl.loop(0, nt)
    def _(t):
        rr = pl.ds(pl.multiple_of(t * T, T), T)
        x1 = r_ref[rr] + dot(o_ref[rr], wo[...])
        dx1[rr] = x1
        b_ref[rr] = (norm_stats(x1)[0] * gain2).astype(B)

    for cp in cps[3:6]:
        cp.wait()

    @pl.loop(0, rows // tall)
    def _(t):
        rr = pl.ds(pl.multiple_of(t * tall, tall), tall)
        x1 = dx1[rr]
        b = b_ref[rr]
        z = dz[rr]
        out = x1
        back = jnp.zeros((tall, D), F)
        C = 512
        for k in range(0, wu.shape[1], C):
            u = dot(b, wu[:, k:k + C])
            h, slope = gelu_both(u)
            h = h.astype(B)
            h_ref[rr, k:k + C] = h
            out = out + dot(h, wd[k:k + C, :])
            d = (slope * dot_nt(z, wd[k:k + C, :])).astype(B)
            du[rr, k:k + C] = d
            back = back + dot_nt(d, wu[:, k:k + C])
        dec[rr] = out.astype(B)
        by_input, by_gain = norm_back(x1, gain2, back)
        acc[1] += by_gain
        dx = z.astype(F) + by_input
        dx1[rr] = dx
        do_ref[rr] = dot_nt(dx.astype(B), wo[...]).astype(B)

    for cp in cps[6:]:
        cp.wait()
    for i in range(wc + nc):
        base, n, out = (i * wide_rows, wide_rows, outw) if i < wc else (
            wc * wide_rows + (i - wc) * narrow_rows, narrow_rows, outn)
        out[i if i < wc else i - wc] = dot_tn(perm[base:base + n, 0:n], dec[base:base + n]).astype(B)

    @pl.loop(0, rows // (nw * AREA))
    def _(g):
        base = pl.multiple_of(g * nw * AREA, nw * AREA)
        rr = pl.ds(base, nw * AREA)
        w16 = [slice(AREA * j, AREA * j + AREA) for j in range(nw)]
        for a in range(D // 256):
            cq = pl.ds(a * 256, 256)
            q, k, v = qkv[rr, cq], qkv[rr, pl.ds(D + a * 256, 256)], qkv[rr, pl.ds(2 * D + a * 256, 256)]
            go_ = do_ref[rr, cq]
            ks = [stack8(k[w], mask) for w in w16]
            qs = [stack8(q[w], mask) for w in w16]
            gs = [stack8(go_[w], mask) for w in w16]
            p = p_ref[rr, pl.ds(a * 128, 128)]
            dp = jnp.concatenate([dot_nt(go_[w], stack8(v[w], mask)) for w in w16], axis=0)
            ds = (p * (dp - group_sums(dp * p, ones))).astype(B)
            dqkv[rr, cq] = (jnp.concatenate([dot(ds[w], m) for w, m in zip(w16, ks)], axis=0) * scale).astype(B)
            s = jnp.concatenate([dot_nt(k[w], m) for w, m in zip(w16, qs)], axis=0) * scale
            s = s.reshape(nw, AREA, 128)
            e = jnp.exp(s - jnp.max(s, axis=1, keepdims=True))
            p = e / jnp.sum(e, axis=1, keepdims=True)
            dp = jnp.concatenate([dot_nt(v[w], m) for w, m in zip(w16, gs)], axis=0).reshape(nw, AREA, 128)
            ds = (p * (dp - jnp.sum(dp * p, axis=1, keepdims=True))).reshape(nw * AREA, 128).astype(B)
            p = p.reshape(nw * AREA, 128).astype(B)
            dqkv[rr, pl.ds(D + a * 256, 256)] = (jnp.concatenate([dot(ds[w], m) for w, m in zip(w16, qs)], axis=0) * scale).astype(B)
            dqkv[rr, pl.ds(2 * D + a * 256, 256)] = jnp.concatenate([dot(p[w], m) for w, m in zip(w16, gs)], axis=0).astype(B)

    @pl.loop(0, nt)
    def _(t):
        rr = pl.ds(pl.multiple_of(t * T, T), T)
        g = group_rows(t)
        by_input, by_gain = norm_back(r_ref[rr], gain1, dot_nt(dqkv[rr], wq[...]))
        acc[0] += by_gain
        dr = dx1[rr] + by_input
        s = sel[rr]
        hidden = 1.0 - jnp.sum(s.astype(F), axis=1, keepdims=True)
        acc[2] += jnp.sum((dr * hidden).reshape(-1, 8, D), axis=0)
        dm_acc[g] += dot_tn(s, dr.astype(B))

    dm_ref[...] = dm_acc[...].astype(B)
    for k in range(3):
        vec_ref[k:k + 1, :] = jnp.sum(acc[k], axis=0, keepdims=True)
    vec_ref[3:, :] = jnp.zeros((5, D), F)
    step = 512
    copies = []

    def leave(k, src, dst):
        cp = pltpu.make_async_copy(src, dst, sems.at[11 + k])
        cp.start()
        copies.append(cp)

    @pl.loop(0, wd.shape[0] // step)
    def _(k):
        kk = pl.ds(pl.multiple_of(k * step, step), step)
        gd[kk, :] = dot_tn(h_ref[:, kk], dz[...]).astype(B)

    leave(0, gd, gd_h)

    @pl.loop(0, wd.shape[0] // step)
    def _(k):
        kk = pl.ds(pl.multiple_of(k * step, step), step)
        gu[:, kk] = dot_tn(b_ref[...], du[:, kk]).astype(B)

    leave(1, gu, gu_h)

    @pl.loop(0, wq.shape[1] // step)
    def _(k):
        kk = pl.ds(pl.multiple_of(k * step, step), step)
        gq[:, kk] = dot_tn(a_ref[...], dqkv[:, kk]).astype(B)

    leave(2, gq, gq_h)
    go[...] = dot_tn(o_ref[...], dx1[...].astype(B)).astype(B)
    leave(3, go, go_h)
    for cp in copies:
        cp.wait()


def decoder(tiles, placed, first, m_shape, wide_shape, narrow_shape, wq, wo, wu, wd, devices):
    wc, wide_rows, D = wide_shape
    nc, narrow_rows, _ = narrow_shape
    FFD = wu.shape[1]
    rows = wc * wide_rows + nc * narrow_rows
    V = pl.BlockSpec(memory_space=pltpu.VMEM)
    A = pl.BlockSpec(memory_space=pl.ANY)
    sds = jax.ShapeDtypeStruct
    weights = [pltpu.VMEM(w.shape, B) for w in (wq, wo, wu, wd)]
    return pl.pallas_call(
        functools.partial(dec_kernel, wc, nc, wide_rows, narrow_rows, devices),
        out_shape=[sds(wide_shape, B), sds(narrow_shape, B), sds(m_shape, B), sds(wq.shape, B), sds(wo.shape, B),
                   sds(wu.shape, B), sds(wd.shape, B), sds((8, D), F)],
        in_specs=[V] * 2 + [A] * 11,
        out_specs=[V] * 3 + [A] * 4 + [V],
        scratch_shapes=weights + [pltpu.VMEM(f.shape, f.dtype) for f in first] + [
            pltpu.VMEM((rows, D), B), pltpu.VMEM((rows, FFD), B), pltpu.VMEM((rows, FFD), B), pltpu.VMEM((rows, D), F),
            pltpu.VMEM((rows, D), B), pltpu.VMEM((rows, 3 * D), B), pltpu.VMEM((rows, D), B),
            pltpu.VMEM(m_shape, F), pltpu.VMEM((3, 8, D), F)] + weights + [
            pltpu.VMEM(placed[0].shape, B), pltpu.VMEM(placed[2].shape, B), pltpu.SemaphoreType.DMA((15,))],
        compiler_params=pltpu.CompilerParams(vmem_limit_bytes=VMEM_LIMIT),
        name="decoder_block",
    )(tiles, placed[1], placed[0], placed[2], *first, wq, wo, wu, wd)


def first_shapes(cotw, cotn):
    rows = cotw.shape[0] * cotw.shape[1] + cotn.shape[0] * cotn.shape[1]
    D = cotw.shape[2]
    sds = jax.ShapeDtypeStruct
    return [sds((rows, D), F), sds((rows, D), B), sds((rows, 3 * D), B), sds((rows, D // 2), F), sds((rows, D), B)]


def decoder_first(wc, nc, wide_rows, narrow_rows, devices, tiles, m_ref, sel, wq, mhi, mlo, r_ref, a_ref, qkv, p_ref, o_ref):
    D = o_ref.shape[1]
    rows = wc * wide_rows + nc * narrow_rows
    T = 256
    nt = rows // T
    wide_tiles = wc * wide_rows // T

    def group_rows(t):
        g = jnp.where(t < wide_tiles, t * T // wide_rows, wc + (t - wide_tiles) // 2)
        return pl.ds(pl.multiple_of(g * 128, 128), 128)

    nw = 32
    while rows % (nw * AREA):
        nw //= 2
    turns = rows // (nw * AREA)

    def enter():
        gain1 = spread_vector(tiles[...], 3, D, devices)
        filler = spread_vector(tiles[...], 2, D, devices)
        mhi[...] = m_ref[...].astype(B)
        mlo[...] = (m_ref[...] - mhi[...].astype(F)).astype(B)

        @pl.loop(0, nt)
        def _(t):
            rr = pl.ds(pl.multiple_of(t * T, T), T)
            g = group_rows(t)
            s = sel[rr]
            seen = jnp.sum(s.astype(F), axis=1, keepdims=True)
            x = dot(s, mhi[g]) + dot(s, mlo[g]) + (1.0 - seen) * filler
            r_ref[rr] = x
            a = (norm_stats(x)[0] * gain1).astype(B)
            a_ref[rr] = a
            qkv[rr] = dot(a, wq[...]).astype(B)

    def attend(half):
        mask = (iota((128, 256), 0) // AREA == iota((128, 256), 1) // HEAD).astype(B)
        scale = HEAD ** -0.5
        ones = (iota((128, 128), 0) // AREA == iota((128, 128), 1) // AREA).astype(B)

        @pl.loop(turns * half // 2, turns * (half + 1) // 2)
        def _(g):
            base = pl.multiple_of(g * nw * AREA, nw * AREA)
            rr = pl.ds(base, nw * AREA)
            for a in range(D // 256):
                cq = pl.ds(a * 256, 256)
                q, k, v = qkv[rr, cq], qkv[rr, pl.ds(D + a * 256, 256)], qkv[rr, pl.ds(2 * D + a * 256, 256)]
                w16 = [slice(AREA * j, AREA * j + AREA) for j in range(nw)]
                s = jnp.concatenate([dot_nt(q[w], stack8(k[w], mask)) for w in w16], axis=0) * scale
                e = jnp.exp(s - lane_groups(s, jnp.maximum))
                p = e / group_sums(e, ones)
                p_ref[rr, pl.ds(a * 128, 128)] = p
                low = p.astype(B)
                o_ref[rr, cq] = jnp.concatenate([dot(low[w], stack8(v[w], mask)) for w in w16], axis=0).astype(B)

    return enter, functools.partial(attend, 0), functools.partial(attend, 1)


def placement(wc, nc, shw, shn, visw, visn, cotw, cotn, perm, sel, dz):
    T = 256
    wide_rows, narrow_rows = cotw.shape[1], cotn.shape[1]
    clips = [(i * wide_rows, wide_rows, 8, shw[i, 0], shw[i, 1], cotw, i, visw, 0) for i in range(wc)]
    clips += [(wc * wide_rows + i * narrow_rows, narrow_rows, 4, shn[i], 0, cotn, i, visn, 64 * (i % 2)) for i in range(nc)]
    for base, n, cols, s, r, cot, i, vis, o in clips:
        seen = vis.shape[1]
        parts = [jnp.full((1, o), -1, jnp.int32)] if o else []
        parts += [vis[i:i + 1, :], jnp.full((1, 128 - o - seen), -1, jnp.int32)]
        shown = jnp.concatenate(parts, axis=1)
        for k in range(0, n, T):
            j = iota((T, 1), 0) + k
            w, q = j >> 4, j & 15
            wf = cols // WIN
            t = ((w // wf) * WIN + (q >> 2) + s) & (TIME - 1)
            f = ((w % wf) * WIN + (q & 3) + r) & (cols - 1)
            patch = t * cols + f
            where = pl.ds(base + k, T)
            hot = jnp.where(iota((T, n), 1) == patch, 1.0, 0.0).astype(B)
            perm[where, 0:n] = hot
            if n < perm.shape[1]:
                perm[where, n:] = jnp.zeros((T, perm.shape[1] - n), B)
            sel[where] = jnp.where(shown == patch, 1.0, 0.0).astype(B)
            dz[where] = dot(hot, cot[i]).astype(B)


def placed_shapes(cotw, cotn):
    rows = cotw.shape[0] * cotw.shape[1] + cotn.shape[0] * cotn.shape[1]
    return [jax.ShapeDtypeStruct((rows, n), B) for n in (cotw.shape[1], 128, cotw.shape[2])]


ENC_HEAD = 64


def valid_keys(kind, wide_seen, narrow_seen):
    q, k = iota((128, 128), 0), iota((128, 128), 1)
    if kind == 0:
        return k < wide_seen
    return ((q // 64) == (k // 64)) & (k % 64 < narrow_seen)


def pair_mask():
    return (iota((256, 128), 0) // 128 == iota((256, 128), 1) // ENC_HEAD).astype(B)


def pair_shares(q, k2, valid):
    s2 = dot_nt(q, k2) * (ENC_HEAD ** -0.5)
    shares = []
    for h in range(2):
        s = jnp.where(valid, s2[:, 128 * h:128 * h + 128], -1e30)
        e = jnp.exp(s - jnp.max(s, axis=1, keepdims=True))
        shares.append(e / jnp.sum(e, axis=1, keepdims=True))
    return shares


def load_rows(dst, pair, wide, narrow, wc, nc):
    dst[...] = jnp.zeros_like(dst)
    for i in range(wc):
        dst[128 * i:128 * i + wide.shape[1], :] = wide[i].astype(F)
    pair[...] = narrow[...].astype(F)
    for i in range(nc):
        o = 128 * wc + 64 * i
        dst[o:o + narrow.shape[0], :] = pair[:, i, :]


def enc_forward_kernel(wc, nc, devices, shw, shn, visw, visn, cotw, cotn, tiles, cw, cn, wq_h, wo_h, wu_h, wd_h, we_h, wqd_h,
                       perm, sel, dz, r_d, a_d, qkv_d, p_d, o_d, m_ref, x_ref, a_ref, qkv, o_ref, x1_ref, b_ref, h_ref, slope_ref, e_ref,
                       wq, wo, wu, wd, we, pair, wqd, mhi, mlo, sems):
    D = wo.shape[0]
    cps = []
    for k, (src, dst) in enumerate((
            (wq_h, wq), (wo_h, wo), (wu_h, wu), (wd_h, wd), (we_h, we), (wqd_h, wqd))):
        cp = pltpu.make_async_copy(src, dst, sems.at[k])
        cp.start()
        cps.append(cp)
    placement(wc, nc, shw, shn, visw, visn, cotw, cotn, perm, sel, dz)
    load_rows(x_ref, pair, cw, cn, wc, nc)
    gain1 = spread_vector(tiles[...], 0, D, devices)
    gain2 = spread_vector(tiles[...], 1, D, devices)
    x = x_ref[...]
    a = (norm_stats(x)[0] * gain1).astype(B)
    a_ref[...] = a
    cps[0].wait()
    for k in range(0, 3 * D, D):
        qkv[:, k:k + D] = dot(a, wq[:, k:k + D]).astype(B)
    mask = pair_mask()
    groups = x_ref.shape[0] // 128
    for g in range(groups):
        rr = slice(128 * g, 128 * g + 128)
        valid = valid_keys(0 if g < wc else 1, cw.shape[1], cn.shape[0])
        for j in range(D // 128):
            q, k, v = (qkv[rr, o + 128 * j:o + 128 * j + 128] for o in (0, D, 2 * D))
            k2 = jnp.concatenate([k, k], axis=0) * mask
            v2 = jnp.concatenate([v, v], axis=0) * mask
            p2 = jnp.concatenate(pair_shares(q, k2, valid), axis=1).astype(B)
            o_ref[rr, 128 * j:128 * j + 128] = dot(p2, v2).astype(B)
    cps[1].wait()
    x1 = x_ref[...] + dot(o_ref[...], wo[...])
    x1_ref[...] = x1
    b = (norm_stats(x1)[0] * gain2).astype(B)
    b_ref[...] = b
    cps[2].wait()
    cps[3].wait()
    out = x1
    C = 512
    for k in range(0, wu.shape[1], C):
        h, slope = gelu_both(dot(b, wu[:, k:k + C]))
        h = h.astype(B)
        h_ref[:, k:k + C] = h
        slope_ref[:, k:k + C] = slope
        out = out + dot(h, wd[k:k + C, :])
    e_ref[...] = out.astype(B)
    cps[4].wait()
    m_ref[...] = dot(e_ref[...], we[...])
    cps[5].wait()
    for step in decoder_first(
            wc, nc, cotw.shape[1], cotn.shape[1], devices, tiles, m_ref, sel, wqd, mhi, mlo, r_d, a_d, qkv_d, p_d, o_d):
        step()


def encoder_forward(place, tiles, cw, cn, wq, wo, wu, wd, we, wqd, devices):
    wc, nc = cw.shape[0], cn.shape[1]
    D = cw.shape[2]
    FFD = wu.shape[1]
    R = 128 * wc + 128 * ((nc + 1) // 2)
    V = pl.BlockSpec(memory_space=pltpu.VMEM)
    S = pl.BlockSpec(memory_space=pltpu.SMEM)
    A = pl.BlockSpec(memory_space=pl.ANY)
    sds = jax.ShapeDtypeStruct
    return pl.pallas_call(
        functools.partial(enc_forward_kernel, wc, nc, devices),
        out_shape=placed_shapes(*place[4:]) + first_shapes(*place[4:]) + [sds((R, we.shape[1]), F), sds((R, D), F), sds((R, D), B), sds((R, 3 * D), B),
                   sds((R, D), B), sds((R, D), F), sds((R, D), B), sds((R, FFD), B), sds((R, FFD), F), sds((R, D), B)],
        in_specs=[S, S] + [V] * 7 + [A] * 6,
        out_specs=[V] * 18,
        scratch_shapes=[pltpu.VMEM(w.shape, B) for w in (wq, wo, wu, wd, we)]
        + [pltpu.VMEM(cn.shape, F), pltpu.VMEM(wqd.shape, B), pltpu.VMEM((R, we.shape[1]), B),
           pltpu.VMEM((R, we.shape[1]), B), pltpu.SemaphoreType.DMA((6,))],
        compiler_params=pltpu.CompilerParams(vmem_limit_bytes=VMEM_LIMIT),
        name="encoder_forward",
    )(*place, tiles, cw, cn, wq, wo, wu, wd, we, wqd)


def enc_backward_kernel(wc, wide_seen, narrow_seen, devices, tiles, dm, dec_vec, x_in, a_ref, qkv, o_ref, x1_ref, b_ref, h_ref, slope_ref, e_ref,
                        wq_h, wo_h, wu_h, wd_h, we_h,
                        dx_ref, gq, go, gu, gd, ge, vec_ref,
                        wq, wo, wu, wd, we, do_ref, dqkv, du, sems):
    D = wo.shape[0]
    cps = []
    for k, (src, dst) in enumerate(((we_h, we), (wd_h, wd), (wu_h, wu), (wo_h, wo), (wq_h, wq))):
        cp = pltpu.make_async_copy(src, dst, sems.at[k])
        cp.start()
        cps.append(cp)
    gain1 = spread_vector(tiles[...], 0, D, devices)
    gain2 = spread_vector(tiles[...], 1, D, devices)
    cps[0].wait()
    grad = dot_nt(dm[...], we[...])
    z = grad.astype(B)
    ge[...] = dot_tn(e_ref[...], dm[...]).astype(B)
    cps[1].wait()
    cps[2].wait()
    back = jnp.zeros_like(grad)
    C = 512
    for k in range(0, wu.shape[1], C):
        d = (slope_ref[:, k:k + C] * dot_nt(z, wd[k:k + C, :])).astype(B)
        du[:, k:k + C] = d
        back = back + dot_nt(d, wu[:, k:k + C])
        gd[k:k + C, :] = dot_tn(h_ref[:, k:k + C], z).astype(B)
        gu[:, k:k + C] = dot_tn(b_ref[...], d).astype(B)
    by_input, by_gain = norm_back(x1_ref[...], gain2, back)
    vec_ref[...] = jnp.zeros_like(vec_ref)
    vec_ref[1:2, :] = jnp.sum(by_gain, axis=0, keepdims=True)
    dx1 = grad + by_input
    y = dx1.astype(B)
    cps[3].wait()
    do_ref[...] = dot_nt(y, wo[...]).astype(B)
    go[...] = dot_tn(o_ref[...], y).astype(B)
    mask = pair_mask()
    groups = x_in.shape[0] // 128
    scale = ENC_HEAD ** -0.5
    lane = iota((128, 128), 1)
    for g in range(groups):
        rr = slice(128 * g, 128 * g + 128)
        valid = valid_keys(0 if g < wc else 1, wide_seen, narrow_seen)
        for j in range(D // 128):
            q, k, v = (qkv[rr, o + 128 * j:o + 128 * j + 128] for o in (0, D, 2 * D))
            g_o = do_ref[rr, 128 * j:128 * j + 128]
            k2 = jnp.concatenate([k, k], axis=0) * mask
            v2 = jnp.concatenate([v, v], axis=0) * mask
            shares = pair_shares(q, k2, valid)
            dp2 = dot_nt(g_o, v2)
            ds, low = [], []
            for h in range(2):
                dp = dp2[:, 128 * h:128 * h + 128]
                p = shares[h]
                ds.append((p * (dp - jnp.sum(dp * p, axis=1, keepdims=True))).astype(B))
                low.append(p.astype(B))
            dq = dot(jnp.concatenate(ds, axis=1), k2) * scale
            dk = jnp.where(lane < ENC_HEAD, dot_tn(ds[0], q), dot_tn(ds[1], q)) * scale
            dv = jnp.where(lane < ENC_HEAD, dot_tn(low[0], g_o), dot_tn(low[1], g_o))
            for o, d in ((0, dq), (D, dk), (2 * D, dv)):
                dqkv[rr, o + 128 * j:o + 128 * j + 128] = d.astype(B)
    cps[4].wait()
    for k in range(0, 3 * D, D):
        gq[:, k:k + D] = dot_tn(a_ref[...], dqkv[:, k:k + D]).astype(B)
    by_input, by_gain = norm_back(x_in[...], gain1, dot_nt(dqkv[...], wq[...]))
    vec_ref[0:1, :] = jnp.sum(by_gain, axis=0, keepdims=True)
    DD = dec_vec.shape[1]
    vec_ref[2:3, 0:DD] = dec_vec[2:3, :]
    vec_ref[3:5, 0:DD] = dec_vec[0:2, :]
    dx_ref[...] = dx1 + by_input


def encoder_backward(tiles, counts, dm, dec_vec, saved, wq, wo, wu, wd, we, devices):
    D = wq.shape[0]
    FFD = wu.shape[1]
    R = dm.shape[0]
    V = pl.BlockSpec(memory_space=pltpu.VMEM)
    A = pl.BlockSpec(memory_space=pl.ANY)
    sds = jax.ShapeDtypeStruct
    return pl.pallas_call(
        functools.partial(enc_backward_kernel, *counts, devices),
        out_shape=[sds((R, D), F)] + [sds(w.shape, B) for w in (wq, wo, wu, wd, we)] + [sds((8, D), F)],
        in_specs=[V] * 12 + [A] * 5,
        out_specs=[V] * 7,
        scratch_shapes=[pltpu.VMEM(w.shape, B) for w in (wq, wo, wu, wd, we)]
        + [pltpu.VMEM((R, D), B), pltpu.VMEM((R, 3 * D), B), pltpu.VMEM((R, FFD), B), pltpu.SemaphoreType.DMA((5,))],
        compiler_params=pltpu.CompilerParams(vmem_limit_bytes=VMEM_LIMIT),
        name="encoder_backward",
    )(tiles, dm, dec_vec, *saved, wq, wo, wu, wd, we)


def results_kernel(wc, nc, sizes, *refs):
    me, e, dx, vec, *refs = refs
    shares, refs = refs[:9], refs[9:]
    encw, encn, gradw, gradn, *refs = refs
    outs, refs = refs[:9], refs[9:]
    vectors, (pair,) = refs[:len(sizes)], refs[len(sizes):]
    for src, wide, narrow in ((e, encw, encn), (dx, gradw, gradn)):
        for i in range(wc):
            rows = src[128 * i:128 * i + encw.shape[1], :]
            if wide is encw:
                wide[i] = rows
            else:
                wide[:, i, :] = rows
        for i in range(nc):
            o = 128 * wc + 64 * i
            pair[:, i, :] = src[o:o + narrow.shape[0], :].astype(F)
        narrow[...] = pair[...].astype(narrow.dtype)
    for src, dst in zip(shares, outs):
        dst[...] = src[...]
    width = vec.shape[1]
    for k, (n, ref) in enumerate(zip(sizes, vectors)):
        ref[...] = pltpu.roll(vec[k:k + 1, :], lax.rem(width - me[0] * n, width), 1)[:, 0:n]


def results(me, e, dx, vec, shares, sizes, wide_shape, narrow_shape):
    wc, nw, D = wide_shape
    nc, nn, _ = narrow_shape
    V = pl.BlockSpec(memory_space=pltpu.VMEM)
    S = pl.BlockSpec(memory_space=pltpu.SMEM)
    sds = jax.ShapeDtypeStruct
    out = pl.pallas_call(
        functools.partial(results_kernel, wc, nc, sizes),
        out_shape=[sds(wide_shape, B), sds((nn, nc, D), B), sds((nw, wc, D), F), sds((nn, nc, D), F)]
        + [sds(s.shape, F) for s in shares] + [sds((1, n), F) for n in sizes],
        in_specs=[S] + [V] * 12,
        out_specs=[V] * (13 + len(sizes)),
        scratch_shapes=[pltpu.VMEM((nn, nc, D), F)],
        compiler_params=pltpu.CompilerParams(vmem_limit_bytes=VMEM_LIMIT),
        name="results",
    )(me.reshape(1), e, dx, vec, *shares)
    swap = functools.partial(jnp.transpose, axes=(1, 0, 2))
    return out[0], swap(out[1]), swap(out[2]), swap(out[3]), out[4:13], [v.reshape(-1) for v in out[13:]]


def gather_ops(nz, pieces, ins, outs, send, recv, sib_send, sib_recv):
    f, c = lax.axis_index("fsdp"), lax.axis_index("dp")
    z, y, x = f // 4, (f // 2) % 2, f % 2
    xn, yn, up, dn, sib = (f + 1 - 2 * x, c), (f + 2 - 4 * y, c), (f + 4, c), (f - 4, c), (f, 1 - c)
    bar = pltpu.get_barrier_semaphore()

    def greet(dev):
        pl.semaphore_signal(bar, inc=1, device_id=dev, device_id_type=MESH)

    greet(xn)
    greet(yn)
    greet(sib)
    pl.when(z < nz - 1)(lambda: greet(up))
    pl.when(z > 0)(lambda: greet(dn))
    pl.semaphore_wait(bar, 3 + (z < nz - 1).astype(jnp.int32) + (z > 0).astype(jnp.int32))
    dest = {"x": xn, "y": yn, "u": up, "d": dn}
    there = {"x": None, "y": None, "u": z < nz - 1, "d": z > 0}
    code = {"x": 0, "y": 0, "u": 1, "d": 2}

    def columns(i, half):
        w, c0, cols, order, share = pieces[i]
        return pl.ds(pl.multiple_of(half * (ins[w].shape[1] // 2) + c0, 128) if share else c0, cols)

    def region(i, s, half):
        w = pieces[i][0]
        r = ins[w].shape[0]
        return outs[w].at[pl.ds(pl.multiple_of(s * r, r), r), columns(i, half)]

    def own(i):
        return ins[pieces[i][0]].at[:, columns(i, c)]

    def remote(i, s, src, d):
        return pltpu.make_async_remote_copy(
            src_ref=src, dst_ref=region(i, s, c), send_sem=send.at[i, code[d]], recv_sem=recv.at[i, s],
            device_id=dest[d], device_id_type=MESH)

    def sibling(i, s, half):
        return pltpu.make_async_remote_copy(
            src_ref=region(i, s, half), dst_ref=region(i, s, half), send_sem=sib_send.at[i],
            recv_sem=sib_recv.at[i], device_id=sib, device_id_type=MESH)

    def some(i, half, count):
        w = pieces[i][0]
        part = outs[w].at[pl.ds(0, count * ins[w].shape[0]), columns(i, half)]
        return lambda a, b: pltpu.make_async_remote_copy(
            src_ref=part, dst_ref=part, send_sem=a, recv_sem=b, device_id=sib, device_id_type=MESH)

    def along(dirs, act):
        for d in dirs:
            if there[d] is None:
                act(d)
            else:
                pl.when(there[d])(lambda d=d: act(d))

    def each(h, i, act):
        for bx, by, sgn in slots():
            k = h - bx - by
            if isinstance(h, int) and not ((k == 0) if sgn == 0 else (1 <= k < nz)):
                continue
            zs = z + sgn * k
            valid = (k == 0) if sgn == 0 else (k >= 1) & (zs >= 0) & (zs < nz)
            s = zs * 4 + (y + by - 2 * by * y) * 2 + (x + bx - 2 * bx * x)
            dirs = forwards(pieces[i][3], bx, by, sgn)
            if isinstance(valid, bool):
                act(i, s, dirs)
            else:
                pl.when(valid)(lambda s=s, dirs=dirs: act(i, s, dirs))

    def start(i):
        along(forwards(pieces[i][3], 0, 0, 0), lambda d: remote(i, f, own(i), d).start())

    def step(i, s, dirs):
        remote(i, s, region(i, s, c), "x").wait_recv()
        along(dirs, lambda d: remote(i, s, region(i, s, c), d).start())
        if pieces[i][4]:
            sibling(i, s, c).start()

    def arrived(i):
        if pieces[i][4]:
            some(i, 1 - c, 4 * nz - 1)(sib_send.at[i], sib_recv.at[i]).wait_recv()

    def finish(i):
        order = pieces[i][3]
        before = {d: order[:order.index(d)] for d in "xyz"}
        size = {"x": 2, "y": 2, "z": nz}

        def blocks(d):
            n = 1
            for e in before[d]:
                n *= size[e]
            return n

        some(i, c, blocks("x") + blocks("y"))(send.at[i, 0], recv.at[i, 0]).wait_send()
        for p in range(nz):
            if p < nz - 1:
                pl.when(z == p)(lambda p=p: some(i, c, blocks("z") * (p + 1))(send.at[i, 1], recv.at[i, 0]).wait_send())
            if p > 0:
                pl.when(z == p)(lambda p=p: some(i, c, blocks("z") * (nz - p))(send.at[i, 2], recv.at[i, 0]).wait_send())
        if pieces[i][4]:
            some(i, c, 4 * nz - 1)(sib_send.at[i], sib_recv.at[i]).wait_send()

    def level(h, indices):
        for i in indices:
            each(h, i, step)

    return start, level, arrived, finish


def gather_encode_kernel(wc, nc, nz, pieces, nw, shw, shn, visw, visn, cotw, cotn, cw, cn, *refs):
    devices = 4 * nz
    vectors, refs = refs[:5], refs[5:]
    ins, refs = list(refs[:nw - 1]), refs[nw - 1:]
    outs, refs = refs[:nw], refs[nw:]
    results_, refs = refs[:18], refs[18:]
    buffers, refs = refs[:18], refs[18:]
    perm, sel, dz, m_ref, x_ref, a_ref, qkv, o_ref, x1_ref, b_ref, h_ref, slope_ref, e_ref, *first = buffers
    wq, wo, wu, wd, we, wqd, mhi, mlo, tiles, sum_ref, pair, tile, send, recv, sib_send, sib_recv, loc, sems, out_sems = refs
    row = iota((16, 128), 0)
    shares = jnp.zeros((16, 128), F)
    for k, v in enumerate(vectors):
        n = v.shape[-1]
        wide = jnp.concatenate([v[...].astype(F).reshape(1, n), jnp.zeros((1, 128 - n), F)], axis=1)
        shares = jnp.where(row == k, wide, shares)
    tile[...] = shares.astype(B)
    ins.append(tile)

    def leave(*which):
        for k in which:
            pltpu.make_async_copy(buffers[k], results_[k], out_sems.at[k]).start()

    D = wo.shape[0]
    start, level, arrived, finish = gather_ops(nz, pieces, ins, outs, send, recv, sib_send, sib_recv)
    sets = {"q": [nw - 1, 0], "u": [2], "d": [3], "o": [1], "e": [4], "5": [5], "6": [6], "7": [7], "8": [8]}
    members = {s: [i for w in ws for i, p in enumerate(pieces) if p[0] == w] for s, ws in sets.items()}
    into = [wq, wo, wu, wd, we, wqd, None, None, None, tiles]
    loads = {}
    gains = []
    locals_ = []
    C = 512
    chunks = wu.shape[1] // C

    def prepare():
        for w in range(nw):
            r = ins[w].shape[0]
            cp = pltpu.make_async_copy(
                ins[w], outs[w].at[pl.ds(pl.multiple_of(lax.axis_index("fsdp") * r, r), r)], loc.at[w])
            cp.start()
            locals_.append(cp)
        placement(wc, nc, shw, shn, visw, visn, cotw, cotn, perm, sel, dz)
        load_rows(x_ref, pair, cw, cn, wc, nc)
        leave(0, 1, 2, 4)

    def ready(s):
        for w, i in zip(sets[s], members[s]):
            arrived(i)
            locals_[w].wait()
            loads[w] = pltpu.make_async_copy(outs[w], into[w], sems.at[w])
            loads[w].start()

    def project():
        loads[nw - 1].wait()
        gains.append(spread_vector(tiles[...], 0, D, devices))
        gains.append(spread_vector(tiles[...], 1, D, devices))
        a = (norm_stats(x_ref[...])[0] * gains[0]).astype(B)
        a_ref[...] = a
        loads[0].wait()
        for k in range(0, 3 * D, D):
            qkv[:, k:k + D] = dot(a, wq[:, k:k + D]).astype(B)
        leave(5, 6)

    def attend(part):
        mask = pair_mask()
        groups = x_ref.shape[0] // 128
        for g in range(groups):
            if g * 2 // groups != part:
                continue
            rr = slice(128 * g, 128 * g + 128)
            valid = valid_keys(0 if g < wc else 1, cw.shape[1], cn.shape[0])
            for j in range(D // 128):
                q, k, v = (qkv[rr, o + 128 * j:o + 128 * j + 128] for o in (0, D, 2 * D))
                k2 = jnp.concatenate([k, k], axis=0) * mask
                v2 = jnp.concatenate([v, v], axis=0) * mask
                p2 = jnp.concatenate(pair_shares(q, k2, valid), axis=1).astype(B)
                o_ref[rr, 128 * j:128 * j + 128] = dot(p2, v2).astype(B)

    def middle():
        loads[1].wait()
        x1 = x_ref[...] + dot(o_ref[...], wo[...])
        x1_ref[...] = x1
        sum_ref[...] = x1
        b_ref[...] = (norm_stats(x1)[0] * gains[1]).astype(B)
        leave(7, 8, 9)

    def feed_forward(j):
        if j == 0:
            loads[2].wait()
            loads[3].wait()
        k = j * C
        h, slope = gelu_both(dot(b_ref[...], wu[:, k:k + C]))
        h = h.astype(B)
        h_ref[:, k:k + C] = h
        slope_ref[:, k:k + C] = slope
        sum_ref[...] += dot(h, wd[k:k + C, :])
        for n in (10, 11):
            pltpu.make_async_copy(buffers[n].at[:, k:k + C], results_[n].at[:, k:k + C], out_sems.at[n]).start()

    def embed():
        e_ref[...] = sum_ref[...].astype(B)
        leave(12)
        loads[4].wait()
        m_ref[...] = dot(e_ref[...], we[...])
        leave(3)

    enter, attend_one, attend_two = decoder_first(
        wc, nc, cotw.shape[1], cotn.shape[1], devices, tiles, m_ref, sel, wqd, mhi, mlo, *first)

    def decode():
        loads[5].wait()
        enter()
        leave(13, 14, 15)

    def decode_end():
        attend_two()
        leave(16, 17)

    compute = [project, functools.partial(attend, 0), functools.partial(attend, 1), middle]
    compute += [functools.partial(feed_forward, j) for j in range(chunks)] + [embed]
    compute += [decode, attend_one, decode_end]
    for token in gather_schedule(nz + 1, len(compute)):
        if token[0] == "S":
            for i in members[token[1]]:
                start(i)
        elif token[0] == "V":
            level(token[1], members[token[2]])
        elif token[0] == "R":
            ready(token[1])
        elif token[0] == "P":
            prepare()
        else:
            compute[token[1]]()
    for w in (6, 7, 8):
        locals_[w].wait()
    for s in "678":
        for i in members[s]:
            arrived(i)
    for i in range(len(pieces)):
        finish(i)
    for n in range(18):
        pltpu.make_async_copy(buffers[n], results_[n], out_sems.at[n]).wait()


def gather_schedule(top, steps):
    if (top, steps) == (5, 14):
        return list(GATHER_SCHEDULE)
    tokens = [("S", s) for s in "qudoe"] + [("P",)] + [("S", s) for s in "5678"]
    tokens += [("V", h, s) for h in range(1, top + 1) for s in "qudoe5678"]
    return tokens + [("R", s) for s in "qoude5"] + [("C", k) for k in range(steps)]


def gather_encode(shards, vectors, pieces, place, cw, cn, nz, cid=1):
    nw, npc, n = len(shards) + 1, len(pieces), 4 * nz
    wc, nc, D = cw.shape[0], cn.shape[1], cw.shape[2]
    R = 128 * wc + 128 * ((nc + 1) // 2)
    V = pl.BlockSpec(memory_space=pltpu.VMEM)
    S = pl.BlockSpec(memory_space=pltpu.SMEM)
    A = pl.BlockSpec(memory_space=pl.ANY)
    sds = jax.ShapeDtypeStruct
    whole = [sds((s.shape[0] * n, s.shape[1]), s.dtype) for s in shards] + [sds((16 * n, 128), B)]
    FFD, DD = shards[2].shape[1], shards[4].shape[1]
    dma = pltpu.SemaphoreType.DMA
    kept = placed_shapes(*place[4:]) + [
        sds((R, DD), F), sds((R, D), F), sds((R, D), B), sds((R, 3 * D), B), sds((R, D), B), sds((R, D), F),
        sds((R, D), B), sds((R, FFD), B), sds((R, FFD), F), sds((R, D), B)] + first_shapes(*place[4:])
    out = pl.pallas_call(
        functools.partial(gather_encode_kernel, wc, nc, nz, pieces, nw),
        out_shape=whole + kept,
        in_specs=[S, S] + [V] * 11 + [A] * (nw - 1),
        out_specs=[A] * (nw + 18),
        scratch_shapes=[pltpu.VMEM(s.shape, s.dtype) for s in kept] + [pltpu.VMEM(w.shape, B) for w in whole[:6]] + [
            pltpu.VMEM((R, DD), B), pltpu.VMEM((R, DD), B), pltpu.VMEM(whole[-1].shape, B), pltpu.VMEM((R, D), F), pltpu.VMEM(cn.shape, F), pltpu.VMEM((16, 128), B),
            dma((npc, 3)), dma((npc, n)), dma((npc,)), dma((npc,)), dma((nw,)), dma((nw,)), dma((18,))],
        compiler_params=pltpu.CompilerParams(collective_id=cid, has_side_effects=True, vmem_limit_bytes=VMEM_LIMIT),
        name="gather_and_encode",
    )(*place, cw, cn, *vectors, *shards)
    return out[:nw], out[nw:nw + 3], out[nw + 4:nw + 13], out[nw + 13:]


def slot_count(order, d, nz):
    size = {"x": 2, "y": 2, "z": nz}
    k = 1
    for e in order[:order.index("z" if d in "ud" else d)]:
        k *= size[e]
    return k * (nz + 1) if d in "ud" else k


def slot_index(order, d, nz, pos):
    size = {"x": 2, "y": 2, "z": nz}
    k = 0
    for e in order[:order.index("z" if d in "ud" else d)]:
        k = k * size[e] + pos[e]
    return k * (nz + 1) + pos["z"] + (1 if d == "d" else 0) if d in "ud" else k


def parent(order, bx, by, sgn):
    differs = {"x": bx, "y": by, "z": int(sgn != 0)}
    last = max(j for j, d in enumerate(order) if differs[d])
    if order[last] == "z":
        return "d" if sgn < 0 else "u"
    return order[last]


def reduce_ops(nz, pieces, rows, mine, other, sibb, rbuf, res, outs, sib_send, sib_recv, send, recv, res_sem, res_send, res_recv):
    f, c = lax.axis_index("fsdp"), lax.axis_index("dp")
    z, y, x = f // 4, (f // 2) % 2, f % 2
    bits = (nz * 4).bit_length() - 1

    def flip(b):
        return f + (1 << b) * (1 - 2 * ((f // (1 << b)) % 2))

    xn, yn, up, dn, sib = (flip(0), c), (flip(1), c), (f + 4, c), (f - 4, c), (f, 1 - c)
    bar = pltpu.get_barrier_semaphore()

    def greet(dev):
        pl.semaphore_signal(bar, inc=1, device_id=dev, device_id_type=MESH)

    greet(xn)
    greet(yn)
    greet(sib)
    pl.when(z < nz - 1)(lambda: greet(up))
    pl.when(z > 0)(lambda: greet(dn))
    far = range(3, bits)
    for b in far:
        greet((flip(b), c))
    pl.semaphore_wait(bar, 3 + len(far) + (z < nz - 1).astype(jnp.int32) + (z > 0).astype(jnp.int32))
    dest = {"x": xn, "y": yn, "u": up, "d": dn}
    there = {"u": z < nz - 1, "d": z > 0}
    opposite = {"u": "d", "d": "u", "x": "x", "y": "y"}
    kind = {"x": 0, "y": 1, "u": 2, "d": 2}

    def give(w):
        return pltpu.make_async_remote_copy(
            src_ref=other[w], dst_ref=sibb[w], send_sem=sib_send.at[w], recv_sem=sib_recv.at[w],
            device_id=sib, device_id_type=MESH)

    def cols(i):
        return pl.ds(pieces[i][1], pieces[i][2])

    def message(i, s, pos, d):
        w, order, b = pieces[i][0], pieces[i][3], kind[d]
        r = rows[w]
        q = slot_index(order, opposite[d], nz, pos)
        return pltpu.make_async_remote_copy(
            src_ref=mine[w].at[pl.ds(pl.multiple_of(s * r, r), r), cols(i)], dst_ref=rbuf[i][b].at[q],
            send_sem=send.at[i], recv_sem=recv.at[i, b, q], device_id=dest[d], device_id_type=MESH)

    def arrival(i, pos, d):
        b = kind[d]
        q = slot_index(pieces[i][3], d, nz, pos)
        return pltpu.make_async_remote_copy(
            src_ref=rbuf[i][b].at[q], dst_ref=rbuf[i][b].at[q], send_sem=send.at[i],
            recv_sem=recv.at[i, b, q], device_id=sib, device_id_type=MESH)

    def add(i, s, pos, children, final):
        w, order = pieces[i][0], pieces[i][3]
        r = rows[w]
        ks = [(kind[d], slot_index(order, d, nz, pos)) for d in children]

        tall = 16
        while r % (2 * tall) == 0 and 2 * tall * pieces[i][2] <= 24 * 16 * 128:
            tall *= 2
        if r % 48 == 0 and 48 * pieces[i][2] <= 27 * 16 * 128:
            tall = max(tall, 48)

        @pl.loop(0, r // tall)
        def _(k):
            rr = pl.ds(pl.multiple_of(k * tall, 16), tall)
            gr = pl.ds(pl.multiple_of(s * r + k * tall, 16), tall)
            t = mine[w][gr, cols(i)].astype(F) + sibb[w][gr, cols(i)].astype(F)
            for b, q in ks:
                t = t + rbuf[i][b][q, rr].astype(F)
            if final:
                res[w][rr, cols(i)] = t
            else:
                mine[w][gr, cols(i)] = t.astype(B)

    def gather_children(i, s, pos, children, final):
        sure = [d for d in children if d in "xy"]
        maybe = [d for d in children if d in "ud"]
        for d in sure:
            arrival(i, pos, d).wait_recv()
        for d in maybe:
            pl.when(there[d])(lambda d=d: arrival(i, pos, d).wait_recv())
        if not maybe:
            add(i, s, pos, sure, final)
        elif len(maybe) == 1:
            pl.when(there[maybe[0]])(lambda: add(i, s, pos, sure + maybe, final))
            pl.when(jnp.logical_not(there[maybe[0]]))(lambda: add(i, s, pos, sure, final))
        else:
            u, d = there["u"], there["d"]
            pl.when(u & d)(lambda: add(i, s, pos, sure + ["u", "d"], final))
            pl.when(u & jnp.logical_not(d))(lambda: add(i, s, pos, sure + ["u"], final))
            pl.when(jnp.logical_not(u) & d)(lambda: add(i, s, pos, sure + ["d"], final))
            if nz == 1:
                add(i, s, pos, sure, final)

    def each(h, i, leaf, act):
        order = pieces[i][3]
        for bx, by, sgn in slots():
            children = forwards(order, bx, by, sgn)
            if leaf is not None and (len(children) == 0) != leaf:
                continue
            k = h - bx - by
            if isinstance(h, int) and not ((k == 0) if sgn == 0 else (1 <= k < nz)):
                continue
            zs = z + sgn * k
            valid = (k == 0) if sgn == 0 else (k >= 1) & (zs >= 0) & (zs < nz)
            pos = {"x": x + bx - 2 * bx * x, "y": y + by - 2 * by * y, "z": zs}
            s = zs * 4 + pos["y"] * 2 + pos["x"]
            p = parent(order, bx, by, sgn)
            if isinstance(valid, bool):
                act(i, s, pos, children, p)
            else:
                pl.when(valid)(lambda s=s, pos=pos, children=children, p=p: act(i, s, pos, children, p))

    def work(i, s, pos, children, p):
        gather_children(i, s, pos, children, False)
        message(i, s, pos, p).start()

    def leaves(h, indices):
        for i in indices:
            each(h, i, True, work)

    def nodes(h, indices):
        for i in indices:
            each(h, i, False, work)

    def out_copy(w):
        n = outs[w].shape[1] // 2
        return pltpu.make_async_copy(res[w], outs[w].at[:, pl.ds(pl.multiple_of(c * n, 128), n)], res_sem.at[w])

    def out_sib(w, half):
        n = outs[w].shape[1] // 2
        return pltpu.make_async_remote_copy(
            src_ref=res[w], dst_ref=outs[w].at[:, pl.ds(pl.multiple_of(half * n, 128), n)], send_sem=res_send.at[w],
            recv_sem=res_recv.at[w], device_id=sib, device_id_type=MESH)

    def total(w):
        for i, piece in enumerate(pieces):
            if piece[0] == w:
                gather_children(i, f, {"x": x, "y": y, "z": z}, forwards(piece[3], 0, 0, 0), True)
        out_sib(w, c).start()
        out_copy(w).start()

    def sent(indices):
        for i in indices:
            w = pieces[i][0]
            part = mine[w].at[pl.ds(0, (4 * nz - 1) * rows[w]), cols(i)]
            pltpu.make_async_remote_copy(
                src_ref=part, dst_ref=part, send_sem=send.at[i], recv_sem=recv.at[i, 0, 0], device_id=sib,
                device_id_type=MESH).wait_send()

    def finish(ws):
        for w in ws:
            give(w).wait_send()
            out_copy(w).wait()
            out_sib(w, c).wait_send()
            out_sib(w, 1 - c).wait_recv()

    return flip, give, leaves, nodes, total, sent, finish


def encode_back_reduce_kernel(wc, wide_seen, narrow_seen, nz, routes, *refs):
    devices = 4 * nz
    dec_vec, *refs = refs
    given, refs = refs[:9], refs[9:]
    h_h, slope_h, we_h, wd_h, wu_h, wo_h, wq_h, *refs = refs
    dec_g, refs = refs[:4], refs[4:]
    (dx_ref, vec_out, *refs) = refs
    outs, refs = refs[:9], refs[9:]
    (we, wo, wq, wd2, wu2, h2, slope2, dx1_ref, z_ref, do_ref, dqkv, *refs) = refs
    tiles, dm, e_ref, b_ref, x1_ref, o_ref, qkv, a_ref, x_ref = refs[:9]
    refs = refs[9:]
    mine, refs = refs[:9], refs[9:]
    enc_other, refs = refs[:5], refs[5:]
    sibb, refs = refs[:9], refs[9:]
    res, refs = refs[:9], refs[9:]
    npc = len(routes)
    rbuf, refs = [refs[3 * i:3 * i + 3] for i in range(npc)], refs[3 * npc:]
    (vbuf, wsem, gsem, dsem, sib_send, sib_recv, send, recv, res_sem, res_send, res_recv, vsend, vrecv) = refs
    c = lax.axis_index("dp")
    held = [tiles, dm, e_ref, b_ref, x1_ref, o_ref, qkv, a_ref, x_ref]
    takes_in = [pltpu.make_async_copy(s, d, gsem.at[k]) for k, (s, d) in enumerate(zip(given, held))]
    for cp in takes_in:
        cp.start()
    D = wo.shape[0]
    n_up = mine[2].shape[1]
    rows = [m.shape[0] // devices for m in mine]

    def half(ref, h):
        n = ref.shape[1] // 2
        return ref.at[:, pl.ds(pl.multiple_of(h * n, 128), n)]

    other = list(enc_other) + [half(g, 1 - c) for g in dec_g]
    flip, give, leaves, nodes, total, sent, finish = reduce_ops(
        nz, routes, rows, mine, other, sibb, rbuf, res, outs, sib_send, sib_recv, send, recv, res_sem, res_send, res_recv)
    dec_ws = [5, 6, 7, 8]
    for w in dec_ws:
        give(w).start()
    takes = [pltpu.make_async_copy(half(dec_g[w - 5], c), mine[w], dsem.at[w - 5]) for w in dec_ws]
    for t in takes:
        t.start()
    loads = [pltpu.make_async_copy(s, d, wsem.at[k]) for k, (s, d) in enumerate(((we_h, we), (wo_h, wo), (wq_h, wq)))]
    C = 512
    chunks = 2 * n_up // C

    def chunk(j):
        h = (1 - c) if j < chunks // 2 else c
        return pl.multiple_of(h * n_up + (j % (chunks // 2)) * C, 128)

    def feed(j):
        k = chunk(j)
        return (pltpu.make_async_copy(wd_h.at[pl.ds(k, C)], wd2.at[j % 2], wsem.at[3 + j % 2]),
                pltpu.make_async_copy(wu_h.at[:, pl.ds(k, C)], wu2.at[j % 2], wsem.at[5 + j % 2]),
                pltpu.make_async_copy(h_h.at[:, pl.ds(k, C)], h2.at[j % 2], wsem.at[7 + j % 2]),
                pltpu.make_async_copy(slope_h.at[:, pl.ds(k, C)], slope2.at[j % 2], wsem.at[9 + j % 2]))

    loads[0].start()
    for j in (0, 1):
        for cp in feed(j):
            cp.start()
    loads[1].start()
    loads[2].start()
    takes_in[0].wait()
    gain1 = spread_vector(tiles[...], 0, D, devices)
    gain2 = spread_vector(tiles[...], 1, D, devices)
    def own_cols(w):
        n = mine[w].shape[1]
        return pl.ds(pl.multiple_of(c * n, 128), n), pl.ds(pl.multiple_of((1 - c) * n, 128), n)

    sets = {"5": [5], "7": [7], "8": [8], "6": [6], "d": [3], "u": [2], "e": [4], "O": [1], "Q": [0]}
    members = {s: [i for i, p in enumerate(routes) if p[0] in ws] for s, ws in sets.items()}
    kept = {}

    def first():
        for cp in takes_in[1:4]:
            cp.wait()
        loads[0].wait()
        grad = dot_nt(dm[...], we[...])
        dx1_ref[...] = grad
        z_ref[...] = grad.astype(B)
        own, rest = own_cols(4)
        enc_other[4][...] = dot_tn(e_ref[...], dm[:, rest]).astype(B)
        mine[4][...] = dot_tn(e_ref[...], dm[:, own]).astype(B)
        give(4).start()
        kept["back"] = jnp.zeros_like(grad)

    def feed_forward(j):
        own, rest = own_cols(3)
        for cp in feed(j):
            cp.wait()
        kk = pl.ds(chunk(j), C)
        d = (slope2[j % 2] * dot_nt(z_ref[...], wd2[j % 2])).astype(B)
        kept["back"] = kept["back"] + dot_nt(d, wu2[j % 2])
        hk = h2[j % 2]
        enc_other[3][kk, :] = dot_tn(hk, z_ref[:, rest]).astype(B)
        mine[3][kk, :] = dot_tn(hk, z_ref[:, own]).astype(B)
        g = dot_tn(b_ref[...], d).astype(B)
        at = (j % (chunks // 2)) * C
        if j < chunks // 2:
            enc_other[2][:, at:at + C] = g
        else:
            mine[2][:, at:at + C] = g
        if j == chunks // 2 - 1:
            give(2).start()
        if j == chunks - 1:
            give(3).start()
        if j + 2 < chunks:
            for cp in feed(j + 2):
                cp.start()

    def project():
        takes_in[4].wait()
        takes_in[5].wait()
        by_input, by_gain = norm_back(x1_ref[...], gain2, kept.pop("back"))
        vbuf[0, 0] = jnp.zeros_like(vbuf[0, 0])
        vbuf[0, 0, 1:2, :] = jnp.sum(by_gain, axis=0, keepdims=True)
        dx1_ref[...] += by_input
        z_ref[...] = dx1_ref[...].astype(B)
        loads[1].wait()
        do_ref[...] = dot_nt(z_ref[...], wo[...]).astype(B)
        own, rest = own_cols(1)
        enc_other[1][...] = dot_tn(o_ref[...], z_ref[:, rest]).astype(B)
        mine[1][...] = dot_tn(o_ref[...], z_ref[:, own]).astype(B)
        give(1).start()

    def attend(part):
        if part == 0:
            takes_in[6].wait()
        mask = pair_mask()
        groups = x_ref.shape[0] // 128
        scale = ENC_HEAD ** -0.5
        lane = iota((128, 128), 1)
        for g in range(groups):
            if g * 2 // groups != part:
                continue
            rr = slice(128 * g, 128 * g + 128)
            valid = valid_keys(0 if g < wc else 1, wide_seen, narrow_seen)
            for j in range(D // 128):
                q, k, v = (qkv[rr, o + 128 * j:o + 128 * j + 128] for o in (0, D, 2 * D))
                g_o = do_ref[rr, 128 * j:128 * j + 128]
                k2 = jnp.concatenate([k, k], axis=0) * mask
                v2 = jnp.concatenate([v, v], axis=0) * mask
                shares = pair_shares(q, k2, valid)
                dp2 = dot_nt(g_o, v2)
                ds, low = [], []
                for h in range(2):
                    dp = dp2[:, 128 * h:128 * h + 128]
                    p = shares[h]
                    ds.append((p * (dp - jnp.sum(dp * p, axis=1, keepdims=True))).astype(B))
                    low.append(p.astype(B))
                dq = dot(jnp.concatenate(ds, axis=1), k2) * scale
                dk = jnp.where(lane < ENC_HEAD, dot_tn(ds[0], q), dot_tn(ds[1], q)) * scale
                dv = jnp.where(lane < ENC_HEAD, dot_tn(low[0], g_o), dot_tn(low[1], g_o))
                for o, d in ((0, dq), (D, dk), (2 * D, dv)):
                    dqkv[rr, o + 128 * j:o + 128 * j + 128] = d.astype(B)

    def mix():
        takes_in[7].wait()
        own, rest = own_cols(0)
        enc_other[0][...] = dot_tn(a_ref[...], dqkv[:, rest]).astype(B)
        give(0).start()
        mine[0][...] = dot_tn(a_ref[...], dqkv[:, own]).astype(B)

    bits = devices.bit_length() - 1

    def vcopy(k):
        return pltpu.make_async_remote_copy(
            src_ref=vbuf.at[0, k], dst_ref=vbuf.at[1, k], send_sem=vsend.at[k], recv_sem=vrecv.at[k],
            device_id=(lax.axis_index("fsdp"), 1 - c) if k == 0 else (flip(k - 1), c), device_id_type=MESH)

    def vstep(k):
        vcopy(k).wait()
        vbuf[0, k + 1] = vbuf[0, k] + vbuf[1, k]
        if k < bits:
            vcopy(k + 1).start()

    def last():
        takes_in[8].wait()
        loads[2].wait()
        by_input, by_gain = norm_back(x_ref[...], gain1, dot_nt(dqkv[...], wq[...]))
        vbuf[0, 0, 0:1, :] = jnp.sum(by_gain, axis=0, keepdims=True)
        DD = dec_vec.shape[1]
        vbuf[0, 0, 2:3, 0:DD] = dec_vec[2:3, :]
        vbuf[0, 0, 3:5, 0:DD] = dec_vec[0:2, :]
        vcopy(0).start()
        dx_ref[...] = dx1_ref[...] + by_input

    compute = [first] + [functools.partial(feed_forward, j) for j in range(chunks)] + [project]
    compute += [functools.partial(attend, 0), functools.partial(attend, 1), mix, last]

    def ready(s):
        if s in "5678":
            for w in sets[s]:
                takes[w - 5].wait()
        for w in sets[s]:
            give(w).wait_recv()

    vectors = []
    for token in schedule(nz + 1, len(compute)):
        if token[0] == "C":
            compute[token[1]]()
            if token[1] == len(compute) - 1:
                vectors = list(range(bits + 1))
        elif token[0] == "R":
            ready(token[1])
        elif token[0] == "L":
            leaves(token[1], members[token[2]])
        elif token[0] == "N":
            nodes(token[1], members[token[2]])
        else:
            for w in sets[token[1]]:
                total(w)
        if vectors and token[0] == "N":
            vstep(vectors.pop(0))
    for k in vectors:
        vstep(k)
    vec_out[...] = vbuf[0, bits + 1]
    sent(range(npc))
    finish(range(9))


def schedule(top, steps):
    if (top, steps) == (5, 12):
        return list(SCHEDULE)
    tokens = [("C", k) for k in range(steps)] + [("R", s) for s in "5786dueOQ"]
    tokens += [("L", top, s) for s in "5786dueOQ"]
    for h in range(top, 0, -1):
        tokens += [("N", h, s) for s in "5786dueOQ"]
        tokens += [("L", h - 1, s) for s in "5786dueOQ"] if h > 1 else []
    return tokens + [("T", s) for s in "5786dueOQ"]


def encode_back_reduce(tiles, counts, dm, dec_vec, saved, enc, dec_grads, routes, nz, cid=2):
    R = dm.shape[0]
    n = 4 * nz
    bits = n.bit_length() - 1
    x, a, qkv, o, x1, b, h, slope, e = saved
    wq, wo, wu, wd, we = enc
    D = wq.shape[0]
    grads = [*enc, *dec_grads]
    shards = [(g.shape[0] // n, g.shape[1]) for g in grads]
    V = pl.BlockSpec(memory_space=pltpu.VMEM)
    A = pl.BlockSpec(memory_space=pl.ANY)
    sds = jax.ShapeDtypeStruct
    dma = pltpu.SemaphoreType.DMA
    most = 1
    rbuf = []
    for w, c0, cols, order in routes:
        for d in "xyu":
            k = slot_count(order, d, nz)
            most = max(most, k)
            rbuf.append(pltpu.VMEM((k, shards[w][0], cols), B))
    npc = len(routes)
    halves = [pltpu.VMEM((g.shape[0], g.shape[1] // 2), B) for g in grads]
    C = 512
    given = [tiles, dm, e, b, x1, o, qkv, a, x]
    out = pl.pallas_call(
        functools.partial(encode_back_reduce_kernel, *counts, nz, routes),
        out_shape=[sds((R, D), F), sds((8, D), F)] + [sds(s, F) for s in shards],
        in_specs=[V] + [A] * 20,
        out_specs=[V] * 2 + [A] * 9,
        scratch_shapes=[
            pltpu.VMEM(we.shape, B), pltpu.VMEM(wo.shape, B), pltpu.VMEM(wq.shape, B),
            pltpu.VMEM((2, C, D), B), pltpu.VMEM((2, D, C), B), pltpu.VMEM((2, R, C), B), pltpu.VMEM((2, R, C), F),
            pltpu.VMEM((R, D), F), pltpu.VMEM((R, D), B), pltpu.VMEM((R, D), B),
            pltpu.VMEM((R, 3 * D), B),
        ] + [pltpu.VMEM(g.shape, g.dtype) for g in given] + halves + halves[:5] + halves + [pltpu.VMEM((s[0], s[1] // 2), F) for s in shards] + rbuf + [
            pltpu.VMEM((2, bits + 2, 8, D), F), dma((11,)), dma((9,)), dma((4,)), dma((9,)), dma((9,)), dma((npc,)),
            dma((npc, 3, most)), dma((9,)), dma((9,)), dma((9,)), dma((bits + 1,)), dma((bits + 1,))],
        compiler_params=pltpu.CompilerParams(collective_id=cid, has_side_effects=True, vmem_limit_bytes=63 * 2**20),
        name="encoder_backward_and_reduce",
    )(dec_vec, *given, h, slope, we, wd, wu, wo, wq, *dec_grads)
    return out[0], out[1], out[2:]


ZXY = ("z", "x", "y")
ZYX = ("z", "y", "x")
XYZ = ("x", "y", "z")
YXZ = ("y", "x", "z")
XZY = ("x", "z", "y")
YZX = ("y", "z", "x")
GATHER = ((0, ZYX), (2, XZY), (3, ZYX), (1, YXZ), (4, YXZ), (5, ZXY), (7, ZXY), (8, YZX), (6, XZY))
GATHER_SCHEDULE = (
    ("S", "o"), ("S", "q"), ("S", "d"), ("P",), ("V", 1, "q"), ("S", "u"), ("V", 1, "o"), ("V", 2, "q"),
    ("S", "e"), ("V", 1, "u"), ("V", 2, "o"), ("V", 3, "q"), ("V", 1, "d"), ("V", 2, "u"), ("V", 4, "q"),
    ("V", 2, "d"), ("V", 5, "q"), ("V", 1, "e"), ("V", 3, "o"), ("S", "5"), ("V", 3, "u"), ("R", "q"), ("C", 0),
    ("V", 3, "d"), ("V", 4, "o"), ("V", 2, "e"), ("V", 1, "5"), ("C", 1), ("V", 4, "u"), ("S", "8"),
    ("V", 5, "o"), ("V", 4, "d"), ("V", 3, "e"), ("V", 2, "5"), ("R", "o"), ("S", "7"), ("C", 2), ("V", 5, "u"),
    ("V", 5, "d"), ("S", "6"), ("V", 1, "8"), ("C", 3), ("V", 3, "5"), ("V", 4, "e"), ("R", "u"), ("R", "d"),
    ("V", 1, "7"), ("V", 1, "6"), ("C", 4), ("C", 5), ("V", 4, "5"), ("V", 2, "8"), ("V", 5, "e"), ("C", 6),
    ("V", 2, "7"), ("C", 7), ("V", 2, "6"), ("V", 5, "5"), ("C", 8), ("V", 3, "8"), ("R", "e"), ("C", 9),
    ("R", "5"), ("V", 3, "7"), ("C", 10), ("V", 3, "6"), ("C", 11), ("V", 4, "8"), ("V", 4, "7"), ("V", 4, "6"),
    ("C", 12), ("V", 5, "6"), ("V", 5, "7"), ("V", 5, "8"), ("C", 13),
)
REDUCE = ((5, YZX), (7, XYZ), (8, ZXY), (6, YZX), (3, YZX), (2, ZXY), (4, ZYX), (1, ZXY), (0, ZXY))
SCHEDULE = (
    ("C", 0), ("C", 1), ("R", "5"), ("L", 5, "5"), ("L", 4, "5"), ("L", 3, "5"), ("R", "7"), ("N", 5, "7"),
    ("C", 2), ("R", "8"), ("L", 5, "8"), ("N", 5, "5"), ("L", 5, "7"), ("N", 5, "8"), ("L", 4, "8"),
    ("L", 4, "7"), ("L", 3, "8"), ("L", 2, "5"), ("R", "6"), ("R", "e"), ("L", 2, "8"), ("N", 5, "6"),
    ("N", 4, "5"), ("C", 3), ("N", 4, "7"), ("N", 4, "8"), ("L", 5, "e"), ("L", 5, "6"), ("L", 4, "e"), ("C", 4),
    ("N", 3, "5"), ("N", 5, "e"), ("L", 3, "e"), ("L", 1, "5"), ("L", 1, "8"), ("N", 3, "8"), ("C", 5), ("C", 6),
    ("N", 4, "e"), ("R", "u"), ("L", 5, "u"), ("N", 4, "6"), ("L", 2, "e"), ("N", 3, "7"), ("L", 4, "6"),
    ("L", 4, "u"), ("L", 3, "6"), ("N", 2, "8"), ("L", 3, "u"), ("N", 5, "u"), ("R", "d"), ("L", 5, "d"),
    ("L", 3, "7"), ("L", 4, "d"), ("N", 5, "d"), ("L", 3, "d"), ("N", 2, "5"), ("L", 2, "u"), ("N", 2, "7"),
    ("C", 7), ("C", 8), ("N", 4, "d"), ("N", 4, "u"), ("L", 2, "d"), ("N", 3, "e"), ("N", 1, "8"), ("R", "O"),
    ("L", 5, "O"), ("N", 5, "O"), ("L", 4, "O"), ("N", 1, "5"), ("C", 9), ("N", 3, "d"), ("L", 1, "e"),
    ("L", 3, "O"), ("N", 3, "6"), ("C", 10), ("L", 2, "7"), ("N", 3, "u"), ("L", 2, "O"), ("R", "Q"),
    ("N", 2, "e"), ("N", 4, "O"), ("L", 5, "Q"), ("N", 1, "7"), ("L", 1, "7"), ("N", 5, "Q"), ("L", 4, "Q"),
    ("N", 2, "d"), ("L", 2, "6"), ("L", 1, "6"), ("N", 4, "Q"), ("N", 2, "6"), ("N", 3, "O"), ("L", 3, "Q"),
    ("N", 2, "u"), ("T", "7"), ("N", 3, "Q"), ("N", 1, "d"), ("T", "5"), ("L", 2, "Q"), ("N", 1, "e"),
    ("L", 1, "d"), ("N", 2, "O"), ("L", 1, "u"), ("N", 2, "Q"), ("N", 1, "u"), ("N", 1, "6"), ("C", 11),
    ("L", 1, "Q"), ("N", 1, "Q"), ("T", "d"), ("T", "8"), ("L", 1, "O"), ("N", 1, "O"), ("T", "e"), ("T", "u"),
    ("T", "6"), ("T", "Q"), ("T", "O"),
)


def whole_tiles(shards, devices):
    return devices % 4 == 0 and all(s.shape[0] % 16 == 0 and s.shape[1] % 256 == 0 for s in shards)


def local(
    clips_wide, clips_narrow, visible_wide, visible_narrow, shift_wide, shift_narrow,
    enc_norm1, enc_qkv, enc_out, enc_norm2, enc_up, enc_down, embed_proj, mask_token,
    dec_norm1, dec_qkv, dec_out, dec_norm2, dec_up, dec_down, cotan_wide, cotan_narrow,
):
    devices = lax.axis_size("fsdp")
    matrices = [enc_qkv, enc_out, enc_up, enc_down, embed_proj, dec_qkv, dec_out, dec_up, dec_down]
    vectors = [enc_norm1, enc_norm2, mask_token, dec_norm1, dec_norm2]
    narrow = jnp.transpose(clips_narrow, (1, 0, 2))
    place = (shift_wide, shift_narrow, visible_wide, visible_narrow, cotan_wide, cotan_narrow)
    counts = (clips_wide.shape[0], clips_wide.shape[1], clips_narrow.shape[1])
    direct = whole_tiles(matrices, devices)
    if direct:
        pieces = [(len(matrices), 0, 128, ZXY, False)]
        pieces += [(w, 0, matrices[w].shape[1] // 2, order, True) for w, order in GATHER]
        whole, placed, saved, first = gather_encode(
            matrices, vectors, pieces, place, clips_wide, narrow, devices // 4
        )
    else:
        packed = jnp.stack([jnp.pad(v, (0, 128 - v.shape[0])) for v in vectors])
        packed = jnp.pad(packed, ((0, 16 - len(vectors)), (0, 0)))
        whole = [lax.all_gather(m, "fsdp", axis=0, tiled=True) for m in (*matrices, packed)]
        got = encoder_forward(place, whole[9], clips_wide, narrow, *whole[:6], devices)
        placed, first, saved = got[:3], got[3:8], got[9:]
    enc, dec, tiles = whole[:5], whole[5:9], whole[9]
    decoded_wide, decoded_narrow, grad_embedded, *dec_grads, gains = decoder(
        tiles, placed, first, (saved[0].shape[0], embed_proj.shape[1]), cotan_wide.shape, cotan_narrow.shape, *dec, devices
    )
    if direct:
        routes = [(w, 0, matrices[w].shape[1] // 2, order) for w, order in REDUCE]
        grad_rows, gains, shares = encode_back_reduce(
            tiles, counts, grad_embedded, gains, saved, enc, dec_grads, routes, devices // 4
        )
    else:
        grad_rows, *enc_grads, gains = encoder_backward(
            tiles, counts, grad_embedded, gains, saved, *enc, devices
        )
        gains = lax.psum(gains, ("fsdp", "dp"))
        shares = [
            lax.psum_scatter(lax.psum(g.astype(F), "dp"), "fsdp", scatter_dimension=0, tiled=True)
            for g in enc_grads + dec_grads
        ]
    encoded_wide, encoded_narrow, grad_wide, grad_narrow, m, v = results(
        lax.axis_index("fsdp"), saved[-1], grad_rows, gains, shares, [v.shape[0] for v in vectors],
        clips_wide.shape, clips_narrow.shape,
    )
    return (
        encoded_wide, encoded_narrow, decoded_wide, decoded_narrow, grad_wide, grad_narrow,
        v[0], m[0], m[1], v[1], m[2], m[3], m[4], v[2], v[3], m[5], m[6], v[4], m[7], m[8],
    )


def solution(mesh):
    clips = ("fsdp", "dp")
    matrix, vector = P("fsdp", None), P("fsdp")
    weights = (
        vector, matrix, matrix, vector, matrix, matrix, matrix, vector,
        vector, matrix, matrix, vector, matrix, matrix,
    )
    rows, pairs = P(clips, None, None), P(clips, None)
    return jax.shard_map(
        local,
        mesh=mesh,
        in_specs=(rows, rows, pairs, pairs, pairs, P(clips), *weights, rows, rows),
        out_specs=(rows,) * 6 + weights,
        check_vma=False,
    )
```

```python
import functools

import jax
import jax.numpy as jnp
from jax import lax
from jax.experimental import pallas as pl
from jax.experimental.pallas import tpu as pltpu
from jax.sharding import PartitionSpec as P

MESH = pl.DeviceIdType.MESH


def slots():
    out=[]
    for bx in (0,1):
        for by in (0,1):
            for sgn in (0,1,-1):
                if (bx,by,sgn)!=(0,0,0): out.append((bx,by,sgn))
    return out

def forwards(order,bx,by,sgn):
    differs={'x':bx,'y':by,'z':int(sgn!=0)}
    last=max([j for j,d in enumerate(order) if differs[d]],default=-1)
    dirs=[]
    for j,d in enumerate(order):
        if j>last:
            dirs += ['u','d'] if d=='z' else [d]
    if last>=0 and order[last]=='z':
        dirs.append('u' if sgn<0 else 'd')
    return dirs


TIME = 64
WIN = 4
EPS = 1e-6
F = jnp.float32
B = jnp.bfloat16
VMEM_LIMIT = 60 * 2**20


def dot(a, b):
    return lax.dot_general(a, b, (((1,), (0,)), ((), ())), preferred_element_type=F)


def dot_nt(a, b):
    return lax.dot_general(a, b, (((1,), (1,)), ((), ())), preferred_element_type=F)


def dot_tn(a, b):
    return lax.dot_general(a, b, (((0,), (0,)), ((), ())), preferred_element_type=F)


def iota(shape, dim):
    return lax.broadcasted_iota(jnp.int32, shape, dim)


def norm_stats(x):
    center = jnp.mean(x, axis=-1, keepdims=True)
    shifted = x - center
    spread = jnp.mean(shifted * shifted, axis=-1, keepdims=True)
    scale = lax.rsqrt(spread + EPS)
    return shifted * scale, scale


def norm_back(x, gain, grad):
    unit, scale = norm_stats(x)
    by_gain = grad * unit
    by_unit = grad * gain
    mean_one = jnp.mean(by_unit, axis=-1, keepdims=True)
    mean_two = jnp.mean(by_unit * unit, axis=-1, keepdims=True)
    by_input = scale * (by_unit - mean_one - unit * mean_two)
    return by_input, jnp.sum(by_gain.reshape(-1, 8, x.shape[1]), axis=0)


def gelu_both(u):
    t = 1.0 / (1.0 + (0.3275911 * 0.7071067811865476) * jnp.abs(u))
    bell = jnp.exp(-0.5 * u * u)
    poly = t * (0.127414796 + t * (-0.142248368 + t * (0.7107068705 + t * (-0.7265760135 + t * 0.5307027145))))
    tail = poly * bell
    phi = jnp.where(u < 0, tail, 1.0 - tail)
    return u * phi, phi + u * (bell * 0.3989422804014327)


def spread_vector(tiles, lane, size, devices):
    part = size // devices
    pick = (iota((128, size), 1) % part == iota((128, size), 0)).astype(B)
    wide = dot(tiles, pick)
    rows = iota((tiles.shape[0], size), 0)
    keep = rows == (iota((tiles.shape[0], size), 1) // part) * 16 + lane
    return jnp.sum(jnp.where(keep, wide, 0.0), axis=0, keepdims=True)


def group_sums(x, ones):
    high = x.astype(B)
    return dot(high, ones) + dot((x - high.astype(F)).astype(B), ones)


def lane_groups(x, op):
    lanes = iota(x.shape, 1)
    width = x.shape[1]
    for d in (1, 2, 4, 8):
        other = jnp.where((lanes & d) != 0, pltpu.roll(x, d, 1), pltpu.roll(x, width - d, 1))
        x = op(x, other)
    return x


HEAD = 32
AREA = WIN * WIN


def stack8(block, mask):
    return jnp.concatenate([block] * 8, axis=0) * mask


def dec_kernel(wc, nc, wide_rows, narrow_rows, devices, tiles, sel, perm_h, dz_h, r_h, a_h, qkv_h, p_h, o_h, wq_h, wo_h, wu_h, wd_h,
               outw_h, outn_h, dm_ref, gq_h, go_h, gu_h, gd_h, vec_ref,
               wq, wo, wu, wd, r_ref, a_ref, qkv, p_ref, o_ref,
               b_ref, h_ref, du, dx1, do_ref, dqkv, dec, dm_acc, acc, gq, go, gu, gd, perm, dz, outw, outn, sems):
    D = wo.shape[0]
    rows = wc * wide_rows + nc * narrow_rows
    T = 256
    tall = 512 if rows % 512 == 0 else T
    nt = rows // T
    wide_tiles = wc * wide_rows // T
    cps = []
    for k, (src, dst) in enumerate((
            (o_h, o_ref), (r_h, r_ref), (wo_h, wo), (wu_h, wu), (dz_h, dz), (wd_h, wd), (perm_h, perm), (qkv_h, qkv),
            (p_h, p_ref), (wq_h, wq), (a_h, a_ref))):
        cp = pltpu.make_async_copy(src, dst, sems.at[k])
        cp.start()
        cps.append(cp)
    gain1 = spread_vector(tiles[...], 3, D, devices)
    gain2 = spread_vector(tiles[...], 4, D, devices)
    dm_acc[...] = jnp.zeros_like(dm_acc)
    acc[...] = jnp.zeros_like(acc)
    def group_rows(t):
        g = jnp.where(t < wide_tiles, t * T // wide_rows, wc + (t - wide_tiles) // 2)
        return pl.ds(pl.multiple_of(g * 128, 128), 128)

    mask = (iota((128, 256), 0) // AREA == iota((128, 256), 1) // HEAD).astype(B)
    scale = HEAD ** -0.5
    nw = 64
    while rows % (nw * AREA):
        nw //= 2
    ones = (iota((128, 128), 0) // AREA == iota((128, 128), 1) // AREA).astype(B)
    for cp in cps[:3]:
        cp.wait()

    @pl.loop(0, nt)
    def _(t):
        rr = pl.ds(pl.multiple_of(t * T, T), T)
        x1 = r_ref[rr] + dot(o_ref[rr], wo[...])
        dx1[rr] = x1
        b_ref[rr] = (norm_stats(x1)[0] * gain2).astype(B)

    for cp in cps[3:6]:
        cp.wait()

    @pl.loop(0, rows // tall)
    def _(t):
        rr = pl.ds(pl.multiple_of(t * tall, tall), tall)
        x1 = dx1[rr]
        b = b_ref[rr]
        z = dz[rr]
        out = x1
        back = jnp.zeros((tall, D), F)
        C = 512
        for k in range(0, wu.shape[1], C):
            u = dot(b, wu[:, k:k + C])
            h, slope = gelu_both(u)
            h = h.astype(B)
            h_ref[rr, k:k + C] = h
            out = out + dot(h, wd[k:k + C, :])
            d = (slope * dot_nt(z, wd[k:k + C, :])).astype(B)
            du[rr, k:k + C] = d
            back = back + dot_nt(d, wu[:, k:k + C])
        dec[rr] = out.astype(B)
        by_input, by_gain = norm_back(x1, gain2, back)
        acc[1] += by_gain
        dx = z.astype(F) + by_input
        dx1[rr] = dx
        do_ref[rr] = dot_nt(dx.astype(B), wo[...]).astype(B)

    for cp in cps[6:]:
        cp.wait()
    for i in range(wc + nc):
        base, n, out = (i * wide_rows, wide_rows, outw) if i < wc else (
            wc * wide_rows + (i - wc) * narrow_rows, narrow_rows, outn)
        out[i if i < wc else i - wc] = dot_tn(perm[base:base + n, 0:n], dec[base:base + n]).astype(B)
    decoded = [pltpu.make_async_copy(outw, outw_h, sems.at[15]), pltpu.make_async_copy(outn, outn_h, sems.at[16])]
    for cp in decoded:
        cp.start()

    @pl.loop(0, rows // (nw * AREA))
    def _(g):
        base = pl.multiple_of(g * nw * AREA, nw * AREA)
        rr = pl.ds(base, nw * AREA)
        w16 = [slice(AREA * j, AREA * j + AREA) for j in range(nw)]
        for a in range(D // 256):
            cq = pl.ds(a * 256, 256)
            q, k, v = qkv[rr, cq], qkv[rr, pl.ds(D + a * 256, 256)], qkv[rr, pl.ds(2 * D + a * 256, 256)]
            go_ = do_ref[rr, cq]
            ks = [stack8(k[w], mask) for w in w16]
            qs = [stack8(q[w], mask) for w in w16]
            gs = [stack8(go_[w], mask) for w in w16]
            p = p_ref[rr, pl.ds(a * 128, 128)]
            dp = jnp.concatenate([dot_nt(go_[w], stack8(v[w], mask)) for w in w16], axis=0)
            ds = (p * (dp - group_sums(dp * p, ones))).astype(B)
            dqkv[rr, cq] = (jnp.concatenate([dot(ds[w], m) for w, m in zip(w16, ks)], axis=0) * scale).astype(B)
            s = jnp.concatenate([dot_nt(k[w], m) for w, m in zip(w16, qs)], axis=0) * scale
            s = s.reshape(nw, AREA, 128)
            e = jnp.exp(s - jnp.max(s, axis=1, keepdims=True))
            p = e / jnp.sum(e, axis=1, keepdims=True)
            dp = jnp.concatenate([dot_nt(v[w], m) for w, m in zip(w16, gs)], axis=0).reshape(nw, AREA, 128)
            ds = (p * (dp - jnp.sum(dp * p, axis=1, keepdims=True))).reshape(nw * AREA, 128).astype(B)
            p = p.reshape(nw * AREA, 128).astype(B)
            dqkv[rr, pl.ds(D + a * 256, 256)] = (jnp.concatenate([dot(ds[w], m) for w, m in zip(w16, qs)], axis=0) * scale).astype(B)
            dqkv[rr, pl.ds(2 * D + a * 256, 256)] = jnp.concatenate([dot(p[w], m) for w, m in zip(w16, gs)], axis=0).astype(B)

    @pl.loop(0, nt)
    def _(t):
        rr = pl.ds(pl.multiple_of(t * T, T), T)
        g = group_rows(t)
        by_input, by_gain = norm_back(r_ref[rr], gain1, dot_nt(dqkv[rr], wq[...]))
        acc[0] += by_gain
        dr = dx1[rr] + by_input
        s = sel[rr]
        hidden = 1.0 - jnp.sum(s.astype(F), axis=1, keepdims=True)
        acc[2] += jnp.sum((dr * hidden).reshape(-1, 8, D), axis=0)
        dm_acc[g] += dot_tn(s, dr.astype(B))

    dm_ref[...] = dm_acc[...].astype(B)
    for k in range(3):
        vec_ref[k:k + 1, :] = jnp.sum(acc[k], axis=0, keepdims=True)
    vec_ref[3:, :] = jnp.zeros((5, D), F)
    step = 512
    copies = []

    def leave(k, src, dst):
        cp = pltpu.make_async_copy(src, dst, sems.at[11 + k])
        cp.start()
        copies.append(cp)

    @pl.loop(0, wd.shape[0] // step)
    def _(k):
        kk = pl.ds(pl.multiple_of(k * step, step), step)
        gd[kk, :] = dot_tn(h_ref[:, kk], dz[...]).astype(B)

    leave(0, gd, gd_h)

    @pl.loop(0, wd.shape[0] // step)
    def _(k):
        kk = pl.ds(pl.multiple_of(k * step, step), step)
        gu[:, kk] = dot_tn(b_ref[...], du[:, kk]).astype(B)

    leave(1, gu, gu_h)

    @pl.loop(0, wq.shape[1] // step)
    def _(k):
        kk = pl.ds(pl.multiple_of(k * step, step), step)
        gq[:, kk] = dot_tn(a_ref[...], dqkv[:, kk]).astype(B)

    leave(2, gq, gq_h)
    go[...] = dot_tn(o_ref[...], dx1[...].astype(B)).astype(B)
    leave(3, go, go_h)
    for cp in copies + decoded:
        cp.wait()


def decoder(tiles, placed, first, m_shape, wide_shape, narrow_shape, wq, wo, wu, wd, devices):
    wc, wide_rows, D = wide_shape
    nc, narrow_rows, _ = narrow_shape
    FFD = wu.shape[1]
    rows = wc * wide_rows + nc * narrow_rows
    V = pl.BlockSpec(memory_space=pltpu.VMEM)
    A = pl.BlockSpec(memory_space=pl.ANY)
    sds = jax.ShapeDtypeStruct
    weights = [pltpu.VMEM(w.shape, B) for w in (wq, wo, wu, wd)]
    return pl.pallas_call(
        functools.partial(dec_kernel, wc, nc, wide_rows, narrow_rows, devices),
        out_shape=[sds(wide_shape, B), sds(narrow_shape, B), sds(m_shape, B), sds(wq.shape, B), sds(wo.shape, B),
                   sds(wu.shape, B), sds(wd.shape, B), sds((8, D), F)],
        in_specs=[V] * 2 + [A] * 11,
        out_specs=[A] * 2 + [V] + [A] * 4 + [V],
        scratch_shapes=weights + [pltpu.VMEM(f.shape, f.dtype) for f in first] + [
            pltpu.VMEM((rows, D), B), pltpu.VMEM((rows, FFD), B), pltpu.VMEM((rows, FFD), B), pltpu.VMEM((rows, D), F),
            pltpu.VMEM((rows, D), B), pltpu.VMEM((rows, 3 * D), B), pltpu.VMEM((rows, D), B),
            pltpu.VMEM(m_shape, F), pltpu.VMEM((3, 8, D), F)] + weights + [
            pltpu.VMEM(placed[0].shape, B), pltpu.VMEM(placed[2].shape, B),
            pltpu.VMEM(wide_shape, B), pltpu.VMEM(narrow_shape, B), pltpu.SemaphoreType.DMA((17,))],
        compiler_params=pltpu.CompilerParams(vmem_limit_bytes=VMEM_LIMIT),
        name="decoder_block",
    )(tiles, placed[1], placed[0], placed[2], *first, wq, wo, wu, wd)


def first_shapes(cotw, cotn):
    rows = cotw.shape[0] * cotw.shape[1] + cotn.shape[0] * cotn.shape[1]
    D = cotw.shape[2]
    sds = jax.ShapeDtypeStruct
    return [sds((rows, D), F), sds((rows, D), B), sds((rows, 3 * D), B), sds((rows, D // 2), F), sds((rows, D), B)]


def decoder_first(wc, nc, wide_rows, narrow_rows, devices, tiles, m_ref, sel, wq, mhi, mlo, r_ref, a_ref, qkv, p_ref, o_ref):
    D = o_ref.shape[1]
    rows = wc * wide_rows + nc * narrow_rows
    T = 256
    nt = rows // T
    wide_tiles = wc * wide_rows // T

    def group_rows(t):
        g = jnp.where(t < wide_tiles, t * T // wide_rows, wc + (t - wide_tiles) // 2)
        return pl.ds(pl.multiple_of(g * 128, 128), 128)

    nw = 32
    while rows % (nw * AREA):
        nw //= 2
    turns = rows // (nw * AREA)

    def enter():
        gain1 = spread_vector(tiles[...], 3, D, devices)
        filler = spread_vector(tiles[...], 2, D, devices)
        mhi[...] = m_ref[...].astype(B)
        mlo[...] = (m_ref[...] - mhi[...].astype(F)).astype(B)

        @pl.loop(0, nt)
        def _(t):
            rr = pl.ds(pl.multiple_of(t * T, T), T)
            g = group_rows(t)
            s = sel[rr]
            seen = jnp.sum(s.astype(F), axis=1, keepdims=True)
            x = dot(s, mhi[g]) + dot(s, mlo[g]) + (1.0 - seen) * filler
            r_ref[rr] = x
            a = (norm_stats(x)[0] * gain1).astype(B)
            a_ref[rr] = a
            qkv[rr] = dot(a, wq[...]).astype(B)

    def attend(half):
        mask = (iota((128, 256), 0) // AREA == iota((128, 256), 1) // HEAD).astype(B)
        scale = HEAD ** -0.5
        ones = (iota((128, 128), 0) // AREA == iota((128, 128), 1) // AREA).astype(B)

        @pl.loop(turns * half // 2, turns * (half + 1) // 2)
        def _(g):
            base = pl.multiple_of(g * nw * AREA, nw * AREA)
            rr = pl.ds(base, nw * AREA)
            for a in range(D // 256):
                cq = pl.ds(a * 256, 256)
                q, k, v = qkv[rr, cq], qkv[rr, pl.ds(D + a * 256, 256)], qkv[rr, pl.ds(2 * D + a * 256, 256)]
                w16 = [slice(AREA * j, AREA * j + AREA) for j in range(nw)]
                s = jnp.concatenate([dot_nt(q[w], stack8(k[w], mask)) for w in w16], axis=0) * scale
                e = jnp.exp(s - lane_groups(s, jnp.maximum))
                p = e / group_sums(e, ones)
                p_ref[rr, pl.ds(a * 128, 128)] = p
                low = p.astype(B)
                o_ref[rr, cq] = jnp.concatenate([dot(low[w], stack8(v[w], mask)) for w in w16], axis=0).astype(B)

    return enter, functools.partial(attend, 0), functools.partial(attend, 1)


def placement(wc, nc, shw, shn, visw, visn, cotw, cotn, perm, sel, dz):
    T = 256
    wide_rows, narrow_rows = cotw.shape[1], cotn.shape[1]
    clips = [(i * wide_rows, wide_rows, 8, shw[i, 0], shw[i, 1], cotw, i, visw, 0) for i in range(wc)]
    clips += [(wc * wide_rows + i * narrow_rows, narrow_rows, 4, shn[i], 0, cotn, i, visn, 64 * (i % 2)) for i in range(nc)]
    for base, n, cols, s, r, cot, i, vis, o in clips:
        seen = vis.shape[1]
        parts = [jnp.full((1, o), -1, jnp.int32)] if o else []
        parts += [vis[i:i + 1, :], jnp.full((1, 128 - o - seen), -1, jnp.int32)]
        shown = jnp.concatenate(parts, axis=1)
        for k in range(0, n, T):
            j = iota((T, 1), 0) + k
            w, q = j >> 4, j & 15
            wf = cols // WIN
            t = ((w // wf) * WIN + (q >> 2) + s) & (TIME - 1)
            f = ((w % wf) * WIN + (q & 3) + r) & (cols - 1)
            patch = t * cols + f
            where = pl.ds(base + k, T)
            hot = jnp.where(iota((T, n), 1) == patch, 1.0, 0.0).astype(B)
            perm[where, 0:n] = hot
            if n < perm.shape[1]:
                perm[where, n:] = jnp.zeros((T, perm.shape[1] - n), B)
            sel[where] = jnp.where(shown == patch, 1.0, 0.0).astype(B)
            dz[where] = dot(hot, cot[i]).astype(B)


def placed_shapes(cotw, cotn):
    rows = cotw.shape[0] * cotw.shape[1] + cotn.shape[0] * cotn.shape[1]
    return [jax.ShapeDtypeStruct((rows, n), B) for n in (cotw.shape[1], 128, cotw.shape[2])]


ENC_HEAD = 64


def valid_keys(kind, wide_seen, narrow_seen):
    q, k = iota((128, 128), 0), iota((128, 128), 1)
    if kind == 0:
        return k < wide_seen
    return ((q // 64) == (k // 64)) & (k % 64 < narrow_seen)


def pair_mask():
    return (iota((256, 128), 0) // 128 == iota((256, 128), 1) // ENC_HEAD).astype(B)


def pair_shares(q, k2, valid):
    s2 = dot_nt(q, k2) * (ENC_HEAD ** -0.5)
    shares = []
    for h in range(2):
        s = jnp.where(valid, s2[:, 128 * h:128 * h + 128], -1e30)
        e = jnp.exp(s - jnp.max(s, axis=1, keepdims=True))
        shares.append(e / jnp.sum(e, axis=1, keepdims=True))
    return shares


def load_rows(dst, pair, wide, narrow, wc, nc):
    dst[...] = jnp.zeros_like(dst)
    for i in range(wc):
        dst[128 * i:128 * i + wide.shape[1], :] = wide[i].astype(F)
    pair[...] = narrow[...].astype(F)
    for i in range(nc):
        o = 128 * wc + 64 * i
        dst[o:o + narrow.shape[0], :] = pair[:, i, :]


def enc_forward_kernel(wc, nc, devices, shw, shn, visw, visn, cotw, cotn, tiles, cw, cn, wq_h, wo_h, wu_h, wd_h, we_h, wqd_h,
                       perm, sel, dz, r_d, a_d, qkv_d, p_d, o_d, m_ref, x_ref, a_ref, qkv, o_ref, x1_ref, b_ref, h_ref, slope_ref, e_ref,
                       wq, wo, wu, wd, we, pair, wqd, mhi, mlo, sems):
    D = wo.shape[0]
    cps = []
    for k, (src, dst) in enumerate((
            (wq_h, wq), (wo_h, wo), (wu_h, wu), (wd_h, wd), (we_h, we), (wqd_h, wqd))):
        cp = pltpu.make_async_copy(src, dst, sems.at[k])
        cp.start()
        cps.append(cp)
    placement(wc, nc, shw, shn, visw, visn, cotw, cotn, perm, sel, dz)
    load_rows(x_ref, pair, cw, cn, wc, nc)
    gain1 = spread_vector(tiles[...], 0, D, devices)
    gain2 = spread_vector(tiles[...], 1, D, devices)
    x = x_ref[...]
    a = (norm_stats(x)[0] * gain1).astype(B)
    a_ref[...] = a
    cps[0].wait()
    for k in range(0, 3 * D, D):
        qkv[:, k:k + D] = dot(a, wq[:, k:k + D]).astype(B)
    mask = pair_mask()
    groups = x_ref.shape[0] // 128
    for g in range(groups):
        rr = slice(128 * g, 128 * g + 128)
        valid = valid_keys(0 if g < wc else 1, cw.shape[1], cn.shape[0])
        for j in range(D // 128):
            q, k, v = (qkv[rr, o + 128 * j:o + 128 * j + 128] for o in (0, D, 2 * D))
            k2 = jnp.concatenate([k, k], axis=0) * mask
            v2 = jnp.concatenate([v, v], axis=0) * mask
            p2 = jnp.concatenate(pair_shares(q, k2, valid), axis=1).astype(B)
            o_ref[rr, 128 * j:128 * j + 128] = dot(p2, v2).astype(B)
    cps[1].wait()
    x1 = x_ref[...] + dot(o_ref[...], wo[...])
    x1_ref[...] = x1
    b = (norm_stats(x1)[0] * gain2).astype(B)
    b_ref[...] = b
    cps[2].wait()
    cps[3].wait()
    out = x1
    C = 512
    for k in range(0, wu.shape[1], C):
        h, slope = gelu_both(dot(b, wu[:, k:k + C]))
        h = h.astype(B)
        h_ref[:, k:k + C] = h
        slope_ref[:, k:k + C] = slope
        out = out + dot(h, wd[k:k + C, :])
    e_ref[...] = out.astype(B)
    cps[4].wait()
    m_ref[...] = dot(e_ref[...], we[...])
    cps[5].wait()
    for step in decoder_first(
            wc, nc, cotw.shape[1], cotn.shape[1], devices, tiles, m_ref, sel, wqd, mhi, mlo, r_d, a_d, qkv_d, p_d, o_d):
        step()


def encoder_forward(place, tiles, cw, cn, wq, wo, wu, wd, we, wqd, devices):
    wc, nc = cw.shape[0], cn.shape[1]
    D = cw.shape[2]
    FFD = wu.shape[1]
    R = 128 * wc + 128 * ((nc + 1) // 2)
    V = pl.BlockSpec(memory_space=pltpu.VMEM)
    S = pl.BlockSpec(memory_space=pltpu.SMEM)
    A = pl.BlockSpec(memory_space=pl.ANY)
    sds = jax.ShapeDtypeStruct
    return pl.pallas_call(
        functools.partial(enc_forward_kernel, wc, nc, devices),
        out_shape=placed_shapes(*place[4:]) + first_shapes(*place[4:]) + [sds((R, we.shape[1]), F), sds((R, D), F), sds((R, D), B), sds((R, 3 * D), B),
                   sds((R, D), B), sds((R, D), F), sds((R, D), B), sds((R, FFD), B), sds((R, FFD), F), sds((R, D), B)],
        in_specs=[S, S] + [V] * 7 + [A] * 6,
        out_specs=[V] * 18,
        scratch_shapes=[pltpu.VMEM(w.shape, B) for w in (wq, wo, wu, wd, we)]
        + [pltpu.VMEM(cn.shape, F), pltpu.VMEM(wqd.shape, B), pltpu.VMEM((R, we.shape[1]), B),
           pltpu.VMEM((R, we.shape[1]), B), pltpu.SemaphoreType.DMA((6,))],
        compiler_params=pltpu.CompilerParams(vmem_limit_bytes=VMEM_LIMIT),
        name="encoder_forward",
    )(*place, tiles, cw, cn, wq, wo, wu, wd, we, wqd)


def enc_backward_kernel(wc, wide_seen, narrow_seen, devices, tiles, dm, dec_vec, x_in, a_ref, qkv, o_ref, x1_ref, b_ref, h_ref, slope_ref, e_ref,
                        wq_h, wo_h, wu_h, wd_h, we_h,
                        dx_ref, gq, go, gu, gd, ge, vec_ref,
                        wq, wo, wu, wd, we, do_ref, dqkv, du, sems):
    D = wo.shape[0]
    cps = []
    for k, (src, dst) in enumerate(((we_h, we), (wd_h, wd), (wu_h, wu), (wo_h, wo), (wq_h, wq))):
        cp = pltpu.make_async_copy(src, dst, sems.at[k])
        cp.start()
        cps.append(cp)
    gain1 = spread_vector(tiles[...], 0, D, devices)
    gain2 = spread_vector(tiles[...], 1, D, devices)
    cps[0].wait()
    grad = dot_nt(dm[...], we[...])
    z = grad.astype(B)
    ge[...] = dot_tn(e_ref[...], dm[...]).astype(B)
    cps[1].wait()
    cps[2].wait()
    back = jnp.zeros_like(grad)
    C = 512
    for k in range(0, wu.shape[1], C):
        d = (slope_ref[:, k:k + C] * dot_nt(z, wd[k:k + C, :])).astype(B)
        du[:, k:k + C] = d
        back = back + dot_nt(d, wu[:, k:k + C])
        gd[k:k + C, :] = dot_tn(h_ref[:, k:k + C], z).astype(B)
        gu[:, k:k + C] = dot_tn(b_ref[...], d).astype(B)
    by_input, by_gain = norm_back(x1_ref[...], gain2, back)
    vec_ref[...] = jnp.zeros_like(vec_ref)
    vec_ref[1:2, :] = jnp.sum(by_gain, axis=0, keepdims=True)
    dx1 = grad + by_input
    y = dx1.astype(B)
    cps[3].wait()
    do_ref[...] = dot_nt(y, wo[...]).astype(B)
    go[...] = dot_tn(o_ref[...], y).astype(B)
    mask = pair_mask()
    groups = x_in.shape[0] // 128
    scale = ENC_HEAD ** -0.5
    lane = iota((128, 128), 1)
    for g in range(groups):
        rr = slice(128 * g, 128 * g + 128)
        valid = valid_keys(0 if g < wc else 1, wide_seen, narrow_seen)
        for j in range(D // 128):
            q, k, v = (qkv[rr, o + 128 * j:o + 128 * j + 128] for o in (0, D, 2 * D))
            g_o = do_ref[rr, 128 * j:128 * j + 128]
            k2 = jnp.concatenate([k, k], axis=0) * mask
            v2 = jnp.concatenate([v, v], axis=0) * mask
            shares = pair_shares(q, k2, valid)
            dp2 = dot_nt(g_o, v2)
            ds, low = [], []
            for h in range(2):
                dp = dp2[:, 128 * h:128 * h + 128]
                p = shares[h]
                ds.append((p * (dp - jnp.sum(dp * p, axis=1, keepdims=True))).astype(B))
                low.append(p.astype(B))
            dq = dot(jnp.concatenate(ds, axis=1), k2) * scale
            dk = jnp.where(lane < ENC_HEAD, dot_tn(ds[0], q), dot_tn(ds[1], q)) * scale
            dv = jnp.where(lane < ENC_HEAD, dot_tn(low[0], g_o), dot_tn(low[1], g_o))
            for o, d in ((0, dq), (D, dk), (2 * D, dv)):
                dqkv[rr, o + 128 * j:o + 128 * j + 128] = d.astype(B)
    cps[4].wait()
    for k in range(0, 3 * D, D):
        gq[:, k:k + D] = dot_tn(a_ref[...], dqkv[:, k:k + D]).astype(B)
    by_input, by_gain = norm_back(x_in[...], gain1, dot_nt(dqkv[...], wq[...]))
    vec_ref[0:1, :] = jnp.sum(by_gain, axis=0, keepdims=True)
    DD = dec_vec.shape[1]
    vec_ref[2:3, 0:DD] = dec_vec[2:3, :]
    vec_ref[3:5, 0:DD] = dec_vec[0:2, :]
    dx_ref[...] = dx1 + by_input


def encoder_backward(tiles, counts, dm, dec_vec, saved, wq, wo, wu, wd, we, devices):
    D = wq.shape[0]
    FFD = wu.shape[1]
    R = dm.shape[0]
    V = pl.BlockSpec(memory_space=pltpu.VMEM)
    A = pl.BlockSpec(memory_space=pl.ANY)
    sds = jax.ShapeDtypeStruct
    return pl.pallas_call(
        functools.partial(enc_backward_kernel, *counts, devices),
        out_shape=[sds((R, D), F)] + [sds(w.shape, B) for w in (wq, wo, wu, wd, we)] + [sds((8, D), F)],
        in_specs=[V] * 12 + [A] * 5,
        out_specs=[V] * 7,
        scratch_shapes=[pltpu.VMEM(w.shape, B) for w in (wq, wo, wu, wd, we)]
        + [pltpu.VMEM((R, D), B), pltpu.VMEM((R, 3 * D), B), pltpu.VMEM((R, FFD), B), pltpu.SemaphoreType.DMA((5,))],
        compiler_params=pltpu.CompilerParams(vmem_limit_bytes=VMEM_LIMIT),
        name="encoder_backward",
    )(tiles, dm, dec_vec, *saved, wq, wo, wu, wd, we)


def results_kernel(wc, nc, sizes, *refs):
    me, e, dx, vec, *refs = refs
    shares, refs = refs[:9], refs[9:]
    encw, encn, gradw, gradn, *refs = refs
    outs, refs = refs[:9], refs[9:]
    vectors, (pair,) = refs[:len(sizes)], refs[len(sizes):]
    for src, wide, narrow in ((e, encw, encn), (dx, gradw, gradn)):
        for i in range(wc):
            rows = src[128 * i:128 * i + encw.shape[1], :]
            if wide is encw:
                wide[i] = rows
            else:
                wide[:, i, :] = rows
        for i in range(nc):
            o = 128 * wc + 64 * i
            pair[:, i, :] = src[o:o + narrow.shape[0], :].astype(F)
        narrow[...] = pair[...].astype(narrow.dtype)
    for src, dst in zip(shares, outs):
        dst[...] = src[...]
    width = vec.shape[1]
    for k, (n, ref) in enumerate(zip(sizes, vectors)):
        ref[...] = pltpu.roll(vec[k:k + 1, :], lax.rem(width - me[0] * n, width), 1)[:, 0:n]


def results(me, e, dx, vec, shares, sizes, wide_shape, narrow_shape):
    wc, nw, D = wide_shape
    nc, nn, _ = narrow_shape
    V = pl.BlockSpec(memory_space=pltpu.VMEM)
    S = pl.BlockSpec(memory_space=pltpu.SMEM)
    sds = jax.ShapeDtypeStruct
    out = pl.pallas_call(
        functools.partial(results_kernel, wc, nc, sizes),
        out_shape=[sds(wide_shape, B), sds((nn, nc, D), B), sds((nw, wc, D), F), sds((nn, nc, D), F)]
        + [sds(s.shape, F) for s in shares] + [sds((1, n), F) for n in sizes],
        in_specs=[S] + [V] * 12,
        out_specs=[V] * (13 + len(sizes)),
        scratch_shapes=[pltpu.VMEM((nn, nc, D), F)],
        compiler_params=pltpu.CompilerParams(vmem_limit_bytes=VMEM_LIMIT),
        name="results",
    )(me.reshape(1), e, dx, vec, *shares)
    swap = functools.partial(jnp.transpose, axes=(1, 0, 2))
    return out[0], swap(out[1]), swap(out[2]), swap(out[3]), out[4:13], [v.reshape(-1) for v in out[13:]]


def gather_ops(nz, pieces, ins, outs, send, recv, sib_send, sib_recv):
    f, c = lax.axis_index("fsdp"), lax.axis_index("dp")
    z, y, x = f // 4, (f // 2) % 2, f % 2
    xn, yn, up, dn, sib = (f + 1 - 2 * x, c), (f + 2 - 4 * y, c), (f + 4, c), (f - 4, c), (f, 1 - c)
    bar = pltpu.get_barrier_semaphore()

    def greet(dev):
        pl.semaphore_signal(bar, inc=1, device_id=dev, device_id_type=MESH)

    greet(xn)
    greet(yn)
    greet(sib)
    pl.when(z < nz - 1)(lambda: greet(up))
    pl.when(z > 0)(lambda: greet(dn))
    pl.semaphore_wait(bar, 3 + (z < nz - 1).astype(jnp.int32) + (z > 0).astype(jnp.int32))
    dest = {"x": xn, "y": yn, "u": up, "d": dn}
    there = {"x": None, "y": None, "u": z < nz - 1, "d": z > 0}
    code = {"x": 0, "y": 0, "u": 1, "d": 2}

    def columns(i, half):
        w, c0, cols, order, share = pieces[i]
        return pl.ds(pl.multiple_of(half * (ins[w].shape[1] // 2) + c0, 128) if share else c0, cols)

    def region(i, s, half):
        w = pieces[i][0]
        r = ins[w].shape[0]
        return outs[w].at[pl.ds(pl.multiple_of(s * r, r), r), columns(i, half)]

    def own(i):
        return ins[pieces[i][0]].at[:, columns(i, c)]

    def remote(i, s, src, d):
        return pltpu.make_async_remote_copy(
            src_ref=src, dst_ref=region(i, s, c), send_sem=send.at[i, code[d]], recv_sem=recv.at[i, s],
            device_id=dest[d], device_id_type=MESH)

    def sibling(i, s, half):
        return pltpu.make_async_remote_copy(
            src_ref=region(i, s, half), dst_ref=region(i, s, half), send_sem=sib_send.at[i],
            recv_sem=sib_recv.at[i], device_id=sib, device_id_type=MESH)

    def some(i, half, count):
        w = pieces[i][0]
        part = outs[w].at[pl.ds(0, count * ins[w].shape[0]), columns(i, half)]
        return lambda a, b: pltpu.make_async_remote_copy(
            src_ref=part, dst_ref=part, send_sem=a, recv_sem=b, device_id=sib, device_id_type=MESH)

    def along(dirs, act):
        for d in dirs:
            if there[d] is None:
                act(d)
            else:
                pl.when(there[d])(lambda d=d: act(d))

    def each(h, i, act):
        for bx, by, sgn in slots():
            k = h - bx - by
            if isinstance(h, int) and not ((k == 0) if sgn == 0 else (1 <= k < nz)):
                continue
            zs = z + sgn * k
            valid = (k == 0) if sgn == 0 else (k >= 1) & (zs >= 0) & (zs < nz)
            s = zs * 4 + (y + by - 2 * by * y) * 2 + (x + bx - 2 * bx * x)
            dirs = forwards(pieces[i][3], bx, by, sgn)
            if isinstance(valid, bool):
                act(i, s, dirs)
            else:
                pl.when(valid)(lambda s=s, dirs=dirs: act(i, s, dirs))

    def start(i):
        along(forwards(pieces[i][3], 0, 0, 0), lambda d: remote(i, f, own(i), d).start())

    def step(i, s, dirs):
        remote(i, s, region(i, s, c), "x").wait_recv()
        along(dirs, lambda d: remote(i, s, region(i, s, c), d).start())
        if pieces[i][4]:
            sibling(i, s, c).start()

    def arrived(i):
        if pieces[i][4]:
            some(i, 1 - c, 4 * nz - 1)(sib_send.at[i], sib_recv.at[i]).wait_recv()

    def finish(i):
        order = pieces[i][3]
        before = {d: order[:order.index(d)] for d in "xyz"}
        size = {"x": 2, "y": 2, "z": nz}

        def blocks(d):
            n = 1
            for e in before[d]:
                n *= size[e]
            return n

        some(i, c, blocks("x") + blocks("y"))(send.at[i, 0], recv.at[i, 0]).wait_send()
        for p in range(nz):
            if p < nz - 1:
                pl.when(z == p)(lambda p=p: some(i, c, blocks("z") * (p + 1))(send.at[i, 1], recv.at[i, 0]).wait_send())
            if p > 0:
                pl.when(z == p)(lambda p=p: some(i, c, blocks("z") * (nz - p))(send.at[i, 2], recv.at[i, 0]).wait_send())
        if pieces[i][4]:
            some(i, c, 4 * nz - 1)(sib_send.at[i], sib_recv.at[i]).wait_send()

    def level(h, indices):
        for i in indices:
            each(h, i, step)

    return start, level, arrived, finish


def gather_encode_kernel(wc, nc, nz, pieces, nw, shw, shn, visw, visn, cotw, cotn, cw, cn, *refs):
    devices = 4 * nz
    vectors, refs = refs[:5], refs[5:]
    ins, refs = list(refs[:nw - 1]), refs[nw - 1:]
    outs, refs = refs[:nw], refs[nw:]
    results_, refs = refs[:18], refs[18:]
    buffers, refs = refs[:18], refs[18:]
    perm, sel, dz, m_ref, x_ref, a_ref, qkv, o_ref, x1_ref, b_ref, h_ref, slope_ref, e_ref, *first = buffers
    wq, wo, wu, wd, we, wqd, mhi, mlo, tiles, sum_ref, pair, tile, send, recv, sib_send, sib_recv, loc, sems, out_sems = refs
    row = iota((16, 128), 0)
    shares = jnp.zeros((16, 128), F)
    for k, v in enumerate(vectors):
        n = v.shape[-1]
        wide = jnp.concatenate([v[...].astype(F).reshape(1, n), jnp.zeros((1, 128 - n), F)], axis=1)
        shares = jnp.where(row == k, wide, shares)
    tile[...] = shares.astype(B)
    ins.append(tile)

    def leave(*which):
        for k in which:
            pltpu.make_async_copy(buffers[k], results_[k], out_sems.at[k]).start()

    D = wo.shape[0]
    start, level, arrived, finish = gather_ops(nz, pieces, ins, outs, send, recv, sib_send, sib_recv)
    sets = {"q": [nw - 1, 0], "u": [2], "d": [3], "o": [1], "e": [4], "5": [5], "6": [6], "7": [7], "8": [8]}
    members = {s: [i for w in ws for i, p in enumerate(pieces) if p[0] == w] for s, ws in sets.items()}
    into = [wq, wo, wu, wd, we, wqd, None, None, None, tiles]
    loads = {}
    gains = []
    locals_ = []
    C = 512
    chunks = wu.shape[1] // C

    def prepare():
        for w in range(nw):
            r = ins[w].shape[0]
            cp = pltpu.make_async_copy(
                ins[w], outs[w].at[pl.ds(pl.multiple_of(lax.axis_index("fsdp") * r, r), r)], loc.at[w])
            cp.start()
            locals_.append(cp)
        placement(wc, nc, shw, shn, visw, visn, cotw, cotn, perm, sel, dz)
        load_rows(x_ref, pair, cw, cn, wc, nc)
        leave(0, 1, 2, 4)

    def ready(s):
        for w, i in zip(sets[s], members[s]):
            arrived(i)
            locals_[w].wait()
            loads[w] = pltpu.make_async_copy(outs[w], into[w], sems.at[w])
            loads[w].start()

    def project():
        loads[nw - 1].wait()
        gains.append(spread_vector(tiles[...], 0, D, devices))
        gains.append(spread_vector(tiles[...], 1, D, devices))
        a = (norm_stats(x_ref[...])[0] * gains[0]).astype(B)
        a_ref[...] = a
        loads[0].wait()
        for k in range(0, 3 * D, D):
            qkv[:, k:k + D] = dot(a, wq[:, k:k + D]).astype(B)
        leave(5, 6)

    def attend(part):
        mask = pair_mask()
        groups = x_ref.shape[0] // 128
        for g in range(groups):
            if g * 2 // groups != part:
                continue
            rr = slice(128 * g, 128 * g + 128)
            valid = valid_keys(0 if g < wc else 1, cw.shape[1], cn.shape[0])
            for j in range(D // 128):
                q, k, v = (qkv[rr, o + 128 * j:o + 128 * j + 128] for o in (0, D, 2 * D))
                k2 = jnp.concatenate([k, k], axis=0) * mask
                v2 = jnp.concatenate([v, v], axis=0) * mask
                p2 = jnp.concatenate(pair_shares(q, k2, valid), axis=1).astype(B)
                o_ref[rr, 128 * j:128 * j + 128] = dot(p2, v2).astype(B)

    def middle():
        loads[1].wait()
        x1 = x_ref[...] + dot(o_ref[...], wo[...])
        x1_ref[...] = x1
        sum_ref[...] = x1
        b_ref[...] = (norm_stats(x1)[0] * gains[1]).astype(B)
        leave(7, 8, 9)

    def feed_forward(j):
        if j == 0:
            loads[2].wait()
            loads[3].wait()
        k = j * C
        h, slope = gelu_both(dot(b_ref[...], wu[:, k:k + C]))
        h = h.astype(B)
        h_ref[:, k:k + C] = h
        slope_ref[:, k:k + C] = slope
        sum_ref[...] += dot(h, wd[k:k + C, :])
        for n in (10, 11):
            pltpu.make_async_copy(buffers[n].at[:, k:k + C], results_[n].at[:, k:k + C], out_sems.at[n]).start()

    def embed():
        e_ref[...] = sum_ref[...].astype(B)
        leave(12)
        loads[4].wait()
        m_ref[...] = dot(e_ref[...], we[...])
        leave(3)

    enter, attend_one, attend_two = decoder_first(
        wc, nc, cotw.shape[1], cotn.shape[1], devices, tiles, m_ref, sel, wqd, mhi, mlo, *first)

    def decode():
        loads[5].wait()
        enter()
        leave(13, 14, 15)

    def decode_end():
        attend_two()
        leave(16, 17)

    compute = [project, functools.partial(attend, 0), functools.partial(attend, 1), middle]
    compute += [functools.partial(feed_forward, j) for j in range(chunks)] + [embed]
    compute += [decode, attend_one, decode_end]
    for token in gather_schedule(nz + 1, len(compute)):
        if token[0] == "S":
            for i in members[token[1]]:
                start(i)
        elif token[0] == "V":
            level(token[1], members[token[2]])
        elif token[0] == "R":
            ready(token[1])
        elif token[0] == "P":
            prepare()
        else:
            compute[token[1]]()
    for w in (6, 7, 8):
        locals_[w].wait()
    for s in "678":
        for i in members[s]:
            arrived(i)
    for i in range(len(pieces)):
        finish(i)
    for n in range(18):
        pltpu.make_async_copy(buffers[n], results_[n], out_sems.at[n]).wait()


def gather_schedule(top, steps):
    if (top, steps) == (5, 14):
        return list(GATHER_SCHEDULE)
    tokens = [("S", s) for s in "qudoe"] + [("P",)] + [("S", s) for s in "5678"]
    tokens += [("V", h, s) for h in range(1, top + 1) for s in "qudoe5678"]
    return tokens + [("R", s) for s in "qoude5"] + [("C", k) for k in range(steps)]


def gather_encode(shards, vectors, pieces, place, cw, cn, nz, cid=1):
    nw, npc, n = len(shards) + 1, len(pieces), 4 * nz
    wc, nc, D = cw.shape[0], cn.shape[1], cw.shape[2]
    R = 128 * wc + 128 * ((nc + 1) // 2)
    V = pl.BlockSpec(memory_space=pltpu.VMEM)
    S = pl.BlockSpec(memory_space=pltpu.SMEM)
    A = pl.BlockSpec(memory_space=pl.ANY)
    sds = jax.ShapeDtypeStruct
    whole = [sds((s.shape[0] * n, s.shape[1]), s.dtype) for s in shards] + [sds((16 * n, 128), B)]
    FFD, DD = shards[2].shape[1], shards[4].shape[1]
    dma = pltpu.SemaphoreType.DMA
    kept = placed_shapes(*place[4:]) + [
        sds((R, DD), F), sds((R, D), F), sds((R, D), B), sds((R, 3 * D), B), sds((R, D), B), sds((R, D), F),
        sds((R, D), B), sds((R, FFD), B), sds((R, FFD), F), sds((R, D), B)] + first_shapes(*place[4:])
    out = pl.pallas_call(
        functools.partial(gather_encode_kernel, wc, nc, nz, pieces, nw),
        out_shape=whole + kept,
        in_specs=[S, S] + [V] * 11 + [A] * (nw - 1),
        out_specs=[A] * (nw + 18),
        scratch_shapes=[pltpu.VMEM(s.shape, s.dtype) for s in kept] + [pltpu.VMEM(w.shape, B) for w in whole[:6]] + [
            pltpu.VMEM((R, DD), B), pltpu.VMEM((R, DD), B), pltpu.VMEM(whole[-1].shape, B), pltpu.VMEM((R, D), F), pltpu.VMEM(cn.shape, F), pltpu.VMEM((16, 128), B),
            dma((npc, 3)), dma((npc, n)), dma((npc,)), dma((npc,)), dma((nw,)), dma((nw,)), dma((18,))],
        compiler_params=pltpu.CompilerParams(collective_id=cid, has_side_effects=True, vmem_limit_bytes=VMEM_LIMIT),
        name="gather_and_encode",
    )(*place, cw, cn, *vectors, *shards)
    return out[:nw], out[nw:nw + 3], out[nw + 4:nw + 13], out[nw + 13:]


def slot_count(order, d, nz):
    size = {"x": 2, "y": 2, "z": nz}
    k = 1
    for e in order[:order.index("z" if d in "ud" else d)]:
        k *= size[e]
    return k * (nz + 1) if d in "ud" else k


def slot_index(order, d, nz, pos):
    size = {"x": 2, "y": 2, "z": nz}
    k = 0
    for e in order[:order.index("z" if d in "ud" else d)]:
        k = k * size[e] + pos[e]
    return k * (nz + 1) + pos["z"] + (1 if d == "d" else 0) if d in "ud" else k


def parent(order, bx, by, sgn):
    differs = {"x": bx, "y": by, "z": int(sgn != 0)}
    last = max(j for j, d in enumerate(order) if differs[d])
    if order[last] == "z":
        return "d" if sgn < 0 else "u"
    return order[last]


def reduce_ops(nz, pieces, rows, mine, other, sibb, rbuf, res, outs, sib_send, sib_recv, send, recv, res_sem, res_send, res_recv):
    f, c = lax.axis_index("fsdp"), lax.axis_index("dp")
    z, y, x = f // 4, (f // 2) % 2, f % 2
    bits = (nz * 4).bit_length() - 1

    def flip(b):
        return f + (1 << b) * (1 - 2 * ((f // (1 << b)) % 2))

    xn, yn, up, dn, sib = (flip(0), c), (flip(1), c), (f + 4, c), (f - 4, c), (f, 1 - c)
    bar = pltpu.get_barrier_semaphore()

    def greet(dev):
        pl.semaphore_signal(bar, inc=1, device_id=dev, device_id_type=MESH)

    greet(xn)
    greet(yn)
    greet(sib)
    pl.when(z < nz - 1)(lambda: greet(up))
    pl.when(z > 0)(lambda: greet(dn))
    far = range(3, bits)
    for b in far:
        greet((flip(b), c))
    pl.semaphore_wait(bar, 3 + len(far) + (z < nz - 1).astype(jnp.int32) + (z > 0).astype(jnp.int32))
    dest = {"x": xn, "y": yn, "u": up, "d": dn}
    there = {"u": z < nz - 1, "d": z > 0}
    opposite = {"u": "d", "d": "u", "x": "x", "y": "y"}
    kind = {"x": 0, "y": 1, "u": 2, "d": 2}

    def give(w):
        return pltpu.make_async_remote_copy(
            src_ref=other[w], dst_ref=sibb[w], send_sem=sib_send.at[w], recv_sem=sib_recv.at[w],
            device_id=sib, device_id_type=MESH)

    def cols(i):
        return pl.ds(pieces[i][1], pieces[i][2])

    def message(i, s, pos, d):
        w, order, b = pieces[i][0], pieces[i][3], kind[d]
        r = rows[w]
        q = slot_index(order, opposite[d], nz, pos)
        return pltpu.make_async_remote_copy(
            src_ref=mine[w].at[pl.ds(pl.multiple_of(s * r, r), r), cols(i)], dst_ref=rbuf[i][b].at[q],
            send_sem=send.at[i], recv_sem=recv.at[i, b, q], device_id=dest[d], device_id_type=MESH)

    def arrival(i, pos, d):
        b = kind[d]
        q = slot_index(pieces[i][3], d, nz, pos)
        return pltpu.make_async_remote_copy(
            src_ref=rbuf[i][b].at[q], dst_ref=rbuf[i][b].at[q], send_sem=send.at[i],
            recv_sem=recv.at[i, b, q], device_id=sib, device_id_type=MESH)

    def add(i, s, pos, children, final):
        w, order = pieces[i][0], pieces[i][3]
        r = rows[w]
        ks = [(kind[d], slot_index(order, d, nz, pos)) for d in children]

        tall = 16
        while r % (2 * tall) == 0 and 2 * tall * pieces[i][2] <= 24 * 16 * 128:
            tall *= 2
        if r % 48 == 0 and 48 * pieces[i][2] <= 27 * 16 * 128:
            tall = max(tall, 48)

        @pl.loop(0, r // tall)
        def _(k):
            rr = pl.ds(pl.multiple_of(k * tall, 16), tall)
            gr = pl.ds(pl.multiple_of(s * r + k * tall, 16), tall)
            t = mine[w][gr, cols(i)].astype(F) + sibb[w][gr, cols(i)].astype(F)
            for b, q in ks:
                t = t + rbuf[i][b][q, rr].astype(F)
            if final:
                res[w][rr, cols(i)] = t
            else:
                mine[w][gr, cols(i)] = t.astype(B)

    def gather_children(i, s, pos, children, final):
        sure = [d for d in children if d in "xy"]
        maybe = [d for d in children if d in "ud"]
        for d in sure:
            arrival(i, pos, d).wait_recv()
        for d in maybe:
            pl.when(there[d])(lambda d=d: arrival(i, pos, d).wait_recv())
        if not maybe:
            add(i, s, pos, sure, final)
        elif len(maybe) == 1:
            pl.when(there[maybe[0]])(lambda: add(i, s, pos, sure + maybe, final))
            pl.when(jnp.logical_not(there[maybe[0]]))(lambda: add(i, s, pos, sure, final))
        else:
            u, d = there["u"], there["d"]
            pl.when(u & d)(lambda: add(i, s, pos, sure + ["u", "d"], final))
            pl.when(u & jnp.logical_not(d))(lambda: add(i, s, pos, sure + ["u"], final))
            pl.when(jnp.logical_not(u) & d)(lambda: add(i, s, pos, sure + ["d"], final))
            if nz == 1:
                add(i, s, pos, sure, final)

    def each(h, i, leaf, act):
        order = pieces[i][3]
        for bx, by, sgn in slots():
            children = forwards(order, bx, by, sgn)
            if leaf is not None and (len(children) == 0) != leaf:
                continue
            k = h - bx - by
            if isinstance(h, int) and not ((k == 0) if sgn == 0 else (1 <= k < nz)):
                continue
            zs = z + sgn * k
            valid = (k == 0) if sgn == 0 else (k >= 1) & (zs >= 0) & (zs < nz)
            pos = {"x": x + bx - 2 * bx * x, "y": y + by - 2 * by * y, "z": zs}
            s = zs * 4 + pos["y"] * 2 + pos["x"]
            p = parent(order, bx, by, sgn)
            if isinstance(valid, bool):
                act(i, s, pos, children, p)
            else:
                pl.when(valid)(lambda s=s, pos=pos, children=children, p=p: act(i, s, pos, children, p))

    def work(i, s, pos, children, p):
        gather_children(i, s, pos, children, False)
        message(i, s, pos, p).start()

    def leaves(h, indices):
        for i in indices:
            each(h, i, True, work)

    def nodes(h, indices):
        for i in indices:
            each(h, i, False, work)

    def out_copy(w):
        n = outs[w].shape[1] // 2
        return pltpu.make_async_copy(res[w], outs[w].at[:, pl.ds(pl.multiple_of(c * n, 128), n)], res_sem.at[w])

    def out_sib(w, half):
        n = outs[w].shape[1] // 2
        return pltpu.make_async_remote_copy(
            src_ref=res[w], dst_ref=outs[w].at[:, pl.ds(pl.multiple_of(half * n, 128), n)], send_sem=res_send.at[w],
            recv_sem=res_recv.at[w], device_id=sib, device_id_type=MESH)

    def total(w):
        for i, piece in enumerate(pieces):
            if piece[0] == w:
                gather_children(i, f, {"x": x, "y": y, "z": z}, forwards(piece[3], 0, 0, 0), True)
        out_sib(w, c).start()
        out_copy(w).start()

    def sent(indices):
        for i in indices:
            w = pieces[i][0]
            part = mine[w].at[pl.ds(0, (4 * nz - 1) * rows[w]), cols(i)]
            pltpu.make_async_remote_copy(
                src_ref=part, dst_ref=part, send_sem=send.at[i], recv_sem=recv.at[i, 0, 0], device_id=sib,
                device_id_type=MESH).wait_send()

    def finish(ws):
        for w in ws:
            give(w).wait_send()
            out_copy(w).wait()
            out_sib(w, c).wait_send()
            out_sib(w, 1 - c).wait_recv()

    return flip, give, leaves, nodes, total, sent, finish


def encode_back_reduce_kernel(wc, wide_seen, narrow_seen, nz, routes, *refs):
    devices = 4 * nz
    dec_vec, *refs = refs
    given, refs = refs[:9], refs[9:]
    h_h, slope_h, we_h, wd_h, wu_h, wo_h, wq_h, *refs = refs
    dec_g, refs = refs[:4], refs[4:]
    (dx_ref, vec_out, *refs) = refs
    outs, refs = refs[:9], refs[9:]
    (we, wo, wq, wd2, wu2, h2, slope2, dx1_ref, z_ref, do_ref, dqkv, *refs) = refs
    tiles, dm, e_ref, b_ref, x1_ref, o_ref, qkv, a_ref, x_ref = refs[:9]
    refs = refs[9:]
    mine, refs = refs[:9], refs[9:]
    enc_other, refs = refs[:5], refs[5:]
    sibb, refs = refs[:9], refs[9:]
    res, refs = refs[:9], refs[9:]
    npc = len(routes)
    rbuf, refs = [refs[3 * i:3 * i + 3] for i in range(npc)], refs[3 * npc:]
    (vbuf, wsem, gsem, dsem, sib_send, sib_recv, send, recv, res_sem, res_send, res_recv, vsend, vrecv) = refs
    c = lax.axis_index("dp")
    held = [tiles, dm, e_ref, b_ref, x1_ref, o_ref, qkv, a_ref, x_ref]
    takes_in = [pltpu.make_async_copy(s, d, gsem.at[k]) for k, (s, d) in enumerate(zip(given, held))]
    for cp in takes_in:
        cp.start()
    D = wo.shape[0]
    n_up = mine[2].shape[1]
    rows = [m.shape[0] // devices for m in mine]

    def half(ref, h):
        n = ref.shape[1] // 2
        return ref.at[:, pl.ds(pl.multiple_of(h * n, 128), n)]

    other = list(enc_other) + [half(g, 1 - c) for g in dec_g]
    flip, give, leaves, nodes, total, sent, finish = reduce_ops(
        nz, routes, rows, mine, other, sibb, rbuf, res, outs, sib_send, sib_recv, send, recv, res_sem, res_send, res_recv)
    dec_ws = [5, 6, 7, 8]
    for w in dec_ws:
        give(w).start()
    takes = [pltpu.make_async_copy(half(dec_g[w - 5], c), mine[w], dsem.at[w - 5]) for w in dec_ws]
    for t in takes:
        t.start()
    loads = [pltpu.make_async_copy(s, d, wsem.at[k]) for k, (s, d) in enumerate(((we_h, we), (wo_h, wo), (wq_h, wq)))]
    C = 512
    chunks = 2 * n_up // C

    def chunk(j):
        h = (1 - c) if j < chunks // 2 else c
        return pl.multiple_of(h * n_up + (j % (chunks // 2)) * C, 128)

    def feed(j):
        k = chunk(j)
        return (pltpu.make_async_copy(wd_h.at[pl.ds(k, C)], wd2.at[j % 2], wsem.at[3 + j % 2]),
                pltpu.make_async_copy(wu_h.at[:, pl.ds(k, C)], wu2.at[j % 2], wsem.at[5 + j % 2]),
                pltpu.make_async_copy(h_h.at[:, pl.ds(k, C)], h2.at[j % 2], wsem.at[7 + j % 2]),
                pltpu.make_async_copy(slope_h.at[:, pl.ds(k, C)], slope2.at[j % 2], wsem.at[9 + j % 2]))

    loads[0].start()
    for j in (0, 1):
        for cp in feed(j):
            cp.start()
    loads[1].start()
    loads[2].start()
    takes_in[0].wait()
    gain1 = spread_vector(tiles[...], 0, D, devices)
    gain2 = spread_vector(tiles[...], 1, D, devices)
    def own_cols(w):
        n = mine[w].shape[1]
        return pl.ds(pl.multiple_of(c * n, 128), n), pl.ds(pl.multiple_of((1 - c) * n, 128), n)

    sets = {"5": [5], "7": [7], "8": [8], "6": [6], "d": [3], "u": [2], "e": [4], "O": [1], "Q": [0]}
    members = {s: [i for i, p in enumerate(routes) if p[0] in ws] for s, ws in sets.items()}
    kept = {}

    def first():
        for cp in takes_in[1:4]:
            cp.wait()
        loads[0].wait()
        grad = dot_nt(dm[...], we[...])
        dx1_ref[...] = grad
        z_ref[...] = grad.astype(B)
        own, rest = own_cols(4)
        enc_other[4][...] = dot_tn(e_ref[...], dm[:, rest]).astype(B)
        mine[4][...] = dot_tn(e_ref[...], dm[:, own]).astype(B)
        give(4).start()
        kept["back"] = jnp.zeros_like(grad)

    def feed_forward(j):
        own, rest = own_cols(3)
        for cp in feed(j):
            cp.wait()
        kk = pl.ds(chunk(j), C)
        d = (slope2[j % 2] * dot_nt(z_ref[...], wd2[j % 2])).astype(B)
        kept["back"] = kept["back"] + dot_nt(d, wu2[j % 2])
        hk = h2[j % 2]
        enc_other[3][kk, :] = dot_tn(hk, z_ref[:, rest]).astype(B)
        mine[3][kk, :] = dot_tn(hk, z_ref[:, own]).astype(B)
        g = dot_tn(b_ref[...], d).astype(B)
        at = (j % (chunks // 2)) * C
        if j < chunks // 2:
            enc_other[2][:, at:at + C] = g
        else:
            mine[2][:, at:at + C] = g
        if j == chunks // 2 - 1:
            give(2).start()
        if j == chunks - 1:
            give(3).start()
        if j + 2 < chunks:
            for cp in feed(j + 2):
                cp.start()

    def project():
        takes_in[4].wait()
        takes_in[5].wait()
        by_input, by_gain = norm_back(x1_ref[...], gain2, kept.pop("back"))
        vbuf[0, 0] = jnp.zeros_like(vbuf[0, 0])
        vbuf[0, 0, 1:2, :] = jnp.sum(by_gain, axis=0, keepdims=True)
        dx1_ref[...] += by_input
        z_ref[...] = dx1_ref[...].astype(B)
        loads[1].wait()
        do_ref[...] = dot_nt(z_ref[...], wo[...]).astype(B)
        own, rest = own_cols(1)
        enc_other[1][...] = dot_tn(o_ref[...], z_ref[:, rest]).astype(B)
        mine[1][...] = dot_tn(o_ref[...], z_ref[:, own]).astype(B)
        give(1).start()

    def attend(part):
        if part == 0:
            takes_in[6].wait()
        mask = pair_mask()
        groups = x_ref.shape[0] // 128
        scale = ENC_HEAD ** -0.5
        lane = iota((128, 128), 1)
        for g in range(groups):
            if g * 2 // groups != part:
                continue
            rr = slice(128 * g, 128 * g + 128)
            valid = valid_keys(0 if g < wc else 1, wide_seen, narrow_seen)
            for j in range(D // 128):
                q, k, v = (qkv[rr, o + 128 * j:o + 128 * j + 128] for o in (0, D, 2 * D))
                g_o = do_ref[rr, 128 * j:128 * j + 128]
                k2 = jnp.concatenate([k, k], axis=0) * mask
                v2 = jnp.concatenate([v, v], axis=0) * mask
                shares = pair_shares(q, k2, valid)
                dp2 = dot_nt(g_o, v2)
                ds, low = [], []
                for h in range(2):
                    dp = dp2[:, 128 * h:128 * h + 128]
                    p = shares[h]
                    ds.append((p * (dp - jnp.sum(dp * p, axis=1, keepdims=True))).astype(B))
                    low.append(p.astype(B))
                dq = dot(jnp.concatenate(ds, axis=1), k2) * scale
                dk = jnp.where(lane < ENC_HEAD, dot_tn(ds[0], q), dot_tn(ds[1], q)) * scale
                dv = jnp.where(lane < ENC_HEAD, dot_tn(low[0], g_o), dot_tn(low[1], g_o))
                for o, d in ((0, dq), (D, dk), (2 * D, dv)):
                    dqkv[rr, o + 128 * j:o + 128 * j + 128] = d.astype(B)

    def mix():
        takes_in[7].wait()
        own, rest = own_cols(0)
        enc_other[0][...] = dot_tn(a_ref[...], dqkv[:, rest]).astype(B)
        give(0).start()
        mine[0][...] = dot_tn(a_ref[...], dqkv[:, own]).astype(B)

    bits = devices.bit_length() - 1

    def vcopy(k):
        return pltpu.make_async_remote_copy(
            src_ref=vbuf.at[0, k], dst_ref=vbuf.at[1, k], send_sem=vsend.at[k], recv_sem=vrecv.at[k],
            device_id=(lax.axis_index("fsdp"), 1 - c) if k == 0 else (flip(k - 1), c), device_id_type=MESH)

    def vstep(k):
        vcopy(k).wait()
        vbuf[0, k + 1] = vbuf[0, k] + vbuf[1, k]
        if k < bits:
            vcopy(k + 1).start()

    def last():
        takes_in[8].wait()
        loads[2].wait()
        by_input, by_gain = norm_back(x_ref[...], gain1, dot_nt(dqkv[...], wq[...]))
        vbuf[0, 0, 0:1, :] = jnp.sum(by_gain, axis=0, keepdims=True)
        DD = dec_vec.shape[1]
        vbuf[0, 0, 2:3, 0:DD] = dec_vec[2:3, :]
        vbuf[0, 0, 3:5, 0:DD] = dec_vec[0:2, :]
        vcopy(0).start()
        dx_ref[...] = dx1_ref[...] + by_input

    compute = [first] + [functools.partial(feed_forward, j) for j in range(chunks)] + [project]
    compute += [functools.partial(attend, 0), functools.partial(attend, 1), mix, last]

    def ready(s):
        if s in "5678":
            for w in sets[s]:
                takes[w - 5].wait()
        for w in sets[s]:
            give(w).wait_recv()

    vectors = []
    for token in schedule(nz + 1, len(compute)):
        if token[0] == "C":
            compute[token[1]]()
            if token[1] == len(compute) - 1:
                vectors = list(range(bits + 1))
        elif token[0] == "R":
            ready(token[1])
        elif token[0] == "L":
            leaves(token[1], members[token[2]])
        elif token[0] == "N":
            nodes(token[1], members[token[2]])
        else:
            for w in sets[token[1]]:
                total(w)
        if vectors and token[0] == "N":
            vstep(vectors.pop(0))
    for k in vectors:
        vstep(k)
    vec_out[...] = vbuf[0, bits + 1]
    sent(range(npc))
    finish(range(9))


def schedule(top, steps):
    if (top, steps) == (5, 12):
        return list(SCHEDULE)
    tokens = [("C", k) for k in range(steps)] + [("R", s) for s in "5786dueOQ"]
    tokens += [("L", top, s) for s in "5786dueOQ"]
    for h in range(top, 0, -1):
        tokens += [("N", h, s) for s in "5786dueOQ"]
        tokens += [("L", h - 1, s) for s in "5786dueOQ"] if h > 1 else []
    return tokens + [("T", s) for s in "5786dueOQ"]


def encode_back_reduce(tiles, counts, dm, dec_vec, saved, enc, dec_grads, routes, nz, cid=2):
    R = dm.shape[0]
    n = 4 * nz
    bits = n.bit_length() - 1
    x, a, qkv, o, x1, b, h, slope, e = saved
    wq, wo, wu, wd, we = enc
    D = wq.shape[0]
    grads = [*enc, *dec_grads]
    shards = [(g.shape[0] // n, g.shape[1]) for g in grads]
    V = pl.BlockSpec(memory_space=pltpu.VMEM)
    A = pl.BlockSpec(memory_space=pl.ANY)
    sds = jax.ShapeDtypeStruct
    dma = pltpu.SemaphoreType.DMA
    most = 1
    rbuf = []
    for w, c0, cols, order in routes:
        for d in "xyu":
            k = slot_count(order, d, nz)
            most = max(most, k)
            rbuf.append(pltpu.VMEM((k, shards[w][0], cols), B))
    npc = len(routes)
    halves = [pltpu.VMEM((g.shape[0], g.shape[1] // 2), B) for g in grads]
    C = 512
    given = [tiles, dm, e, b, x1, o, qkv, a, x]
    out = pl.pallas_call(
        functools.partial(encode_back_reduce_kernel, *counts, nz, routes),
        out_shape=[sds((R, D), F), sds((8, D), F)] + [sds(s, F) for s in shards],
        in_specs=[V] + [A] * 20,
        out_specs=[V] * 2 + [A] * 9,
        scratch_shapes=[
            pltpu.VMEM(we.shape, B), pltpu.VMEM(wo.shape, B), pltpu.VMEM(wq.shape, B),
            pltpu.VMEM((2, C, D), B), pltpu.VMEM((2, D, C), B), pltpu.VMEM((2, R, C), B), pltpu.VMEM((2, R, C), F),
            pltpu.VMEM((R, D), F), pltpu.VMEM((R, D), B), pltpu.VMEM((R, D), B),
            pltpu.VMEM((R, 3 * D), B),
        ] + [pltpu.VMEM(g.shape, g.dtype) for g in given] + halves + halves[:5] + halves + [pltpu.VMEM((s[0], s[1] // 2), F) for s in shards] + rbuf + [
            pltpu.VMEM((2, bits + 2, 8, D), F), dma((11,)), dma((9,)), dma((4,)), dma((9,)), dma((9,)), dma((npc,)),
            dma((npc, 3, most)), dma((9,)), dma((9,)), dma((9,)), dma((bits + 1,)), dma((bits + 1,))],
        compiler_params=pltpu.CompilerParams(collective_id=cid, has_side_effects=True, vmem_limit_bytes=63 * 2**20),
        name="encoder_backward_and_reduce",
    )(dec_vec, *given, h, slope, we, wd, wu, wo, wq, *dec_grads)
    return out[0], out[1], out[2:]


ZXY = ("z", "x", "y")
ZYX = ("z", "y", "x")
XYZ = ("x", "y", "z")
YXZ = ("y", "x", "z")
XZY = ("x", "z", "y")
YZX = ("y", "z", "x")
GATHER = ((0, ZYX), (2, XZY), (3, ZYX), (1, YXZ), (4, YXZ), (5, ZXY), (7, ZXY), (8, YZX), (6, XZY))
GATHER_SCHEDULE = (
    ("S", "o"), ("S", "q"), ("S", "d"), ("P",), ("V", 1, "q"), ("S", "u"), ("V", 1, "o"), ("V", 2, "q"),
    ("S", "e"), ("V", 1, "u"), ("V", 2, "o"), ("V", 3, "q"), ("V", 1, "d"), ("V", 2, "u"), ("V", 4, "q"),
    ("V", 2, "d"), ("V", 5, "q"), ("V", 1, "e"), ("V", 3, "o"), ("S", "5"), ("V", 3, "u"), ("R", "q"), ("C", 0),
    ("V", 3, "d"), ("V", 4, "o"), ("V", 2, "e"), ("V", 1, "5"), ("C", 1), ("V", 4, "u"), ("S", "8"),
    ("V", 5, "o"), ("V", 4, "d"), ("V", 3, "e"), ("V", 2, "5"), ("R", "o"), ("S", "7"), ("C", 2), ("V", 5, "u"),
    ("V", 5, "d"), ("S", "6"), ("V", 1, "8"), ("C", 3), ("V", 3, "5"), ("V", 4, "e"), ("R", "u"), ("R", "d"),
    ("V", 1, "7"), ("V", 1, "6"), ("C", 4), ("C", 5), ("V", 4, "5"), ("V", 2, "8"), ("V", 5, "e"), ("C", 6),
    ("V", 2, "7"), ("C", 7), ("V", 2, "6"), ("V", 5, "5"), ("C", 8), ("V", 3, "8"), ("R", "e"), ("C", 9),
    ("R", "5"), ("V", 3, "7"), ("C", 10), ("V", 3, "6"), ("C", 11), ("V", 4, "8"), ("V", 4, "7"), ("V", 4, "6"),
    ("C", 12), ("V", 5, "6"), ("V", 5, "7"), ("V", 5, "8"), ("C", 13),
)
REDUCE = ((5, YZX), (7, XYZ), (8, ZXY), (6, YZX), (3, YZX), (2, ZXY), (4, ZYX), (1, ZXY), (0, ZXY))
SCHEDULE = (
    ("C", 0), ("C", 1), ("R", "5"), ("L", 5, "5"), ("L", 4, "5"), ("L", 3, "5"), ("R", "7"), ("N", 5, "7"),
    ("C", 2), ("R", "8"), ("L", 5, "8"), ("N", 5, "5"), ("L", 5, "7"), ("N", 5, "8"), ("L", 4, "8"),
    ("L", 4, "7"), ("L", 3, "8"), ("L", 2, "5"), ("R", "6"), ("R", "e"), ("L", 2, "8"), ("N", 5, "6"),
    ("N", 4, "5"), ("C", 3), ("N", 4, "7"), ("N", 4, "8"), ("L", 5, "e"), ("L", 5, "6"), ("L", 4, "e"), ("C", 4),
    ("N", 3, "5"), ("N", 5, "e"), ("L", 3, "e"), ("L", 1, "5"), ("L", 1, "8"), ("N", 3, "8"), ("C", 5), ("C", 6),
    ("N", 4, "e"), ("R", "u"), ("L", 5, "u"), ("N", 4, "6"), ("L", 2, "e"), ("N", 3, "7"), ("L", 4, "6"),
    ("L", 4, "u"), ("L", 3, "6"), ("N", 2, "8"), ("L", 3, "u"), ("N", 5, "u"), ("R", "d"), ("L", 5, "d"),
    ("L", 3, "7"), ("L", 4, "d"), ("N", 5, "d"), ("L", 3, "d"), ("N", 2, "5"), ("L", 2, "u"), ("N", 2, "7"),
    ("C", 7), ("C", 8), ("N", 4, "d"), ("N", 4, "u"), ("L", 2, "d"), ("N", 3, "e"), ("N", 1, "8"), ("R", "O"),
    ("L", 5, "O"), ("N", 5, "O"), ("L", 4, "O"), ("N", 1, "5"), ("C", 9), ("N", 3, "d"), ("L", 1, "e"),
    ("L", 3, "O"), ("N", 3, "6"), ("C", 10), ("L", 2, "7"), ("N", 3, "u"), ("L", 2, "O"), ("R", "Q"),
    ("N", 2, "e"), ("N", 4, "O"), ("L", 5, "Q"), ("N", 1, "7"), ("L", 1, "7"), ("N", 5, "Q"), ("L", 4, "Q"),
    ("N", 2, "d"), ("L", 2, "6"), ("L", 1, "6"), ("N", 4, "Q"), ("N", 2, "6"), ("N", 3, "O"), ("L", 3, "Q"),
    ("N", 2, "u"), ("T", "7"), ("N", 3, "Q"), ("N", 1, "d"), ("T", "5"), ("L", 2, "Q"), ("N", 1, "e"),
    ("L", 1, "d"), ("N", 2, "O"), ("L", 1, "u"), ("N", 2, "Q"), ("N", 1, "u"), ("N", 1, "6"), ("C", 11),
    ("L", 1, "Q"), ("N", 1, "Q"), ("T", "d"), ("T", "8"), ("L", 1, "O"), ("N", 1, "O"), ("T", "e"), ("T", "u"),
    ("T", "6"), ("T", "Q"), ("T", "O"),
)


def whole_tiles(shards, devices):
    return devices % 4 == 0 and all(s.shape[0] % 16 == 0 and s.shape[1] % 256 == 0 for s in shards)


def local(
    clips_wide, clips_narrow, visible_wide, visible_narrow, shift_wide, shift_narrow,
    enc_norm1, enc_qkv, enc_out, enc_norm2, enc_up, enc_down, embed_proj, mask_token,
    dec_norm1, dec_qkv, dec_out, dec_norm2, dec_up, dec_down, cotan_wide, cotan_narrow,
):
    devices = lax.axis_size("fsdp")
    matrices = [enc_qkv, enc_out, enc_up, enc_down, embed_proj, dec_qkv, dec_out, dec_up, dec_down]
    vectors = [enc_norm1, enc_norm2, mask_token, dec_norm1, dec_norm2]
    narrow = jnp.transpose(clips_narrow, (1, 0, 2))
    place = (shift_wide, shift_narrow, visible_wide, visible_narrow, cotan_wide, cotan_narrow)
    counts = (clips_wide.shape[0], clips_wide.shape[1], clips_narrow.shape[1])
    direct = whole_tiles(matrices, devices)
    if direct:
        pieces = [(len(matrices), 0, 128, ZXY, False)]
        pieces += [(w, 0, matrices[w].shape[1] // 2, order, True) for w, order in GATHER]
        whole, placed, saved, first = gather_encode(
            matrices, vectors, pieces, place, clips_wide, narrow, devices // 4
        )
    else:
        packed = jnp.stack([jnp.pad(v, (0, 128 - v.shape[0])) for v in vectors])
        packed = jnp.pad(packed, ((0, 16 - len(vectors)), (0, 0)))
        whole = [lax.all_gather(m, "fsdp", axis=0, tiled=True) for m in (*matrices, packed)]
        got = encoder_forward(place, whole[9], clips_wide, narrow, *whole[:6], devices)
        placed, first, saved = got[:3], got[3:8], got[9:]
    enc, dec, tiles = whole[:5], whole[5:9], whole[9]
    decoded_wide, decoded_narrow, grad_embedded, *dec_grads, gains = decoder(
        tiles, placed, first, (saved[0].shape[0], embed_proj.shape[1]), cotan_wide.shape, cotan_narrow.shape, *dec, devices
    )
    if direct:
        routes = [(w, 0, matrices[w].shape[1] // 2, order) for w, order in REDUCE]
        grad_rows, gains, shares = encode_back_reduce(
            tiles, counts, grad_embedded, gains, saved, enc, dec_grads, routes, devices // 4
        )
    else:
        grad_rows, *enc_grads, gains = encoder_backward(
            tiles, counts, grad_embedded, gains, saved, *enc, devices
        )
        gains = lax.psum(gains, ("fsdp", "dp"))
        shares = [
            lax.psum_scatter(lax.psum(g.astype(F), "dp"), "fsdp", scatter_dimension=0, tiled=True)
            for g in enc_grads + dec_grads
        ]
    encoded_wide, encoded_narrow, grad_wide, grad_narrow, m, v = results(
        lax.axis_index("fsdp"), saved[-1], grad_rows, gains, shares, [v.shape[0] for v in vectors],
        clips_wide.shape, clips_narrow.shape,
    )
    return (
        encoded_wide, encoded_narrow, decoded_wide, decoded_narrow, grad_wide, grad_narrow,
        v[0], m[0], m[1], v[1], m[2], m[3], m[4], v[2], v[3], m[5], m[6], v[4], m[7], m[8],
    )


def solution(mesh):
    clips = ("fsdp", "dp")
    matrix, vector = P("fsdp", None), P("fsdp")
    weights = (
        vector, matrix, matrix, vector, matrix, matrix, matrix, vector,
        vector, matrix, matrix, vector, matrix, matrix,
    )
    rows, pairs = P(clips, None, None), P(clips, None)
    return jax.shard_map(
        local,
        mesh=mesh,
        in_specs=(rows, rows, pairs, pairs, pairs, P(clips), *weights, rows, rows),
        out_specs=(rows,) * 6 + weights,
        check_vma=False,
    )
```
